32 devices in a mesh: dp: 8 (over y, x, core), seq: 4 (over z).
Axes of the slice: x: 2, y: 2, z: 4, core: 2. Of those that a mesh axis runs over, the one named last changes fastest.
Arguments:
- hidden_in: bfloat16 [8, 1024, 1536], P('dp', 'seq'), may hold values from -6 to 6
- out_grad: bfloat16 [8, 1024, 1536], P('dp', 'seq'), may hold values from -6 to 6
- prenorm: float32 [1536], P('dp'), may hold values from 0.5 to 1.5
- inproject: float32 [1536, 6448], P('dp'), may hold values from -0.15625 to 0.15625
- convtaps: float32 [5, 3328], P(None, 'dp'), may hold values from -0.5 to 0.5
- headcoefs: float32 [3, 48], replicated, may hold values from -12 to 3, as said below
- postnorm: float32 [3072], P('dp'), may hold values from 0.5 to 1.5
- outproject: float32 [3072, 1536], P('dp'), may hold values from -0.109375 to 0.109375
- prenorm_first: float32 [1536], P('dp'), may hold values from -56 to 56
- inproject_first: float32 [1536, 6448], P('dp'), may hold values from -56 to 56
- convtaps_first: float32 [5, 3328], P(None, 'dp'), may hold values from -56 to 56
- headcoefs_first: float32 [3, 48], replicated, may hold values from -56 to 56
- postnorm_first: float32 [3072], P('dp'), may hold values from -56 to 56
- outproject_first: float32 [3072, 1536], P('dp'), may hold values from -56 to 56
- prenorm_second: float32 [1536], P('dp'), may hold values from 16.384 to 163.84
- inproject_second: float32 [1536, 6448], P('dp'), may hold values from 16.384 to 163.84
- convtaps_second: float32 [5, 3328], P(None, 'dp'), may hold values from 16.384 to 163.84
- headcoefs_second: float32 [3, 48], replicated, may hold values from 16.384 to 163.84
- postnorm_second: float32 [3072], P('dp'), may hold values from 16.384 to 163.84
- outproject_second: float32 [3072, 1536], P('dp'), may hold values from 16.384 to 163.84
Outputs:
- output: float32 [8, 1024, 1536], P('dp', 'seq')
- input_gradient: float32 [8, 1024, 1536], P('dp', 'seq')
- prenorm_gradient: float32 [1536], P('dp')
- inproject_gradient: float32 [1536, 6448], P('dp')
- convtaps_gradient: float32 [5, 3328], P(None, 'dp')
- headcoefs_gradient: float32 [3, 48], replicated
- postnorm_gradient: float32 [3072], P('dp')
- outproject_gradient: float32 [3072, 1536], P('dp')
- prenorm_updated: float32 [1536], P('dp')
- inproject_updated: float32 [1536, 6448], P('dp')
- convtaps_updated: float32 [5, 3328], P(None, 'dp')
- headcoefs_updated: float32 [3, 48], replicated
- postnorm_updated: float32 [3072], P('dp')
- outproject_updated: float32 [3072, 1536], P('dp')
- prenorm_moment: float32 [1536], P('dp')
- inproject_moment: float32 [1536, 6448], P('dp')
- convtaps_moment: float32 [5, 3328], P(None, 'dp')
- headcoefs_moment: float32 [3, 48], replicated
- postnorm_moment: float32 [3072], P('dp')
- outproject_moment: float32 [3072, 1536], P('dp')
- prenorm_square: float32 [1536], P('dp')
- inproject_square: float32 [1536, 6448], P('dp')
- convtaps_square: float32 [5, 3328], P(None, 'dp')
- headcoefs_square: float32 [3, 48], replicated
- postnorm_square: float32 [3072], P('dp')
- outproject_square: float32 [3072, 1536], P('dp')
The draws below stay inside these ranges and needn't reach their ends.
Inputs may be any that keep to these rules, and one draw needn't show every extreme that they name: `headcoefs`: row 0 holds step biases, row 1 logarithms of decay rates, row 2 skip weights.
All inputs are finite; a program needn't handle non-finite values.
Results may differ from the reference program's by a relative error of at most 0.00155.
The reference program's roundings to bfloat16 on the way count: a program that leaves them out, or rounds other values in their place, can miss the bound.
Values may be sent and summed in bfloat16 or wider, within the bound.
A program may use at most 320 MiB of HBM per device.

```python
import math
import jax
import jax.numpy as jnp
from jax import lax

D = 1536
H = 48
N = 128
K = 4
SPAN = 256
SEQ_LEN = 1024
DI = 3072
CONV = 3328
PROJ = 6448
SEQUENCES = 8
TOKENS = 8192


def draw_headcoefs(key, part):
    step_key = jax.random.fold_in(key, 11)
    rate_key = jax.random.fold_in(key, 12)
    skip_key = jax.random.fold_in(key, 13)
    log_step = jax.random.uniform(step_key, (H,), jnp.float32, -7.0, -2.3)
    step_size = jnp.exp(log_step)
    bias_row = jnp.log(jnp.expm1(step_size))
    decay_row = jnp.log(jax.random.uniform(rate_key, (H,), jnp.float32, 1.0, 16.0))
    skip_row = jax.random.uniform(skip_key, (H,), jnp.float32, 0.5, 1.5)
    return jnp.stack([bias_row, decay_row, skip_row])


def levels(stream_key, extent, split, smallest, largest):
    level, own = 1.0, jax.random.fold_in(stream_key, 6)
    for axis_at, parts in split:
        draws = jnp.exp(jax.random.uniform(jax.random.fold_in(own, axis_at), (parts,), jnp.float32, smallest / len(split), largest / len(split)))
        level = level * jnp.repeat(draws, extent[axis_at] // parts).reshape([-1 if axis == axis_at else 1 for axis in range(len(extent))])
    return level


def scatter_about(stream_key, shape, scale, reach, cuts=(), dtype=jnp.bfloat16):
    array = scale * jax.random.normal(stream_key, shape, jnp.float32)
    if cuts:
        array = array * levels(stream_key, shape, cuts, -0.22, 0.18)
    return jnp.clip(array, -reach, reach).astype(dtype)


def setup_inputs(seed: int = 0) -> dict:
    streams_of = jax.random.split(jax.random.key(seed), 21)
    return {
        "hidden_in": scatter_about(streams_of[0], (SEQUENCES, SEQ_LEN, D), 1.0, 6.0, ((0, 8), (1, 4))),
        "out_grad": scatter_about(streams_of[1], (SEQUENCES, SEQ_LEN, D), 1.0, 6.0, ((0, 8), (1, 4))),
        "prenorm": jnp.clip(1.0 + 0.1 * jax.random.normal(streams_of[2], (D,), jnp.float32), 0.5, 1.5),
        "inproject": scatter_about(streams_of[3], (D, PROJ), D ** -0.5, 0.15625, ((0, 8),), jnp.float32),
        "convtaps": jnp.clip(jax.random.uniform(streams_of[4], (K + 1, CONV), jnp.float32, -0.5, 0.5) * levels(streams_of[4], (K + 1, CONV), ((1, 8),), -0.4, 0.0), -0.5, 0.5),
        "headcoefs": draw_headcoefs(jax.random.fold_in(streams_of[20], 71), 0),
        "postnorm": jnp.clip(1.0 + 0.1 * jax.random.normal(streams_of[6], (DI,), jnp.float32), 0.5, 1.5),
        "outproject": scatter_about(streams_of[7], (DI, D), DI ** -0.5, 0.109375, ((0, 8),), jnp.float32),
        "prenorm_first": scatter_about(streams_of[8], (D,), (0.1 * TOKENS ** 0.5), 56.0, ((0, 8),), jnp.float32),
        "inproject_first": scatter_about(streams_of[9], (D, PROJ), (0.1 * TOKENS ** 0.5), 56.0, ((0, 8),), jnp.float32),
        "convtaps_first": scatter_about(streams_of[10], (K + 1, CONV), (0.1 * TOKENS ** 0.5), 56.0, ((1, 8),), jnp.float32),
        "headcoefs_first": scatter_about(streams_of[11], (3, H), (0.1 * TOKENS ** 0.5), 56.0, (), jnp.float32),
        "postnorm_first": scatter_about(streams_of[12], (DI,), (0.1 * TOKENS ** 0.5), 56.0, ((0, 8),), jnp.float32),
        "outproject_first": scatter_about(streams_of[13], (DI, D), (0.1 * TOKENS ** 0.5), 56.0, ((0, 8),), jnp.float32),
        "prenorm_second": jnp.clip(jnp.exp(math.log(163.84) - 2.30258502 * jax.random.uniform(streams_of[14], (D,), jnp.float32) ** levels(streams_of[14], (D,), ((0, 8),), -0.2, 0.2)), 16.384, 163.84),
        "inproject_second": jnp.clip(jnp.exp(math.log(163.84) - 2.30258502 * jax.random.uniform(streams_of[15], (D, PROJ), jnp.float32) ** levels(streams_of[15], (D, PROJ), ((0, 8),), -0.2, 0.2)), 16.384, 163.84),
        "convtaps_second": jnp.clip(jnp.exp(math.log(163.84) - 2.30258502 * jax.random.uniform(streams_of[16], (K + 1, CONV), jnp.float32) ** levels(streams_of[16], (K + 1, CONV), ((1, 8),), -0.2, 0.2)), 16.384, 163.84),
        "headcoefs_second": jnp.clip(jnp.exp(jax.random.uniform(streams_of[17], (3, H), jnp.float32, math.log(16.384), math.log(163.84))), 16.384, 163.84),
        "postnorm_second": jnp.clip(jnp.exp(math.log(163.84) - 2.30258502 * jax.random.uniform(streams_of[18], (DI,), jnp.float32) ** levels(streams_of[18], (DI,), ((0, 8),), -0.2, 0.2)), 16.384, 163.84),
        "outproject_second": jnp.clip(jnp.exp(math.log(163.84) - 2.30258502 * jax.random.uniform(streams_of[19], (DI, D), jnp.float32) ** levels(streams_of[19], (DI, D), ((0, 8),), -0.2, 0.2)), 16.384, 163.84),
    }


@jax.custom_vjp
def low(v):
    return lax.optimization_barrier(v.astype(jnp.bfloat16)).astype(jnp.float32)

@jax.custom_vjp
def low_back(v):
    return v

def low_keep(v):
    return (low(v), None)

def low_pass(kept, grad):
    return (grad,)

def back_keep(v):
    return (v, None)

def back_low(kept, grad):
    return (low(grad),)
low.defvjp(low_keep, low_pass)
low_back.defvjp(back_keep, back_low)
norm_eps = 1e-05
highest = lax.Precision.HIGHEST
beta_moment = 0.9
beta_square = 0.95
adam_eps = 1e-08
adam_step = 3.0
rate_matrix = 0.005
rate_vector = 0.05
weight_decay = 0.1

def causal_conv(signal, conv_taps):
    tap_count = conv_taps.shape[0] - 1
    length = signal.shape[0]
    padded = jnp.pad(signal, ((tap_count - 1, 0), (0, 0)))
    summed = jnp.broadcast_to(conv_taps[tap_count][None, :], signal.shape)
    for offset in range(tap_count):
        summed = summed + conv_taps[offset][None, :] * padded[offset:offset + length]
    return jax.nn.silu(summed)

def mix_heads(inner_seq, shared_seq, rate_seq, inner_taps, shared_taps, head_rows):
    length = inner_seq.shape[0]
    head_count = rate_seq.shape[1]
    head_width = inner_seq.shape[1] // head_count
    state_count = shared_seq.shape[1] // 2
    blocks = length // SPAN
    conv_inner = causal_conv(inner_seq, inner_taps)
    conv_shared = causal_conv(shared_seq, shared_taps)
    step_size = jax.nn.softplus(rate_seq + head_rows[0][None, :])
    log_decay = -step_size * jnp.exp(head_rows[1])[None, :]
    values = conv_inner.reshape(blocks, SPAN, head_count, head_width)
    writes = conv_shared[:, :state_count].reshape(blocks, SPAN, state_count)
    readouts = conv_shared[:, state_count:].reshape(blocks, SPAN, state_count)
    cumulative = jnp.cumsum(log_decay.reshape(blocks, SPAN, head_count), axis=1)
    scaled = values * step_size.reshape(blocks, SPAN, head_count)[:, :, :, None]
    pair_scores = jnp.einsum('bln,bsn->bls', readouts, writes, precision=highest)
    position = jnp.arange(SPAN)
    causal = position[:, None] >= position[None, :]
    spread = cumulative[:, :, None, :] - cumulative[:, None, :, :]
    kernel = jnp.exp(jnp.where(causal[None, :, :, None], spread, -1e+30)) * pair_scores[:, :, :, None]
    within = jnp.einsum('blsh,bshp->blhp', kernel, scaled, precision=highest)
    to_end = jnp.exp(cumulative[:, -1:, :] - cumulative)
    block_states = jnp.einsum('bsn,bsh,bshp->bhnp', writes, to_end, scaled, precision=highest)
    block_decay = jnp.exp(cumulative[:, -1, :])

    def advance(carried, pieces):
        decay_now, fresh_state = pieces
        return (carried * decay_now[:, None, None] + fresh_state, carried)
    initial = jnp.zeros((head_count, state_count, head_width), jnp.float32)
    final_state, entering = lax.scan(advance, initial, (block_decay, block_states))
    across = jnp.einsum('bln,blh,bhnp->blhp', readouts, jnp.exp(cumulative), entering, precision=highest)
    result = within + across + head_rows[2][None, None, :, None] * values
    return result.reshape(length, head_count * head_width)

def rms_scale(values, scales):
    return values * lax.rsqrt(lax.optimization_barrier(jnp.mean(values * values, axis=-1, keepdims=True)) + norm_eps) * scales

def gated_norm(mixer_out, gate_values, scales):
    return rms_scale(mixer_out * jax.nn.silu(gate_values), scales)

def adam_update(weight, moment, square, gradient, step_rate, decay_rate):
    moment_new = beta_moment * moment + (1.0 - beta_moment) * gradient
    square_new = beta_square * square + (1.0 - beta_square) * gradient * gradient
    moment_hat = moment_new / (1.0 - beta_moment ** adam_step)
    square_hat = square_new / (1.0 - beta_square ** adam_step)
    updated = weight - step_rate * (moment_hat / (jnp.sqrt(square_hat) + adam_eps) + decay_rate * weight)
    return (updated, moment_new, square_new)

def layer_forward(params, sequence):
    pre_scale, in_matrix, conv_taps, head_rows, post_scale, out_matrix = params
    pre_scale = low(pre_scale)
    in_matrix = low(in_matrix)
    conv_taps = low(conv_taps)
    post_scale = low(post_scale)
    out_matrix = low(out_matrix)
    normed = low(rms_scale(sequence, pre_scale))
    project = low_back(jnp.dot(normed, in_matrix, precision=highest, preferred_element_type=jnp.float32))
    gate_values = project[:, :DI]
    inner_part = low(project[:, DI:2 * DI])
    shared_part = low(project[:, 2 * DI:2 * DI + 2 * N])
    rate_part = low(project[:, 2 * DI + 2 * N:])
    mixer_out = mix_heads(inner_part, shared_part, rate_part, conv_taps[:, :DI], conv_taps[:, DI:], head_rows)
    mixer_out = low(low_back(mixer_out))
    gated = low(gated_norm(mixer_out, gate_values, post_scale))
    return sequence + jnp.dot(gated, out_matrix, precision=highest, preferred_element_type=jnp.float32)

def reference(hidden_in, out_grad, prenorm, inproject, convtaps, headcoefs, postnorm, outproject, prenorm_first, inproject_first, convtaps_first, headcoefs_first, postnorm_first, outproject_first, prenorm_second, inproject_second, convtaps_second, headcoefs_second, postnorm_second, outproject_second):
    params = (prenorm, inproject, convtaps, headcoefs, postnorm, outproject)
    hidden = hidden_in.astype(jnp.float32)
    cotangent = out_grad.astype(jnp.float32)
    zero_grads = jax.tree.map(jnp.zeros_like, params)

    def per_sequence(totals, pieces):
        sequence, seq_cot = pieces
        output, pullback = jax.vjp(layer_forward, params, sequence)
        param_grads, input_grad = pullback(seq_cot)
        totals = jax.tree.map(jnp.add, totals, param_grads)
        return (totals, (output, input_grad))
    gradients, (outputs, input_grads) = lax.scan(per_sequence, zero_grads, (hidden, cotangent))
    prenorm_grad, inproj_grad, conv_grad, head_grad, postnorm_grad, outproj_grad = gradients
    prenorm_new, prenorm_mom, prenorm_sq = adam_update(prenorm, prenorm_first, prenorm_second, prenorm_grad, rate_vector, 0.0)
    inproj_new, inproj_mom, inproj_sq = adam_update(inproject, inproject_first, inproject_second, inproj_grad, rate_matrix, weight_decay)
    conv_new, conv_mom, conv_sq = adam_update(convtaps, convtaps_first, convtaps_second, conv_grad, rate_vector, 0.0)
    head_new, head_mom, head_sq = adam_update(headcoefs, headcoefs_first, headcoefs_second, head_grad, rate_vector, 0.0)
    postnorm_new, postnorm_mom, postnorm_sq = adam_update(postnorm, postnorm_first, postnorm_second, postnorm_grad, rate_vector, 0.0)
    outproj_new, outproj_mom, outproj_sq = adam_update(outproject, outproject_first, outproject_second, outproj_grad, rate_matrix, weight_decay)
    return (outputs, input_grads, prenorm_grad, inproj_grad, conv_grad, head_grad, postnorm_grad, outproj_grad, prenorm_new, inproj_new, conv_new, head_new, postnorm_new, outproj_new, prenorm_mom, inproj_mom, conv_mom, head_mom, postnorm_mom, outproj_mom, prenorm_sq, inproj_sq, conv_sq, head_sq, postnorm_sq, outproj_sq)
```

```python
import functools

import jax
import jax.numpy as jnp
from jax import lax
from jax.experimental import pallas as pl
from jax.experimental.pallas import tpu as pltpu
from jax.sharding import PartitionSpec as P

N = 128
LANES = 128
HALO = 16

norm_eps = 1e-05
beta_moment = 0.9
beta_square = 0.95
adam_eps = 1e-08
adam_step = 3.0
rate_matrix = 0.005
rate_vector = 0.05
weight_decay = 0.1

f32 = jnp.float32
bf16 = jnp.bfloat16
MESH = pl.DeviceIdType.MESH


def adam_update(weight, moment, square, gradient, step_rate, decay_rate):
    moment_new = beta_moment * moment + (1.0 - beta_moment) * gradient
    square_new = beta_square * square + (1.0 - beta_square) * gradient * gradient
    moment_hat = moment_new / (1.0 - beta_moment**adam_step)
    square_hat = square_new / (1.0 - beta_square**adam_step)
    updated = weight - step_rate * (
        moment_hat / (jnp.sqrt(square_hat) + adam_eps) + decay_rate * weight
    )
    return (updated, moment_new, square_new)


def mm(a, b, ca, cb):
    return lax.dot_general(a, b, (((ca,), (cb,)), ((), ())), preferred_element_type=f32)


def halves(a):
    hi = a.astype(bf16)
    return hi, (a - hi.astype(f32)).astype(bf16)


def thirds(a):
    hi = a.astype(bf16)
    rest = a - hi.astype(f32)
    mid = rest.astype(bf16)
    return hi, mid, (rest - mid.astype(f32)).astype(bf16)


def mm3(a, b, ca, cb):
    return mm(a[0], b[0], ca, cb) + mm(a[0], b[1], ca, cb) + mm(a[1], b[0], ca, cb)


def iota(shape, dim):
    return lax.broadcasted_iota(jnp.int32, shape, dim)


def head_lanes(tile, heads_a_tile, copies):
    rows = iota((copies * LANES, LANES), 0)
    lane_head = tile * heads_a_tile + iota((copies * LANES, LANES), 1) // (LANES // heads_a_tile)
    return (rows % LANES == lane_head).astype(f32).astype(bf16)


def conv_tile(conv_ref, halo_ref, u_ref, taps_ref, start, rows):
    cols = pl.ds(start, LANES)
    conv_ref[0:HALO, :] = halo_ref[:, cols].astype(f32)
    conv_ref[HALO : HALO + rows, :] = u_ref[:, cols].astype(f32)
    taps = taps_ref[:, cols]
    pre = taps[4:5, :] + taps[0:1, :] * conv_ref[HALO - 3 : HALO - 3 + rows, :]
    for k in range(1, 4):
        pre = pre + taps[k : k + 1, :] * conv_ref[HALO - 3 + k : HALO - 3 + k + rows, :]
    return pre, jax.nn.sigmoid(pre)


def seq_copy(src, dst, send, recv, to):
    return pltpu.make_async_remote_copy(
        src_ref=src,
        dst_ref=dst,
        send_sem=send,
        recv_sem=recv,
        device_id={"seq": to},
        device_id_type=MESH,
    )


def greet_seq(barrier, rank, last):
    @pl.when(rank > 0)
    def _():
        pl.semaphore_signal(barrier, inc=1, device_id={"seq": rank - 1}, device_id_type=MESH)

    @pl.when(rank < last)
    def _():
        pl.semaphore_signal(barrier, inc=1, device_id={"seq": rank + 1}, device_id_type=MESH)


def seq_neighbours(rank, last):
    return jnp.minimum(rank, 1) + jnp.minimum(last - rank, 1)


def forward_kernel(
    sizes,
    u_ref,
    rate_ref,
    heads_ref,
    skip_ref,
    taps_ref,
    mixer_ref,
    ypre_ref,
    enter_ref,
    halo_ref,
    step_ref,
    cum_ref,
    cumt_ref,
    conv_ref,
    score_ref,
    leave_ref,
    send_sem,
    recv_sem,
    halo_sem,
):
    rows, inner, tiles, per_tile = sizes
    conv_width = inner + 2 * N
    rank = lax.axis_index("seq")
    last = lax.axis_size("seq") - 1
    barrier = pltpu.get_barrier_semaphore()
    greet_seq(barrier, rank, last)
    pl.semaphore_wait(barrier, seq_neighbours(rank, last))
    right = jnp.minimum(rank + 1, last)
    halo_copy = seq_copy(
        u_ref.at[pl.ds(rows - HALO, HALO), pl.ds(0, conv_width)],
        halo_ref,
        halo_sem.at[0],
        halo_sem.at[1],
        right,
    )

    @pl.when(rank < last)
    def _():
        halo_copy.start()

    step = jax.nn.softplus(rate_ref[...] + heads_ref[0:1, :])
    decay = -step * jnp.exp(heads_ref[1:2, :])
    lower = (iota((rows, rows), 0) >= iota((rows, rows), 1)).astype(f32).astype(bf16)
    cum = sum(mm(lower, part, 1, 0) for part in thirds(decay))
    step_ref[...] = step
    cum_ref[...] = cum
    cumt_ref[...] = cum.T

    @pl.when(rank > 0)
    def _():
        halo_copy.wait_recv()

    @pl.when(rank == 0)
    def _():
        halo_ref[...] = jnp.zeros_like(halo_ref)

    pre_b, sig_b = conv_tile(conv_ref, halo_ref, u_ref, taps_ref, inner, rows)
    b_parts = halves(pre_b * sig_b)
    pre_c, sig_c = conv_tile(conv_ref, halo_ref, u_ref, taps_ref, inner + N, rows)
    c_parts = halves(pre_c * sig_c)
    scores = mm3(c_parts, b_parts, 1, 1)
    causal = iota((rows, rows), 0) >= iota((rows, rows), 1)
    score_ref[...] = jnp.where(causal, scores, 0.0)
    cum_parts = jnp.concatenate(thirds(cum), axis=1)
    step_parts = jnp.concatenate(thirds(step), axis=1)
    lane = iota((rows, LANES), 1)
    width = LANES // per_tile

    def chain(tile):
        return seq_copy(
            leave_ref.at[tile], enter_ref.at[tile], send_sem.at[tile], recv_sem.at[tile], right
        )

    def one(tile, carry):
        start = pl.multiple_of(tile * LANES, LANES)
        cols = pl.ds(start, LANES)
        pick = head_lanes(tile, per_tile, 3)
        cum_l = mm(cum_parts, pick, 1, 0)
        step_l = mm(step_parts, pick, 1, 0)
        pre, sig = conv_tile(conv_ref, halo_ref, u_ref, taps_ref, start, rows)
        values = pre * sig
        x = values * step_l
        total = cum_l[rows - 1 : rows, :]
        fresh = mm3(b_parts, halves(x * jnp.exp(total - cum_l)), 0, 0)

        @pl.when(rank > 0)
        def _():
            chain(tile).wait_recv()

        @pl.when(rank == 0)
        def _():
            enter_ref[tile] = jnp.zeros((N, LANES), f32)

        enter = enter_ref[tile]
        leave_ref[tile] = jnp.exp(total) * enter + fresh

        @pl.when(rank < last)
        def _():
            chain(tile).start()

        result = mm3(c_parts, halves(enter), 1, 0) * jnp.exp(cum_l)
        for h in range(per_tile):
            row = cumt_ref[pl.ds(tile * per_tile + h, 1), :]
            col = cum_l[:, h * width : h * width + 1]
            kernel = jnp.exp(jnp.minimum(col - row, 0.0)) * score_ref[...]
            own = (lane // width) == h
            result = result + mm3(halves(kernel), halves(jnp.where(own, x, 0.0)), 1, 0)
        ypre_ref[:, cols] = result
        mixer_ref[:, cols] = (result + skip_ref[0:1, cols] * values).astype(bf16)
        return carry

    lax.fori_loop(0, tiles, one, 0)

    @pl.when(rank < last)
    def _():
        halo_copy.wait_send()

        def drain(tile, carry):
            chain(tile).wait_send()
            return carry

        lax.fori_loop(0, tiles, drain, 0)


def backward_kernel(
    sizes,
    u_ref,
    halo_ref,
    rate_ref,
    step_ref,
    cum_ref,
    cumt_ref,
    heads_ref,
    skip_ref,
    taps_ref,
    dy_ref,
    ypre_ref,
    enter_ref,
    turn_ref,
    dproj_ref,
    conv_grad_ref,
    head_grad_ref,
    turned_ref,
    conv_ref,
    score_ref,
    dscore_ref,
    dread_ref,
    dwrite_ref,
    dcum_ref,
    dstep_ref,
    dpre_ref,
    leave_ref,
    arrive_ref,
    send_sem,
    recv_sem,
    halo_sem,
    turn_send,
    turn_recv,
    own_sem,
):
    rows, inner, tiles, per_tile = sizes
    conv_width = inner + 2 * N
    rank = lax.axis_index("seq")
    last = lax.axis_size("seq") - 1
    me = lax.axis_index("dp")
    group = lax.axis_size("dp")
    barrier = pltpu.get_barrier_semaphore()
    greet_seq(barrier, rank, last)
    for i in range(1, group):
        pl.semaphore_signal(
            barrier, inc=1, device_id={"dp": lax.rem(me + i, group)}, device_id_type=MESH
        )
    pl.semaphore_wait(barrier, seq_neighbours(rank, last) + group - 1)

    def turn(i):
        peer = lax.rem(me + i, group)
        return pltpu.make_async_remote_copy(
            src_ref=turn_ref.at[peer],
            dst_ref=turned_ref.at[:, pl.ds(pl.multiple_of(me * rows, rows), rows)],
            send_sem=turn_send.at[i],
            recv_sem=turn_recv.at[i],
            device_id={"dp": peer},
            device_id_type=MESH,
        )

    for i in range(1, group):
        turn(i).start()
    own_copy = pltpu.make_async_copy(
        turn_ref.at[me],
        turned_ref.at[:, pl.ds(pl.multiple_of(me * rows, rows), rows)],
        own_sem,
    )
    own_copy.start()

    left = jnp.maximum(rank - 1, 0)
    cum = cum_ref[...]
    step = step_ref[...]
    pre_b, sig_b = conv_tile(conv_ref, halo_ref, u_ref, taps_ref, inner, rows)
    b_parts = halves(pre_b * sig_b)
    pre_c, sig_c = conv_tile(conv_ref, halo_ref, u_ref, taps_ref, inner + N, rows)
    c_parts = halves(pre_c * sig_c)
    later = iota((rows, rows), 1) >= iota((rows, rows), 0)
    score_ref[...] = jnp.where(later, mm3(b_parts, c_parts, 1, 1), 0.0)
    dscore_ref[...] = jnp.zeros_like(dscore_ref)
    dread_ref[...] = jnp.zeros_like(dread_ref)
    dwrite_ref[...] = jnp.zeros_like(dwrite_ref)
    dcum_ref[...] = jnp.zeros_like(dcum_ref)
    dstep_ref[...] = jnp.zeros_like(dstep_ref)
    cum_parts = jnp.concatenate(thirds(cum), axis=1)
    step_parts = jnp.concatenate(thirds(step), axis=1)
    lane = iota((rows, LANES), 1)
    final_row = iota((rows, LANES), 0) == rows - 1
    width = LANES // per_tile

    def chain(tile):
        return seq_copy(
            leave_ref.at[tile], arrive_ref.at[tile], send_sem.at[tile], recv_sem.at[tile], left
        )

    def tap_grads(dpre, extra):
        sums = [
            jnp.sum(
                dpre * conv_ref[HALO - 3 + k : HALO - 3 + k + rows, :], axis=0, keepdims=True
            )
            for k in range(4)
        ]
        sums.append(jnp.sum(dpre, axis=0, keepdims=True))
        sums.append(extra)
        sums.append(jnp.zeros((2, LANES), f32))
        return jnp.concatenate(sums, axis=0)

    def one(tile, carry):
        start = pl.multiple_of(tile * LANES, LANES)
        cols = pl.ds(start, LANES)
        pick = head_lanes(tile, per_tile, 3)
        cum_l = mm(cum_parts, pick, 1, 0)
        step_l = mm(step_parts, pick, 1, 0)
        total = cum_l[rows - 1 : rows, :]
        dy = dy_ref[:, cols].astype(f32)
        reads = halves(dy * jnp.exp(cum_l))
        denter = mm3(c_parts, reads, 0, 0)

        @pl.when(rank < last)
        def _():
            chain(tile).wait_recv()

        @pl.when(rank == last)
        def _():
            arrive_ref[tile] = jnp.zeros((N, LANES), f32)

        arrive = arrive_ref[tile]
        leave_ref[tile] = jnp.exp(total) * arrive + denter

        @pl.when(rank > 0)
        def _():
            chain(tile).start()

        pre, sig = conv_tile(conv_ref, halo_ref, u_ref, taps_ref, start, rows)
        values = pre * sig
        x = values * step_l
        x_parts = halves(x)
        tail = jnp.exp(total - cum_l)
        enter = enter_ref[tile]
        arrive_parts = halves(arrive)
        dx_state = mm3(b_parts, arrive_parts, 1, 0) * tail
        dx = dx_state
        for h in range(per_tile):
            row = cumt_ref[pl.ds(tile * per_tile + h, 1), :]
            col = cum_l[:, h * width : h * width + 1]
            spread = jnp.exp(jnp.minimum(row - col, 0.0))
            kernel = halves(spread * score_ref[...])
            own = jnp.where((lane // width) == h, dy, 0.0).astype(bf16)
            dx = dx + (mm(kernel[0], own, 1, 0) + mm(kernel[1], own, 1, 0))
            pairs = mm(x_parts[0], own, 1, 1) + mm(x_parts[1], own, 1, 1)
            dscore_ref[...] += spread * pairs
        dread_ref[...] += mm3(reads, halves(enter), 1, 1)
        dwrite_ref[...] += mm3(halves(x * tail), arrive_parts, 1, 1)
        ends = jnp.sum(x * dx_state, axis=0, keepdims=True) + jnp.exp(total) * jnp.sum(
            enter * arrive, axis=0, keepdims=True
        )
        dcum = dy * ypre_ref[:, cols] - x * dx + jnp.where(final_row, ends, 0.0)
        own_head = pick[0:LANES, :]
        for part in halves(dcum):
            dcum_ref[...] += mm(part, own_head, 1, 1)
        for part in halves(dx * values):
            dstep_ref[...] += mm(part, own_head, 1, 1)
        dvalues = step_l * dx + skip_ref[0:1, cols] * dy
        dpre = dvalues * sig * (1.0 + pre * (1.0 - sig))
        dpre_ref[0:rows, cols] = dpre
        conv_grad_ref[:, cols] = tap_grads(dpre, jnp.sum(dy * values, axis=0, keepdims=True))
        return carry

    lax.fori_loop(0, tiles, one, 0)

    dscore = halves(jnp.where(later, dscore_ref[...], 0.0))
    dshared = (
        dwrite_ref[...] + mm3(dscore, c_parts, 1, 0),
        dread_ref[...] + mm3(dscore, b_parts, 0, 0),
    )
    for i in range(2):
        start = inner + i * N
        pre, sig = conv_tile(conv_ref, halo_ref, u_ref, taps_ref, start, rows)
        dpre = dshared[i] * sig * (1.0 + pre * (1.0 - sig))
        dpre_ref[0:rows, start : start + N] = dpre
        conv_grad_ref[:, start : start + N] = tap_grads(dpre, jnp.zeros((1, LANES), f32))

    edge = seq_copy(
        dpre_ref.at[pl.ds(0, 8), :],
        dpre_ref.at[pl.ds(rows, 8), :],
        halo_sem.at[0],
        halo_sem.at[1],
        left,
    )

    @pl.when(rank > 0)
    def _():
        edge.start()

    upper = (iota((rows, rows), 1) >= iota((rows, rows), 0)).astype(f32).astype(bf16)
    ddecay = sum(mm(upper, part, 1, 0) for part in thirds(dcum_ref[...]))
    exp_rate = jnp.exp(heads_ref[1:2, :])
    drate = (dstep_ref[...] - ddecay * exp_rate) * jax.nn.sigmoid(rate_ref[...] + heads_ref[0:1, :])
    head_grad_ref[...] = jnp.concatenate(
        [
            jnp.sum(drate, axis=0, keepdims=True),
            jnp.sum(ddecay * (-step * exp_rate), axis=0, keepdims=True),
            jnp.zeros((6, LANES), f32),
        ],
        axis=0,
    )
    heads = tiles * per_tile
    dproj_ref[:, conv_width : conv_width + heads] = drate[:, 0:heads].astype(bf16)

    @pl.when(rank == last)
    def _():
        dpre_ref[rows : rows + 8, :] = jnp.zeros((8, conv_width), f32)

    @pl.when(rank < last)
    def _():
        edge.wait_recv()

    def unconv(tile, carry):
        cols = pl.ds(pl.multiple_of(tile * LANES, LANES), LANES)
        taps = taps_ref[:, cols]
        du = taps[3:4, :] * dpre_ref[0:rows, cols]
        for k in range(3):
            du = du + taps[k : k + 1, :] * dpre_ref[3 - k : 3 - k + rows, cols]
        dproj_ref[:, cols] = du.astype(bf16)
        return carry

    lax.fori_loop(0, conv_width // LANES, unconv, 0)

    @pl.when(rank > 0)
    def _():
        edge.wait_send()

        def drain(tile, carry):
            chain(tile).wait_send()
            return carry

        lax.fori_loop(0, tiles, drain, 0)

    own_copy.wait()
    for i in range(1, group):
        turn(i).wait_send()
        origin = lax.rem(me + group - i, group)
        pltpu.make_async_remote_copy(
            src_ref=turn_ref.at[origin],
            dst_ref=turned_ref.at[:, pl.ds(pl.multiple_of(origin * rows, rows), rows)],
            send_sem=turn_send.at[i],
            recv_sem=turn_recv.at[i],
            device_id={"dp": origin},
            device_id_type=MESH,
        ).wait_recv()


def vmem(count):
    return [pl.BlockSpec(memory_space=pltpu.VMEM)] * count


def scan_forward(u, rate, heads, skip, taps, sizes):
    rows, inner, tiles, _ = sizes
    conv_width = inner + 2 * N
    shape = jax.ShapeDtypeStruct
    return pl.pallas_call(
        functools.partial(forward_kernel, sizes),
        out_shape=(
            shape((rows, inner), bf16),
            shape((rows, inner), f32),
            shape((tiles, N, LANES), f32),
            shape((HALO, conv_width), bf16),
            shape((rows, LANES), f32),
            shape((rows, LANES), f32),
            shape((LANES, rows), f32),
        ),
        in_specs=vmem(5),
        out_specs=tuple(vmem(7)),
        scratch_shapes=[
            pltpu.VMEM((HALO + rows, LANES), f32),
            pltpu.VMEM((rows, rows), f32),
            pltpu.VMEM((tiles, N, LANES), f32),
            pltpu.SemaphoreType.DMA((tiles,)),
            pltpu.SemaphoreType.DMA((tiles,)),
            pltpu.SemaphoreType.DMA((2,)),
        ],
        compiler_params=pltpu.CompilerParams(
            collective_id=1, has_side_effects=True, vmem_limit_bytes=40 * 2**20
        ),
        cost_estimate=pl.CostEstimate(flops=4 * 10**9, bytes_accessed=10**7, transcendentals=4 * 10**6),
    )(u, rate, heads, skip, taps)


def scan_backward(u, halo, rate, step, cum, cumt, heads, skip, taps, dy, ypre, enter, turn, sizes):
    rows, inner, tiles, _ = sizes
    conv_width = inner + 2 * N
    shape = jax.ShapeDtypeStruct
    group, turn_rows, _ = turn.shape
    return pl.pallas_call(
        functools.partial(backward_kernel, sizes),
        out_shape=(
            shape(u.shape, bf16),
            shape((8, conv_width), f32),
            shape((8, LANES), f32),
            shape((turn_rows, group * rows), bf16),
        ),
        in_specs=vmem(12) + [pl.BlockSpec(memory_space=pl.ANY)],
        out_specs=tuple(vmem(3) + [pl.BlockSpec(memory_space=pl.ANY)]),
        scratch_shapes=[
            pltpu.VMEM((HALO + rows, LANES), f32),
            pltpu.VMEM((rows, rows), f32),
            pltpu.VMEM((rows, rows), f32),
            pltpu.VMEM((rows, N), f32),
            pltpu.VMEM((rows, N), f32),
            pltpu.VMEM((rows, LANES), f32),
            pltpu.VMEM((rows, LANES), f32),
            pltpu.VMEM((rows + 8, conv_width), f32),
            pltpu.VMEM((tiles, N, LANES), f32),
            pltpu.VMEM((tiles, N, LANES), f32),
            pltpu.SemaphoreType.DMA((tiles,)),
            pltpu.SemaphoreType.DMA((tiles,)),
            pltpu.SemaphoreType.DMA((2,)),
            pltpu.SemaphoreType.DMA((group,)),
            pltpu.SemaphoreType.DMA((group,)),
            pltpu.SemaphoreType.DMA,
        ],
        compiler_params=pltpu.CompilerParams(
            collective_id=2, has_side_effects=True, vmem_limit_bytes=40 * 2**20
        ),
        cost_estimate=pl.CostEstimate(flops=6 * 10**9, bytes_accessed=2 * 10**7, transcendentals=4 * 10**6),
    )(u, halo, rate, step, cum, cumt, heads, skip, taps, dy, ypre, enter, turn)


def on_device(
    hidden_in,
    out_grad,
    prenorm,
    inproject,
    convtaps,
    headcoefs,
    postnorm,
    outproject,
    prenorm_first,
    inproject_first,
    convtaps_first,
    headcoefs_first,
    postnorm_first,
    outproject_first,
    prenorm_second,
    inproject_second,
    convtaps_second,
    headcoefs_second,
    postnorm_second,
    outproject_second,
):
    group = lax.axis_size("dp")
    me = lax.axis_index("dp")
    seq_here, rows, model_width = hidden_in.shape
    assert seq_here == 1
    heads = headcoefs.shape[1]
    own_in, proj_width = inproject.shape
    own_out = outproject.shape[0]
    inner = own_out * group
    width = inner // heads
    per_tile = LANES // width
    tiles = inner // LANES
    sizes = (rows, inner, tiles, per_tile)
    conv_own = convtaps.shape[1]
    conv_width = conv_own * group

    in_low = inproject.astype(bf16)
    scan_matrix = lax.all_gather(in_low[:, inner:], "dp", axis=0, tiled=True)
    small = jnp.concatenate([prenorm, postnorm, convtaps.reshape(-1)]).astype(bf16)
    small = lax.all_gather(small, "dp", axis=0).astype(f32)
    pre_scale = small[:, :own_in].reshape(-1)
    post_scale = small[:, own_in : own_in + own_out].reshape(-1)
    taps = small[:, own_in + own_out :].reshape(group, -1, conv_own)
    taps = jnp.swapaxes(taps, 0, 1).reshape(-1, conv_width)
    tap_rows = taps.shape[0]
    gate_matrix = lax.all_gather(in_low[:, :inner], "dp", axis=0, tiled=True)
    out_matrix = lax.all_gather(outproject.astype(bf16), "dp", axis=0, tiled=True)

    hidden = hidden_in.reshape(rows, model_width).astype(f32)
    cot_low = out_grad.reshape(rows, model_width)
    cot_all = lax.all_gather(cot_low, "dp", axis=0, tiled=True)
    root = lax.rsqrt(jnp.mean(hidden * hidden, axis=-1, keepdims=True) + norm_eps)
    normed_low = (hidden * root * pre_scale).astype(bf16)

    scan_in = jnp.dot(normed_low, scan_matrix, preferred_element_type=f32).astype(bf16)
    pad_heads = ((0, 0), (0, LANES - heads))
    rate = jnp.pad(scan_in[:, conv_width:].astype(f32), pad_heads)
    head_rows = jnp.pad(headcoefs, ((0, 8 - headcoefs.shape[0]), (0, LANES - heads)))
    skip = jnp.repeat(headcoefs[2:3], width, axis=1)
    taps_pad = jnp.pad(taps, ((0, 8 - tap_rows), (0, 0)))
    mixer_low, ypre, enter, halo, step, cum, cumt = scan_forward(
        scan_in, rate, head_rows, skip, taps_pad, sizes
    )

    gate = jnp.dot(normed_low, gate_matrix, preferred_element_type=f32)
    mixer = mixer_low.astype(f32)
    gate_sig = jax.nn.sigmoid(gate)
    gate_act = gate * gate_sig
    gated = mixer * gate_act
    post_root = lax.rsqrt(jnp.mean(gated * gated, axis=-1, keepdims=True) + norm_eps)
    whitened = gated * post_root
    post_low = (whitened * post_scale).astype(bf16)
    output = hidden + jnp.dot(post_low, out_matrix, preferred_element_type=f32)

    post_grad = mm(cot_low, out_matrix, 1, 1)
    postnorm_grad = jnp.sum(post_grad * whitened, axis=0)
    dwhite = post_grad * post_scale
    dgated = post_root * (dwhite - whitened * jnp.mean(dwhite * whitened, axis=-1, keepdims=True))
    dy = (dgated * gate_act).astype(bf16)
    gate_grad = (dgated * mixer * gate_sig * (1.0 + gate * (1.0 - gate_sig))).astype(bf16)

    turn = jnp.concatenate(
        [
            normed_low.T.reshape(group, own_in, rows),
            post_low.T.reshape(group, own_out, rows),
        ],
        axis=1,
    )
    scan_grad, conv_grad, head_grad, turned = scan_backward(
        scan_in, halo, rate, step, cum, cumt, head_rows, skip, taps_pad, dy, ypre, enter, turn, sizes
    )
    gate_all = lax.all_gather(gate_grad, "dp", axis=0, tiled=True)
    scan_all = lax.all_gather(scan_grad, "dp", axis=0, tiled=True)
    normed_turned = turned[:own_in]
    outproj_owned = lax.psum(
        jnp.dot(turned[own_in:], cot_all, preferred_element_type=f32), "seq"
    )
    gate_owned = lax.psum(jnp.dot(normed_turned, gate_all, preferred_element_type=f32), "seq")
    scan_owned = lax.psum(jnp.dot(normed_turned, scan_all, preferred_element_type=f32), "seq")
    inproj_owned = jnp.concatenate([gate_owned, scan_owned], axis=1)

    normed_grad = mm(gate_grad, gate_matrix, 1, 1) + mm(scan_grad, scan_matrix, 1, 1)
    plain = hidden * root
    prenorm_grad = jnp.sum(normed_grad * plain, axis=0)
    dplain = normed_grad * pre_scale
    input_gradient = root * (
        dplain - plain * jnp.mean(dplain * plain, axis=-1, keepdims=True)
    ) + cot_low.astype(f32)

    head_sums = jnp.concatenate(
        [
            head_grad[:2, :heads],
            jnp.sum(conv_grad[tap_rows : tap_rows + 1, :inner].reshape(1, heads, width), axis=-1),
        ],
        axis=0,
    )
    packed = jnp.concatenate(
        [
            prenorm_grad,
            postnorm_grad,
            conv_grad[:tap_rows].reshape(-1),
            head_sums.reshape(-1),
        ]
    )
    packed = lax.psum(packed, ("dp", "seq"))
    prenorm_owned = lax.dynamic_slice_in_dim(packed, me * own_in, own_in, 0)
    postnorm_owned = lax.dynamic_slice_in_dim(packed, model_width + me * own_out, own_out, 0)
    conv_at = model_width + inner
    conv_end = conv_at + tap_rows * conv_width
    conv_owned = lax.dynamic_slice_in_dim(
        packed[conv_at:conv_end].reshape(tap_rows, conv_width), me * conv_own, conv_own, 1
    )
    head_total = packed[conv_end:].reshape(3, heads)

    prenorm_new, prenorm_mom, prenorm_sq = adam_update(
        prenorm, prenorm_first, prenorm_second, prenorm_owned, rate_vector, 0.0
    )
    inproj_new, inproj_mom, inproj_sq = adam_update(
        inproject, inproject_first, inproject_second, inproj_owned, rate_matrix, weight_decay
    )
    conv_new, conv_mom, conv_sq = adam_update(
        convtaps, convtaps_first, convtaps_second, conv_owned, rate_vector, 0.0
    )
    head_new, head_mom, head_sq = adam_update(
        headcoefs, headcoefs_first, headcoefs_second, head_total, rate_vector, 0.0
    )
    postnorm_new, postnorm_mom, postnorm_sq = adam_update(
        postnorm, postnorm_first, postnorm_second, postnorm_owned, rate_vector, 0.0
    )
    outproj_new, outproj_mom, outproj_sq = adam_update(
        outproject, outproject_first, outproject_second, outproj_owned, rate_matrix, weight_decay
    )
    return (
        output.reshape(seq_here, rows, model_width),
        input_gradient.reshape(seq_here, rows, model_width),
        prenorm_owned,
        inproj_owned,
        conv_owned,
        head_total,
        postnorm_owned,
        outproj_owned,
        prenorm_new,
        inproj_new,
        conv_new,
        head_new,
        postnorm_new,
        outproj_new,
        prenorm_mom,
        inproj_mom,
        conv_mom,
        head_mom,
        postnorm_mom,
        outproj_mom,
        prenorm_sq,
        inproj_sq,
        conv_sq,
        head_sq,
        postnorm_sq,
        outproj_sq,
    )


def solution(mesh):
    weights = (P("dp"), P("dp", None), P(None, "dp"), P(), P("dp"), P("dp", None))
    tokens = (P("dp", "seq", None), P("dp", "seq", None))
    return jax.shard_map(
        on_device,
        mesh=mesh,
        in_specs=tokens + weights * 3,
        out_specs=tokens + weights * 4,
        check_vma=False,
    )
```

```python
import functools

import jax
import jax.numpy as jnp
from jax import lax
from jax.experimental import pallas as pl
from jax.experimental.pallas import tpu as pltpu
from jax.sharding import PartitionSpec as P

N = 128
LANES = 128
HALO = 16

norm_eps = 1e-05
beta_moment = 0.9
beta_square = 0.95
adam_eps = 1e-08
adam_step = 3.0
rate_matrix = 0.005
rate_vector = 0.05
weight_decay = 0.1

f32 = jnp.float32
bf16 = jnp.bfloat16
MESH = pl.DeviceIdType.MESH


def adam_update(weight, moment, square, gradient, step_rate, decay_rate):
    moment_new = beta_moment * moment + (1.0 - beta_moment) * gradient
    square_new = beta_square * square + (1.0 - beta_square) * gradient * gradient
    moment_hat = moment_new / (1.0 - beta_moment**adam_step)
    square_hat = square_new / (1.0 - beta_square**adam_step)
    updated = weight - step_rate * (
        moment_hat / (jnp.sqrt(square_hat) + adam_eps) + decay_rate * weight
    )
    return (updated, moment_new, square_new)


def mm(a, b, ca, cb):
    return lax.dot_general(a, b, (((ca,), (cb,)), ((), ())), preferred_element_type=f32)


def halves(a):
    hi = a.astype(bf16)
    return hi, (a - hi.astype(f32)).astype(bf16)


def thirds(a):
    hi = a.astype(bf16)
    rest = a - hi.astype(f32)
    mid = rest.astype(bf16)
    return hi, mid, (rest - mid.astype(f32)).astype(bf16)


def mm3(a, b, ca, cb):
    return mm(a[0], b[0], ca, cb) + mm(a[0], b[1], ca, cb) + mm(a[1], b[0], ca, cb)


def iota(shape, dim):
    return lax.broadcasted_iota(jnp.int32, shape, dim)


def head_lanes(tile, heads_a_tile, copies):
    rows = iota((copies * LANES, LANES), 0)
    lane_head = tile * heads_a_tile + iota((copies * LANES, LANES), 1) // (LANES // heads_a_tile)
    return (rows % LANES == lane_head).astype(f32).astype(bf16)


def conv_tile(conv_ref, halo_ref, u_ref, taps_ref, start, rows):
    cols = pl.ds(start, LANES)
    conv_ref[0:HALO, :] = halo_ref[:, cols].astype(f32)
    conv_ref[HALO : HALO + rows, :] = u_ref[:, cols].astype(f32)
    taps = taps_ref[:, cols]
    pre = taps[4:5, :] + taps[0:1, :] * conv_ref[HALO - 3 : HALO - 3 + rows, :]
    for k in range(1, 4):
        pre = pre + taps[k : k + 1, :] * conv_ref[HALO - 3 + k : HALO - 3 + k + rows, :]
    return pre, jax.nn.sigmoid(pre)


def seq_copy(src, dst, send, recv, to):
    return pltpu.make_async_remote_copy(
        src_ref=src,
        dst_ref=dst,
        send_sem=send,
        recv_sem=recv,
        device_id={"seq": to},
        device_id_type=MESH,
    )


def greet_seq(barrier, rank, last):
    @pl.when(rank > 0)
    def _():
        pl.semaphore_signal(barrier, inc=1, device_id={"seq": rank - 1}, device_id_type=MESH)

    @pl.when(rank < last)
    def _():
        pl.semaphore_signal(barrier, inc=1, device_id={"seq": rank + 1}, device_id_type=MESH)


def seq_neighbours(rank, last):
    return jnp.minimum(rank, 1) + jnp.minimum(last - rank, 1)


def forward_kernel(
    sizes,
    u_ref,
    rate_ref,
    heads_ref,
    skip_ref,
    taps_ref,
    mixer_ref,
    ypre_ref,
    enter_ref,
    halo_ref,
    step_ref,
    cum_ref,
    cumt_ref,
    conv_ref,
    score_ref,
    leave_ref,
    send_sem,
    recv_sem,
    halo_sem,
):
    rows, inner, tiles, per_tile = sizes
    conv_width = inner + 2 * N
    rank = lax.axis_index("seq")
    last = lax.axis_size("seq") - 1
    barrier = pltpu.get_barrier_semaphore()
    greet_seq(barrier, rank, last)
    pl.semaphore_wait(barrier, seq_neighbours(rank, last))
    right = jnp.minimum(rank + 1, last)
    halo_copy = seq_copy(
        u_ref.at[pl.ds(rows - HALO, HALO), pl.ds(0, conv_width)],
        halo_ref,
        halo_sem.at[0],
        halo_sem.at[1],
        right,
    )

    @pl.when(rank < last)
    def _():
        halo_copy.start()

    step = jax.nn.softplus(rate_ref[...] + heads_ref[0:1, :])
    decay = -step * jnp.exp(heads_ref[1:2, :])
    lower = (iota((rows, rows), 0) >= iota((rows, rows), 1)).astype(f32).astype(bf16)
    cum = sum(mm(lower, part, 1, 0) for part in thirds(decay))
    step_ref[...] = step
    cum_ref[...] = cum
    cumt_ref[...] = cum.T

    @pl.when(rank > 0)
    def _():
        halo_copy.wait_recv()

    @pl.when(rank == 0)
    def _():
        halo_ref[...] = jnp.zeros_like(halo_ref)

    pre_b, sig_b = conv_tile(conv_ref, halo_ref, u_ref, taps_ref, inner, rows)
    b_parts = halves(pre_b * sig_b)
    pre_c, sig_c = conv_tile(conv_ref, halo_ref, u_ref, taps_ref, inner + N, rows)
    c_parts = halves(pre_c * sig_c)
    scores = mm3(c_parts, b_parts, 1, 1)
    causal = iota((rows, rows), 0) >= iota((rows, rows), 1)
    score_ref[...] = jnp.where(causal, scores, 0.0)
    cum_parts = jnp.concatenate(thirds(cum), axis=1)
    step_parts = jnp.concatenate(thirds(step), axis=1)
    lane = iota((rows, LANES), 1)
    width = LANES // per_tile

    def chain(tile):
        return seq_copy(
            leave_ref.at[tile], enter_ref.at[tile], send_sem.at[tile], recv_sem.at[tile], right
        )

    def one(tile, carry):
        start = pl.multiple_of(tile * LANES, LANES)
        cols = pl.ds(start, LANES)
        pick = head_lanes(tile, per_tile, 3)
        cum_l = mm(cum_parts, pick, 1, 0)
        step_l = mm(step_parts, pick, 1, 0)
        pre, sig = conv_tile(conv_ref, halo_ref, u_ref, taps_ref, start, rows)
        values = pre * sig
        x = values * step_l
        total = cum_l[rows - 1 : rows, :]
        fresh = mm3(b_parts, halves(x * jnp.exp(total - cum_l)), 0, 0)

        @pl.when(rank > 0)
        def _():
            chain(tile).wait_recv()

        @pl.when(rank == 0)
        def _():
            enter_ref[tile] = jnp.zeros((N, LANES), f32)

        enter = enter_ref[tile]
        leave_ref[tile] = jnp.exp(total) * enter + fresh

        @pl.when(rank < last)
        def _():
            chain(tile).start()

        result = mm3(c_parts, halves(enter), 1, 0) * jnp.exp(cum_l)
        for h in range(per_tile):
            row = cumt_ref[pl.ds(tile * per_tile + h, 1), :]
            col = cum_l[:, h * width : h * width + 1]
            kernel = jnp.exp(jnp.minimum(col - row, 0.0)) * score_ref[...]
            own = (lane // width) == h
            result = result + mm3(halves(kernel), halves(jnp.where(own, x, 0.0)), 1, 0)
        ypre_ref[:, cols] = result
        mixer_ref[:, cols] = (result + skip_ref[0:1, cols] * values).astype(bf16)
        return carry

    lax.fori_loop(0, tiles, one, 0)

    @pl.when(rank < last)
    def _():
        halo_copy.wait_send()

        def drain(tile, carry):
            chain(tile).wait_send()
            return carry

        lax.fori_loop(0, tiles, drain, 0)


def backward_kernel(
    sizes,
    u_ref,
    halo_ref,
    rate_ref,
    step_ref,
    cum_ref,
    cumt_ref,
    heads_ref,
    skip_ref,
    taps_ref,
    dy_ref,
    ypre_ref,
    enter_ref,
    turn_ref,
    dproj_ref,
    conv_grad_ref,
    head_grad_ref,
    turned_ref,
    conv_ref,
    score_ref,
    dscore_ref,
    dread_ref,
    dwrite_ref,
    dcum_ref,
    dstep_ref,
    dpre_ref,
    leave_ref,
    arrive_ref,
    send_sem,
    recv_sem,
    halo_sem,
    turn_send,
    turn_recv,
    own_sem,
):
    rows, inner, tiles, per_tile = sizes
    conv_width = inner + 2 * N
    rank = lax.axis_index("seq")
    last = lax.axis_size("seq") - 1
    me = lax.axis_index("dp")
    group = lax.axis_size("dp")
    barrier = pltpu.get_barrier_semaphore()
    greet_seq(barrier, rank, last)
    for i in range(1, group):
        pl.semaphore_signal(
            barrier, inc=1, device_id={"dp": lax.rem(me + i, group)}, device_id_type=MESH
        )
    pl.semaphore_wait(barrier, seq_neighbours(rank, last) + group - 1)

    def turn(i):
        peer = lax.rem(me + i, group)
        return pltpu.make_async_remote_copy(
            src_ref=turn_ref.at[peer],
            dst_ref=turned_ref.at[:, pl.ds(pl.multiple_of(me * rows, rows), rows)],
            send_sem=turn_send.at[i],
            recv_sem=turn_recv.at[i],
            device_id={"dp": peer},
            device_id_type=MESH,
        )

    for i in range(1, group):
        turn(i).start()
    own_copy = pltpu.make_async_copy(
        turn_ref.at[me],
        turned_ref.at[:, pl.ds(pl.multiple_of(me * rows, rows), rows)],
        own_sem,
    )
    own_copy.start()

    left = jnp.maximum(rank - 1, 0)
    cum = cum_ref[...]
    step = step_ref[...]
    pre_b, sig_b = conv_tile(conv_ref, halo_ref, u_ref, taps_ref, inner, rows)
    b_parts = halves(pre_b * sig_b)
    pre_c, sig_c = conv_tile(conv_ref, halo_ref, u_ref, taps_ref, inner + N, rows)
    c_parts = halves(pre_c * sig_c)
    later = iota((rows, rows), 1) >= iota((rows, rows), 0)
    score_ref[...] = jnp.where(later, mm3(b_parts, c_parts, 1, 1), 0.0)
    dscore_ref[...] = jnp.zeros_like(dscore_ref)
    dread_ref[...] = jnp.zeros_like(dread_ref)
    dwrite_ref[...] = jnp.zeros_like(dwrite_ref)
    dcum_ref[...] = jnp.zeros_like(dcum_ref)
    dstep_ref[...] = jnp.zeros_like(dstep_ref)
    cum_parts = jnp.concatenate(thirds(cum), axis=1)
    step_parts = jnp.concatenate(thirds(step), axis=1)
    lane = iota((rows, LANES), 1)
    final_row = iota((rows, LANES), 0) == rows - 1
    width = LANES // per_tile

    def chain(tile):
        return seq_copy(
            leave_ref.at[tile], arrive_ref.at[tile], send_sem.at[tile], recv_sem.at[tile], left
        )

    def tap_grads(dpre, extra):
        sums = [
            jnp.sum(
                dpre * conv_ref[HALO - 3 + k : HALO - 3 + k + rows, :], axis=0, keepdims=True
            )
            for k in range(4)
        ]
        sums.append(jnp.sum(dpre, axis=0, keepdims=True))
        sums.append(extra)
        sums.append(jnp.zeros((2, LANES), f32))
        return jnp.concatenate(sums, axis=0)

    def one(tile, carry):
        start = pl.multiple_of(tile * LANES, LANES)
        cols = pl.ds(start, LANES)
        pick = head_lanes(tile, per_tile, 3)
        cum_l = mm(cum_parts, pick, 1, 0)
        step_l = mm(step_parts, pick, 1, 0)
        total = cum_l[rows - 1 : rows, :]
        dy = dy_ref[:, cols].astype(f32)
        reads = halves(dy * jnp.exp(cum_l))
        denter = mm3(c_parts, reads, 0, 0)

        @pl.when(rank < last)
        def _():
            chain(tile).wait_recv()

        @pl.when(rank == last)
        def _():
            arrive_ref[tile] = jnp.zeros((N, LANES), f32)

        arrive = arrive_ref[tile]
        leave_ref[tile] = jnp.exp(total) * arrive + denter

        @pl.when(rank > 0)
        def _():
            chain(tile).start()

        pre, sig = conv_tile(conv_ref, halo_ref, u_ref, taps_ref, start, rows)
        values = pre * sig
        x = values * step_l
        x_parts = halves(x)
        tail = jnp.exp(total - cum_l)
        enter = enter_ref[tile]
        arrive_parts = halves(arrive)
        dx_state = mm3(b_parts, arrive_parts, 1, 0) * tail
        dx = dx_state
        for h in range(per_tile):
            row = cumt_ref[pl.ds(tile * per_tile + h, 1), :]
            col = cum_l[:, h * width : h * width + 1]
            spread = jnp.exp(jnp.minimum(row - col, 0.0))
            kernel = halves(spread * score_ref[...])
            own = jnp.where((lane // width) == h, dy, 0.0).astype(bf16)
            dx = dx + (mm(kernel[0], own, 1, 0) + mm(kernel[1], own, 1, 0))
            pairs = mm(x_parts[0], own, 1, 1) + mm(x_parts[1], own, 1, 1)
            dscore_ref[...] += spread * pairs
        dread_ref[...] += mm3(reads, halves(enter), 1, 1)
        dwrite_ref[...] += mm3(halves(x * tail), arrive_parts, 1, 1)
        ends = jnp.sum(x * dx_state, axis=0, keepdims=True) + jnp.exp(total) * jnp.sum(
            enter * arrive, axis=0, keepdims=True
        )
        dcum = dy * ypre_ref[:, cols] - x * dx + jnp.where(final_row, ends, 0.0)
        own_head = pick[0:LANES, :]
        for part in halves(dcum):
            dcum_ref[...] += mm(part, own_head, 1, 1)
        for part in halves(dx * values):
            dstep_ref[...] += mm(part, own_head, 1, 1)
        dvalues = step_l * dx + skip_ref[0:1, cols] * dy
        dpre = dvalues * sig * (1.0 + pre * (1.0 - sig))
        dpre_ref[0:rows, cols] = dpre
        conv_grad_ref[:, cols] = tap_grads(dpre, jnp.sum(dy * values, axis=0, keepdims=True))
        return carry

    lax.fori_loop(0, tiles, one, 0)

    dscore = halves(jnp.where(later, dscore_ref[...], 0.0))
    dshared = (
        dwrite_ref[...] + mm3(dscore, c_parts, 1, 0),
        dread_ref[...] + mm3(dscore, b_parts, 0, 0),
    )
    for i in range(2):
        start = inner + i * N
        pre, sig = conv_tile(conv_ref, halo_ref, u_ref, taps_ref, start, rows)
        dpre = dshared[i] * sig * (1.0 + pre * (1.0 - sig))
        dpre_ref[0:rows, start : start + N] = dpre
        conv_grad_ref[:, start : start + N] = tap_grads(dpre, jnp.zeros((1, LANES), f32))

    edge = seq_copy(
        dpre_ref.at[pl.ds(0, 8), :],
        dpre_ref.at[pl.ds(rows, 8), :],
        halo_sem.at[0],
        halo_sem.at[1],
        left,
    )

    @pl.when(rank > 0)
    def _():
        edge.start()

    upper = (iota((rows, rows), 1) >= iota((rows, rows), 0)).astype(f32).astype(bf16)
    ddecay = sum(mm(upper, part, 1, 0) for part in thirds(dcum_ref[...]))
    exp_rate = jnp.exp(heads_ref[1:2, :])
    drate = (dstep_ref[...] - ddecay * exp_rate) * jax.nn.sigmoid(rate_ref[...] + heads_ref[0:1, :])
    head_grad_ref[...] = jnp.concatenate(
        [
            jnp.sum(drate, axis=0, keepdims=True),
            jnp.sum(ddecay * (-step * exp_rate), axis=0, keepdims=True),
            jnp.zeros((6, LANES), f32),
        ],
        axis=0,
    )
    heads = tiles * per_tile
    dproj_ref[:, conv_width : conv_width + heads] = drate[:, 0:heads].astype(bf16)

    @pl.when(rank == last)
    def _():
        dpre_ref[rows : rows + 8, :] = jnp.zeros((8, conv_width), f32)

    @pl.when(rank < last)
    def _():
        edge.wait_recv()

    def unconv(tile, carry):
        cols = pl.ds(pl.multiple_of(tile * LANES, LANES), LANES)
        taps = taps_ref[:, cols]
        du = taps[3:4, :] * dpre_ref[0:rows, cols]
        for k in range(3):
            du = du + taps[k : k + 1, :] * dpre_ref[3 - k : 3 - k + rows, cols]
        dproj_ref[:, cols] = du.astype(bf16)
        return carry

    lax.fori_loop(0, conv_width // LANES, unconv, 0)

    @pl.when(rank > 0)
    def _():
        edge.wait_send()

        def drain(tile, carry):
            chain(tile).wait_send()
            return carry

        lax.fori_loop(0, tiles, drain, 0)

    own_copy.wait()
    for i in range(1, group):
        turn(i).wait_send()
        origin = lax.rem(me + group - i, group)
        pltpu.make_async_remote_copy(
            src_ref=turn_ref.at[origin],
            dst_ref=turned_ref.at[:, pl.ds(pl.multiple_of(origin * rows, rows), rows)],
            send_sem=turn_send.at[i],
            recv_sem=turn_recv.at[i],
            device_id={"dp": origin},
            device_id_type=MESH,
        ).wait_recv()


def vmem(count):
    return [pl.BlockSpec(memory_space=pltpu.VMEM)] * count


def scan_forward(u, rate, heads, skip, taps, sizes):
    rows, inner, tiles, _ = sizes
    conv_width = inner + 2 * N
    shape = jax.ShapeDtypeStruct
    return pl.pallas_call(
        functools.partial(forward_kernel, sizes),
        out_shape=(
            shape((rows, inner), bf16),
            shape((rows, inner), f32),
            shape((tiles, N, LANES), f32),
            shape((HALO, conv_width), bf16),
            shape((rows, LANES), f32),
            shape((rows, LANES), f32),
            shape((LANES, rows), f32),
        ),
        in_specs=vmem(5),
        out_specs=tuple(vmem(7)),
        scratch_shapes=[
            pltpu.VMEM((HALO + rows, LANES), f32),
            pltpu.VMEM((rows, rows), f32),
            pltpu.VMEM((tiles, N, LANES), f32),
            pltpu.SemaphoreType.DMA((tiles,)),
            pltpu.SemaphoreType.DMA((tiles,)),
            pltpu.SemaphoreType.DMA((2,)),
        ],
        compiler_params=pltpu.CompilerParams(
            collective_id=1, has_side_effects=True, vmem_limit_bytes=40 * 2**20
        ),
        cost_estimate=pl.CostEstimate(flops=4 * 10**9, bytes_accessed=10**7, transcendentals=4 * 10**6),
    )(u, rate, heads, skip, taps)


def scan_backward(u, halo, rate, step, cum, cumt, heads, skip, taps, dy, ypre, enter, turn, sizes):
    rows, inner, tiles, _ = sizes
    conv_width = inner + 2 * N
    shape = jax.ShapeDtypeStruct
    group, turn_rows, _ = turn.shape
    return pl.pallas_call(
        functools.partial(backward_kernel, sizes),
        out_shape=(
            shape(u.shape, bf16),
            shape((8, conv_width), f32),
            shape((8, LANES), f32),
            shape((turn_rows, group * rows), bf16),
        ),
        in_specs=vmem(12) + [pl.BlockSpec(memory_space=pl.ANY)],
        out_specs=tuple(vmem(3) + [pl.BlockSpec(memory_space=pl.ANY)]),
        scratch_shapes=[
            pltpu.VMEM((HALO + rows, LANES), f32),
            pltpu.VMEM((rows, rows), f32),
            pltpu.VMEM((rows, rows), f32),
            pltpu.VMEM((rows, N), f32),
            pltpu.VMEM((rows, N), f32),
            pltpu.VMEM((rows, LANES), f32),
            pltpu.VMEM((rows, LANES), f32),
            pltpu.VMEM((rows + 8, conv_width), f32),
            pltpu.VMEM((tiles, N, LANES), f32),
            pltpu.VMEM((tiles, N, LANES), f32),
            pltpu.SemaphoreType.DMA((tiles,)),
            pltpu.SemaphoreType.DMA((tiles,)),
            pltpu.SemaphoreType.DMA((2,)),
            pltpu.SemaphoreType.DMA((group,)),
            pltpu.SemaphoreType.DMA((group,)),
            pltpu.SemaphoreType.DMA,
        ],
        compiler_params=pltpu.CompilerParams(
            collective_id=2, has_side_effects=True, vmem_limit_bytes=40 * 2**20
        ),
        cost_estimate=pl.CostEstimate(flops=6 * 10**9, bytes_accessed=2 * 10**7, transcendentals=4 * 10**6),
    )(u, halo, rate, step, cum, cumt, heads, skip, taps, dy, ypre, enter, turn)


def line_kernel(shapes, root, lag, has_small, *refs):
    count = len(shapes)
    refs = list(refs)
    parts = [refs.pop(0) for _ in range(count - has_small)]
    small_ref = refs.pop(0) if has_small else None
    outs = [refs.pop(0) for _ in range(count)]
    from_left = [refs.pop(0) for _ in range(count)]
    from_right = [refs.pop(0) for _ in range(count)]
    if has_small:
        small_sum, small_all, small_send, small_recv = (refs.pop(0) for _ in range(4))
        parts.append(small_sum)
    up_send, left_recv, right_recv, total_recv, down_left, down_right = refs

    rank = lax.axis_index("seq")
    last = lax.axis_size("seq") - 1
    me = lax.axis_index("dp")
    group = lax.axis_size("dp")
    barrier = pltpu.get_barrier_semaphore()
    greet_seq(barrier, rank, last)
    if has_small:
        for i in range(1, group):
            pl.semaphore_signal(
                barrier, inc=1, device_id={"dp": lax.rem(me + i, group)}, device_id_type=MESH
            )
        pl.semaphore_wait(barrier, seq_neighbours(rank, last) + group - 1)
    else:
        pl.semaphore_wait(barrier, seq_neighbours(rank, last))
    left = jnp.maximum(rank - 1, 0)
    right = jnp.minimum(rank + 1, last)

    def small_copy(i, peer, slot):
        return pltpu.make_async_remote_copy(
            src_ref=small_ref.at[peer],
            dst_ref=small_all.at[slot],
            send_sem=small_send.at[i],
            recv_sem=small_recv.at[i],
            device_id={"dp": peer},
            device_id_type=MESH,
        )

    if has_small:
        for i in range(1, group):
            small_copy(i, lax.rem(me + i, group), me).start()
        small_all[me] = small_ref[me]

    def rows_of(array, chunk):
        size = shapes[array][1]
        return pl.ds(pl.multiple_of(chunk * size, size), size)

    def up_copy(array, chunk, step, source, target, recv, to):
        rows = rows_of(array, chunk)
        return seq_copy(
            source[array].at[rows, :], target[array].at[rows, :], up_send.at[step], recv.at[step], to
        )

    def down_copy(array, chunk, step, send, to):
        rows = rows_of(array, chunk)
        return seq_copy(
            outs[array].at[rows, :], outs[array].at[rows, :], send.at[step], total_recv.at[step], to
        )

    def up_side(array, chunk, step, inbox, recv, edge, to):
        rows = rows_of(array, chunk)

        @pl.when(rank == edge)
        def _():
            up_copy(array, chunk, step, parts, inbox, recv, to).start()

        @pl.when(rank != edge)
        def _():
            up_copy(array, chunk, step, inbox, inbox, recv, to).wait_recv()
            inbox[array][rows, :] += parts[array][rows, :]
            up_copy(array, chunk, step, inbox, inbox, recv, to).start()

    def up(array, chunk, step):
        rows = rows_of(array, chunk)
        if has_small and array == count - 1:
            for i in range(1, group):
                small_copy(i, lax.rem(me + i, group), me).wait_send()
                origin = lax.rem(me + group - i, group)
                small_copy(i, origin, origin).wait_recv()
            small_sum[...] = jnp.sum(small_all[...], axis=0)

        @pl.when(rank < root)
        def _():
            up_side(array, chunk, step, from_left, left_recv, 0, right)

        @pl.when(rank > root)
        def _():
            up_side(array, chunk, step, from_right, right_recv, last, left)

        @pl.when(rank == root)
        def _():
            total = parts[array][rows, :]
            if root > 0:
                up_copy(array, chunk, step, from_left, from_left, left_recv, left).wait_recv()
                total = total + from_left[array][rows, :]
            if root < last:
                up_copy(array, chunk, step, from_right, from_right, right_recv, right).wait_recv()
                total = total + from_right[array][rows, :]
            outs[array][rows, :] = total
            if root > 0:
                down_copy(array, chunk, step, down_left, left).start()
            if root < last:
                down_copy(array, chunk, step, down_right, right).start()

    def down(array, chunk, step):
        @pl.when(rank < root)
        def _():
            down_copy(array, chunk, step, down_left, left).wait_recv()

            @pl.when(rank > 0)
            def _():
                down_copy(array, chunk, step, down_left, left).start()

        @pl.when(rank > root)
        def _():
            down_copy(array, chunk, step, down_right, right).wait_recv()

            @pl.when(rank < last)
            def _():
                down_copy(array, chunk, step, down_right, right).start()

    def drain(array, chunk, step):
        @pl.when(rank < root)
        def _():
            up_copy(array, chunk, step, parts, from_left, left_recv, right).wait_send()

        @pl.when(rank > root)
        def _():
            up_copy(array, chunk, step, parts, from_right, right_recv, left).wait_send()

        @pl.when((rank <= root) & (rank > 0))
        def _():
            down_copy(array, chunk, step, down_left, left).wait_send()

        @pl.when((rank >= root) & (rank < last))
        def _():
            down_copy(array, chunk, step, down_right, right).wait_send()

    def each(step, action):
        first = 0
        for array in range(count):
            chunks = shapes[array][0] // shapes[array][1]

            @pl.when((step >= first) & (step < first + chunks))
            def _(array=array, first=first):
                action(array, step - first, step)

            first += chunks
        return first

    steps = sum(shape[0] // shape[1] for shape in shapes)

    def forward(step, carry):
        each(step, up)
        each(step - lag, down)
        return carry

    lax.fori_loop(0, steps + lag, forward, 0)

    def finish(step, carry):
        each(step, drain)
        return carry

    lax.fori_loop(0, steps, finish, 0)


def line_reduce(parts, small, ident):
    size = lax.axis_size("seq")
    group = lax.axis_size("dp")
    shapes = [(part.shape[0], part.shape[0] // 12) for part in parts]
    full = [part.shape for part in parts]
    args = list(parts)
    extra = []
    if small is not None:
        shapes.append((8, 8))
        full.append(small.shape[1:])
        args.append(small)
        extra = [
            pltpu.VMEM(small.shape[1:], f32),
            pltpu.VMEM(small.shape, f32),
            pltpu.SemaphoreType.DMA((group,)),
            pltpu.SemaphoreType.DMA((group,)),
        ]
    steps = sum(shape[0] // shape[1] for shape in shapes)
    return pl.pallas_call(
        functools.partial(line_kernel, shapes, size // 2, 4, small is not None),
        out_shape=tuple(jax.ShapeDtypeStruct(shape, f32) for shape in full),
        in_specs=vmem(len(args)),
        out_specs=tuple(vmem(len(full))),
        scratch_shapes=[pltpu.VMEM(shape, f32) for shape in full] * 2
        + extra
        + [pltpu.SemaphoreType.DMA((steps,))] * 6,
        compiler_params=pltpu.CompilerParams(
            collective_id=ident, has_side_effects=True, vmem_limit_bytes=40 * 2**20
        ),
        cost_estimate=pl.CostEstimate(flops=10**10, bytes_accessed=2 * 10**8, transcendentals=0),
    )(*args)


def on_device(
    hidden_in,
    out_grad,
    prenorm,
    inproject,
    convtaps,
    headcoefs,
    postnorm,
    outproject,
    prenorm_first,
    inproject_first,
    convtaps_first,
    headcoefs_first,
    postnorm_first,
    outproject_first,
    prenorm_second,
    inproject_second,
    convtaps_second,
    headcoefs_second,
    postnorm_second,
    outproject_second,
):
    group = lax.axis_size("dp")
    me = lax.axis_index("dp")
    seq_here, rows, model_width = hidden_in.shape
    assert seq_here == 1
    heads = headcoefs.shape[1]
    own_in, proj_width = inproject.shape
    own_out = outproject.shape[0]
    inner = own_out * group
    width = inner // heads
    per_tile = LANES // width
    tiles = inner // LANES
    sizes = (rows, inner, tiles, per_tile)
    conv_own = convtaps.shape[1]
    conv_width = conv_own * group

    in_low = inproject.astype(bf16)
    scan_matrix = lax.all_gather(in_low[:, inner:], "dp", axis=0, tiled=True)
    small = jnp.concatenate([prenorm, postnorm, convtaps.reshape(-1)]).astype(bf16)
    small = lax.all_gather(small, "dp", axis=0).astype(f32)
    pre_scale = small[:, :own_in].reshape(-1)
    post_scale = small[:, own_in : own_in + own_out].reshape(-1)
    taps = small[:, own_in + own_out :].reshape(group, -1, conv_own)
    taps = jnp.swapaxes(taps, 0, 1).reshape(-1, conv_width)
    tap_rows = taps.shape[0]
    gate_matrix = lax.all_gather(in_low[:, :inner], "dp", axis=0, tiled=True)
    out_matrix = lax.all_gather(outproject.astype(bf16), "dp", axis=0, tiled=True)

    hidden = hidden_in.reshape(rows, model_width).astype(f32)
    cot_low = out_grad.reshape(rows, model_width)
    cot_all = lax.all_gather(cot_low, "dp", axis=0, tiled=True)
    root = lax.rsqrt(jnp.mean(hidden * hidden, axis=-1, keepdims=True) + norm_eps)
    normed_low = (hidden * root * pre_scale).astype(bf16)

    scan_in = jnp.dot(normed_low, scan_matrix, preferred_element_type=f32).astype(bf16)
    pad_heads = ((0, 0), (0, LANES - heads))
    rate = jnp.pad(scan_in[:, conv_width:].astype(f32), pad_heads)
    head_rows = jnp.pad(headcoefs, ((0, 8 - headcoefs.shape[0]), (0, LANES - heads)))
    skip = jnp.repeat(headcoefs[2:3], width, axis=1)
    taps_pad = jnp.pad(taps, ((0, 8 - tap_rows), (0, 0)))
    mixer_low, ypre, enter, halo, step, cum, cumt = scan_forward(
        scan_in, rate, head_rows, skip, taps_pad, sizes
    )

    gate = jnp.dot(normed_low, gate_matrix, preferred_element_type=f32)
    mixer = mixer_low.astype(f32)
    gate_sig = jax.nn.sigmoid(gate)
    gate_act = gate * gate_sig
    gated = mixer * gate_act
    post_root = lax.rsqrt(jnp.mean(gated * gated, axis=-1, keepdims=True) + norm_eps)
    whitened = gated * post_root
    post_low = (whitened * post_scale).astype(bf16)
    output = hidden + jnp.dot(post_low, out_matrix, preferred_element_type=f32)

    post_grad = mm(cot_low, out_matrix, 1, 1)
    postnorm_grad = jnp.sum(post_grad * whitened, axis=0)
    dwhite = post_grad * post_scale
    dgated = post_root * (dwhite - whitened * jnp.mean(dwhite * whitened, axis=-1, keepdims=True))
    dy = (dgated * gate_act).astype(bf16)
    gate_grad = (dgated * mixer * gate_sig * (1.0 + gate * (1.0 - gate_sig))).astype(bf16)

    turn = jnp.concatenate(
        [
            normed_low.T.reshape(group, own_in, rows),
            post_low.T.reshape(group, own_out, rows),
        ],
        axis=1,
    )
    scan_grad, conv_grad, head_grad, turned = scan_backward(
        scan_in, halo, rate, step, cum, cumt, head_rows, skip, taps_pad, dy, ypre, enter, turn, sizes
    )
    gate_all = lax.all_gather(gate_grad, "dp", axis=0, tiled=True)
    scan_all = lax.all_gather(scan_grad, "dp", axis=0, tiled=True)
    normed_turned = turned[:own_in]
    outproj_owned, gate_owned = line_reduce(
        [
            jnp.dot(turned[own_in:], cot_all, preferred_element_type=f32),
            jnp.dot(normed_turned, gate_all, preferred_element_type=f32),
        ],
        None,
        3,
    )

    normed_grad = mm(gate_grad, gate_matrix, 1, 1) + mm(scan_grad, scan_matrix, 1, 1)
    plain = hidden * root
    prenorm_grad = jnp.sum(normed_grad * plain, axis=0)
    dplain = normed_grad * pre_scale
    input_gradient = root * (
        dplain - plain * jnp.mean(dplain * plain, axis=-1, keepdims=True)
    ) + cot_low.astype(f32)

    head_sums = jnp.concatenate(
        [
            head_grad[:2, :heads],
            jnp.sum(conv_grad[tap_rows : tap_rows + 1, :inner].reshape(1, heads, width), axis=-1),
        ],
        axis=0,
    )
    conv_sums = conv_grad[:tap_rows].reshape(tap_rows, group, conv_own)
    packed = jnp.concatenate(
        [
            prenorm_grad.reshape(group, own_in),
            postnorm_grad.reshape(group, own_out),
            jnp.swapaxes(conv_sums, 0, 1).reshape(group, -1),
            jnp.broadcast_to(head_sums.reshape(1, -1), (group, 3 * heads)),
        ],
        axis=1,
    )
    packed_size = packed.shape[1]
    packed_lanes = -(-packed_size // (8 * LANES)) * LANES
    packed = jnp.pad(packed, ((0, 0), (0, 8 * packed_lanes - packed_size)))
    scan_owned, packed = line_reduce(
        [jnp.dot(normed_turned, scan_all, preferred_element_type=f32)],
        packed.reshape(group, 8, packed_lanes),
        4,
    )
    inproj_owned = jnp.concatenate([gate_owned, scan_owned], axis=1)
    packed = packed.reshape(-1)
    prenorm_owned = packed[:own_in]
    postnorm_owned = packed[own_in : own_in + own_out]
    conv_at = own_in + own_out
    conv_end = conv_at + tap_rows * conv_own
    conv_owned = packed[conv_at:conv_end].reshape(tap_rows, conv_own)
    head_total = packed[conv_end:packed_size].reshape(3, heads)

    prenorm_new, prenorm_mom, prenorm_sq = adam_update(
        prenorm, prenorm_first, prenorm_second, prenorm_owned, rate_vector, 0.0
    )
    inproj_new, inproj_mom, inproj_sq = adam_update(
        inproject, inproject_first, inproject_second, inproj_owned, rate_matrix, weight_decay
    )
    conv_new, conv_mom, conv_sq = adam_update(
        convtaps, convtaps_first, convtaps_second, conv_owned, rate_vector, 0.0
    )
    head_new, head_mom, head_sq = adam_update(
        headcoefs, headcoefs_first, headcoefs_second, head_total, rate_vector, 0.0
    )
    postnorm_new, postnorm_mom, postnorm_sq = adam_update(
        postnorm, postnorm_first, postnorm_second, postnorm_owned, rate_vector, 0.0
    )
    outproj_new, outproj_mom, outproj_sq = adam_update(
        outproject, outproject_first, outproject_second, outproj_owned, rate_matrix, weight_decay
    )
    return (
        output.reshape(seq_here, rows, model_width),
        input_gradient.reshape(seq_here, rows, model_width),
        prenorm_owned,
        inproj_owned,
        conv_owned,
        head_total,
        postnorm_owned,
        outproj_owned,
        prenorm_new,
        inproj_new,
        conv_new,
        head_new,
        postnorm_new,
        outproj_new,
        prenorm_mom,
        inproj_mom,
        conv_mom,
        head_mom,
        postnorm_mom,
        outproj_mom,
        prenorm_sq,
        inproj_sq,
        conv_sq,
        head_sq,
        postnorm_sq,
        outproj_sq,
    )


def solution(mesh):
    weights = (P("dp"), P("dp", None), P(None, "dp"), P(), P("dp"), P("dp", None))
    tokens = (P("dp", "seq", None), P("dp", "seq", None))
    return jax.shard_map(
        on_device,
        mesh=mesh,
        in_specs=tokens + weights * 3,
        out_specs=tokens + weights * 4,
        check_vma=False,
    )
```

```python
import functools

import jax
import jax.numpy as jnp
from jax import lax
from jax.experimental import pallas as pl
from jax.experimental.pallas import tpu as pltpu
from jax.sharding import PartitionSpec as P

N = 128
LANES = 128
HALO = 16
WIDE = 256

norm_eps = 1e-05
beta_moment = 0.9
beta_square = 0.95
adam_eps = 1e-08
adam_step = 3.0
rate_matrix = 0.005
rate_vector = 0.05
weight_decay = 0.1

f32 = jnp.float32
bf16 = jnp.bfloat16
MESH = pl.DeviceIdType.MESH


def adam_update(weight, moment, square, gradient, step_rate, decay_rate):
    moment_new = beta_moment * moment + (1.0 - beta_moment) * gradient
    square_new = beta_square * square + (1.0 - beta_square) * gradient * gradient
    moment_hat = moment_new / (1.0 - beta_moment**adam_step)
    square_hat = square_new / (1.0 - beta_square**adam_step)
    updated = weight - step_rate * (
        moment_hat / (jnp.sqrt(square_hat) + adam_eps) + decay_rate * weight
    )
    return (updated, moment_new, square_new)


def mm(a, b, ca, cb):
    return lax.dot_general(a, b, (((ca,), (cb,)), ((), ())), preferred_element_type=f32)


def halves(a):
    hi = a.astype(bf16)
    return hi, (a - hi.astype(f32)).astype(bf16)


def thirds(a):
    hi = a.astype(bf16)
    rest = a - hi.astype(f32)
    mid = rest.astype(bf16)
    return hi, mid, (rest - mid.astype(f32)).astype(bf16)


def mm3(a, b, ca, cb):
    return mm(a[0], b[0], ca, cb) + mm(a[0], b[1], ca, cb) + mm(a[1], b[0], ca, cb)


def iota(shape, dim):
    return lax.broadcasted_iota(jnp.int32, shape, dim)


def head_lanes(tile, heads_a_tile, copies):
    rows = iota((copies * LANES, LANES), 0)
    lane_head = tile * heads_a_tile + iota((copies * LANES, LANES), 1) // (LANES // heads_a_tile)
    return (rows % LANES == lane_head).astype(f32).astype(bf16)


def conv_tile(conv_ref, halo_ref, u_ref, taps_ref, start, rows):
    cols = pl.ds(start, LANES)
    conv_ref[0:HALO, :] = halo_ref[:, cols].astype(f32)
    conv_ref[HALO : HALO + rows, :] = u_ref[:, cols].astype(f32)
    taps = taps_ref[:, cols]
    pre = taps[4:5, :] + taps[0:1, :] * conv_ref[HALO - 3 : HALO - 3 + rows, :]
    for k in range(1, 4):
        pre = pre + taps[k : k + 1, :] * conv_ref[HALO - 3 + k : HALO - 3 + k + rows, :]
    return pre, jax.nn.sigmoid(pre)


def seq_copy(src, dst, send, recv, to):
    return pltpu.make_async_remote_copy(
        src_ref=src,
        dst_ref=dst,
        send_sem=send,
        recv_sem=recv,
        device_id={"seq": to},
        device_id_type=MESH,
    )


def greet_seq(barrier, rank, last):
    @pl.when(rank > 0)
    def _():
        pl.semaphore_signal(barrier, inc=1, device_id={"seq": rank - 1}, device_id_type=MESH)

    @pl.when(rank < last)
    def _():
        pl.semaphore_signal(barrier, inc=1, device_id={"seq": rank + 1}, device_id_type=MESH)


def seq_neighbours(rank, last):
    return jnp.minimum(rank, 1) + jnp.minimum(last - rank, 1)


def greet_plane(barrier, me, group):
    for i in range(1, group):
        pl.semaphore_signal(
            barrier, inc=1, device_id={"dp": lax.rem(me + i, group)}, device_id_type=MESH
        )


def slot_of(device, group):
    return lax.rem(device, 2) * (group // 2) + device // 2


def ring_place(at, chips):
    half = chips // 2
    turned = at // half
    return at * (1 - turned) + turned * (3 * half - 1 - at)


def forward_kernel(
    sizes,
    u_ref,
    rate_ref,
    heads_ref,
    skip_ref,
    taps_ref,
    mixer_ref,
    ypre_ref,
    enter_ref,
    halo_ref,
    step_ref,
    cum_ref,
    cumt_ref,
    conv_ref,
    score_ref,
    leave_ref,
    send_sem,
    recv_sem,
    halo_sem,
):
    rows, inner, tiles, per_tile = sizes
    conv_width = inner + 2 * N
    rank = lax.axis_index("seq")
    last = lax.axis_size("seq") - 1
    barrier = pltpu.get_barrier_semaphore()
    greet_seq(barrier, rank, last)
    pl.semaphore_wait(barrier, seq_neighbours(rank, last))
    right = jnp.minimum(rank + 1, last)
    halo_copy = seq_copy(
        u_ref.at[pl.ds(rows - HALO, HALO), pl.ds(0, conv_width)],
        halo_ref,
        halo_sem.at[0],
        halo_sem.at[1],
        right,
    )

    @pl.when(rank < last)
    def _():
        halo_copy.start()

    step = jax.nn.softplus(rate_ref[...] + heads_ref[0:1, :])
    decay = -step * jnp.exp(heads_ref[1:2, :])
    lower = (iota((rows, rows), 0) >= iota((rows, rows), 1)).astype(f32).astype(bf16)
    cum = sum(mm(lower, part, 1, 0) for part in thirds(decay))
    step_ref[...] = step
    cum_ref[...] = cum
    cumt_ref[...] = cum.T

    @pl.when(rank > 0)
    def _():
        halo_copy.wait_recv()

    @pl.when(rank == 0)
    def _():
        halo_ref[...] = jnp.zeros_like(halo_ref)

    pre_b, sig_b = conv_tile(conv_ref, halo_ref, u_ref, taps_ref, inner, rows)
    b_parts = halves(pre_b * sig_b)
    pre_c, sig_c = conv_tile(conv_ref, halo_ref, u_ref, taps_ref, inner + N, rows)
    c_parts = halves(pre_c * sig_c)
    scores = mm3(c_parts, b_parts, 1, 1)
    causal = iota((rows, rows), 0) >= iota((rows, rows), 1)
    score_ref[...] = jnp.where(causal, scores, 0.0)
    cum_parts = jnp.concatenate(thirds(cum), axis=1)
    step_parts = jnp.concatenate(thirds(step), axis=1)
    lane = iota((rows, LANES), 1)
    width = LANES // per_tile

    def chain(tile):
        return seq_copy(
            leave_ref.at[tile], enter_ref.at[tile], send_sem.at[tile], recv_sem.at[tile], right
        )

    def one(tile, carry):
        start = pl.multiple_of(tile * LANES, LANES)
        cols = pl.ds(start, LANES)
        pick = head_lanes(tile, per_tile, 3)
        cum_l = mm(cum_parts, pick, 1, 0)
        step_l = mm(step_parts, pick, 1, 0)
        pre, sig = conv_tile(conv_ref, halo_ref, u_ref, taps_ref, start, rows)
        values = pre * sig
        x = values * step_l
        total = cum_l[rows - 1 : rows, :]
        fresh = mm3(b_parts, halves(x * jnp.exp(total - cum_l)), 0, 0)

        @pl.when(rank > 0)
        def _():
            chain(tile).wait_recv()

        @pl.when(rank == 0)
        def _():
            enter_ref[tile] = jnp.zeros((N, LANES), f32)

        enter = enter_ref[tile]
        leave_ref[tile] = jnp.exp(total) * enter + fresh

        @pl.when(rank < last)
        def _():
            chain(tile).start()

        result = mm3(c_parts, halves(enter), 1, 0) * jnp.exp(cum_l)
        for h in range(per_tile):
            row = cumt_ref[pl.ds(tile * per_tile + h, 1), :]
            col = cum_l[:, h * width : h * width + 1]
            kernel = jnp.exp(jnp.minimum(col - row, 0.0)) * score_ref[...]
            own = (lane // width) == h
            result = result + mm3(halves(kernel), halves(jnp.where(own, x, 0.0)), 1, 0)
        ypre_ref[:, cols] = result
        mixer_ref[:, cols] = (result + skip_ref[0:1, cols] * values).astype(bf16)
        return carry

    lax.fori_loop(0, tiles, one, 0)

    @pl.when(rank < last)
    def _():
        halo_copy.wait_send()

        def drain(tile, carry):
            chain(tile).wait_send()
            return carry

        lax.fori_loop(0, tiles, drain, 0)


def backward_kernel(
    sizes,
    u_ref,
    halo_ref,
    rate_ref,
    step_ref,
    cum_ref,
    cumt_ref,
    heads_ref,
    skip_ref,
    taps_ref,
    dy_ref,
    ypre_ref,
    enter_ref,
    turn_ref,
    dproj_ref,
    conv_grad_ref,
    head_grad_ref,
    turned_ref,
    conv_ref,
    score_ref,
    dscore_ref,
    dread_ref,
    dwrite_ref,
    dcum_ref,
    dstep_ref,
    dpre_ref,
    leave_ref,
    arrive_ref,
    send_sem,
    recv_sem,
    halo_sem,
    turn_send,
    turn_recv,
    own_sem,
):
    rows, inner, tiles, per_tile = sizes
    conv_width = inner + 2 * N
    rank = lax.axis_index("seq")
    last = lax.axis_size("seq") - 1
    me = lax.axis_index("dp")
    group = lax.axis_size("dp")
    barrier = pltpu.get_barrier_semaphore()
    greet_seq(barrier, rank, last)
    greet_plane(barrier, me, group)
    pl.semaphore_wait(barrier, seq_neighbours(rank, last) + group - 1)

    def landing(device):
        return turned_ref.at[:, pl.ds(pl.multiple_of(slot_of(device, group) * rows, rows), rows)]

    def turn(i):
        peer = lax.rem(me + i, group)
        return pltpu.make_async_remote_copy(
            src_ref=turn_ref.at[peer],
            dst_ref=landing(me),
            send_sem=turn_send.at[i],
            recv_sem=turn_recv.at[i],
            device_id={"dp": peer},
            device_id_type=MESH,
        )

    for i in range(1, group):
        turn(i).start()
    own_copy = pltpu.make_async_copy(turn_ref.at[me], landing(me), own_sem)
    own_copy.start()

    left = jnp.maximum(rank - 1, 0)
    cum = cum_ref[...]
    step = step_ref[...]
    pre_b, sig_b = conv_tile(conv_ref, halo_ref, u_ref, taps_ref, inner, rows)
    b_parts = halves(pre_b * sig_b)
    pre_c, sig_c = conv_tile(conv_ref, halo_ref, u_ref, taps_ref, inner + N, rows)
    c_parts = halves(pre_c * sig_c)
    later = iota((rows, rows), 1) >= iota((rows, rows), 0)
    score_ref[...] = jnp.where(later, mm3(b_parts, c_parts, 1, 1), 0.0)
    dscore_ref[...] = jnp.zeros_like(dscore_ref)
    dread_ref[...] = jnp.zeros_like(dread_ref)
    dwrite_ref[...] = jnp.zeros_like(dwrite_ref)
    dcum_ref[...] = jnp.zeros_like(dcum_ref)
    dstep_ref[...] = jnp.zeros_like(dstep_ref)
    cum_parts = jnp.concatenate(thirds(cum), axis=1)
    step_parts = jnp.concatenate(thirds(step), axis=1)
    lane = iota((rows, LANES), 1)
    final_row = iota((rows, LANES), 0) == rows - 1
    width = LANES // per_tile

    def chain(tile):
        return seq_copy(
            leave_ref.at[tile], arrive_ref.at[tile], send_sem.at[tile], recv_sem.at[tile], left
        )

    def tap_grads(dpre, extra):
        sums = [
            jnp.sum(
                dpre * conv_ref[HALO - 3 + k : HALO - 3 + k + rows, :], axis=0, keepdims=True
            )
            for k in range(4)
        ]
        sums.append(jnp.sum(dpre, axis=0, keepdims=True))
        sums.append(extra)
        sums.append(jnp.zeros((2, LANES), f32))
        return jnp.concatenate(sums, axis=0)

    def one(tile, carry):
        start = pl.multiple_of(tile * LANES, LANES)
        cols = pl.ds(start, LANES)
        pick = head_lanes(tile, per_tile, 3)
        cum_l = mm(cum_parts, pick, 1, 0)
        step_l = mm(step_parts, pick, 1, 0)
        total = cum_l[rows - 1 : rows, :]
        dy = dy_ref[:, cols].astype(f32)
        reads = halves(dy * jnp.exp(cum_l))
        denter = mm3(c_parts, reads, 0, 0)

        @pl.when(rank < last)
        def _():
            chain(tile).wait_recv()

        @pl.when(rank == last)
        def _():
            arrive_ref[tile] = jnp.zeros((N, LANES), f32)

        arrive = arrive_ref[tile]
        leave_ref[tile] = jnp.exp(total) * arrive + denter

        @pl.when(rank > 0)
        def _():
            chain(tile).start()

        pre, sig = conv_tile(conv_ref, halo_ref, u_ref, taps_ref, start, rows)
        values = pre * sig
        x = values * step_l
        x_parts = halves(x)
        tail = jnp.exp(total - cum_l)
        enter = enter_ref[tile]
        arrive_parts = halves(arrive)
        dx_state = mm3(b_parts, arrive_parts, 1, 0) * tail
        dx = dx_state
        for h in range(per_tile):
            row = cumt_ref[pl.ds(tile * per_tile + h, 1), :]
            col = cum_l[:, h * width : h * width + 1]
            spread = jnp.exp(jnp.minimum(row - col, 0.0))
            kernel = halves(spread * score_ref[...])
            own = jnp.where((lane // width) == h, dy, 0.0).astype(bf16)
            dx = dx + (mm(kernel[0], own, 1, 0) + mm(kernel[1], own, 1, 0))
            pairs = mm(x_parts[0], own, 1, 1) + mm(x_parts[1], own, 1, 1)
            dscore_ref[...] += spread * pairs
        dread_ref[...] += mm3(reads, halves(enter), 1, 1)
        dwrite_ref[...] += mm3(halves(x * tail), arrive_parts, 1, 1)
        ends = jnp.sum(x * dx_state, axis=0, keepdims=True) + jnp.exp(total) * jnp.sum(
            enter * arrive, axis=0, keepdims=True
        )
        dcum = dy * ypre_ref[:, cols] - x * dx + jnp.where(final_row, ends, 0.0)
        own_head = pick[0:LANES, :]
        for part in halves(dcum):
            dcum_ref[...] += mm(part, own_head, 1, 1)
        for part in halves(dx * values):
            dstep_ref[...] += mm(part, own_head, 1, 1)
        dvalues = step_l * dx + skip_ref[0:1, cols] * dy
        dpre = dvalues * sig * (1.0 + pre * (1.0 - sig))
        dpre_ref[0:rows, cols] = dpre
        conv_grad_ref[:, cols] = tap_grads(dpre, jnp.sum(dy * values, axis=0, keepdims=True))
        return carry

    lax.fori_loop(0, tiles, one, 0)

    dscore = halves(jnp.where(later, dscore_ref[...], 0.0))
    dshared = (
        dwrite_ref[...] + mm3(dscore, c_parts, 1, 0),
        dread_ref[...] + mm3(dscore, b_parts, 0, 0),
    )
    for i in range(2):
        start = inner + i * N
        pre, sig = conv_tile(conv_ref, halo_ref, u_ref, taps_ref, start, rows)
        dpre = dshared[i] * sig * (1.0 + pre * (1.0 - sig))
        dpre_ref[0:rows, start : start + N] = dpre
        conv_grad_ref[:, start : start + N] = tap_grads(dpre, jnp.zeros((1, LANES), f32))

    edge = seq_copy(
        dpre_ref.at[pl.ds(0, 8), :],
        dpre_ref.at[pl.ds(rows, 8), :],
        halo_sem.at[0],
        halo_sem.at[1],
        left,
    )

    @pl.when(rank > 0)
    def _():
        edge.start()

    upper = (iota((rows, rows), 1) >= iota((rows, rows), 0)).astype(f32).astype(bf16)
    ddecay = sum(mm(upper, part, 1, 0) for part in thirds(dcum_ref[...]))
    exp_rate = jnp.exp(heads_ref[1:2, :])
    drate = (dstep_ref[...] - ddecay * exp_rate) * jax.nn.sigmoid(rate_ref[...] + heads_ref[0:1, :])
    head_grad_ref[...] = jnp.concatenate(
        [
            jnp.sum(drate, axis=0, keepdims=True),
            jnp.sum(ddecay * (-step * exp_rate), axis=0, keepdims=True),
            jnp.zeros((6, LANES), f32),
        ],
        axis=0,
    )
    dproj_ref[:, conv_width : conv_width + LANES] = drate.astype(bf16)
    dproj_ref[:, conv_width + LANES :] = jnp.zeros(
        (rows, dproj_ref.shape[1] - conv_width - LANES), bf16
    )

    @pl.when(rank == last)
    def _():
        dpre_ref[rows : rows + 8, :] = jnp.zeros((8, conv_width), f32)

    @pl.when(rank < last)
    def _():
        edge.wait_recv()

    def unconv(tile, carry):
        cols = pl.ds(pl.multiple_of(tile * LANES, LANES), LANES)
        taps = taps_ref[:, cols]
        du = taps[3:4, :] * dpre_ref[0:rows, cols]
        for k in range(3):
            du = du + taps[k : k + 1, :] * dpre_ref[3 - k : 3 - k + rows, cols]
        dproj_ref[:, cols] = du.astype(bf16)
        return carry

    lax.fori_loop(0, conv_width // LANES, unconv, 0)

    @pl.when(rank > 0)
    def _():
        edge.wait_send()

        def drain(tile, carry):
            chain(tile).wait_send()
            return carry

        lax.fori_loop(0, tiles, drain, 0)

    own_copy.wait()
    for i in range(1, group):
        turn(i).wait_send()
        origin = lax.rem(me + group - i, group)
        pltpu.make_async_remote_copy(
            src_ref=turn_ref.at[origin],
            dst_ref=landing(origin),
            send_sem=turn_send.at[i],
            recv_sem=turn_recv.at[i],
            device_id={"dp": origin},
            device_id_type=MESH,
        ).wait_recv()


def vmem(count):
    return [pl.BlockSpec(memory_space=pltpu.VMEM)] * count


def scan_forward(u, rate, heads, skip, taps, sizes):
    rows, inner, tiles, _ = sizes
    conv_width = inner + 2 * N
    shape = jax.ShapeDtypeStruct
    return pl.pallas_call(
        functools.partial(forward_kernel, sizes),
        out_shape=(
            shape((rows, inner), bf16),
            shape((rows, inner), f32),
            shape((tiles, N, LANES), f32),
            shape((HALO, conv_width), bf16),
            shape((rows, LANES), f32),
            shape((rows, LANES), f32),
            shape((LANES, rows), f32),
        ),
        in_specs=vmem(5),
        out_specs=tuple(vmem(7)),
        scratch_shapes=[
            pltpu.VMEM((HALO + rows, LANES), f32),
            pltpu.VMEM((rows, rows), f32),
            pltpu.VMEM((tiles, N, LANES), f32),
            pltpu.SemaphoreType.DMA((tiles,)),
            pltpu.SemaphoreType.DMA((tiles,)),
            pltpu.SemaphoreType.DMA((2,)),
        ],
        compiler_params=pltpu.CompilerParams(
            collective_id=1, has_side_effects=True, vmem_limit_bytes=40 * 2**20
        ),
        cost_estimate=pl.CostEstimate(flops=4 * 10**9, bytes_accessed=10**7, transcendentals=4 * 10**6),
    )(u, rate, heads, skip, taps)


def scan_backward(u, halo, rate, step, cum, cumt, heads, skip, taps, dy, ypre, enter, turn, sizes):
    rows, inner, tiles, _ = sizes
    conv_width = inner + 2 * N
    shape = jax.ShapeDtypeStruct
    group, turn_rows, _ = turn.shape
    return pl.pallas_call(
        functools.partial(backward_kernel, sizes),
        out_shape=(
            shape((rows, -(-u.shape[1] // WIDE) * WIDE), bf16),
            shape((8, conv_width), f32),
            shape((8, LANES), f32),
            shape((turn_rows, group * rows), bf16),
        ),
        in_specs=vmem(12) + [pl.BlockSpec(memory_space=pl.ANY)],
        out_specs=tuple(vmem(3) + [pl.BlockSpec(memory_space=pl.ANY)]),
        scratch_shapes=[
            pltpu.VMEM((HALO + rows, LANES), f32),
            pltpu.VMEM((rows, rows), f32),
            pltpu.VMEM((rows, rows), f32),
            pltpu.VMEM((rows, N), f32),
            pltpu.VMEM((rows, N), f32),
            pltpu.VMEM((rows, LANES), f32),
            pltpu.VMEM((rows, LANES), f32),
            pltpu.VMEM((rows + 8, conv_width), f32),
            pltpu.VMEM((tiles, N, LANES), f32),
            pltpu.VMEM((tiles, N, LANES), f32),
            pltpu.SemaphoreType.DMA((tiles,)),
            pltpu.SemaphoreType.DMA((tiles,)),
            pltpu.SemaphoreType.DMA((2,)),
            pltpu.SemaphoreType.DMA((group,)),
            pltpu.SemaphoreType.DMA((group,)),
            pltpu.SemaphoreType.DMA,
        ],
        compiler_params=pltpu.CompilerParams(
            collective_id=2, has_side_effects=True, vmem_limit_bytes=40 * 2**20
        ),
        cost_estimate=pl.CostEstimate(flops=6 * 10**9, bytes_accessed=2 * 10**7, transcendentals=4 * 10**6),
    )(u, halo, rate, step, cum, cumt, heads, skip, taps, dy, ypre, enter, turn)


def tail_kernel(
    sizes,
    turned_ref,
    cot_ref,
    gate_ref,
    scan_ref,
    small_ref,
    in_ref,
    out_ref,
    small_out_ref,
    gathered_ref,
    value_ref,
    inbox_ref,
    other_ref,
    total_ref,
    loaded_ref,
    small_value_ref,
    small_inbox_ref,
    small_other_ref,
    small_all_ref,
    up_send,
    inbox_recv,
    other_recv,
    total_recv,
    left_send,
    right_send,
    store_sem,
    ring_send,
    ring_recv,
    pair_send,
    pair_recv,
    own_sem,
    load_sem,
    small_send,
    small_recv,
):
    rows, own_in, out_steps, gate_steps, steps, root, lag, spacing = sizes
    chunks = steps - out_steps
    rank = lax.axis_index("seq")
    last = lax.axis_size("seq") - 1
    me = lax.axis_index("dp")
    group = lax.axis_size("dp")
    chips = group // 2
    reach = chips // 2
    core = lax.rem(me, 2)
    chip = me // 2
    place = ring_place(chip, chips)
    barrier = pltpu.get_barrier_semaphore()
    greet_seq(barrier, rank, last)
    greet_plane(barrier, me, group)
    pl.semaphore_wait(barrier, seq_neighbours(rank, last) + group - 1)
    left = jnp.maximum(rank - 1, 0)
    right = jnp.minimum(rank + 1, last)

    def plane_copy(src, dst, send, recv, to):
        return pltpu.make_async_remote_copy(
            src_ref=src,
            dst_ref=dst,
            send_sem=send,
            recv_sem=recv,
            device_id={"dp": to},
            device_id_type=MESH,
        )

    def small_copy(i, peer, slot):
        return plane_copy(
            small_ref.at[peer], small_all_ref.at[slot], small_send.at[i], small_recv.at[i], peer
        )

    for i in range(1, group):
        small_copy(i, lax.rem(me + i, group), me).start()
    small_all_ref[me] = small_ref[me]

    def ring_chip(ahead):
        return ring_place(lax.rem(place + ahead + chips, chips), chips)

    def block(chunk, origin, part):
        ref = gathered_ref.at[chunk, core, origin]
        return ref if part is None else ref.at[pl.ds(part * (rows // 2), rows // 2), :]

    def hop(chunk, number, way, source=None):
        origin = ring_chip(-way * (number - 1))
        part = None if number < reach else (0 if way == 1 else 1)
        at = 2 * (number - 1) + (0 if way == 1 else 1)
        return plane_copy(
            block(chunk, origin, part) if source is None else source,
            block(chunk, origin, part),
            ring_send.at[chunk, at],
            ring_recv.at[chunk, at],
            2 * ring_chip(way) + core,
        )

    def hop_in(chunk, number, way):
        origin = ring_chip(-way * number)
        part = None if number < reach else (0 if way == 1 else 1)
        at = 2 * (number - 1) + (0 if way == 1 else 1)
        return plane_copy(
            block(chunk, origin, part),
            block(chunk, origin, part),
            ring_send.at[chunk, at],
            ring_recv.at[chunk, at],
            2 * ring_chip(way) + core,
        )

    def own_source(chunk, part, action):
        part_rows = pl.ds(0, rows) if part is None else pl.ds(part * (rows // 2), rows // 2)

        @pl.when(chunk < gate_steps)
        def _():
            start = pl.multiple_of(chunk * WIDE, WIDE)
            action(gate_ref.at[part_rows, pl.ds(start, WIDE)])

        @pl.when(chunk >= gate_steps)
        def _():
            start = pl.multiple_of((chunk - gate_steps) * WIDE, WIDE)
            action(scan_ref.at[part_rows, pl.ds(start, WIDE)])

    def own_copy(chunk, source):
        return pltpu.make_async_copy(source, block(chunk, chip, None), own_sem.at[chunk])

    def pair_copy(chunk, half):
        return plane_copy(
            gathered_ref.at[chunk, half],
            gathered_ref.at[chunk, half],
            pair_send.at[chunk],
            pair_recv.at[chunk],
            me + 1 - 2 * core,
        )

    def load_copy(chunk):
        slot = lax.rem(chunk, 2)
        return pltpu.make_async_copy(
            gathered_ref.at[chunk], loaded_ref.at[slot], load_sem.at[slot]
        )

    def ring_stage(chunk, stage):
        if stage == 0:
            own_source(chunk, None, lambda source: own_copy(chunk, source).start())
            for way in (1, -1):
                part = None if reach > 1 else (0 if way == 1 else 1)
                own_source(
                    chunk, part, lambda source, way=way: hop(chunk, 1, way, source).start()
                )
        elif stage < reach:
            for way in (1, -1):
                hop_in(chunk, stage, way).wait_recv()
                hop(chunk, stage + 1, way).start()
        else:
            for way in (1, -1):
                hop_in(chunk, stage, way).wait_recv()
            own_copy(chunk, block(chunk, chip, None)).wait()
            pair_copy(chunk, core).start()

    def compute(step):
        @pl.when(step < out_steps)
        def _():
            cols = pl.ds(pl.multiple_of(step * LANES, LANES), LANES)
            cot = jnp.concatenate(
                [
                    cot_ref[pl.ds((2 * (slot % chips) + slot // chips) * rows, rows), cols]
                    for slot in range(group)
                ],
                axis=0,
            )
            for half in range(2):
                rows_at = own_in * (1 + half)
                value_ref[:, half * LANES : (half + 1) * LANES] = mm(
                    turned_ref[rows_at : rows_at + own_in, :], cot, 1, 0
                )

        @pl.when(step >= out_steps)
        def _():
            chunk = step - out_steps
            load_copy(chunk).wait()
            arrived = loaded_ref[lax.rem(chunk, 2)].reshape(group * rows, WIDE)
            value_ref[...] = mm(turned_ref[0:own_in, :], arrived, 1, 0)

    def up_copy(source, target, step, recv, to):
        return seq_copy(source, target, up_send.at[step], recv.at[step], to)

    def up(value, inbox, other, total, step):
        edge = ((rank == 0) | (rank == last)) & (rank != root)
        inner = (rank != root) & (rank > 0) & (rank < last)

        @pl.when(edge)
        def _():
            inbox[...] = value[...]

        @pl.when(inner)
        def _():
            up_copy(inbox, inbox, step, inbox_recv, left).wait_recv()
            inbox[...] += value[...]

        @pl.when(rank < root)
        def _():
            up_copy(inbox, inbox, step, inbox_recv, right).start()

        @pl.when(rank == root + 1)
        def _():
            up_copy(inbox, other, step, other_recv, left).start()

        @pl.when(rank > root + 1)
        def _():
            up_copy(inbox, inbox, step, inbox_recv, left).start()

        @pl.when(rank == root)
        def _():
            result = value[...]
            if root > 0:
                up_copy(inbox, inbox, step, inbox_recv, left).wait_recv()
                result = result + inbox[...]
            if root < last:
                up_copy(other, other, step, other_recv, right).wait_recv()
                result = result + other[...]
            total[...] = result
            if root > 0:
                down_copy(total, step, left_send, left).start()
            if root < last:
                down_copy(total, step, right_send, right).start()

    def down_copy(total, step, send, to):
        return seq_copy(total, total, send.at[step], total_recv.at[step], to)

    def down(total, step):
        @pl.when(rank < root)
        def _():
            down_copy(total, step, left_send, left).wait_recv()

            @pl.when(rank > 0)
            def _():
                down_copy(total, step, left_send, left).start()

        @pl.when(rank > root)
        def _():
            down_copy(total, step, right_send, right).wait_recv()

            @pl.when(rank < last)
            def _():
                down_copy(total, step, right_send, right).start()

    def store_out(step, half):
        cols = pl.ds(pl.multiple_of(step * LANES, LANES), LANES)
        return pltpu.make_async_copy(
            total_ref.at[step, :, pl.ds(half * LANES, LANES)],
            out_ref.at[pl.ds(half * own_in, own_in), cols],
            store_sem.at[step, half],
        )

    def store_in(step):
        cols = pl.ds(pl.multiple_of((step - out_steps) * WIDE, WIDE), WIDE)
        return pltpu.make_async_copy(
            total_ref.at[step], in_ref.at[:, cols], store_sem.at[step, 0]
        )

    def stored(step, action):
        @pl.when(step < out_steps)
        def _():
            for half in range(2):
                action(store_out(step, half))

        @pl.when(step >= out_steps)
        def _():
            action(store_in(step))

    def drain(inbox, other, total, step):
        @pl.when(rank < root)
        def _():
            up_copy(inbox, inbox, step, inbox_recv, right).wait_send()

        @pl.when(rank > root)
        def _():
            up_copy(inbox, inbox, step, inbox_recv, left).wait_send()

        @pl.when((rank <= root) & (rank > 0))
        def _():
            down_copy(total, step, left_send, left).wait_send()

        @pl.when((rank >= root) & (rank < last))
        def _():
            down_copy(total, step, right_send, right).wait_send()

    behind = lag * (jnp.maximum(rank - root, 0) + jnp.maximum(root - rank, 0))

    def round_(step, carry):
        for stage in range(reach, -1, -1):
            chunk = step - stage * spacing

            @pl.when((chunk >= 0) & (chunk < chunks))
            def _(chunk=chunk, stage=stage):
                ring_stage(chunk, stage)

        ready = step - (out_steps - 1)

        @pl.when((ready >= 0) & (ready < chunks))
        def _():
            pair_copy(ready, 1 - core).wait_recv()
            load_copy(ready).start()

        @pl.when(step < steps)
        def _():
            compute(step)
            up(value_ref, inbox_ref.at[step], other_ref.at[step], total_ref.at[step], step)

        @pl.when(step == steps)
        def _():
            for i in range(1, group):
                small_copy(i, lax.rem(me + i, group), me).wait_send()
                origin = lax.rem(me + group - i, group)
                small_copy(i, origin, origin).wait_recv()
            small_value_ref[...] = jnp.sum(small_all_ref[...], axis=0)
            up(small_value_ref, small_inbox_ref, small_other_ref, small_out_ref, steps)

        late = step - behind

        @pl.when((late >= 0) & (late < steps))
        def _():
            down(total_ref.at[late], late)
            stored(late, lambda copy: copy.start())

        @pl.when(late == steps)
        def _():
            down(small_out_ref, steps)

        return carry

    lax.fori_loop(0, steps + 1 + behind, round_, 0)

    def finish(step, carry):
        drain(inbox_ref.at[step], other_ref.at[step], total_ref.at[step], step)
        stored(step, lambda copy: copy.wait())
        return carry

    lax.fori_loop(0, steps, finish, 0)
    drain(small_inbox_ref, small_other_ref, small_out_ref, steps)

    def finish_ring(chunk, carry):
        for number in range(1, reach + 1):
            for way in (1, -1):
                hop(chunk, number, way).wait_send()
        pair_copy(chunk, core).wait_send()
        return carry

    lax.fori_loop(0, chunks, finish_ring, 0)


def reduce_gradients(turned, cot_all, gate_grad, scan_grad, small, own_in):
    size = lax.axis_size("seq")
    group = lax.axis_size("dp")
    rows = gate_grad.shape[0]
    model_width = cot_all.shape[1]
    out_steps = model_width // LANES
    gate_steps = gate_grad.shape[1] // WIDE
    chunks = gate_steps + scan_grad.shape[1] // WIDE
    steps = out_steps + chunks
    reach = group // 4
    spacing = min(3, (out_steps - 2) // reach)
    sizes = (rows, own_in, out_steps, gate_steps, steps, size // 2, 3, spacing)
    shape = jax.ShapeDtypeStruct
    dma = pltpu.SemaphoreType.DMA
    small_shape = small.shape[1:]
    anywhere = pl.BlockSpec(memory_space=pl.ANY)
    return pl.pallas_call(
        functools.partial(tail_kernel, sizes),
        out_shape=(
            shape((own_in, chunks * WIDE), f32),
            shape((2 * own_in, model_width), f32),
            shape(small_shape, f32),
            shape((chunks, 2, group // 2, rows, WIDE), bf16),
        ),
        in_specs=vmem(2) + [anywhere] * 2 + vmem(1),
        out_specs=(anywhere, anywhere, vmem(1)[0], anywhere),
        scratch_shapes=[
            pltpu.VMEM((own_in, WIDE), f32),
            pltpu.VMEM((steps, own_in, WIDE), f32),
            pltpu.VMEM((steps, own_in, WIDE), f32),
            pltpu.VMEM((steps, own_in, WIDE), f32),
            pltpu.VMEM((2, 2, group // 2, rows, WIDE), bf16),
            pltpu.VMEM(small_shape, f32),
            pltpu.VMEM(small_shape, f32),
            pltpu.VMEM(small_shape, f32),
            pltpu.VMEM(small.shape, f32),
        ]
        + [dma((steps + 1,))] * 6
        + [
            dma((steps, 2)),
            dma((chunks, 2 * reach)),
            dma((chunks, 2 * reach)),
            dma((chunks,)),
            dma((chunks,)),
            dma((chunks,)),
            dma((2,)),
            dma((group,)),
            dma((group,)),
        ],
        compiler_params=pltpu.CompilerParams(
            collective_id=3, has_side_effects=True, vmem_limit_bytes=52 * 2**20
        ),
        cost_estimate=pl.CostEstimate(
            flops=2 * 10**10, bytes_accessed=2 * 10**8, transcendentals=0
        ),
    )(turned, cot_all, gate_grad, scan_grad, small)


def on_device(
    hidden_in,
    out_grad,
    prenorm,
    inproject,
    convtaps,
    headcoefs,
    postnorm,
    outproject,
    prenorm_first,
    inproject_first,
    convtaps_first,
    headcoefs_first,
    postnorm_first,
    outproject_first,
    prenorm_second,
    inproject_second,
    convtaps_second,
    headcoefs_second,
    postnorm_second,
    outproject_second,
):
    group = lax.axis_size("dp")
    me = lax.axis_index("dp")
    seq_here, rows, model_width = hidden_in.shape
    assert seq_here == 1
    heads = headcoefs.shape[1]
    own_in, proj_width = inproject.shape
    own_out = outproject.shape[0]
    inner = own_out * group
    width = inner // heads
    per_tile = LANES // width
    tiles = inner // LANES
    sizes = (rows, inner, tiles, per_tile)
    conv_own = convtaps.shape[1]
    conv_width = conv_own * group

    in_low = inproject.astype(bf16)
    scan_matrix = lax.all_gather(in_low[:, inner:], "dp", axis=0, tiled=True)
    small = jnp.concatenate([prenorm, postnorm, convtaps.reshape(-1)]).astype(bf16)
    small = lax.all_gather(small, "dp", axis=0).astype(f32)
    pre_scale = small[:, :own_in].reshape(-1)
    post_scale = small[:, own_in : own_in + own_out].reshape(-1)
    taps = small[:, own_in + own_out :].reshape(group, -1, conv_own)
    taps = jnp.swapaxes(taps, 0, 1).reshape(-1, conv_width)
    tap_rows = taps.shape[0]
    gate_matrix = lax.all_gather(in_low[:, :inner], "dp", axis=0, tiled=True)
    out_matrix = lax.all_gather(outproject.astype(bf16), "dp", axis=0, tiled=True)

    hidden = hidden_in.reshape(rows, model_width).astype(f32)
    cot_low = out_grad.reshape(rows, model_width)
    cot_all = lax.all_gather(cot_low, "dp", axis=0, tiled=True)
    root = lax.rsqrt(jnp.mean(hidden * hidden, axis=-1, keepdims=True) + norm_eps)
    normed_low = (hidden * root * pre_scale).astype(bf16)

    scan_in = jnp.dot(normed_low, scan_matrix, preferred_element_type=f32).astype(bf16)
    pad_heads = ((0, 0), (0, LANES - heads))
    rate = jnp.pad(scan_in[:, conv_width:].astype(f32), pad_heads)
    head_rows = jnp.pad(headcoefs, ((0, 8 - headcoefs.shape[0]), (0, LANES - heads)))
    skip = jnp.repeat(headcoefs[2:3], width, axis=1)
    taps_pad = jnp.pad(taps, ((0, 8 - tap_rows), (0, 0)))
    mixer_low, ypre, enter, halo, step, cum, cumt = scan_forward(
        scan_in, rate, head_rows, skip, taps_pad, sizes
    )

    gate = jnp.dot(normed_low, gate_matrix, preferred_element_type=f32)
    mixer = mixer_low.astype(f32)
    gate_sig = jax.nn.sigmoid(gate)
    gate_act = gate * gate_sig
    gated = mixer * gate_act
    post_root = lax.rsqrt(jnp.mean(gated * gated, axis=-1, keepdims=True) + norm_eps)
    whitened = gated * post_root
    post_low = (whitened * post_scale).astype(bf16)
    output = hidden + jnp.dot(post_low, out_matrix, preferred_element_type=f32)

    post_grad = mm(cot_low, out_matrix, 1, 1)
    postnorm_grad = jnp.sum(post_grad * whitened, axis=0)
    dwhite = post_grad * post_scale
    dgated = post_root * (dwhite - whitened * jnp.mean(dwhite * whitened, axis=-1, keepdims=True))
    dy = (dgated * gate_act).astype(bf16)
    gate_grad = (dgated * mixer * gate_sig * (1.0 + gate * (1.0 - gate_sig))).astype(bf16)

    turn = jnp.concatenate(
        [
            normed_low.T.reshape(group, own_in, rows),
            post_low.T.reshape(group, own_out, rows),
        ],
        axis=1,
    )
    scan_grad, conv_grad, head_grad, turned = scan_backward(
        scan_in, halo, rate, step, cum, cumt, head_rows, skip, taps_pad, dy, ypre, enter, turn, sizes
    )
    normed_grad = mm(gate_grad, gate_matrix, 1, 1) + mm(
        scan_grad[:, : scan_matrix.shape[1]], scan_matrix, 1, 1
    )
    plain = hidden * root
    prenorm_grad = jnp.sum(normed_grad * plain, axis=0)
    dplain = normed_grad * pre_scale
    input_gradient = root * (
        dplain - plain * jnp.mean(dplain * plain, axis=-1, keepdims=True)
    ) + cot_low.astype(f32)

    head_sums = jnp.concatenate(
        [
            head_grad[:2, :heads],
            jnp.sum(conv_grad[tap_rows : tap_rows + 1, :inner].reshape(1, heads, width), axis=-1),
        ],
        axis=0,
    )
    conv_sums = conv_grad[:tap_rows].reshape(tap_rows, group, conv_own)
    packed = jnp.concatenate(
        [
            prenorm_grad.reshape(group, own_in),
            postnorm_grad.reshape(group, own_out),
            jnp.swapaxes(conv_sums, 0, 1).reshape(group, -1),
            jnp.broadcast_to(head_sums.reshape(1, -1), (group, 3 * heads)),
        ],
        axis=1,
    )
    packed_size = packed.shape[1]
    packed_lanes = -(-packed_size // (8 * LANES)) * LANES
    packed = jnp.pad(packed, ((0, 0), (0, 8 * packed_lanes - packed_size)))
    inproj_padded, outproj_owned, packed, _ = reduce_gradients(
        turned, cot_all, gate_grad, scan_grad, packed.reshape(group, 8, packed_lanes), own_in
    )
    inproj_owned = inproj_padded[:, :proj_width]
    packed = packed.reshape(-1)
    prenorm_owned = packed[:own_in]
    postnorm_owned = packed[own_in : own_in + own_out]
    conv_at = own_in + own_out
    conv_end = conv_at + tap_rows * conv_own
    conv_owned = packed[conv_at:conv_end].reshape(tap_rows, conv_own)
    head_total = packed[conv_end:packed_size].reshape(3, heads)

    prenorm_new, prenorm_mom, prenorm_sq = adam_update(
        prenorm, prenorm_first, prenorm_second, prenorm_owned, rate_vector, 0.0
    )
    inproj_new, inproj_mom, inproj_sq = adam_update(
        inproject, inproject_first, inproject_second, inproj_owned, rate_matrix, weight_decay
    )
    conv_new, conv_mom, conv_sq = adam_update(
        convtaps, convtaps_first, convtaps_second, conv_owned, rate_vector, 0.0
    )
    head_new, head_mom, head_sq = adam_update(
        headcoefs, headcoefs_first, headcoefs_second, head_total, rate_vector, 0.0
    )
    postnorm_new, postnorm_mom, postnorm_sq = adam_update(
        postnorm, postnorm_first, postnorm_second, postnorm_owned, rate_vector, 0.0
    )
    outproj_new, outproj_mom, outproj_sq = adam_update(
        outproject, outproject_first, outproject_second, outproj_owned, rate_matrix, weight_decay
    )
    return (
        output.reshape(seq_here, rows, model_width),
        input_gradient.reshape(seq_here, rows, model_width),
        prenorm_owned,
        inproj_owned,
        conv_owned,
        head_total,
        postnorm_owned,
        outproj_owned,
        prenorm_new,
        inproj_new,
        conv_new,
        head_new,
        postnorm_new,
        outproj_new,
        prenorm_mom,
        inproj_mom,
        conv_mom,
        head_mom,
        postnorm_mom,
        outproj_mom,
        prenorm_sq,
        inproj_sq,
        conv_sq,
        head_sq,
        postnorm_sq,
        outproj_sq,
    )


def solution(mesh):
    weights = (P("dp"), P("dp", None), P(None, "dp"), P(), P("dp"), P("dp", None))
    tokens = (P("dp", "seq", None), P("dp", "seq", None))
    return jax.shard_map(
        on_device,
        mesh=mesh,
        in_specs=tokens + weights * 3,
        out_specs=tokens + weights * 4,
        check_vma=False,
    )
```

```python
import functools

import jax
import jax.numpy as jnp
from jax import lax
from jax.experimental import pallas as pl
from jax.experimental.pallas import tpu as pltpu
from jax.sharding import PartitionSpec as P

N = 128
LANES = 128
HALO = 16
WIDE = 256
HEIGHT = 32

norm_eps = 1e-05
beta_moment = 0.9
beta_square = 0.95
adam_eps = 1e-08
adam_step = 3.0
rate_matrix = 0.005
rate_vector = 0.05
weight_decay = 0.1

f32 = jnp.float32
bf16 = jnp.bfloat16
MESH = pl.DeviceIdType.MESH


def adam_update(weight, moment, square, gradient, step_rate, decay_rate):
    moment_new = beta_moment * moment + (1.0 - beta_moment) * gradient
    square_new = beta_square * square + (1.0 - beta_square) * gradient * gradient
    moment_hat = moment_new / (1.0 - beta_moment**adam_step)
    square_hat = square_new / (1.0 - beta_square**adam_step)
    updated = weight - step_rate * (
        moment_hat / (jnp.sqrt(square_hat) + adam_eps) + decay_rate * weight
    )
    return (updated, moment_new, square_new)


def mm(a, b, ca, cb):
    return lax.dot_general(a, b, (((ca,), (cb,)), ((), ())), preferred_element_type=f32)


def halves(a):
    hi = a.astype(bf16)
    return hi, (a - hi.astype(f32)).astype(bf16)


def thirds(a):
    hi = a.astype(bf16)
    rest = a - hi.astype(f32)
    mid = rest.astype(bf16)
    return hi, mid, (rest - mid.astype(f32)).astype(bf16)


def mm3(a, b, ca, cb):
    return mm(a[0], b[0], ca, cb) + mm(a[0], b[1], ca, cb) + mm(a[1], b[0], ca, cb)


def iota(shape, dim):
    return lax.broadcasted_iota(jnp.int32, shape, dim)


def head_lanes(tile, heads_a_tile, copies):
    rows = iota((copies * LANES, LANES), 0)
    lane_head = tile * heads_a_tile + iota((copies * LANES, LANES), 1) // (LANES // heads_a_tile)
    return (rows % LANES == lane_head).astype(f32).astype(bf16)


def conv_tile(conv_ref, halo_ref, u_ref, taps_ref, start, rows):
    cols = pl.ds(start, LANES)
    conv_ref[0:HALO, :] = halo_ref[:, cols].astype(f32)
    conv_ref[HALO : HALO + rows, :] = u_ref[:, cols].astype(f32)
    taps = taps_ref[:, cols]
    pre = taps[4:5, :] + taps[0:1, :] * conv_ref[HALO - 3 : HALO - 3 + rows, :]
    for k in range(1, 4):
        pre = pre + taps[k : k + 1, :] * conv_ref[HALO - 3 + k : HALO - 3 + k + rows, :]
    return pre, jax.nn.sigmoid(pre)


def seq_copy(src, dst, send, recv, to):
    return pltpu.make_async_remote_copy(
        src_ref=src,
        dst_ref=dst,
        send_sem=send,
        recv_sem=recv,
        device_id={"seq": to},
        device_id_type=MESH,
    )


def greet_seq(barrier, rank, last):
    @pl.when(rank > 0)
    def _():
        pl.semaphore_signal(barrier, inc=1, device_id={"seq": rank - 1}, device_id_type=MESH)

    @pl.when(rank < last)
    def _():
        pl.semaphore_signal(barrier, inc=1, device_id={"seq": rank + 1}, device_id_type=MESH)


def seq_neighbours(rank, last):
    return jnp.minimum(rank, 1) + jnp.minimum(last - rank, 1)


def greet_plane(barrier, me, group):
    for i in range(1, group):
        pl.semaphore_signal(
            barrier, inc=1, device_id={"dp": lax.rem(me + i, group)}, device_id_type=MESH
        )


def slot_of(device, group):
    return lax.rem(device, 2) * (group // 2) + device // 2


def ring_place(at, chips):
    half = chips // 2
    turned = at // half
    return at * (1 - turned) + turned * (3 * half - 1 - at)


def front_kernel(
    sizes,
    in_shard_ref,
    out_shard_ref,
    small_ref,
    hidden_ref,
    cot_ref,
    heads_ref,
    skip_ref,
    u_ref,
    ypre_ref,
    enter_ref,
    halo_ref,
    step_ref,
    cum_ref,
    cumt_ref,
    taps_ref,
    pre_scale_ref,
    dy_ref,
    gate_grad_ref,
    post_grad_ref,
    post_ref,
    normed_t_ref,
    post_t_ref,
    token_ref,
    scan_all_ref,
    gate_all_ref,
    out_all_ref,
    in_wide_ref,
    out_wide_ref,
    scan_shard_ref,
    gate_shard_ref,
    out_low_ref,
    small_all_ref,
    post_scale_ref,
    normed_ref,
    weights_ref,
    out_weights_ref,
    conv_ref,
    score_ref,
    leave_ref,
    mixer_ref,
    gate_ref,
    gated_ref,
    dpost_ref,
    send_sem,
    recv_sem,
    halo_sem,
    small_send,
    small_recv,
    wide_sem,
    weight_sem,
    *ring_sems,
):
    rows, inner, tiles, per_tile = sizes
    conv_width = inner + 2 * N
    own_in = in_shard_ref.shape[0]
    own_out, model_width = out_shard_ref.shape
    scan_width = in_shard_ref.shape[1] - inner
    rank = lax.axis_index("seq")
    last = lax.axis_size("seq") - 1
    me = lax.axis_index("dp")
    group = lax.axis_size("dp")
    in_chunks = own_in // HEIGHT
    out_height = 2 * HEIGHT
    out_chunks = own_out // out_height

    def wide_rows(chunk):
        return pl.ds(pl.multiple_of(chunk * HEIGHT, HEIGHT), HEIGHT)

    def in_wide(chunk):
        some = wide_rows(chunk)
        return pltpu.make_async_copy(
            in_shard_ref.at[some, :], in_wide_ref.at[some, :], wide_sem.at[chunk]
        )

    out_wide = pltpu.make_async_copy(out_shard_ref, out_wide_ref, wide_sem.at[in_chunks])
    for chunk in range(in_chunks):
        in_wide(chunk).start()
    out_wide.start()
    barrier = pltpu.get_barrier_semaphore()
    greet_seq(barrier, rank, last)
    greet_plane(barrier, me, group)
    pl.semaphore_wait(barrier, seq_neighbours(rank, last) + group - 1)
    right = jnp.minimum(rank + 1, last)
    left = jnp.maximum(rank - 1, 0)

    def small_copy(i, peer, slot):
        return plane_copy(
            small_ref, small_all_ref.at[slot], small_send.at[i], small_recv.at[i], peer
        )

    for i in range(1, group):
        small_copy(i, lax.rem(me + i, group), me).start()
    small_all_ref[me] = small_ref[...]
    scan_shard_ref[:, scan_width - scan_width % LANES :] = jnp.zeros(
        (own_in, scan_shard_ref.shape[1] - scan_width + scan_width % LANES), bf16
    )

    def prepare_scan(chunk):
        some = wide_rows(chunk)
        in_wide(chunk).wait()
        scan_shard_ref[some, 0:scan_width] = in_wide_ref[some, inner:].astype(bf16)

    def prepare_gate(chunk):
        some = wide_rows(chunk)
        gate_shard_ref[some, :] = in_wide_ref[some, 0:inner].astype(bf16)

    def prepare_out(chunk):
        @pl.when(chunk == 0)
        def _():
            out_wide.wait()

        some = pl.ds(pl.multiple_of(chunk * out_height, out_height), out_height)
        out_low_ref[some, :] = out_wide_ref[some, :].astype(bf16)

    scan_ring = weight_ring(scan_shard_ref, scan_all_ref, HEIGHT, ring_sems[0:5], prepare_scan)
    gate_ring = weight_ring(gate_shard_ref, gate_all_ref, HEIGHT, ring_sems[5:10], prepare_gate)
    out_ring = weight_ring(out_low_ref, out_all_ref, out_height, ring_sems[10:15], prepare_out)
    spacing = 2
    rings = (
        (scan_ring, 0, in_chunks),
        (gate_ring, in_chunks, in_chunks),
        (out_ring, 2 * in_chunks, out_chunks),
    )

    def round_(step):
        for ring, first, chunks in rings:
            ring.round(step - first, chunks, spacing)

    def rounds(first, end):
        def one(step, carry):
            round_(step)
            return carry

        lax.fori_loop(first, end, one, 0)

    def complete(at):
        ring, first, chunks = rings[at]
        return first + chunks + spacing * ring.reach

    def wait_pairs(at):
        ring, _, chunks = rings[at]

        def one(chunk, carry):
            ring.wait_pair(chunk)
            return carry

        lax.fori_loop(0, chunks, one, 0)

    rounds(0, 2)

    for i in range(1, group):
        small_copy(i, lax.rem(me + i, group), me).wait_send()
        small_copy(i, me, lax.rem(me + group - i, group)).wait_recv()
    conv_own = conv_width // group
    taps_ref[...] = jnp.zeros_like(taps_ref)
    for device in range(group):
        small = small_all_ref[device].astype(f32)
        pre_scale_ref[0:1, device * own_in : (device + 1) * own_in] = small[0:1, 0:own_in]
        taps_ref[0:5, device * conv_own : (device + 1) * conv_own] = small[1:6, 0:conv_own]
        post_scale_ref[0:1, device * own_out : (device + 1) * own_out] = small[6:7, 0:own_out]
    pre_scale_ref[1:8, :] = jnp.zeros((7, model_width), f32)
    token_ref[...] = jnp.zeros_like(token_ref)

    def norm(at, carry):
        some = pl.ds(pl.multiple_of(at * HEIGHT, HEIGHT), HEIGHT)
        hidden = hidden_ref[some, :].astype(f32)
        root = lax.rsqrt(jnp.mean(hidden * hidden, axis=-1, keepdims=True) + norm_eps)
        normed_ref[some, :] = (hidden * root * pre_scale_ref[0:1, :]).astype(bf16)
        return carry

    lax.fori_loop(0, rows // HEIGHT, norm, 0)

    def turn(source_ref, target_ref):
        def one(at, carry):
            cols = pl.ds(pl.multiple_of(at * LANES, LANES), LANES)
            target_ref[cols, :] = source_ref[:, cols].astype(f32).T.astype(bf16)
            return carry

        lax.fori_loop(0, source_ref.shape[1] // LANES, one, 0)

    turn(normed_ref, normed_t_ref)
    rounds(2, complete(0))
    wait_pairs(0)

    def weight_copy(all_ref, at, width):
        slot = lax.rem(at, 2)
        cols = pl.ds(pl.multiple_of(at * WIDE, WIDE), width)
        return pltpu.make_async_copy(
            all_ref.at[:, :, :, cols],
            weights_ref.at[slot, :, :, :, pl.ds(0, width)],
            weight_sem.at[slot],
        )

    def columns(all_ref, action):
        total = all_ref.shape[3]
        full = total // WIDE
        rest = total % WIDE

        def fetch(at, act):
            @pl.when(at < full)
            def _():
                act(weight_copy(all_ref, at, WIDE))

            if rest:

                @pl.when(at == full)
                def _():
                    act(weight_copy(all_ref, at, rest))

        fetch(0, lambda copy: copy.start())

        def one(at, carry):
            fetch(at + 1, lambda copy: copy.start())
            fetch(at, lambda copy: copy.wait())
            weights = weights_ref[lax.rem(at, 2)].reshape(model_width, WIDE)
            action(at, WIDE, mm(normed_ref[...], weights, 1, 0))
            return carry

        lax.fori_loop(0, full, one, 0)
        if rest:
            fetch(full, lambda copy: copy.wait())
            weights = weights_ref[full % 2, :, :, :, 0:rest].reshape(model_width, rest)
            action(full, rest, mm(normed_ref[...], weights, 1, 0))

    def keep_scan(at, width, product):
        cols = pl.ds(at * WIDE if isinstance(at, int) else pl.multiple_of(at * WIDE, WIDE), width)
        u_ref[:, cols] = product.astype(bf16)

    columns(scan_all_ref, keep_scan)
    halo_copy = seq_copy(
        u_ref.at[pl.ds(rows - HALO, HALO), pl.ds(0, conv_width)],
        halo_ref,
        halo_sem.at[0],
        halo_sem.at[1],
        right,
    )

    @pl.when(rank < last)
    def _():
        halo_copy.start()

    round_(complete(0))
    step = jax.nn.softplus(u_ref[:, conv_width:].astype(f32) + heads_ref[0:1, :])
    decay = -step * jnp.exp(heads_ref[1:2, :])
    lower = (iota((rows, rows), 0) >= iota((rows, rows), 1)).astype(f32).astype(bf16)
    cum = sum(mm(lower, part, 1, 0) for part in thirds(decay))
    step_ref[...] = step
    cum_ref[...] = cum
    cumt_ref[...] = cum.T

    @pl.when(rank > 0)
    def _():
        halo_copy.wait_recv()

    @pl.when(rank == 0)
    def _():
        halo_ref[...] = jnp.zeros_like(halo_ref)

    pre_b, sig_b = conv_tile(conv_ref, halo_ref, u_ref, taps_ref, inner, rows)
    b_parts = halves(pre_b * sig_b)
    pre_c, sig_c = conv_tile(conv_ref, halo_ref, u_ref, taps_ref, inner + N, rows)
    c_parts = halves(pre_c * sig_c)
    scores = mm3(c_parts, b_parts, 1, 1)
    causal = iota((rows, rows), 0) >= iota((rows, rows), 1)
    score_ref[...] = jnp.where(causal, scores, 0.0)
    cum_parts = jnp.concatenate(thirds(cum), axis=1)
    step_parts = jnp.concatenate(thirds(step), axis=1)
    lane = iota((rows, LANES), 1)
    width = LANES // per_tile

    def chain(tile):
        return seq_copy(
            leave_ref.at[tile], enter_ref.at[tile], send_sem.at[tile], recv_sem.at[tile], right
        )

    def one(tile, carry):
        start = pl.multiple_of(tile * LANES, LANES)
        cols = pl.ds(start, LANES)
        pick = head_lanes(tile, per_tile, 3)
        cum_l = mm(cum_parts, pick, 1, 0)
        step_l = mm(step_parts, pick, 1, 0)
        pre, sig = conv_tile(conv_ref, halo_ref, u_ref, taps_ref, start, rows)
        values = pre * sig
        x = values * step_l
        total = cum_l[rows - 1 : rows, :]
        fresh = mm3(b_parts, halves(x * jnp.exp(total - cum_l)), 0, 0)

        @pl.when(rank > 0)
        def _():
            chain(tile).wait_recv()

        @pl.when(rank == 0)
        def _():
            enter_ref[tile] = jnp.zeros((N, LANES), f32)

        enter = enter_ref[tile]
        leave_ref[tile] = jnp.exp(total) * enter + fresh

        @pl.when(rank < last)
        def _():
            chain(tile).start()

        result = mm3(c_parts, halves(enter), 1, 0) * jnp.exp(cum_l)
        for h in range(per_tile):
            row = cumt_ref[pl.ds(tile * per_tile + h, 1), :]
            col = cum_l[:, h * width : h * width + 1]
            kernel = jnp.exp(jnp.minimum(col - row, 0.0)) * score_ref[...]
            own = (lane // width) == h
            result = result + mm3(halves(kernel), halves(jnp.where(own, x, 0.0)), 1, 0)
        ypre_ref[:, cols] = result
        mixer_ref[:, cols] = (result + skip_ref[0:1, cols] * values).astype(bf16)

        @pl.when(lax.rem(tile, pace) == pace - 1)
        def _():
            round_(in_loop + tile // pace)

        return carry

    in_loop = complete(0) + 1
    pace = 4
    lax.fori_loop(0, tiles, one, 0)
    at_round = in_loop + tiles // pace
    rounds(at_round, max(at_round, complete(1)))
    at_round = max(at_round, complete(1))
    wait_pairs(1)

    gated_ref_sum = score_ref

    def keep_gate(at, width, product):
        cols = pl.ds(at * WIDE if isinstance(at, int) else pl.multiple_of(at * WIDE, WIDE), width)
        gated = mixer_ref[:, cols].astype(f32) * (product * jax.nn.sigmoid(product))
        gate_ref[:, cols] = product
        gated_ref[:, cols] = gated
        square = gated * gated
        total = square[:, 0:LANES]
        for part in range(1, width // LANES):
            total = total + square[:, part * LANES : (part + 1) * LANES]
        gated_ref_sum[:, 0:LANES] += total

    gated_ref_sum[:, 0:LANES] = jnp.zeros((rows, LANES), f32)
    columns(gate_all_ref, keep_gate)
    end_round = complete(2)
    rounds(at_round, min(at_round + 1, end_round))
    at_round = min(at_round + 1, end_round)
    root = lax.rsqrt(
        jnp.sum(gated_ref_sum[:, 0:LANES], axis=-1, keepdims=True) / inner + norm_eps
    )

    def keep_post(at, carry):
        cols = pl.ds(pl.multiple_of(at * WIDE, WIDE), WIDE)
        whitened = gated_ref[:, cols] * root
        gated_ref[:, cols] = whitened
        post_ref[:, cols] = (whitened * post_scale_ref[0:1, cols]).astype(bf16)
        return carry

    lax.fori_loop(0, inner // WIDE, keep_post, 0)
    turn(post_ref, post_t_ref)
    rounds(at_round, end_round)
    wait_pairs(2)

    span = 2 * own_out

    def out_copy(chip):
        slot = chip % 2
        return pltpu.make_async_copy(
            out_all_ref.at[chip], out_weights_ref.at[slot], weight_sem.at[slot]
        )

    out_copy(0).start()
    overlap = jnp.zeros((rows, LANES), f32)
    for chip in range(group // 2):
        if chip + 1 < group // 2:
            out_copy(chip + 1).start()
        out_copy(chip).wait()
        cols = slice(chip * span, (chip + 1) * span)
        weights = out_weights_ref[chip % 2].reshape(span, model_width)
        dpost = mm(cot_ref[...], weights, 1, 1)
        dpost_ref[:, cols] = dpost
        pulled = dpost * gated_ref[:, cols]
        post_grad_ref[0:1, cols] = jnp.sum(pulled, axis=0, keepdims=True)
        pulled = pulled * post_scale_ref[0:1, cols]
        for part in range(span // LANES):
            overlap = overlap + pulled[:, part * LANES : (part + 1) * LANES]
    mean = jnp.sum(overlap, axis=-1, keepdims=True) / inner

    def keep_back(at, carry):
        cols = pl.ds(pl.multiple_of(at * WIDE, WIDE), WIDE)
        gate = gate_ref[:, cols]
        sig = jax.nn.sigmoid(gate)
        dgated = root * (dpost_ref[:, cols] * post_scale_ref[0:1, cols] - gated_ref[:, cols] * mean)
        dy_ref[:, cols] = (dgated * (gate * sig)).astype(bf16)
        gate_grad_ref[:, cols] = (
            dgated * mixer_ref[:, cols].astype(f32) * sig * (1.0 + gate * (1.0 - sig))
        ).astype(bf16)
        return carry

    lax.fori_loop(0, inner // WIDE, keep_back, 0)

    @pl.when(rank < last)
    def _():
        halo_copy.wait_send()

        def drain(tile, carry):
            chain(tile).wait_send()
            return carry

        lax.fori_loop(0, tiles, drain, 0)

    for ring, _, chunks in rings:

        def finish(chunk, carry, ring=ring):
            ring.finish(chunk)
            return carry

        lax.fori_loop(0, chunks, finish, 0)


def backward_kernel(
    sizes,
    u_ref,
    halo_ref,
    step_ref,
    cum_ref,
    cumt_ref,
    heads_ref,
    skip_ref,
    taps_ref,
    dy_ref,
    ypre_ref,
    enter_ref,
    normed_t_ref,
    post_t_ref,
    dproj_ref,
    conv_grad_ref,
    head_grad_ref,
    turned_ref,
    conv_ref,
    score_ref,
    dscore_ref,
    dread_ref,
    dwrite_ref,
    dcum_ref,
    dstep_ref,
    dpre_ref,
    leave_ref,
    arrive_ref,
    send_sem,
    recv_sem,
    halo_sem,
    turn_send,
    turn_recv,
    own_sem,
):
    rows, inner, tiles, per_tile = sizes
    conv_width = inner + 2 * N
    rank = lax.axis_index("seq")
    last = lax.axis_size("seq") - 1
    me = lax.axis_index("dp")
    group = lax.axis_size("dp")
    barrier = pltpu.get_barrier_semaphore()
    greet_seq(barrier, rank, last)
    greet_plane(barrier, me, group)
    pl.semaphore_wait(barrier, seq_neighbours(rank, last) + group - 1)

    own_in = normed_t_ref.shape[0] // group
    own_out = post_t_ref.shape[0] // group
    turns = ((normed_t_ref, 0, own_in), (post_t_ref, own_in, own_out))

    def landing(device, which):
        _, first, height = turns[which]
        cols = pl.ds(pl.multiple_of(slot_of(device, group) * rows, rows), rows)
        return turned_ref.at[pl.ds(first, height), cols]

    def leaving(device, which):
        source, _, height = turns[which]
        return source.at[pl.ds(pl.multiple_of(device * height, height), height), :]

    def turn(i, which, peer, source):
        return plane_copy(
            leaving(peer, which),
            landing(source, which),
            turn_send.at[i, which],
            turn_recv.at[i, which],
            peer,
        )

    own_copies = [
        pltpu.make_async_copy(leaving(me, which), landing(me, which), own_sem.at[which])
        for which in range(2)
    ]
    for which in range(2):
        for i in range(1, group):
            turn(i, which, lax.rem(me + i, group), me).start()
        own_copies[which].start()

    left = jnp.maximum(rank - 1, 0)
    cum = cum_ref[...]
    step = step_ref[...]
    pre_b, sig_b = conv_tile(conv_ref, halo_ref, u_ref, taps_ref, inner, rows)
    b_parts = halves(pre_b * sig_b)
    pre_c, sig_c = conv_tile(conv_ref, halo_ref, u_ref, taps_ref, inner + N, rows)
    c_parts = halves(pre_c * sig_c)
    later = iota((rows, rows), 1) >= iota((rows, rows), 0)
    score_ref[...] = jnp.where(later, mm3(b_parts, c_parts, 1, 1), 0.0)
    dscore_ref[...] = jnp.zeros_like(dscore_ref)
    dread_ref[...] = jnp.zeros_like(dread_ref)
    dwrite_ref[...] = jnp.zeros_like(dwrite_ref)
    dcum_ref[...] = jnp.zeros_like(dcum_ref)
    dstep_ref[...] = jnp.zeros_like(dstep_ref)
    cum_parts = jnp.concatenate(thirds(cum), axis=1)
    step_parts = jnp.concatenate(thirds(step), axis=1)
    lane = iota((rows, LANES), 1)
    final_row = iota((rows, LANES), 0) == rows - 1
    width = LANES // per_tile

    def chain(tile):
        return seq_copy(
            leave_ref.at[tile], arrive_ref.at[tile], send_sem.at[tile], recv_sem.at[tile], left
        )

    def tap_grads(dpre, extra):
        sums = [
            jnp.sum(
                dpre * conv_ref[HALO - 3 + k : HALO - 3 + k + rows, :], axis=0, keepdims=True
            )
            for k in range(4)
        ]
        sums.append(jnp.sum(dpre, axis=0, keepdims=True))
        sums.append(extra)
        sums.append(jnp.zeros((2, LANES), f32))
        return jnp.concatenate(sums, axis=0)

    def one(tile, carry):
        start = pl.multiple_of(tile * LANES, LANES)
        cols = pl.ds(start, LANES)
        pick = head_lanes(tile, per_tile, 3)
        cum_l = mm(cum_parts, pick, 1, 0)
        step_l = mm(step_parts, pick, 1, 0)
        total = cum_l[rows - 1 : rows, :]
        dy = dy_ref[:, cols].astype(f32)
        reads = halves(dy * jnp.exp(cum_l))
        denter = mm3(c_parts, reads, 0, 0)

        @pl.when(rank < last)
        def _():
            chain(tile).wait_recv()

        @pl.when(rank == last)
        def _():
            arrive_ref[tile] = jnp.zeros((N, LANES), f32)

        arrive = arrive_ref[tile]
        leave_ref[tile] = jnp.exp(total) * arrive + denter

        @pl.when(rank > 0)
        def _():
            chain(tile).start()

        pre, sig = conv_tile(conv_ref, halo_ref, u_ref, taps_ref, start, rows)
        values = pre * sig
        x = values * step_l
        x_parts = halves(x)
        tail = jnp.exp(total - cum_l)
        enter = enter_ref[tile]
        arrive_parts = halves(arrive)
        dx_state = mm3(b_parts, arrive_parts, 1, 0) * tail
        dx = dx_state
        for h in range(per_tile):
            row = cumt_ref[pl.ds(tile * per_tile + h, 1), :]
            col = cum_l[:, h * width : h * width + 1]
            spread = jnp.exp(jnp.minimum(row - col, 0.0))
            kernel = halves(spread * score_ref[...])
            own = jnp.where((lane // width) == h, dy, 0.0).astype(bf16)
            dx = dx + (mm(kernel[0], own, 1, 0) + mm(kernel[1], own, 1, 0))
            pairs = mm(x_parts[0], own, 1, 1) + mm(x_parts[1], own, 1, 1)
            dscore_ref[...] += spread * pairs
        dread_ref[...] += mm3(reads, halves(enter), 1, 1)
        dwrite_ref[...] += mm3(halves(x * tail), arrive_parts, 1, 1)
        ends = jnp.sum(x * dx_state, axis=0, keepdims=True) + jnp.exp(total) * jnp.sum(
            enter * arrive, axis=0, keepdims=True
        )
        dcum = dy * ypre_ref[:, cols] - x * dx + jnp.where(final_row, ends, 0.0)
        own_head = pick[0:LANES, :]
        for part in halves(dcum):
            dcum_ref[...] += mm(part, own_head, 1, 1)
        for part in halves(dx * values):
            dstep_ref[...] += mm(part, own_head, 1, 1)
        dvalues = step_l * dx + skip_ref[0:1, cols] * dy
        dpre = dvalues * sig * (1.0 + pre * (1.0 - sig))
        dpre_ref[0:rows, cols] = dpre
        conv_grad_ref[:, cols] = tap_grads(dpre, jnp.sum(dy * values, axis=0, keepdims=True))
        return carry

    lax.fori_loop(0, tiles, one, 0)

    dscore = halves(jnp.where(later, dscore_ref[...], 0.0))
    dshared = (
        dwrite_ref[...] + mm3(dscore, c_parts, 1, 0),
        dread_ref[...] + mm3(dscore, b_parts, 0, 0),
    )
    for i in range(2):
        start = inner + i * N
        pre, sig = conv_tile(conv_ref, halo_ref, u_ref, taps_ref, start, rows)
        dpre = dshared[i] * sig * (1.0 + pre * (1.0 - sig))
        dpre_ref[0:rows, start : start + N] = dpre
        conv_grad_ref[:, start : start + N] = tap_grads(dpre, jnp.zeros((1, LANES), f32))

    edge = seq_copy(
        dpre_ref.at[pl.ds(0, 8), :],
        dpre_ref.at[pl.ds(rows, 8), :],
        halo_sem.at[0],
        halo_sem.at[1],
        left,
    )

    @pl.when(rank > 0)
    def _():
        edge.start()

    upper = (iota((rows, rows), 1) >= iota((rows, rows), 0)).astype(f32).astype(bf16)
    ddecay = sum(mm(upper, part, 1, 0) for part in thirds(dcum_ref[...]))
    exp_rate = jnp.exp(heads_ref[1:2, :])
    drate = (dstep_ref[...] - ddecay * exp_rate) * jax.nn.sigmoid(
        u_ref[:, conv_width:].astype(f32) + heads_ref[0:1, :]
    )
    head_grad_ref[...] = jnp.concatenate(
        [
            jnp.sum(drate, axis=0, keepdims=True),
            jnp.sum(ddecay * (-step * exp_rate), axis=0, keepdims=True),
            jnp.zeros((6, LANES), f32),
        ],
        axis=0,
    )
    dproj_ref[:, conv_width : conv_width + LANES] = drate.astype(bf16)
    dproj_ref[:, conv_width + LANES :] = jnp.zeros(
        (rows, dproj_ref.shape[1] - conv_width - LANES), bf16
    )

    @pl.when(rank == last)
    def _():
        dpre_ref[rows : rows + 8, :] = jnp.zeros((8, conv_width), f32)

    @pl.when(rank < last)
    def _():
        edge.wait_recv()

    def unconv(tile, carry):
        cols = pl.ds(pl.multiple_of(tile * LANES, LANES), LANES)
        taps = taps_ref[:, cols]
        du = taps[3:4, :] * dpre_ref[0:rows, cols]
        for k in range(3):
            du = du + taps[k : k + 1, :] * dpre_ref[3 - k : 3 - k + rows, cols]
        dproj_ref[:, cols] = du.astype(bf16)
        return carry

    lax.fori_loop(0, conv_width // LANES, unconv, 0)

    @pl.when(rank > 0)
    def _():
        edge.wait_send()

        def drain(tile, carry):
            chain(tile).wait_send()
            return carry

        lax.fori_loop(0, tiles, drain, 0)

    for which in range(2):
        own_copies[which].wait()
        for i in range(1, group):
            turn(i, which, lax.rem(me + i, group), me).wait_send()
            origin = lax.rem(me + group - i, group)
            turn(i, which, origin, origin).wait_recv()


def vmem(count):
    return [pl.BlockSpec(memory_space=pltpu.VMEM)] * count


def front(in_shard, out_shard, small, hidden, cot, heads, skip, sizes):
    rows, inner, tiles, _ = sizes
    conv_width = inner + 2 * N
    shape = jax.ShapeDtypeStruct
    group = lax.axis_size("dp")
    own_in, proj_width = in_shard.shape
    own_out, model_width = out_shard.shape
    scan_width = -(-(proj_width - inner) // LANES) * LANES
    in_chunks = own_in // HEIGHT
    out_chunks = own_out // (2 * HEIGHT)
    anywhere = pl.BlockSpec(memory_space=pl.ANY)
    dma = pltpu.SemaphoreType.DMA
    return pl.pallas_call(
        functools.partial(front_kernel, sizes),
        out_shape=(
            shape((rows, scan_width), bf16),
            shape((rows, inner), f32),
            shape((tiles, N, LANES), f32),
            shape((HALO, conv_width), bf16),
            shape((rows, LANES), f32),
            shape((rows, LANES), f32),
            shape((LANES, rows), f32),
            shape((8, conv_width), f32),
            shape((8, model_width), f32),
            shape((rows, inner), bf16),
            shape((rows, inner), bf16),
            shape((1, inner), f32),
            shape((rows, inner), bf16),
            shape((model_width, rows), bf16),
            shape((inner, rows), bf16),
            shape((8, LANES), f32),
            shape((group // 2, 2, own_in, scan_width), bf16),
            shape((group // 2, 2, own_in, inner), bf16),
            shape((group // 2, 2, own_out, model_width), bf16),
        ),
        in_specs=[anywhere] * 2 + vmem(5),
        out_specs=tuple(vmem(16) + [anywhere] * 3),
        scratch_shapes=[
            pltpu.VMEM(in_shard.shape, f32),
            pltpu.VMEM(out_shard.shape, f32),
            pltpu.VMEM((own_in, scan_width), bf16),
            pltpu.VMEM((own_in, inner), bf16),
            pltpu.VMEM((own_out, model_width), bf16),
            pltpu.VMEM((group,) + small.shape, bf16),
            pltpu.VMEM((1, inner), f32),
            pltpu.VMEM((rows, model_width), bf16),
            pltpu.VMEM((2, group // 2, 2, own_in, WIDE), bf16),
            pltpu.VMEM((2, 2, own_out, model_width), bf16),
            pltpu.VMEM((HALO + rows, LANES), f32),
            pltpu.VMEM((rows, rows), f32),
            pltpu.VMEM((tiles, N, LANES), f32),
            pltpu.VMEM((rows, inner), bf16),
            pltpu.VMEM((rows, inner), f32),
            pltpu.VMEM((rows, inner), f32),
            pltpu.VMEM((rows, inner), f32),
            dma((tiles,)),
            dma((tiles,)),
            dma((2,)),
            dma((group,)),
            dma((group,)),
            dma((in_chunks + 1,)),
            dma((2,)),
        ]
        + PlaneRing.semaphores(in_chunks)
        + PlaneRing.semaphores(in_chunks)
        + PlaneRing.semaphores(out_chunks),
        compiler_params=pltpu.CompilerParams(
            collective_id=1, has_side_effects=True, vmem_limit_bytes=58 * 2**20
        ),
        cost_estimate=pl.CostEstimate(
            flops=10**10, bytes_accessed=10**8, transcendentals=4 * 10**6
        ),
    )(in_shard, out_shard, small, hidden, cot, heads, skip)


def scan_backward(
    u, halo, step, cum, cumt, heads, skip, taps, dy, ypre, enter, normed_t, post_t, sizes
):
    rows, inner, tiles, _ = sizes
    conv_width = inner + 2 * N
    shape = jax.ShapeDtypeStruct
    group = lax.axis_size("dp")
    turn_rows = (normed_t.shape[0] + post_t.shape[0]) // group
    return pl.pallas_call(
        functools.partial(backward_kernel, sizes),
        out_shape=(
            shape((rows, -(-u.shape[1] // WIDE) * WIDE), bf16),
            shape((8, conv_width), f32),
            shape((8, LANES), f32),
            shape((turn_rows, group * rows), bf16),
        ),
        in_specs=vmem(11) + [pl.BlockSpec(memory_space=pl.ANY)] * 2,
        out_specs=tuple(vmem(3) + [pl.BlockSpec(memory_space=pl.ANY)]),
        scratch_shapes=[
            pltpu.VMEM((HALO + rows, LANES), f32),
            pltpu.VMEM((rows, rows), f32),
            pltpu.VMEM((rows, rows), f32),
            pltpu.VMEM((rows, N), f32),
            pltpu.VMEM((rows, N), f32),
            pltpu.VMEM((rows, LANES), f32),
            pltpu.VMEM((rows, LANES), f32),
            pltpu.VMEM((rows + 8, conv_width), f32),
            pltpu.VMEM((tiles, N, LANES), f32),
            pltpu.VMEM((tiles, N, LANES), f32),
            pltpu.SemaphoreType.DMA((tiles,)),
            pltpu.SemaphoreType.DMA((tiles,)),
            pltpu.SemaphoreType.DMA((2,)),
            pltpu.SemaphoreType.DMA((group, 2)),
            pltpu.SemaphoreType.DMA((group, 2)),
            pltpu.SemaphoreType.DMA((2,)),
        ],
        compiler_params=pltpu.CompilerParams(
            collective_id=2, has_side_effects=True, vmem_limit_bytes=40 * 2**20
        ),
        cost_estimate=pl.CostEstimate(flops=6 * 10**9, bytes_accessed=2 * 10**7, transcendentals=4 * 10**6),
    )(u, halo, step, cum, cumt, heads, skip, taps, dy, ypre, enter, normed_t, post_t)


def plane_copy(src, dst, send, recv, to):
    return pltpu.make_async_remote_copy(
        src_ref=src,
        dst_ref=dst,
        send_sem=send,
        recv_sem=recv,
        device_id={"dp": to},
        device_id_type=MESH,
    )


class PlaneRing:
    def __init__(self, block, source, pair_block, sems, prepare=None):
        group = lax.axis_size("dp")
        me = lax.axis_index("dp")
        self.block, self.source, self.pair_block = block, source, pair_block
        self.prepare = prepare
        self.ring_send, self.ring_recv, self.pair_send, self.pair_recv, self.own_sem = sems
        self.chips = group // 2
        self.reach = self.chips // 2
        self.me = me
        self.core = lax.rem(me, 2)
        self.chip = me // 2
        self.place = ring_place(self.chip, self.chips)

    @staticmethod
    def semaphores(chunks):
        group = lax.axis_size("dp")
        dma = pltpu.SemaphoreType.DMA
        return [dma((chunks, group // 2)), dma((chunks, group // 2))] + [dma((chunks,))] * 3

    def ring_chip(self, ahead):
        return ring_place(lax.rem(self.place + ahead + self.chips, self.chips), self.chips)

    def part(self, number, way):
        return None if number < self.reach else (0 if way == 1 else 1)

    def copy(self, chunk, number, way, origin, source=None):
        block = self.block(chunk, origin, self.part(number, way))
        at = 2 * (number - 1) + (0 if way == 1 else 1)
        return plane_copy(
            block if source is None else source,
            block,
            self.ring_send.at[chunk, at],
            self.ring_recv.at[chunk, at],
            2 * self.ring_chip(way) + self.core,
        )

    def hop(self, chunk, number, way, source=None):
        return self.copy(chunk, number, way, self.ring_chip(-way * (number - 1)), source)

    def hop_in(self, chunk, number, way):
        return self.copy(chunk, number, way, self.ring_chip(-way * number))

    def own_copy(self, chunk, source):
        return pltpu.make_async_copy(
            source, self.block(chunk, self.chip, None), self.own_sem.at[chunk]
        )

    def pair_copy(self, chunk, core):
        block = self.pair_block(chunk, core)
        return plane_copy(
            block,
            block,
            self.pair_send.at[chunk],
            self.pair_recv.at[chunk],
            self.me + 1 - 2 * self.core,
        )

    def stage(self, chunk, number):
        if number == 0:
            if self.prepare is not None:
                self.prepare(chunk)
            self.source(chunk, None, lambda ref: self.own_copy(chunk, ref).start())
            for way in (1, -1):
                self.source(
                    chunk,
                    self.part(1, way),
                    lambda ref, way=way: self.hop(chunk, 1, way, ref).start(),
                )
            return
        for way in (1, -1):
            self.hop_in(chunk, number, way).wait_recv()
            if number < self.reach:
                self.hop(chunk, number + 1, way).start()
        if number == self.reach:
            self.own_copy(chunk, self.block(chunk, self.chip, None)).wait()
            self.pair_copy(chunk, self.core).start()

    def wait_pair(self, chunk):
        self.pair_copy(chunk, 1 - self.core).wait_recv()

    def finish(self, chunk):
        for number in range(1, self.reach + 1):
            for way in (1, -1):
                self.hop(chunk, number, way).wait_send()
        self.pair_copy(chunk, self.core).wait_send()

    def round(self, step, chunks, spacing):
        for number in range(self.reach, -1, -1):
            chunk = step - number * spacing

            @pl.when((chunk >= 0) & (chunk < chunks))
            def _(chunk=chunk, number=number):
                self.stage(chunk, number)


def weight_ring(shard_ref, all_ref, height, sems, prepare):
    core = lax.rem(lax.axis_index("dp"), 2)

    def rows_of(chunk, part):
        size = height if part is None else height // 2
        start = chunk * height + (0 if part is None else part * size)
        return pl.ds(pl.multiple_of(start, size), size)

    return PlaneRing(
        lambda chunk, origin, part: all_ref.at[origin, core, rows_of(chunk, part), :],
        lambda chunk, part, action: action(shard_ref.at[rows_of(chunk, part), :]),
        lambda chunk, half: all_ref.at[:, half, rows_of(chunk, None), :],
        sems,
        prepare,
    )


HEIGHT = 32


def tail_kernel(
    sizes,
    turned_ref,
    cot_ref,
    gate_ref,
    scan_ref,
    small_ref,
    hidden_ref,
    own_cot_ref,
    post_ref,
    scale_ref,
    gate_matrix_ref,
    scan_matrix_ref,
    out_matrix_ref,
    in_ref,
    out_ref,
    small_out_ref,
    output_ref,
    input_grad_ref,
    gathered_ref,
    value_ref,
    inbox_ref,
    total_ref,
    loaded_ref,
    small_value_ref,
    small_inbox_ref,
    small_all_ref,
    weights_ref,
    normed_grad_ref,
    scale_grad_ref,
    up_send,
    inbox_recv,
    other_recv,
    total_recv,
    left_send,
    right_send,
    store_sem,
    ring_send,
    ring_recv,
    pair_send,
    pair_recv,
    own_sem,
    load_sem,
    small_send,
    small_recv,
    scale_send,
    scale_recv,
    weight_sem,
):
    rows, own_in, out_steps, gate_steps, steps, root, lag, spacing = sizes
    chunks = steps - out_steps
    rank = lax.axis_index("seq")
    last = lax.axis_size("seq") - 1
    me = lax.axis_index("dp")
    group = lax.axis_size("dp")
    chips = group // 2
    reach = chips // 2
    core = lax.rem(me, 2)
    barrier = pltpu.get_barrier_semaphore()
    greet_seq(barrier, rank, last)
    greet_plane(barrier, me, group)
    pl.semaphore_wait(barrier, seq_neighbours(rank, last) + group - 1)
    left = jnp.maximum(rank - 1, 0)
    right = jnp.minimum(rank + 1, last)

    packed = small_ref.shape[2]
    model_width = hidden_ref.shape[1]

    def small_copy(i, peer, slot):
        return plane_copy(
            small_ref.at[peer],
            small_all_ref.at[slot, :, pl.ds(0, packed)],
            small_send.at[i],
            small_recv.at[i],
            peer,
        )

    def scale_copy(i, peer, slot):
        return plane_copy(
            scale_grad_ref,
            small_all_ref.at[slot, :, pl.ds(packed, model_width)],
            scale_send.at[i],
            scale_recv.at[i],
            peer,
        )

    for i in range(1, group):
        small_copy(i, lax.rem(me + i, group), me).start()
    small_all_ref[me, :, 0:packed] = small_ref[me]

    def block(chunk, origin, part):
        ref = gathered_ref.at[chunk, core, origin]
        return ref if part is None else ref.at[pl.ds(part * (rows // 2), rows // 2), :]

    def source(chunk, part, action):
        part_rows = pl.ds(0, rows) if part is None else pl.ds(part * (rows // 2), rows // 2)

        @pl.when(chunk < gate_steps)
        def _():
            start = pl.multiple_of(chunk * WIDE, WIDE)
            action(gate_ref.at[part_rows, pl.ds(start, WIDE)])

        @pl.when(chunk >= gate_steps)
        def _():
            start = pl.multiple_of((chunk - gate_steps) * WIDE, WIDE)
            action(scan_ref.at[part_rows, pl.ds(start, WIDE)])

    ring = PlaneRing(
        block,
        source,
        lambda chunk, half: gathered_ref.at[chunk, half],
        (ring_send, ring_recv, pair_send, pair_recv, own_sem),
    )

    def load_copy(chunk):
        slot = lax.rem(chunk, 2)
        return pltpu.make_async_copy(
            gathered_ref.at[chunk], loaded_ref.at[slot], load_sem.at[slot]
        )

    def compute(step):
        @pl.when(step < out_steps)
        def _():
            cols = pl.ds(pl.multiple_of(step * LANES, LANES), LANES)
            cot = jnp.concatenate(
                [
                    cot_ref[pl.ds((2 * (slot % chips) + slot // chips) * rows, rows), cols]
                    for slot in range(group)
                ],
                axis=0,
            )
            for half in range(2):
                rows_at = own_in * (1 + half)
                value_ref[:, half * LANES : (half + 1) * LANES] = mm(
                    turned_ref[rows_at : rows_at + own_in, :], cot, 1, 0
                )

        @pl.when(step >= out_steps)
        def _():
            chunk = step - out_steps
            load_copy(chunk).wait()
            arrived = loaded_ref[lax.rem(chunk, 2)].reshape(group * rows, WIDE)
            value_ref[...] = mm(turned_ref[0:own_in, :], arrived, 1, 0)

    def weight_copy(item, action):
        slot = lax.rem(item, 2)
        narrow = scan_matrix_ref.shape[1] % WIDE

        def one(matrix_ref, first, width):
            height = matrix_ref.shape[0]
            start = pl.multiple_of((item - first) * WIDE, WIDE)
            action(
                pltpu.make_async_copy(
                    matrix_ref.at[:, pl.ds(start, width)],
                    weights_ref.at[slot, pl.ds(0, height), pl.ds(0, width)],
                    weight_sem.at[slot],
                )
            )

        full = chunks - 1 if narrow else chunks

        @pl.when(item < gate_steps)
        def _():
            one(gate_matrix_ref, 0, WIDE)

        @pl.when((item >= gate_steps) & (item < full))
        def _():
            one(scan_matrix_ref, gate_steps, WIDE)

        if narrow:

            @pl.when(item == full)
            def _():
                one(scan_matrix_ref, gate_steps, narrow)

        @pl.when((item >= chunks) & (item < items))
        def _():
            one(out_matrix_ref, chunks, WIDE)

    items = chunks + model_width // WIDE

    def back_product(grad_ref, item, first, width):
        cols = pl.ds(pl.multiple_of((item - first) * WIDE, WIDE), width)
        weights = weights_ref[lax.rem(item, 2), 0:model_width, 0:width]
        normed_grad_ref[...] += mm(grad_ref[:, cols], weights, 1, 1)

    def norm_backward():
        def block(at, carry):
            some = pl.ds(pl.multiple_of(at * HEIGHT, HEIGHT), HEIGHT)
            hidden = hidden_ref[some, :].astype(f32)
            root_mean = lax.rsqrt(jnp.mean(hidden * hidden, axis=-1, keepdims=True) + norm_eps)
            plain = hidden * root_mean
            grad = normed_grad_ref[some, :]
            scaled = grad * scale_ref[0:1, :]
            input_grad_ref[some, :] = root_mean * (
                scaled - plain * jnp.mean(scaled * plain, axis=-1, keepdims=True)
            ) + own_cot_ref[some, :].astype(f32)
            return carry + jnp.sum(grad * plain, axis=0, keepdims=True)

        total = lax.fori_loop(0, rows // HEIGHT, block, jnp.zeros((1, model_width), f32))
        first = iota((8, model_width), 0) == 0
        scale_grad_ref[...] = jnp.where(first, total, 0.0)
        for i in range(1, group):
            scale_copy(i, lax.rem(me + i, group), me).start()
        small_all_ref[me, :, packed:] = scale_grad_ref[...]

    def local_product(item):
        narrow = scan_matrix_ref.shape[1] % WIDE
        full = chunks - 1 if narrow else chunks

        @pl.when(item == 0)
        def _():
            normed_grad_ref[...] = jnp.zeros_like(normed_grad_ref)

        weight_copy(item, lambda copy: copy.wait())
        weight_copy(item + 1, lambda copy: copy.start())

        @pl.when(item < gate_steps)
        def _():
            back_product(gate_ref, item, 0, WIDE)

        @pl.when((item >= gate_steps) & (item < full))
        def _():
            back_product(scan_ref, item, gate_steps, WIDE)

        if narrow:

            @pl.when(item == full)
            def _():
                back_product(scan_ref, item, gate_steps, narrow)

        @pl.when(item == chunks - 1)
        def _():
            norm_backward()

        @pl.when(item >= chunks)
        def _():
            cols = pl.ds(pl.multiple_of((item - chunks) * WIDE, WIDE), WIDE)
            output_ref[:, cols] = hidden_ref[:, cols].astype(f32) + mm(
                post_ref[...], weights_ref[lax.rem(item, 2)], 1, 0
            )

    weight_copy(0, lambda copy: copy.start())

    def up_copy(source, target, step, recv, to):
        return seq_copy(source, target, up_send.at[step], recv.at[step], to)

    def up(value, inbox, total, step):
        edge = ((rank == 0) | (rank == last)) & (rank != root)
        inner = (rank != root) & (rank > 0) & (rank < last)

        @pl.when(edge)
        def _():
            inbox[...] = value[...]

        @pl.when(inner)
        def _():
            up_copy(inbox, inbox, step, inbox_recv, left).wait_recv()
            inbox[...] += value[...]

        @pl.when(rank < root)
        def _():
            up_copy(inbox, inbox, step, inbox_recv, right).start()

        @pl.when(rank == root + 1)
        def _():
            up_copy(inbox, total, step, other_recv, left).start()

        @pl.when(rank > root + 1)
        def _():
            up_copy(inbox, inbox, step, inbox_recv, left).start()

        @pl.when(rank == root)
        def _():
            result = value[...]
            if root > 0:
                up_copy(inbox, inbox, step, inbox_recv, left).wait_recv()
                result = result + inbox[...]
            if root < last:
                up_copy(total, total, step, other_recv, right).wait_recv()
                result = result + total[...]
            total[...] = result
            if root > 0:
                down_copy(total, step, left_send, left).start()
            if root < last:
                down_copy(total, step, right_send, right).start()

    def down_copy(total, step, send, to):
        return seq_copy(total, total, send.at[step], total_recv.at[step], to)

    def down(total, step):
        @pl.when(rank < root)
        def _():
            down_copy(total, step, left_send, left).wait_recv()

            @pl.when(rank > 0)
            def _():
                down_copy(total, step, left_send, left).start()

        @pl.when(rank > root)
        def _():
            down_copy(total, step, right_send, right).wait_recv()

            @pl.when(rank < last)
            def _():
                down_copy(total, step, right_send, right).start()

    def store_out(step, half):
        cols = pl.ds(pl.multiple_of(step * LANES, LANES), LANES)
        return pltpu.make_async_copy(
            total_ref.at[step, :, pl.ds(half * LANES, LANES)],
            out_ref.at[pl.ds(half * own_in, own_in), cols],
            store_sem.at[step, half],
        )

    def store_in(step):
        cols = pl.ds(pl.multiple_of((step - out_steps) * WIDE, WIDE), WIDE)
        return pltpu.make_async_copy(
            total_ref.at[step], in_ref.at[:, cols], store_sem.at[step, 0]
        )

    def stored(step, action):
        @pl.when(step < out_steps)
        def _():
            for half in range(2):
                action(store_out(step, half))

        @pl.when(step >= out_steps)
        def _():
            action(store_in(step))

    def drain(inbox, total, step):
        @pl.when(rank < root)
        def _():
            up_copy(inbox, inbox, step, inbox_recv, right).wait_send()

        @pl.when(rank > root)
        def _():
            up_copy(inbox, inbox, step, inbox_recv, left).wait_send()

        @pl.when((rank <= root) & (rank > 0))
        def _():
            down_copy(total, step, left_send, left).wait_send()

        @pl.when((rank >= root) & (rank < last))
        def _():
            down_copy(total, step, right_send, right).wait_send()

    behind = lag * (jnp.maximum(rank - root, 0) + jnp.maximum(root - rank, 0))

    def round_(step, carry):
        for stage in range(reach, -1, -1):
            chunk = step - stage * spacing

            @pl.when((chunk >= 0) & (chunk < chunks))
            def _(chunk=chunk, stage=stage):
                ring.stage(chunk, stage)

        ready = step - (out_steps - 1)

        @pl.when((ready >= 0) & (ready < chunks))
        def _():
            ring.wait_pair(ready)
            load_copy(ready).start()

        @pl.when(step < steps)
        def _():
            compute(step)
            up(value_ref, inbox_ref.at[step], total_ref.at[step], step)

        @pl.when(step == steps)
        def _():
            for i in range(1, group):
                small_copy(i, lax.rem(me + i, group), me).wait_send()
                origin = lax.rem(me + group - i, group)
                small_copy(i, origin, origin).wait_recv()
                scale_copy(i, origin, me).wait_send()
                scale_copy(i, origin, origin).wait_recv()
            small_value_ref[...] = jnp.sum(small_all_ref[...], axis=0)
            up(small_value_ref, small_inbox_ref, small_out_ref, steps)

        @pl.when(step < items)
        def _():
            local_product(step)

        late = step - behind

        @pl.when((late >= 0) & (late < steps))
        def _():
            down(total_ref.at[late], late)
            stored(late, lambda copy: copy.start())

        @pl.when(late == steps)
        def _():
            down(small_out_ref, steps)

        return carry

    lax.fori_loop(0, steps + 1 + behind, round_, 0)

    def finish(step, carry):
        drain(inbox_ref.at[step], total_ref.at[step], step)
        stored(step, lambda copy: copy.wait())
        return carry

    lax.fori_loop(0, steps, finish, 0)
    drain(small_inbox_ref, small_out_ref, steps)

    def finish_ring(chunk, carry):
        ring.finish(chunk)
        return carry

    lax.fori_loop(0, chunks, finish_ring, 0)


def reduce_gradients(
    turned, cot_all, gate_grad, scan_grad, small, hidden, cot, post, scale, matrices, own_in
):
    size = lax.axis_size("seq")
    group = lax.axis_size("dp")
    rows = gate_grad.shape[0]
    model_width = cot_all.shape[1]
    out_steps = model_width // LANES
    gate_steps = gate_grad.shape[1] // WIDE
    chunks = gate_steps + scan_grad.shape[1] // WIDE
    steps = out_steps + chunks
    reach = group // 4
    spacing = min(3, (out_steps - 2) // reach)
    sizes = (rows, own_in, out_steps, gate_steps, steps, size // 2, 3, spacing)
    assert chunks + model_width // WIDE <= steps
    shape = jax.ShapeDtypeStruct
    dma = pltpu.SemaphoreType.DMA
    small_shape = (8, small.shape[2] + model_width)
    anywhere = pl.BlockSpec(memory_space=pl.ANY)
    return pl.pallas_call(
        functools.partial(tail_kernel, sizes),
        out_shape=(
            shape((own_in, chunks * WIDE), f32),
            shape((2 * own_in, model_width), f32),
            shape(small_shape, f32),
            shape((rows, model_width), f32),
            shape((rows, model_width), f32),
            shape((chunks, 2, group // 2, rows, WIDE), bf16),
        ),
        in_specs=vmem(9) + [anywhere] * 3,
        out_specs=(anywhere, anywhere) + tuple(vmem(3)) + (anywhere,),
        scratch_shapes=[
            pltpu.VMEM((own_in, WIDE), f32),
            pltpu.VMEM((steps, own_in, WIDE), f32),
            pltpu.VMEM((steps, own_in, WIDE), f32),
            pltpu.VMEM((2, 2, group // 2, rows, WIDE), bf16),
            pltpu.VMEM(small_shape, f32),
            pltpu.VMEM(small_shape, f32),
            pltpu.VMEM((group,) + small_shape, f32),
            pltpu.VMEM((2, matrices[2].shape[0], WIDE), bf16),
            pltpu.VMEM((rows, model_width), f32),
            pltpu.VMEM((8, model_width), f32),
        ]
        + [dma((steps + 1,))] * 6
        + [
            dma((steps, 2)),
            *PlaneRing.semaphores(chunks),
            dma((2,)),
            *[dma((group,))] * 4,
            dma((2,)),
        ],
        compiler_params=pltpu.CompilerParams(
            collective_id=3, has_side_effects=True, vmem_limit_bytes=56 * 2**20
        ),
        cost_estimate=pl.CostEstimate(
            flops=2 * 10**10, bytes_accessed=2 * 10**8, transcendentals=0
        ),
    )(turned, cot_all, gate_grad, scan_grad, small, hidden, cot, post, scale, *matrices)


def on_device(
    hidden_in,
    out_grad,
    prenorm,
    inproject,
    convtaps,
    headcoefs,
    postnorm,
    outproject,
    prenorm_first,
    inproject_first,
    convtaps_first,
    headcoefs_first,
    postnorm_first,
    outproject_first,
    prenorm_second,
    inproject_second,
    convtaps_second,
    headcoefs_second,
    postnorm_second,
    outproject_second,
):
    group = lax.axis_size("dp")
    me = lax.axis_index("dp")
    seq_here, rows, model_width = hidden_in.shape
    assert seq_here == 1
    heads = headcoefs.shape[1]
    own_in, proj_width = inproject.shape
    own_out = outproject.shape[0]
    inner = own_out * group
    width = inner // heads
    per_tile = LANES // width
    tiles = inner // LANES
    sizes = (rows, inner, tiles, per_tile)
    conv_own = convtaps.shape[1]
    conv_width = conv_own * group

    tap_rows = convtaps.shape[0]
    small_lanes = -(-max(own_in, own_out, conv_own) // LANES) * LANES
    small = jnp.concatenate(
        [
            jnp.pad(part, ((0, 0), (0, small_lanes - part.shape[1])))
            for part in (prenorm.reshape(1, -1), convtaps, postnorm.reshape(1, -1))
        ]
    )
    small = jnp.pad(small, ((0, 16 - small.shape[0]), (0, 0))).astype(bf16)
    hidden_low = hidden_in.reshape(rows, model_width)
    cot_low = out_grad.reshape(rows, model_width)
    head_rows = jnp.pad(headcoefs, ((0, 8 - headcoefs.shape[0]), (0, LANES - heads)))
    skip = jnp.repeat(headcoefs[2:3], width, axis=1)
    (
        scan_in,
        ypre,
        enter,
        halo,
        step,
        cum,
        cumt,
        taps,
        pre_scale,
        dy,
        gate_grad,
        postnorm_grad,
        post_low,
        normed_t,
        post_t,
        token,
        scan_matrix,
        gate_matrix,
        out_matrix,
    ) = front(inproject, outproject, small, hidden_low, cot_low, head_rows, skip, sizes)
    scan_matrix = scan_matrix.reshape(model_width, -1)
    gate_matrix = gate_matrix.reshape(model_width, inner)
    out_matrix = out_matrix.reshape(inner, model_width)
    cot_all = lax.all_gather(cot_low + token[0, 0].astype(bf16), "dp", axis=0, tiled=True)
    scan_grad, conv_grad, head_grad, turned = scan_backward(
        scan_in, halo, step, cum, cumt, head_rows, skip, taps, dy, ypre, enter, normed_t, post_t, sizes
    )

    head_sums = jnp.concatenate(
        [
            head_grad[:2, :heads],
            jnp.sum(conv_grad[tap_rows : tap_rows + 1, :inner].reshape(1, heads, width), axis=-1),
        ],
        axis=0,
    )
    conv_sums = conv_grad[:tap_rows].reshape(tap_rows, group, conv_own)
    packed = jnp.concatenate(
        [
            postnorm_grad.reshape(group, own_out),
            jnp.swapaxes(conv_sums, 0, 1).reshape(group, -1),
            jnp.broadcast_to(head_sums.reshape(1, -1), (group, 3 * heads)),
        ],
        axis=1,
    )
    packed_size = packed.shape[1]
    packed_lanes = -(-packed_size // (8 * LANES)) * LANES
    packed = jnp.pad(packed, ((0, 0), (0, 8 * packed_lanes - packed_size)))
    inproj_padded, outproj_owned, packed, output, input_gradient, _ = reduce_gradients(
        turned,
        cot_all,
        gate_grad,
        scan_grad,
        packed.reshape(group, 8, packed_lanes),
        hidden_low,
        cot_low,
        post_low,
        pre_scale,
        (gate_matrix, scan_matrix, out_matrix),
        own_in,
    )
    inproj_owned = inproj_padded[:, :proj_width]
    prenorm_owned = lax.dynamic_slice_in_dim(packed[0, packed_lanes:], me * own_in, own_in, 0)
    packed = packed[:, :packed_lanes].reshape(-1)
    postnorm_owned = packed[:own_out]
    conv_at = own_out
    conv_end = conv_at + tap_rows * conv_own
    conv_owned = packed[conv_at:conv_end].reshape(tap_rows, conv_own)
    head_total = packed[conv_end:packed_size].reshape(3, heads)

    prenorm_new, prenorm_mom, prenorm_sq = adam_update(
        prenorm, prenorm_first, prenorm_second, prenorm_owned, rate_vector, 0.0
    )
    inproj_new, inproj_mom, inproj_sq = adam_update(
        inproject, inproject_first, inproject_second, inproj_owned, rate_matrix, weight_decay
    )
    conv_new, conv_mom, conv_sq = adam_update(
        convtaps, convtaps_first, convtaps_second, conv_owned, rate_vector, 0.0
    )
    head_new, head_mom, head_sq = adam_update(
        headcoefs, headcoefs_first, headcoefs_second, head_total, rate_vector, 0.0
    )
    postnorm_new, postnorm_mom, postnorm_sq = adam_update(
        postnorm, postnorm_first, postnorm_second, postnorm_owned, rate_vector, 0.0
    )
    outproj_new, outproj_mom, outproj_sq = adam_update(
        outproject, outproject_first, outproject_second, outproj_owned, rate_matrix, weight_decay
    )
    return (
        output.reshape(seq_here, rows, model_width),
        input_gradient.reshape(seq_here, rows, model_width),
        prenorm_owned,
        inproj_owned,
        conv_owned,
        head_total,
        postnorm_owned,
        outproj_owned,
        prenorm_new,
        inproj_new,
        conv_new,
        head_new,
        postnorm_new,
        outproj_new,
        prenorm_mom,
        inproj_mom,
        conv_mom,
        head_mom,
        postnorm_mom,
        outproj_mom,
        prenorm_sq,
        inproj_sq,
        conv_sq,
        head_sq,
        postnorm_sq,
        outproj_sq,
    )


def solution(mesh):
    weights = (P("dp"), P("dp", None), P(None, "dp"), P(), P("dp"), P("dp", None))
    tokens = (P("dp", "seq", None), P("dp", "seq", None))
    return jax.shard_map(
        on_device,
        mesh=mesh,
        in_specs=tokens + weights * 3,
        out_specs=tokens + weights * 4,
        check_vma=False,
    )
```

```python
import functools

import jax
import jax.numpy as jnp
from jax import lax
from jax.experimental import pallas as pl
from jax.experimental.pallas import tpu as pltpu
from jax.sharding import PartitionSpec as P

N = 128
LANES = 128
HALO = 16
WIDE = 256
HEIGHT = 32
PARTS = 2
LAG = 4
COT_AT = 4
COT_SPACING = 7

norm_eps = 1e-05
beta_moment = 0.9
beta_square = 0.95
adam_eps = 1e-08
adam_step = 3.0
rate_matrix = 0.005
rate_vector = 0.05
weight_decay = 0.1

f32 = jnp.float32
bf16 = jnp.bfloat16
MESH = pl.DeviceIdType.MESH


def adam_update(weight, moment, square, gradient, step_rate, decay_rate):
    moment_new = beta_moment * moment + (1.0 - beta_moment) * gradient
    square_new = beta_square * square + (1.0 - beta_square) * gradient * gradient
    moment_hat = moment_new / (1.0 - beta_moment**adam_step)
    square_hat = square_new / (1.0 - beta_square**adam_step)
    updated = weight - step_rate * (
        moment_hat / (jnp.sqrt(square_hat) + adam_eps) + decay_rate * weight
    )
    return (updated, moment_new, square_new)


def mm(a, b, ca, cb):
    return lax.dot_general(a, b, (((ca,), (cb,)), ((), ())), preferred_element_type=f32)


def halves(a):
    hi = a.astype(bf16)
    return hi, (a - hi.astype(f32)).astype(bf16)


def thirds(a):
    hi = a.astype(bf16)
    rest = a - hi.astype(f32)
    mid = rest.astype(bf16)
    return hi, mid, (rest - mid.astype(f32)).astype(bf16)


def mm3(a, b, ca, cb):
    return mm(a[0], b[0], ca, cb) + mm(a[0], b[1], ca, cb) + mm(a[1], b[0], ca, cb)


def iota(shape, dim):
    return lax.broadcasted_iota(jnp.int32, shape, dim)


def head_lanes(tile, heads_a_tile, copies):
    rows = iota((copies * LANES, LANES), 0)
    lane_head = tile * heads_a_tile + iota((copies * LANES, LANES), 1) // (LANES // heads_a_tile)
    return (rows % LANES == lane_head).astype(f32).astype(bf16)


def conv_tile(conv_ref, halo_ref, u_ref, taps_ref, start, rows):
    cols = pl.ds(start, LANES)
    conv_ref[0:HALO, :] = halo_ref[:, cols].astype(f32)
    conv_ref[HALO : HALO + rows, :] = u_ref[:, cols].astype(f32)
    taps = taps_ref[:, cols]
    pre = taps[4:5, :] + taps[0:1, :] * conv_ref[HALO - 3 : HALO - 3 + rows, :]
    for k in range(1, 4):
        pre = pre + taps[k : k + 1, :] * conv_ref[HALO - 3 + k : HALO - 3 + k + rows, :]
    return pre, jax.nn.sigmoid(pre)


def seq_copy(src, dst, send, recv, to):
    return pltpu.make_async_remote_copy(
        src_ref=src,
        dst_ref=dst,
        send_sem=send,
        recv_sem=recv,
        device_id={"seq": to},
        device_id_type=MESH,
    )


def greet_seq(barrier, rank, last):
    @pl.when(rank > 0)
    def _():
        pl.semaphore_signal(barrier, inc=1, device_id={"seq": rank - 1}, device_id_type=MESH)

    @pl.when(rank < last)
    def _():
        pl.semaphore_signal(barrier, inc=1, device_id={"seq": rank + 1}, device_id_type=MESH)


def seq_neighbours(rank, last):
    return jnp.minimum(rank, 1) + jnp.minimum(last - rank, 1)


def greet_plane(barrier, me, group):
    for i in range(1, group):
        pl.semaphore_signal(
            barrier, inc=1, device_id={"dp": lax.rem(me + i, group)}, device_id_type=MESH
        )


def slot_of(device, group):
    return lax.rem(device, 2) * (group // 2) + device // 2


def ring_place(at, chips):
    half = chips // 2
    turned = at // half
    return at * (1 - turned) + turned * (3 * half - 1 - at)


def front_kernel(
    sizes,
    in_shard_ref,
    out_shard_ref,
    small_ref,
    hidden_ref,
    cot_ref,
    heads_ref,
    skip_ref,
    pre_scale_ref,
    gate_grad_ref,
    post_grad_ref,
    post_ref,
    normed_turned_ref,
    post_turned_ref,
    dproj_ref,
    conv_grad_ref,
    head_grad_ref,
    scan_all_ref,
    gate_all_ref,
    out_all_ref,
    cot_all_ref,
    u_ref,
    ypre_ref,
    enter_ref,
    halo_ref,
    step_ref,
    cum_ref,
    cumt_ref,
    taps_ref,
    dy_ref,
    post_t_ref,
    in_wide_ref,
    out_wide_ref,
    scan_shard_ref,
    gate_shard_ref,
    out_low_ref,
    small_all_ref,
    post_scale_ref,
    normed_ref,
    weights_ref,
    out_weights_ref,
    conv_ref,
    score_ref,
    leave_ref,
    mixer_ref,
    gate_ref,
    gated_ref,
    dpost_ref,
    normed_t_ref,
    dscore_ref,
    dread_ref,
    dwrite_ref,
    dcum_ref,
    dstep_ref,
    dpre_ref,
    arrive_ref,
    send_sem,
    recv_sem,
    halo_sem,
    back_send,
    back_recv,
    edge_sem,
    small_send,
    small_recv,
    turn_send,
    turn_recv,
    own_sem,
    wide_sem,
    weight_sem,
    *ring_sems,
):
    rows, inner, tiles, per_tile = sizes
    conv_width = inner + 2 * N
    own_in = in_shard_ref.shape[0]
    own_out, model_width = out_shard_ref.shape
    scan_width = in_shard_ref.shape[1] - inner
    rank = lax.axis_index("seq")
    last = lax.axis_size("seq") - 1
    me = lax.axis_index("dp")
    group = lax.axis_size("dp")
    in_chunks = own_in // HEIGHT
    out_height = 2 * HEIGHT
    out_chunks = own_out // out_height

    def wide_rows(chunk):
        return pl.ds(pl.multiple_of(chunk * HEIGHT, HEIGHT), HEIGHT)

    def in_wide(chunk):
        some = wide_rows(chunk)
        return pltpu.make_async_copy(
            in_shard_ref.at[some, :], in_wide_ref.at[some, :], wide_sem.at[chunk]
        )

    out_wide = pltpu.make_async_copy(out_shard_ref, out_wide_ref, wide_sem.at[in_chunks])
    for chunk in range(in_chunks):
        in_wide(chunk).start()
    out_wide.start()
    barrier = pltpu.get_barrier_semaphore()
    greet_seq(barrier, rank, last)
    greet_plane(barrier, me, group)
    pl.semaphore_wait(barrier, seq_neighbours(rank, last) + group - 1)
    right = jnp.minimum(rank + 1, last)
    left = jnp.maximum(rank - 1, 0)

    def small_copy(i, peer, slot):
        return plane_copy(
            small_ref, small_all_ref.at[slot], small_send.at[i], small_recv.at[i], peer
        )

    for i in range(1, group):
        small_copy(i, lax.rem(me + i, group), me).start()
    small_all_ref[me] = small_ref[...]
    scan_shard_ref[:, scan_width - scan_width % LANES :] = jnp.zeros(
        (own_in, scan_shard_ref.shape[1] - scan_width + scan_width % LANES), bf16
    )

    def prepare_scan(chunk):
        some = wide_rows(chunk)
        in_wide(chunk).wait()
        scan_shard_ref[some, 0:scan_width] = in_wide_ref[some, inner:].astype(bf16)

    def prepare_gate(chunk):
        some = wide_rows(chunk)
        gate_shard_ref[some, :] = in_wide_ref[some, 0:inner].astype(bf16)

    def prepare_out(chunk):
        @pl.when(chunk == 0)
        def _():
            out_wide.wait()

        some = pl.ds(pl.multiple_of(chunk * out_height, out_height), out_height)
        out_low_ref[some, :] = out_wide_ref[some, :].astype(bf16)

    scan_ring = weight_ring(scan_shard_ref, scan_all_ref, HEIGHT, ring_sems[0:5], prepare_scan)
    gate_ring = weight_ring(gate_shard_ref, gate_all_ref, HEIGHT, ring_sems[5:10], prepare_gate)
    out_ring = weight_ring(out_low_ref, out_all_ref, out_height, ring_sems[10:15], prepare_out)
    spacing = 2
    rings = (
        (scan_ring, 0, in_chunks),
        (gate_ring, in_chunks, in_chunks),
        (out_ring, 2 * in_chunks, out_chunks),
    )

    def round_(step):
        for ring, first, chunks in rings:
            ring.round(step - first, chunks, spacing)

    def rounds(first, end):
        def one(step, carry):
            round_(step)
            return carry

        lax.fori_loop(first, end, one, 0)

    def complete(at):
        ring, first, chunks = rings[at]
        return first + chunks + spacing * ring.reach

    def wait_pairs(at):
        ring, _, chunks = rings[at]

        def one(chunk, carry):
            ring.wait_pair(chunk)
            return carry

        lax.fori_loop(0, chunks, one, 0)

    rounds(0, 2)

    for i in range(1, group):
        small_copy(i, lax.rem(me + i, group), me).wait_send()
        small_copy(i, me, lax.rem(me + group - i, group)).wait_recv()
    conv_own = conv_width // group
    taps_ref[...] = jnp.zeros_like(taps_ref)
    for device in range(group):
        small = small_all_ref[device].astype(f32)
        pre_scale_ref[0:1, device * own_in : (device + 1) * own_in] = small[0:1, 0:own_in]
        taps_ref[0:5, device * conv_own : (device + 1) * conv_own] = small[1:6, 0:conv_own]
        post_scale_ref[0:1, device * own_out : (device + 1) * own_out] = small[6:7, 0:own_out]
    pre_scale_ref[1:8, :] = jnp.zeros((7, model_width), f32)

    def norm(at, carry):
        some = pl.ds(pl.multiple_of(at * HEIGHT, HEIGHT), HEIGHT)
        hidden = hidden_ref[some, :].astype(f32)
        root = lax.rsqrt(jnp.mean(hidden * hidden, axis=-1, keepdims=True) + norm_eps)
        normed_ref[some, :] = (hidden * root * pre_scale_ref[0:1, :]).astype(bf16)
        return carry

    lax.fori_loop(0, rows // HEIGHT, norm, 0)

    def turn(source_ref, target_ref):
        def one(at, carry):
            cols = pl.ds(pl.multiple_of(at * LANES, LANES), LANES)
            target_ref[cols, :] = source_ref[:, cols].astype(f32).T.astype(bf16)
            return carry

        lax.fori_loop(0, source_ref.shape[1] // LANES, one, 0)

    turn(normed_ref, normed_t_ref)
    rounds(2, complete(0))
    wait_pairs(0)

    def weight_copy(all_ref, at, width):
        slot = lax.rem(at, 2)
        cols = pl.ds(pl.multiple_of(at * WIDE, WIDE), width)
        return pltpu.make_async_copy(
            all_ref.at[:, :, :, cols],
            weights_ref.at[slot, :, :, :, pl.ds(0, width)],
            weight_sem.at[slot],
        )

    def columns(all_ref, action):
        total = all_ref.shape[3]
        full = total // WIDE
        rest = total % WIDE

        def fetch(at, act):
            @pl.when(at < full)
            def _():
                act(weight_copy(all_ref, at, WIDE))

            if rest:

                @pl.when(at == full)
                def _():
                    act(weight_copy(all_ref, at, rest))

        fetch(0, lambda copy: copy.start())

        def one(at, carry):
            fetch(at + 1, lambda copy: copy.start())
            fetch(at, lambda copy: copy.wait())
            weights = weights_ref[lax.rem(at, 2)].reshape(model_width, WIDE)
            action(at, WIDE, mm(normed_ref[...], weights, 1, 0))
            return carry

        lax.fori_loop(0, full, one, 0)
        if rest:
            fetch(full, lambda copy: copy.wait())
            weights = weights_ref[full % 2, :, :, :, 0:rest].reshape(model_width, rest)
            action(full, rest, mm(normed_ref[...], weights, 1, 0))

    def keep_scan(at, width, product):
        cols = pl.ds(at * WIDE if isinstance(at, int) else pl.multiple_of(at * WIDE, WIDE), width)
        u_ref[:, cols] = product.astype(bf16)

    columns(scan_all_ref, keep_scan)
    halo_copy = seq_copy(
        u_ref.at[pl.ds(rows - HALO, HALO), pl.ds(0, conv_width)],
        halo_ref,
        halo_sem.at[0],
        halo_sem.at[1],
        right,
    )

    @pl.when(rank < last)
    def _():
        halo_copy.start()

    round_(complete(0))
    step = jax.nn.softplus(u_ref[:, conv_width:].astype(f32) + heads_ref[0:1, :])
    decay = -step * jnp.exp(heads_ref[1:2, :])
    lower = (iota((rows, rows), 0) >= iota((rows, rows), 1)).astype(f32).astype(bf16)
    cum = sum(mm(lower, part, 1, 0) for part in thirds(decay))
    step_ref[...] = step
    cum_ref[...] = cum
    cumt_ref[...] = cum.T

    @pl.when(rank > 0)
    def _():
        halo_copy.wait_recv()

    @pl.when(rank == 0)
    def _():
        halo_ref[...] = jnp.zeros_like(halo_ref)

    pre_b, sig_b = conv_tile(conv_ref, halo_ref, u_ref, taps_ref, inner, rows)
    b_parts = halves(pre_b * sig_b)
    pre_c, sig_c = conv_tile(conv_ref, halo_ref, u_ref, taps_ref, inner + N, rows)
    c_parts = halves(pre_c * sig_c)
    scores = mm3(c_parts, b_parts, 1, 1)
    causal = iota((rows, rows), 0) >= iota((rows, rows), 1)
    score_ref[...] = jnp.where(causal, scores, 0.0)
    cum_parts = jnp.concatenate(thirds(cum), axis=1)
    step_parts = jnp.concatenate(thirds(step), axis=1)
    lane = iota((rows, LANES), 1)
    width = LANES // per_tile

    def chain(tile):
        return seq_copy(
            leave_ref.at[tile], enter_ref.at[tile], send_sem.at[tile], recv_sem.at[tile], right
        )

    def one(tile, carry):
        start = pl.multiple_of(tile * LANES, LANES)
        cols = pl.ds(start, LANES)
        pick = head_lanes(tile, per_tile, 3)
        cum_l = mm(cum_parts, pick, 1, 0)
        step_l = mm(step_parts, pick, 1, 0)
        pre, sig = conv_tile(conv_ref, halo_ref, u_ref, taps_ref, start, rows)
        values = pre * sig
        x = values * step_l
        total = cum_l[rows - 1 : rows, :]
        fresh = mm3(b_parts, halves(x * jnp.exp(total - cum_l)), 0, 0)

        @pl.when(rank > 0)
        def _():
            chain(tile).wait_recv()

        @pl.when(rank == 0)
        def _():
            enter_ref[tile] = jnp.zeros((N, LANES), f32)

        enter = enter_ref[tile]
        leave_ref[tile] = jnp.exp(total) * enter + fresh

        @pl.when(rank < last)
        def _():
            chain(tile).start()

        result = mm3(c_parts, halves(enter), 1, 0) * jnp.exp(cum_l)
        for h in range(per_tile):
            row = cumt_ref[pl.ds(tile * per_tile + h, 1), :]
            col = cum_l[:, h * width : h * width + 1]
            kernel = jnp.exp(jnp.minimum(col - row, 0.0)) * score_ref[...]
            own = (lane // width) == h
            result = result + mm3(halves(kernel), halves(jnp.where(own, x, 0.0)), 1, 0)
        ypre_ref[:, cols] = result
        mixer_ref[:, cols] = (result + skip_ref[0:1, cols] * values).astype(bf16)

        @pl.when(lax.rem(tile, pace) == pace - 1)
        def _():
            round_(in_loop + tile // pace)

        return carry

    in_loop = complete(0) + 1
    pace = 4
    lax.fori_loop(0, tiles, one, 0)
    at_round = in_loop + tiles // pace
    rounds(at_round, max(at_round, complete(1)))
    at_round = max(at_round, complete(1))
    wait_pairs(1)

    gated_ref_sum = score_ref

    def keep_gate(at, width, product):
        cols = pl.ds(at * WIDE if isinstance(at, int) else pl.multiple_of(at * WIDE, WIDE), width)
        gated = mixer_ref[:, cols].astype(f32) * (product * jax.nn.sigmoid(product))
        gate_ref[:, cols] = product
        gated_ref[:, cols] = gated
        square = gated * gated
        total = square[:, 0:LANES]
        for part in range(1, width // LANES):
            total = total + square[:, part * LANES : (part + 1) * LANES]
        gated_ref_sum[:, 0:LANES] += total

    gated_ref_sum[:, 0:LANES] = jnp.zeros((rows, LANES), f32)
    columns(gate_all_ref, keep_gate)
    end_round = complete(2)
    rounds(at_round, min(at_round + 1, end_round))
    at_round = min(at_round + 1, end_round)
    root = lax.rsqrt(
        jnp.sum(gated_ref_sum[:, 0:LANES], axis=-1, keepdims=True) / inner + norm_eps
    )

    def keep_post(at, carry):
        cols = pl.ds(pl.multiple_of(at * WIDE, WIDE), WIDE)
        whitened = gated_ref[:, cols] * root
        gated_ref[:, cols] = whitened
        post_ref[:, cols] = (whitened * post_scale_ref[0:1, cols]).astype(bf16)
        return carry

    lax.fori_loop(0, inner // WIDE, keep_post, 0)
    turn(post_ref, post_t_ref)
    rounds(at_round, end_round)
    wait_pairs(2)
    normed_turn = PlaneTurn(
        normed_t_ref,
        normed_turned_ref,
        own_in,
        rows,
        (turn_send.at[0], turn_recv.at[0], own_sem.at[0]),
    )
    post_turn = PlaneTurn(
        post_t_ref,
        post_turned_ref,
        own_out,
        rows,
        (turn_send.at[1], turn_recv.at[1], own_sem.at[1]),
    )
    post_turn.start()
    normed_turn.start()

    span = 2 * own_out

    def out_copy(chip):
        slot = chip % 2
        return pltpu.make_async_copy(
            out_all_ref.at[chip], out_weights_ref.at[slot], weight_sem.at[slot]
        )

    out_copy(0).start()
    overlap = jnp.zeros((rows, LANES), f32)
    for chip in range(group // 2):
        if chip + 1 < group // 2:
            out_copy(chip + 1).start()
        out_copy(chip).wait()
        cols = slice(chip * span, (chip + 1) * span)
        weights = out_weights_ref[chip % 2].reshape(span, model_width)
        dpost = mm(cot_ref[...], weights, 1, 1)
        dpost_ref[:, cols] = dpost
        pulled = dpost * gated_ref[:, cols]
        post_grad_ref[0:1, cols] = jnp.sum(pulled, axis=0, keepdims=True)
        pulled = pulled * post_scale_ref[0:1, cols]
        for part in range(span // LANES):
            overlap = overlap + pulled[:, part * LANES : (part + 1) * LANES]
    mean = jnp.sum(overlap, axis=-1, keepdims=True) / inner

    def keep_back(at, carry):
        cols = pl.ds(pl.multiple_of(at * WIDE, WIDE), WIDE)
        gate = gate_ref[:, cols]
        sig = jax.nn.sigmoid(gate)
        dgated = root * (dpost_ref[:, cols] * post_scale_ref[0:1, cols] - gated_ref[:, cols] * mean)
        dy_ref[:, cols] = (dgated * (gate * sig)).astype(bf16)
        gate_grad_ref[:, cols] = (
            dgated * mixer_ref[:, cols].astype(f32) * sig * (1.0 + gate * (1.0 - sig))
        ).astype(bf16)
        return carry

    lax.fori_loop(0, inner // WIDE, keep_back, 0)

    @pl.when(rank < last)
    def _():
        halo_copy.wait_send()

        def drain(tile, carry):
            chain(tile).wait_send()
            return carry

        lax.fori_loop(0, tiles, drain, 0)

    for ring, _, chunks in rings:

        def finish(chunk, carry, ring=ring):
            ring.finish(chunk)
            return carry

        lax.fori_loop(0, chunks, finish, 0)

    def backward():
        core = lax.rem(me, 2)
        cot_chunks = cot_ref.shape[1] // WIDE

        def cot_block(chunk, origin, part):
            ref = cot_all_ref.at[chunk, core, origin]
            return ref if part is None else ref.at[pl.ds(part * (rows // 2), rows // 2), :]

        def cot_source(chunk, part, action):
            part_rows = pl.ds(0, rows) if part is None else pl.ds(part * (rows // 2), rows // 2)
            cols = pl.ds(pl.multiple_of(chunk * WIDE, WIDE), WIDE)
            action(cot_ref.at[part_rows, cols])

        ring = PlaneRing(
            cot_block, cot_source, lambda chunk, half: cot_all_ref.at[chunk, half], cot_ring_sems
        )

        left = jnp.maximum(rank - 1, 0)
        cum = cum_ref[...]
        step = step_ref[...]
        pre_b, sig_b = conv_tile(conv_ref, halo_ref, u_ref, taps_ref, inner, rows)
        b_parts = halves(pre_b * sig_b)
        pre_c, sig_c = conv_tile(conv_ref, halo_ref, u_ref, taps_ref, inner + N, rows)
        c_parts = halves(pre_c * sig_c)
        later = iota((rows, rows), 1) >= iota((rows, rows), 0)
        score_ref[...] = jnp.where(later, mm3(b_parts, c_parts, 1, 1), 0.0)
        dscore_ref[...] = jnp.zeros_like(dscore_ref)
        dread_ref[...] = jnp.zeros_like(dread_ref)
        dwrite_ref[...] = jnp.zeros_like(dwrite_ref)
        dcum_ref[...] = jnp.zeros_like(dcum_ref)
        dstep_ref[...] = jnp.zeros_like(dstep_ref)
        cum_parts = jnp.concatenate(thirds(cum), axis=1)
        step_parts = jnp.concatenate(thirds(step), axis=1)
        lane = iota((rows, LANES), 1)
        final_row = iota((rows, LANES), 0) == rows - 1
        width = LANES // per_tile

        def chain(tile):
            return seq_copy(
                leave_ref.at[tile], arrive_ref.at[tile], back_send.at[tile], back_recv.at[tile], left
            )

        def tap_grads(dpre, extra):
            sums = [
                jnp.sum(
                    dpre * conv_ref[HALO - 3 + k : HALO - 3 + k + rows, :], axis=0, keepdims=True
                )
                for k in range(4)
            ]
            sums.append(jnp.sum(dpre, axis=0, keepdims=True))
            sums.append(extra)
            sums.append(jnp.zeros((2, LANES), f32))
            return jnp.concatenate(sums, axis=0)

        def one(tile, carry):
            start = pl.multiple_of(tile * LANES, LANES)
            cols = pl.ds(start, LANES)
            pick = head_lanes(tile, per_tile, 3)
            cum_l = mm(cum_parts, pick, 1, 0)
            step_l = mm(step_parts, pick, 1, 0)
            total = cum_l[rows - 1 : rows, :]
            dy = dy_ref[:, cols].astype(f32)
            reads = halves(dy * jnp.exp(cum_l))
            denter = mm3(c_parts, reads, 0, 0)

            @pl.when(rank < last)
            def _():
                chain(tile).wait_recv()

            @pl.when(rank == last)
            def _():
                arrive_ref[tile] = jnp.zeros((N, LANES), f32)

            arrive = arrive_ref[tile]
            leave_ref[tile] = jnp.exp(total) * arrive + denter

            @pl.when(rank > 0)
            def _():
                chain(tile).start()

            pre, sig = conv_tile(conv_ref, halo_ref, u_ref, taps_ref, start, rows)
            values = pre * sig
            x = values * step_l
            x_parts = halves(x)
            tail = jnp.exp(total - cum_l)
            enter = enter_ref[tile]
            arrive_parts = halves(arrive)
            dx_state = mm3(b_parts, arrive_parts, 1, 0) * tail
            dx = dx_state
            for h in range(per_tile):
                row = cumt_ref[pl.ds(tile * per_tile + h, 1), :]
                col = cum_l[:, h * width : h * width + 1]
                spread = jnp.exp(jnp.minimum(row - col, 0.0))
                kernel = halves(spread * score_ref[...])
                own = jnp.where((lane // width) == h, dy, 0.0).astype(bf16)
                dx = dx + (mm(kernel[0], own, 1, 0) + mm(kernel[1], own, 1, 0))
                pairs = mm(x_parts[0], own, 1, 1) + mm(x_parts[1], own, 1, 1)
                dscore_ref[...] += spread * pairs
            dread_ref[...] += mm3(reads, halves(enter), 1, 1)
            dwrite_ref[...] += mm3(halves(x * tail), arrive_parts, 1, 1)
            ends = jnp.sum(x * dx_state, axis=0, keepdims=True) + jnp.exp(total) * jnp.sum(
                enter * arrive, axis=0, keepdims=True
            )
            dcum = dy * ypre_ref[:, cols] - x * dx + jnp.where(final_row, ends, 0.0)
            own_head = pick[0:LANES, :]
            for part in halves(dcum):
                dcum_ref[...] += mm(part, own_head, 1, 1)
            for part in halves(dx * values):
                dstep_ref[...] += mm(part, own_head, 1, 1)
            dvalues = step_l * dx + skip_ref[0:1, cols] * dy
            dpre = dvalues * sig * (1.0 + pre * (1.0 - sig))
            dpre_ref[0:rows, cols] = dpre
            conv_grad_ref[:, cols] = tap_grads(dpre, jnp.sum(dy * values, axis=0, keepdims=True))

            ring.round(tile - COT_AT, cot_chunks, COT_SPACING)

            return carry

        lax.fori_loop(0, tiles, one, 0)
        for at in range(tiles - COT_AT, cot_chunks + COT_SPACING * ring.reach):
            ring.round(at, cot_chunks, COT_SPACING)

        dscore = halves(jnp.where(later, dscore_ref[...], 0.0))
        dshared = (
            dwrite_ref[...] + mm3(dscore, c_parts, 1, 0),
            dread_ref[...] + mm3(dscore, b_parts, 0, 0),
        )
        for i in range(2):
            start = inner + i * N
            pre, sig = conv_tile(conv_ref, halo_ref, u_ref, taps_ref, start, rows)
            dpre = dshared[i] * sig * (1.0 + pre * (1.0 - sig))
            dpre_ref[0:rows, start : start + N] = dpre
            conv_grad_ref[:, start : start + N] = tap_grads(dpre, jnp.zeros((1, LANES), f32))

        edge = seq_copy(
            dpre_ref.at[pl.ds(0, 8), :],
            dpre_ref.at[pl.ds(rows, 8), :],
            edge_sem.at[0],
            edge_sem.at[1],
            left,
        )

        @pl.when(rank > 0)
        def _():
            edge.start()

        upper = (iota((rows, rows), 1) >= iota((rows, rows), 0)).astype(f32).astype(bf16)
        ddecay = sum(mm(upper, part, 1, 0) for part in thirds(dcum_ref[...]))
        exp_rate = jnp.exp(heads_ref[1:2, :])
        drate = (dstep_ref[...] - ddecay * exp_rate) * jax.nn.sigmoid(
            u_ref[:, conv_width:].astype(f32) + heads_ref[0:1, :]
        )
        head_grad_ref[...] = jnp.concatenate(
            [
                jnp.sum(drate, axis=0, keepdims=True),
                jnp.sum(ddecay * (-step * exp_rate), axis=0, keepdims=True),
                jnp.zeros((6, LANES), f32),
            ],
            axis=0,
        )
        dproj_ref[:, conv_width : conv_width + LANES] = drate.astype(bf16)
        dproj_ref[:, conv_width + LANES :] = jnp.zeros(
            (rows, dproj_ref.shape[1] - conv_width - LANES), bf16
        )

        @pl.when(rank == last)
        def _():
            dpre_ref[rows : rows + 8, :] = jnp.zeros((8, conv_width), f32)

        @pl.when(rank < last)
        def _():
            edge.wait_recv()

        def unconv(tile, carry):
            cols = pl.ds(pl.multiple_of(tile * LANES, LANES), LANES)
            taps = taps_ref[:, cols]
            du = taps[3:4, :] * dpre_ref[0:rows, cols]
            for k in range(3):
                du = du + taps[k : k + 1, :] * dpre_ref[3 - k : 3 - k + rows, cols]
            dproj_ref[:, cols] = du.astype(bf16)
            return carry

        lax.fori_loop(0, conv_width // LANES, unconv, 0)

        @pl.when(rank > 0)
        def _():
            edge.wait_send()

            def drain(tile, carry):
                chain(tile).wait_send()
                return carry

            lax.fori_loop(0, tiles, drain, 0)


        def finish_ring(chunk, carry):
            ring.wait_pair(chunk)
            ring.finish(chunk)
            return carry

        lax.fori_loop(0, cot_chunks, finish_ring, 0)

    cot_ring_sems = ring_sems[15:]
    backward()
    post_turn.finish()
    normed_turn.finish()


def vmem(count):
    return [pl.BlockSpec(memory_space=pltpu.VMEM)] * count


def front(in_shard, out_shard, small, hidden, cot, heads, skip, sizes):
    rows, inner, tiles, _ = sizes
    conv_width = inner + 2 * N
    shape = jax.ShapeDtypeStruct
    group = lax.axis_size("dp")
    own_in, proj_width = in_shard.shape
    own_out, model_width = out_shard.shape
    scan_width = -(-(proj_width - inner) // LANES) * LANES
    in_chunks = own_in // HEIGHT
    out_chunks = own_out // (2 * HEIGHT)
    anywhere = pl.BlockSpec(memory_space=pl.ANY)
    dma = pltpu.SemaphoreType.DMA
    return pl.pallas_call(
        functools.partial(front_kernel, sizes),
        out_shape=(
            shape((8, model_width), f32),
            shape((rows, inner), bf16),
            shape((1, inner), f32),
            shape((rows, inner), bf16),
            shape((own_in, group * rows), bf16),
            shape((own_out, group * rows), bf16),
            shape((rows, -(-scan_width // WIDE) * WIDE), bf16),
            shape((8, conv_width), f32),
            shape((8, LANES), f32),
            shape((group // 2, 2, own_in, scan_width), bf16),
            shape((group // 2, 2, own_in, inner), bf16),
            shape((group // 2, 2, own_out, model_width), bf16),
            shape((model_width // WIDE, 2, group // 2, rows, WIDE), bf16),
        ),
        in_specs=[anywhere] * 2 + vmem(5),
        out_specs=tuple(vmem(9) + [anywhere] * 4),
        scratch_shapes=[
            pltpu.VMEM((rows, scan_width), bf16),
            pltpu.VMEM((rows, inner), f32),
            pltpu.VMEM((tiles, N, LANES), f32),
            pltpu.VMEM((HALO, conv_width), bf16),
            pltpu.VMEM((rows, LANES), f32),
            pltpu.VMEM((rows, LANES), f32),
            pltpu.VMEM((LANES, rows), f32),
            pltpu.VMEM((8, conv_width), f32),
            pltpu.VMEM((rows, inner), bf16),
            pltpu.VMEM((inner, rows), bf16),
            pltpu.VMEM(in_shard.shape, f32),
            pltpu.VMEM(out_shard.shape, f32),
            pltpu.VMEM((own_in, scan_width), bf16),
            pltpu.VMEM((own_in, inner), bf16),
            pltpu.VMEM((own_out, model_width), bf16),
            pltpu.VMEM((group,) + small.shape, bf16),
            pltpu.VMEM((1, inner), f32),
            pltpu.VMEM((rows, model_width), bf16),
            pltpu.VMEM((2, group // 2, 2, own_in, WIDE), bf16),
            pltpu.VMEM((2, 2, own_out, model_width), bf16),
            pltpu.VMEM((HALO + rows, LANES), f32),
            pltpu.VMEM((rows, rows), f32),
            pltpu.VMEM((tiles, N, LANES), f32),
            pltpu.VMEM((rows, inner), bf16),
            pltpu.VMEM((rows, inner), f32),
            pltpu.VMEM((rows, inner), f32),
            pltpu.VMEM((rows, inner), f32),
            pltpu.VMEM((model_width, rows), bf16),
            pltpu.VMEM((rows, rows), f32),
            pltpu.VMEM((rows, N), f32),
            pltpu.VMEM((rows, N), f32),
            pltpu.VMEM((rows, LANES), f32),
            pltpu.VMEM((rows, LANES), f32),
            pltpu.VMEM((rows + 8, conv_width), f32),
            pltpu.VMEM((tiles, N, LANES), f32),
            dma((tiles,)),
            dma((tiles,)),
            dma((2,)),
            dma((tiles,)),
            dma((tiles,)),
            dma((2,)),
            dma((group,)),
            dma((group,)),
            dma((2, group)),
            dma((2, group)),
            dma((2,)),
            dma((in_chunks + 1,)),
            dma((2,)),
        ]
        + PlaneRing.semaphores(in_chunks)
        + PlaneRing.semaphores(in_chunks)
        + PlaneRing.semaphores(out_chunks)
        + PlaneRing.semaphores(model_width // WIDE),
        compiler_params=pltpu.CompilerParams(
            collective_id=1, has_side_effects=True, vmem_limit_bytes=60 * 2**20
        ),
        cost_estimate=pl.CostEstimate(
            flops=10**10, bytes_accessed=10**8, transcendentals=4 * 10**6
        ),
    )(in_shard, out_shard, small, hidden, cot, heads, skip)


def plane_copy(src, dst, send, recv, to):
    return pltpu.make_async_remote_copy(
        src_ref=src,
        dst_ref=dst,
        send_sem=send,
        recv_sem=recv,
        device_id={"dp": to},
        device_id_type=MESH,
    )


class PlaneTurn:
    def __init__(self, source, target, height, width, sems):
        self.source, self.target, self.height, self.width = source, target, height, width
        self.send, self.recv, self.own_sem = sems
        self.me = lax.axis_index("dp")
        self.group = lax.axis_size("dp")

    def rows_for(self, device):
        return self.source.at[
            pl.ds(pl.multiple_of(device * self.height, self.height), self.height), :
        ]

    def columns_of(self, device):
        start = pl.multiple_of(slot_of(device, self.group) * self.width, self.width)
        return self.target.at[:, pl.ds(start, self.width)]

    def copy(self, i, peer, origin):
        return plane_copy(
            self.rows_for(peer), self.columns_of(origin), self.send.at[i], self.recv.at[i], peer
        )

    def own(self):
        return pltpu.make_async_copy(
            self.rows_for(self.me), self.columns_of(self.me), self.own_sem
        )

    def start(self):
        for i in range(1, self.group):
            self.copy(i, lax.rem(self.me + i, self.group), self.me).start()
        self.own().start()

    def arrive(self):
        for i in range(1, self.group):
            origin = lax.rem(self.me + self.group - i, self.group)
            self.copy(i, origin, origin).wait_recv()
        self.own().wait()

    def sent(self):
        for i in range(1, self.group):
            self.copy(i, lax.rem(self.me + i, self.group), self.me).wait_send()

    def finish(self):
        self.arrive()
        self.sent()


class PlaneRing:
    def __init__(self, block, source, pair_block, sems, prepare=None):
        group = lax.axis_size("dp")
        me = lax.axis_index("dp")
        self.block, self.source, self.pair_block = block, source, pair_block
        self.prepare = prepare
        self.ring_send, self.ring_recv, self.pair_send, self.pair_recv, self.own_sem = sems
        self.chips = group // 2
        self.reach = self.chips // 2
        self.me = me
        self.core = lax.rem(me, 2)
        self.chip = me // 2
        self.place = ring_place(self.chip, self.chips)

    @staticmethod
    def semaphores(chunks):
        group = lax.axis_size("dp")
        dma = pltpu.SemaphoreType.DMA
        return [dma((chunks, group // 2)), dma((chunks, group // 2))] + [dma((chunks,))] * 3

    def ring_chip(self, ahead):
        return ring_place(lax.rem(self.place + ahead + self.chips, self.chips), self.chips)

    def part(self, number, way):
        return None if number < self.reach else (0 if way == 1 else 1)

    def copy(self, chunk, number, way, origin, source=None):
        block = self.block(chunk, origin, self.part(number, way))
        at = 2 * (number - 1) + (0 if way == 1 else 1)
        return plane_copy(
            block if source is None else source,
            block,
            self.ring_send.at[chunk, at],
            self.ring_recv.at[chunk, at],
            2 * self.ring_chip(way) + self.core,
        )

    def hop(self, chunk, number, way, source=None):
        return self.copy(chunk, number, way, self.ring_chip(-way * (number - 1)), source)

    def hop_in(self, chunk, number, way):
        return self.copy(chunk, number, way, self.ring_chip(-way * number))

    def own_copy(self, chunk, source):
        return pltpu.make_async_copy(
            source, self.block(chunk, self.chip, None), self.own_sem.at[chunk]
        )

    def pair_copy(self, chunk, core):
        block = self.pair_block(chunk, core)
        return plane_copy(
            block,
            block,
            self.pair_send.at[chunk],
            self.pair_recv.at[chunk],
            self.me + 1 - 2 * self.core,
        )

    def stage(self, chunk, number):
        if number == 0:
            if self.prepare is not None:
                self.prepare(chunk)
            self.source(chunk, None, lambda ref: self.own_copy(chunk, ref).start())
            for way in (1, -1):
                self.source(
                    chunk,
                    self.part(1, way),
                    lambda ref, way=way: self.hop(chunk, 1, way, ref).start(),
                )
            return
        for way in (1, -1):
            self.hop_in(chunk, number, way).wait_recv()
            if number < self.reach:
                self.hop(chunk, number + 1, way).start()
        if number == self.reach:
            self.own_copy(chunk, self.block(chunk, self.chip, None)).wait()
            self.pair_copy(chunk, self.core).start()

    def wait_pair(self, chunk):
        self.pair_copy(chunk, 1 - self.core).wait_recv()

    def finish(self, chunk):
        for number in range(1, self.reach + 1):
            for way in (1, -1):
                self.hop(chunk, number, way).wait_send()
        self.pair_copy(chunk, self.core).wait_send()

    def round(self, step, chunks, spacing):
        for number in range(self.reach, -1, -1):
            chunk = step - number * spacing

            @pl.when((chunk >= 0) & (chunk < chunks))
            def _(chunk=chunk, number=number):
                self.stage(chunk, number)


def weight_ring(shard_ref, all_ref, height, sems, prepare):
    core = lax.rem(lax.axis_index("dp"), 2)

    def rows_of(chunk, part):
        size = height if part is None else height // 2
        start = chunk * height + (0 if part is None else part * size)
        return pl.ds(pl.multiple_of(start, size), size)

    return PlaneRing(
        lambda chunk, origin, part: all_ref.at[origin, core, rows_of(chunk, part), :],
        lambda chunk, part, action: action(shard_ref.at[rows_of(chunk, part), :]),
        lambda chunk, half: all_ref.at[:, half, rows_of(chunk, None), :],
        sems,
        prepare,
    )


HEIGHT = 32


def tail_kernel(
    sizes,
    normed_turned_ref,
    post_turned_ref,
    cot_ref,
    gate_ref,
    scan_ref,
    small_ref,
    hidden_ref,
    own_cot_ref,
    post_ref,
    scale_ref,
    gate_matrix_ref,
    scan_matrix_ref,
    out_matrix_ref,
    in_ref,
    out_ref,
    small_out_ref,
    output_ref,
    input_grad_ref,
    gathered_ref,
    value_ref,
    inbox_ref,
    total_ref,
    loaded_ref,
    small_value_ref,
    small_inbox_ref,
    small_all_ref,
    weights_ref,
    normed_grad_ref,
    scale_grad_ref,
    up_send,
    inbox_recv,
    other_recv,
    total_recv,
    left_send,
    right_send,
    store_sem,
    ring_send,
    ring_recv,
    pair_send,
    pair_recv,
    own_sem,
    load_sem,
    small_send,
    small_recv,
    scale_send,
    scale_recv,
    weight_sem,
):
    rows, own_in, out_steps, gate_steps, steps, root, lag, spacing = sizes
    chunks = steps - out_steps
    rank = lax.axis_index("seq")
    last = lax.axis_size("seq") - 1
    me = lax.axis_index("dp")
    group = lax.axis_size("dp")
    chips = group // 2
    reach = chips // 2
    core = lax.rem(me, 2)
    barrier = pltpu.get_barrier_semaphore()
    greet_seq(barrier, rank, last)
    greet_plane(barrier, me, group)
    pl.semaphore_wait(barrier, seq_neighbours(rank, last) + group - 1)
    left = jnp.maximum(rank - 1, 0)
    right = jnp.minimum(rank + 1, last)

    packed = small_ref.shape[2]
    model_width = hidden_ref.shape[1]

    def small_copy(i, peer, slot):
        return plane_copy(
            small_ref.at[peer],
            small_all_ref.at[slot, :, pl.ds(0, packed)],
            small_send.at[i],
            small_recv.at[i],
            peer,
        )

    def scale_copy(i, peer, slot):
        return plane_copy(
            scale_grad_ref,
            small_all_ref.at[slot, :, pl.ds(packed, model_width)],
            scale_send.at[i],
            scale_recv.at[i],
            peer,
        )

    for i in range(1, group):
        small_copy(i, lax.rem(me + i, group), me).start()
    small_all_ref[me, :, 0:packed] = small_ref[me]

    def block(chunk, origin, part):
        ref = gathered_ref.at[chunk, core, origin]
        return ref if part is None else ref.at[pl.ds(part * (rows // 2), rows // 2), :]

    def source(chunk, part, action):
        part_rows = pl.ds(0, rows) if part is None else pl.ds(part * (rows // 2), rows // 2)

        @pl.when(chunk < gate_steps)
        def _():
            start = pl.multiple_of(chunk * WIDE, WIDE)
            action(gate_ref.at[part_rows, pl.ds(start, WIDE)])

        @pl.when(chunk >= gate_steps)
        def _():
            start = pl.multiple_of((chunk - gate_steps) * WIDE, WIDE)
            action(scan_ref.at[part_rows, pl.ds(start, WIDE)])

    ring = PlaneRing(
        block,
        source,
        lambda chunk, half: gathered_ref.at[chunk, half],
        (ring_send, ring_recv, pair_send, pair_recv, own_sem),
    )

    def fetch(step, action):
        order = jnp.where(step < out_steps, step // 2, step - out_steps + out_steps // 2)
        slot = lax.rem(order, 2)

        @pl.when((step < out_steps) & (lax.rem(step, 2) == 0))
        def _():
            action(
                pltpu.make_async_copy(
                    cot_ref.at[step // 2], loaded_ref.at[slot], load_sem.at[slot]
                )
            )

        @pl.when(step >= out_steps)
        def _():
            action(
                pltpu.make_async_copy(
                    gathered_ref.at[step - out_steps], loaded_ref.at[slot], load_sem.at[slot]
                )
            )

        return slot

    def compute(step):
        arrived = loaded_ref.at[fetch(step, lambda copy: copy.wait())]

        @pl.when(step < out_steps)
        def _():
            some = pl.ds(pl.multiple_of(lax.rem(step, 2) * own_in, own_in), own_in)
            value_ref[...] = mm(
                post_turned_ref[some, :], arrived[...].reshape(group * rows, WIDE), 1, 0
            )

        @pl.when(step >= out_steps)
        def _():
            value_ref[...] = mm(
                normed_turned_ref[...], arrived[...].reshape(group * rows, WIDE), 1, 0
            )

    fetch(0, lambda copy: copy.start())

    def weight_copy(item, action):
        slot = lax.rem(item, 2)
        narrow = scan_matrix_ref.shape[1] % WIDE

        def one(matrix_ref, first, width):
            height = matrix_ref.shape[0]
            start = pl.multiple_of((item - first) * WIDE, WIDE)
            action(
                pltpu.make_async_copy(
                    matrix_ref.at[:, pl.ds(start, width)],
                    weights_ref.at[slot, pl.ds(0, height), pl.ds(0, width)],
                    weight_sem.at[slot],
                )
            )

        full = chunks - 1 if narrow else chunks

        @pl.when(item < gate_steps)
        def _():
            one(gate_matrix_ref, 0, WIDE)

        @pl.when((item >= gate_steps) & (item < full))
        def _():
            one(scan_matrix_ref, gate_steps, WIDE)

        if narrow:

            @pl.when(item == full)
            def _():
                one(scan_matrix_ref, gate_steps, narrow)

        @pl.when((item >= chunks) & (item < items))
        def _():
            one(out_matrix_ref, chunks, WIDE)

    items = chunks + model_width // WIDE

    def back_product(grad_ref, item, first, width):
        cols = pl.ds(pl.multiple_of((item - first) * WIDE, WIDE), width)
        weights = weights_ref[lax.rem(item, 2), 0:model_width, 0:width]
        normed_grad_ref[...] += mm(grad_ref[:, cols], weights, 1, 1)

    def norm_backward():
        def block(at, carry):
            some = pl.ds(pl.multiple_of(at * HEIGHT, HEIGHT), HEIGHT)
            hidden = hidden_ref[some, :].astype(f32)
            root_mean = lax.rsqrt(jnp.mean(hidden * hidden, axis=-1, keepdims=True) + norm_eps)
            plain = hidden * root_mean
            grad = normed_grad_ref[some, :]
            scaled = grad * scale_ref[0:1, :]
            input_grad_ref[some, :] = root_mean * (
                scaled - plain * jnp.mean(scaled * plain, axis=-1, keepdims=True)
            ) + own_cot_ref[some, :].astype(f32)
            return carry + jnp.sum(grad * plain, axis=0, keepdims=True)

        total = lax.fori_loop(0, rows // HEIGHT, block, jnp.zeros((1, model_width), f32))
        first = iota((8, model_width), 0) == 0
        scale_grad_ref[...] = jnp.where(first, total, 0.0)
        for i in range(1, group):
            scale_copy(i, lax.rem(me + i, group), me).start()
        small_all_ref[me, :, packed:] = scale_grad_ref[...]

    def local_product(item):
        narrow = scan_matrix_ref.shape[1] % WIDE
        full = chunks - 1 if narrow else chunks

        @pl.when(item == 0)
        def _():
            normed_grad_ref[...] = jnp.zeros_like(normed_grad_ref)

        weight_copy(item, lambda copy: copy.wait())
        weight_copy(item + 1, lambda copy: copy.start())

        @pl.when(item < gate_steps)
        def _():
            back_product(gate_ref, item, 0, WIDE)

        @pl.when((item >= gate_steps) & (item < full))
        def _():
            back_product(scan_ref, item, gate_steps, WIDE)

        if narrow:

            @pl.when(item == full)
            def _():
                back_product(scan_ref, item, gate_steps, narrow)

        @pl.when(item == chunks - 1)
        def _():
            norm_backward()

        @pl.when(item >= chunks)
        def _():
            cols = pl.ds(pl.multiple_of((item - chunks) * WIDE, WIDE), WIDE)
            output_ref[:, cols] = hidden_ref[:, cols].astype(f32) + mm(
                post_ref[...], weights_ref[lax.rem(item, 2)], 1, 0
            )

    weight_copy(0, lambda copy: copy.start())

    def piece(ref, part, parts):
        if parts == 1:
            return ref
        size = own_in // parts
        start = part * size if isinstance(part, int) else pl.multiple_of(part * size, size)
        return ref.at[pl.ds(start, size), :]

    def up_copy(source, target, step, part, parts, recv, to):
        return seq_copy(
            piece(source, part, parts),
            piece(target, part, parts),
            up_send.at[step, part],
            recv.at[step, part],
            to,
        )

    def down_copy(total, step, part, parts, send, to):
        return seq_copy(
            piece(total, part, parts),
            piece(total, part, parts),
            send.at[step, part],
            total_recv.at[step, part],
            to,
        )

    def up(value, inbox, total, step, parts, after):
        edge = ((rank == 0) | (rank == last)) & (rank != root)
        inner_place = (rank != root) & (rank > 0) & (rank < last)
        for part in range(parts):
            here = piece(value, part, parts)
            inbox_here = piece(inbox, part, parts)
            total_here = piece(total, part, parts)

            @pl.when(edge)
            def _(here=here, inbox_here=inbox_here):
                inbox_here[...] = here[...]

            @pl.when(inner_place)
            def _(here=here, inbox_here=inbox_here, part=part):
                up_copy(inbox, inbox, step, part, parts, inbox_recv, left).wait_recv()
                inbox_here[...] += here[...]

            @pl.when(rank < root)
            def _(part=part):
                up_copy(inbox, inbox, step, part, parts, inbox_recv, right).start()

            @pl.when(rank == root + 1)
            def _(part=part):
                up_copy(inbox, total, step, part, parts, other_recv, left).start()

            @pl.when(rank > root + 1)
            def _(part=part):
                up_copy(inbox, inbox, step, part, parts, inbox_recv, left).start()

            @pl.when(rank == root)
            def _(here=here, inbox_here=inbox_here, total_here=total_here, part=part):
                result = here[...]
                if root > 0:
                    up_copy(inbox, inbox, step, part, parts, inbox_recv, left).wait_recv()
                    result = result + inbox_here[...]
                if root < last:
                    up_copy(total, total, step, part, parts, other_recv, right).wait_recv()
                    result = result + total_here[...]
                total_here[...] = result
                if root > 0:
                    down_copy(total, step, part, parts, left_send, left).start()
                if root < last:
                    down_copy(total, step, part, parts, right_send, right).start()

            after(part)

    def down(total, step, part, parts):
        @pl.when(rank < root)
        def _():
            down_copy(total, step, part, parts, left_send, left).wait_recv()

            @pl.when(rank > 0)
            def _():
                down_copy(total, step, part, parts, left_send, left).start()

        @pl.when(rank > root)
        def _():
            down_copy(total, step, part, parts, right_send, right).wait_recv()

            @pl.when(rank < last)
            def _():
                down_copy(total, step, part, parts, right_send, right).start()

    def drain(inbox, total, step, parts):
        for part in range(parts):

            @pl.when(rank < root)
            def _(part=part):
                up_copy(inbox, inbox, step, part, parts, inbox_recv, right).wait_send()

            @pl.when(rank > root)
            def _(part=part):
                up_copy(inbox, inbox, step, part, parts, inbox_recv, left).wait_send()

            @pl.when((rank <= root) & (rank > 0))
            def _(part=part):
                down_copy(total, step, part, parts, left_send, left).wait_send()

            @pl.when((rank >= root) & (rank < last))
            def _(part=part):
                down_copy(total, step, part, parts, right_send, right).wait_send()

    def stored(step, action):
        @pl.when(step < out_steps)
        def _():
            some = pl.ds(pl.multiple_of(lax.rem(step, 2) * own_in, own_in), own_in)
            cols = pl.ds(pl.multiple_of(step // 2 * WIDE, WIDE), WIDE)
            action(
                pltpu.make_async_copy(
                    total_ref.at[step], out_ref.at[some, cols], store_sem.at[step]
                )
            )

        @pl.when(step >= out_steps)
        def _():
            cols = pl.ds(pl.multiple_of((step - out_steps) * WIDE, WIDE), WIDE)
            action(
                pltpu.make_async_copy(total_ref.at[step], in_ref.at[:, cols], store_sem.at[step])
            )

    behind = lag * (jnp.maximum(rank - root, 0) + jnp.maximum(root - rank, 0))

    def round_(step, carry):
        for stage in range(reach, -1, -1):
            chunk = step - stage * spacing

            @pl.when((chunk >= 0) & (chunk < chunks))
            def _(chunk=chunk, stage=stage):
                ring.stage(chunk, stage)

        @pl.when((step + 1 >= out_steps) & (step + 1 < steps))
        def _():
            ring.wait_pair(step + 1 - out_steps)

        @pl.when(step + 1 < steps)
        def _():
            fetch(step + 1, lambda copy: copy.start())

        def down_late(part):
            late = PARTS * step + part - behind
            late_step = late // PARTS
            late_part = lax.rem(late, PARTS)

            @pl.when((late >= 0) & (late_step < steps))
            def _():
                down(total_ref.at[late_step], late_step, late_part, PARTS)

                @pl.when(late_part == PARTS - 1)
                def _():
                    stored(late_step, lambda copy: copy.start())

            @pl.when(late == PARTS * steps)
            def _():
                down(small_out_ref, steps, 0, 1)

        @pl.when(step < steps)
        def _():
            compute(step)
            up(value_ref, inbox_ref.at[step], total_ref.at[step], step, PARTS, down_late)

        @pl.when(step == steps)
        def _():
            for i in range(1, group):
                small_copy(i, lax.rem(me + i, group), me).wait_send()
                origin = lax.rem(me + group - i, group)
                small_copy(i, origin, origin).wait_recv()
                scale_copy(i, origin, me).wait_send()
                scale_copy(i, origin, origin).wait_recv()
            small_value_ref[...] = jnp.sum(small_all_ref[...], axis=0)
            up(small_value_ref, small_inbox_ref, small_out_ref, steps, 1, lambda part: None)

        @pl.when(step >= steps)
        def _():
            for part in range(PARTS):
                down_late(part)

        @pl.when(step < items)
        def _():
            local_product(step)

        return carry

    lax.fori_loop(0, steps + 1 + (behind + PARTS - 1) // PARTS, round_, 0)

    def finish(step, carry):
        drain(inbox_ref.at[step], total_ref.at[step], step, PARTS)
        stored(step, lambda copy: copy.wait())
        return carry

    lax.fori_loop(0, steps, finish, 0)
    drain(small_inbox_ref, small_out_ref, steps, 1)

    def finish_ring(chunk, carry):
        ring.finish(chunk)
        return carry

    lax.fori_loop(0, chunks, finish_ring, 0)


def reduce_gradients(
    normed_turned, post_turned, cot_all, gate_grad, scan_grad, small, hidden, cot, post, scale, matrices
):
    size = lax.axis_size("seq")
    group = lax.axis_size("dp")
    rows = gate_grad.shape[0]
    own_in = normed_turned.shape[0]
    model_width = hidden.shape[1]
    out_steps = 2 * (model_width // WIDE)
    gate_steps = gate_grad.shape[1] // WIDE
    chunks = gate_steps + scan_grad.shape[1] // WIDE
    steps = out_steps + chunks
    reach = group // 4
    spacing = min(3, (out_steps - 2) // reach)
    sizes = (rows, own_in, out_steps, gate_steps, steps, size // 2, LAG, spacing)
    assert chunks + model_width // WIDE <= steps
    shape = jax.ShapeDtypeStruct
    dma = pltpu.SemaphoreType.DMA
    small_shape = (8, small.shape[2] + model_width)
    anywhere = pl.BlockSpec(memory_space=pl.ANY)
    return pl.pallas_call(
        functools.partial(tail_kernel, sizes),
        out_shape=(
            shape((own_in, chunks * WIDE), f32),
            shape((2 * own_in, model_width), f32),
            shape(small_shape, f32),
            shape((rows, model_width), f32),
            shape((rows, model_width), f32),
            shape((chunks, 2, group // 2, rows, WIDE), bf16),
        ),
        in_specs=vmem(2) + [anywhere] + vmem(7) + [anywhere] * 3,
        out_specs=(anywhere, anywhere) + tuple(vmem(3)) + (anywhere,),
        scratch_shapes=[
            pltpu.VMEM((own_in, WIDE), f32),
            pltpu.VMEM((steps, own_in, WIDE), f32),
            pltpu.VMEM((steps, own_in, WIDE), f32),
            pltpu.VMEM((2, 2, group // 2, rows, WIDE), bf16),
            pltpu.VMEM(small_shape, f32),
            pltpu.VMEM(small_shape, f32),
            pltpu.VMEM((group,) + small_shape, f32),
            pltpu.VMEM((2, matrices[2].shape[0], WIDE), bf16),
            pltpu.VMEM((rows, model_width), f32),
            pltpu.VMEM((8, model_width), f32),
        ]
        + [dma((steps + 1, PARTS))] * 6
        + [
            dma((steps,)),
            *PlaneRing.semaphores(chunks),
            dma((2,)),
            *[dma((group,))] * 4,
            dma((2,)),
        ],
        compiler_params=pltpu.CompilerParams(
            collective_id=3, has_side_effects=True, vmem_limit_bytes=56 * 2**20
        ),
        cost_estimate=pl.CostEstimate(
            flops=2 * 10**10, bytes_accessed=2 * 10**8, transcendentals=0
        ),
    )(
        normed_turned,
        post_turned,
        cot_all,
        gate_grad,
        scan_grad,
        small,
        hidden,
        cot,
        post,
        scale,
        *matrices,
    )


def on_device(
    hidden_in,
    out_grad,
    prenorm,
    inproject,
    convtaps,
    headcoefs,
    postnorm,
    outproject,
    prenorm_first,
    inproject_first,
    convtaps_first,
    headcoefs_first,
    postnorm_first,
    outproject_first,
    prenorm_second,
    inproject_second,
    convtaps_second,
    headcoefs_second,
    postnorm_second,
    outproject_second,
):
    group = lax.axis_size("dp")
    me = lax.axis_index("dp")
    seq_here, rows, model_width = hidden_in.shape
    assert seq_here == 1
    heads = headcoefs.shape[1]
    own_in, proj_width = inproject.shape
    own_out = outproject.shape[0]
    inner = own_out * group
    width = inner // heads
    per_tile = LANES // width
    tiles = inner // LANES
    sizes = (rows, inner, tiles, per_tile)
    conv_own = convtaps.shape[1]
    conv_width = conv_own * group

    tap_rows = convtaps.shape[0]
    small_lanes = -(-max(own_in, own_out, conv_own) // LANES) * LANES
    small = jnp.concatenate(
        [
            jnp.pad(part, ((0, 0), (0, small_lanes - part.shape[1])))
            for part in (prenorm.reshape(1, -1), convtaps, postnorm.reshape(1, -1))
        ]
    )
    small = jnp.pad(small, ((0, 16 - small.shape[0]), (0, 0))).astype(bf16)
    hidden_low = hidden_in.reshape(rows, model_width)
    cot_low = out_grad.reshape(rows, model_width)
    head_rows = jnp.pad(headcoefs, ((0, 8 - headcoefs.shape[0]), (0, LANES - heads)))
    skip = jnp.repeat(headcoefs[2:3], width, axis=1)
    (
        pre_scale,
        gate_grad,
        postnorm_grad,
        post_low,
        normed_turned,
        post_turned,
        scan_grad,
        conv_grad,
        head_grad,
        scan_matrix,
        gate_matrix,
        out_matrix,
        cot_all,
    ) = front(inproject, outproject, small, hidden_low, cot_low, head_rows, skip, sizes)
    scan_matrix = scan_matrix.reshape(model_width, -1)
    gate_matrix = gate_matrix.reshape(model_width, inner)
    out_matrix = out_matrix.reshape(inner, model_width)
    head_sums = jnp.concatenate(
        [
            head_grad[:2, :heads],
            jnp.sum(conv_grad[tap_rows : tap_rows + 1, :inner].reshape(1, heads, width), axis=-1),
        ],
        axis=0,
    )
    conv_sums = conv_grad[:tap_rows].reshape(tap_rows, group, conv_own)
    packed = jnp.concatenate(
        [
            postnorm_grad.reshape(group, own_out),
            jnp.swapaxes(conv_sums, 0, 1).reshape(group, -1),
            jnp.broadcast_to(head_sums.reshape(1, -1), (group, 3 * heads)),
        ],
        axis=1,
    )
    packed_size = packed.shape[1]
    packed_lanes = -(-packed_size // (8 * LANES)) * LANES
    packed = jnp.pad(packed, ((0, 0), (0, 8 * packed_lanes - packed_size)))
    inproj_padded, outproj_owned, packed, output, input_gradient, _ = reduce_gradients(
        normed_turned,
        post_turned,
        cot_all,
        gate_grad,
        scan_grad,
        packed.reshape(group, 8, packed_lanes),
        hidden_low,
        cot_low,
        post_low,
        pre_scale,
        (gate_matrix, scan_matrix, out_matrix),
    )
    inproj_owned = inproj_padded[:, :proj_width]
    prenorm_owned = lax.dynamic_slice_in_dim(packed[0, packed_lanes:], me * own_in, own_in, 0)
    packed = packed[:, :packed_lanes].reshape(-1)
    postnorm_owned = packed[:own_out]
    conv_at = own_out
    conv_end = conv_at + tap_rows * conv_own
    conv_owned = packed[conv_at:conv_end].reshape(tap_rows, conv_own)
    head_total = packed[conv_end:packed_size].reshape(3, heads)

    prenorm_new, prenorm_mom, prenorm_sq = adam_update(
        prenorm, prenorm_first, prenorm_second, prenorm_owned, rate_vector, 0.0
    )
    inproj_new, inproj_mom, inproj_sq = adam_update(
        inproject, inproject_first, inproject_second, inproj_owned, rate_matrix, weight_decay
    )
    conv_new, conv_mom, conv_sq = adam_update(
        convtaps, convtaps_first, convtaps_second, conv_owned, rate_vector, 0.0
    )
    head_new, head_mom, head_sq = adam_update(
        headcoefs, headcoefs_first, headcoefs_second, head_total, rate_vector, 0.0
    )
    postnorm_new, postnorm_mom, postnorm_sq = adam_update(
        postnorm, postnorm_first, postnorm_second, postnorm_owned, rate_vector, 0.0
    )
    outproj_new, outproj_mom, outproj_sq = adam_update(
        outproject, outproject_first, outproject_second, outproj_owned, rate_matrix, weight_decay
    )
    return (
        output.reshape(seq_here, rows, model_width),
        input_gradient.reshape(seq_here, rows, model_width),
        prenorm_owned,
        inproj_owned,
        conv_owned,
        head_total,
        postnorm_owned,
        outproj_owned,
        prenorm_new,
        inproj_new,
        conv_new,
        head_new,
        postnorm_new,
        outproj_new,
        prenorm_mom,
        inproj_mom,
        conv_mom,
        head_mom,
        postnorm_mom,
        outproj_mom,
        prenorm_sq,
        inproj_sq,
        conv_sq,
        head_sq,
        postnorm_sq,
        outproj_sq,
    )


def solution(mesh):
    weights = (P("dp"), P("dp", None), P(None, "dp"), P(), P("dp"), P("dp", None))
    tokens = (P("dp", "seq", None), P("dp", "seq", None))
    return jax.shard_map(
        on_device,
        mesh=mesh,
        in_specs=tokens + weights * 3,
        out_specs=tokens + weights * 4,
        check_vma=False,
    )
```

```python
import functools

import jax
import jax.numpy as jnp
from jax import lax
from jax.experimental import pallas as pl
from jax.experimental.pallas import tpu as pltpu
from jax.sharding import PartitionSpec as P

N = 128
LANES = 128
HALO = 16
WIDE = 256
HEIGHT = 32
PARTS = 2
LAG = 4
COT_AT = 8
EARLY = 6
COT_SPACING = 5

norm_eps = 1e-05
beta_moment = 0.9
beta_square = 0.95
adam_eps = 1e-08
adam_step = 3.0
rate_matrix = 0.005
rate_vector = 0.05
weight_decay = 0.1

f32 = jnp.float32
bf16 = jnp.bfloat16
MESH = pl.DeviceIdType.MESH


def adam_update(weight, moment, square, gradient, step_rate, decay_rate):
    moment_new = beta_moment * moment + (1.0 - beta_moment) * gradient
    square_new = beta_square * square + (1.0 - beta_square) * gradient * gradient
    moment_hat = moment_new / (1.0 - beta_moment**adam_step)
    square_hat = square_new / (1.0 - beta_square**adam_step)
    updated = weight - step_rate * (
        moment_hat / (jnp.sqrt(square_hat) + adam_eps) + decay_rate * weight
    )
    return (updated, moment_new, square_new)


def mm(a, b, ca, cb):
    return lax.dot_general(a, b, (((ca,), (cb,)), ((), ())), preferred_element_type=f32)


def halves(a):
    hi = a.astype(bf16)
    return hi, (a - hi.astype(f32)).astype(bf16)


def thirds(a):
    hi = a.astype(bf16)
    rest = a - hi.astype(f32)
    mid = rest.astype(bf16)
    return hi, mid, (rest - mid.astype(f32)).astype(bf16)


def mm3(a, b, ca, cb):
    return mm(a[0], b[0], ca, cb) + mm(a[0], b[1], ca, cb) + mm(a[1], b[0], ca, cb)


def iota(shape, dim):
    return lax.broadcasted_iota(jnp.int32, shape, dim)


def head_lanes(tile, heads_a_tile, copies):
    rows = iota((copies * LANES, LANES), 0)
    lane_head = tile * heads_a_tile + iota((copies * LANES, LANES), 1) // (LANES // heads_a_tile)
    return (rows % LANES == lane_head).astype(f32).astype(bf16)


def conv_tile(conv_ref, halo_ref, u_ref, taps_ref, start, rows):
    cols = pl.ds(start, LANES)
    conv_ref[0:HALO, :] = halo_ref[:, cols].astype(f32)
    conv_ref[HALO : HALO + rows, :] = u_ref[:, cols].astype(f32)
    taps = taps_ref[:, cols]
    pre = taps[4:5, :] + taps[0:1, :] * conv_ref[HALO - 3 : HALO - 3 + rows, :]
    for k in range(1, 4):
        pre = pre + taps[k : k + 1, :] * conv_ref[HALO - 3 + k : HALO - 3 + k + rows, :]
    return pre, jax.nn.sigmoid(pre)


def seq_copy(src, dst, send, recv, to):
    return pltpu.make_async_remote_copy(
        src_ref=src,
        dst_ref=dst,
        send_sem=send,
        recv_sem=recv,
        device_id={"seq": to},
        device_id_type=MESH,
    )


def greet_seq(barrier, rank, last):
    @pl.when(rank > 0)
    def _():
        pl.semaphore_signal(barrier, inc=1, device_id={"seq": rank - 1}, device_id_type=MESH)

    @pl.when(rank < last)
    def _():
        pl.semaphore_signal(barrier, inc=1, device_id={"seq": rank + 1}, device_id_type=MESH)


def seq_neighbours(rank, last):
    return jnp.minimum(rank, 1) + jnp.minimum(last - rank, 1)


def greet_plane(barrier, me, group):
    for i in range(1, group):
        pl.semaphore_signal(
            barrier, inc=1, device_id={"dp": lax.rem(me + i, group)}, device_id_type=MESH
        )


def slot_of(device, group):
    return lax.rem(device, 2) * (group // 2) + device // 2


def ring_place(at, chips):
    half = chips // 2
    turned = at // half
    return at * (1 - turned) + turned * (3 * half - 1 - at)


def front_kernel(
    sizes,
    in_shard_ref,
    out_shard_ref,
    prenorm_ref,
    convtaps_ref,
    postnorm_ref,
    hidden_ref,
    cot_ref,
    headcoefs_ref,
    pre_scale_ref,
    gate_grad_out_ref,
    post_out_ref,
    normed_turned_ref,
    post_turned_ref,
    dproj_ref,
    packed_ref,
    scan_all_ref,
    gate_all_ref,
    out_all_ref,
    cot_all_ref,
    u_ref,
    ypre_ref,
    enter_ref,
    halo_ref,
    step_ref,
    cum_ref,
    cumt_ref,
    taps_ref,
    dy_ref,
    post_t_ref,
    in_wide_ref,
    out_wide_ref,
    scan_shard_ref,
    gate_shard_ref,
    out_low_ref,
    small_all_ref,
    post_scale_ref,
    normed_ref,
    weights_ref,
    out_weights_ref,
    conv_ref,
    score_ref,
    leave_ref,
    mixer_ref,
    gate_ref,
    gated_ref,
    dpost_ref,
    normed_t_ref,
    dscore_ref,
    dread_ref,
    dwrite_ref,
    dcum_ref,
    dstep_ref,
    dpre_ref,
    arrive_ref,
    post_grad_ref,
    gate_grad_ref,
    post_ref,
    small_ref,
    heads_ref,
    skip_ref,
    send_sem,
    recv_sem,
    halo_sem,
    back_send,
    back_recv,
    edge_sem,
    leave_sem,
    small_send,
    small_recv,
    turn_send,
    turn_recv,
    own_sem,
    wide_sem,
    weight_sem,
    *ring_sems,
):
    rows, inner, tiles, per_tile = sizes
    conv_width = inner + 2 * N
    own_in = in_shard_ref.shape[0]
    own_out, model_width = out_shard_ref.shape
    scan_width = in_shard_ref.shape[1] - inner
    rank = lax.axis_index("seq")
    last = lax.axis_size("seq") - 1
    me = lax.axis_index("dp")
    group = lax.axis_size("dp")
    in_chunks = own_in // HEIGHT
    out_height = 2 * HEIGHT
    out_chunks = own_out // out_height

    def wide_rows(chunk):
        return pl.ds(pl.multiple_of(chunk * HEIGHT, HEIGHT), HEIGHT)

    def in_wide(chunk):
        some = wide_rows(chunk)
        return pltpu.make_async_copy(
            in_shard_ref.at[some, :], in_wide_ref.at[some, :], wide_sem.at[chunk]
        )

    out_wide = pltpu.make_async_copy(out_shard_ref, out_wide_ref, wide_sem.at[in_chunks])
    for chunk in range(in_chunks):
        in_wide(chunk).start()
    out_wide.start()
    conv_own = convtaps_ref.shape[1]
    small_rows = [
        jnp.concatenate([part, jnp.zeros((part.shape[0], width), f32)], axis=1)
        if width
        else part
        for part, width in (
            (ref[...], small_ref.shape[1] - ref.shape[1])
            for ref in (prenorm_ref, convtaps_ref, postnorm_ref)
        )
    ]
    small_rows.append(jnp.zeros((9, small_ref.shape[1]), f32))
    small_ref[...] = jnp.concatenate(small_rows, axis=0).astype(bf16)
    heads_ref[...] = jnp.zeros_like(heads_ref)
    heads_ref[0:3, 0 : headcoefs_ref.shape[1]] = headcoefs_ref[...]
    barrier = pltpu.get_barrier_semaphore()
    greet_seq(barrier, rank, last)
    greet_plane(barrier, me, group)
    pl.semaphore_wait(barrier, seq_neighbours(rank, last) + group - 1)
    right = jnp.minimum(rank + 1, last)
    left = jnp.maximum(rank - 1, 0)

    def small_copy(i, peer, slot):
        return plane_copy(
            small_ref, small_all_ref.at[slot], small_send.at[i], small_recv.at[i], peer
        )

    for i in range(1, group):
        small_copy(i, lax.rem(me + i, group), me).start()
    small_all_ref[me] = small_ref[...]
    scan_shard_ref[:, scan_width - scan_width % LANES :] = jnp.zeros(
        (own_in, scan_shard_ref.shape[1] - scan_width + scan_width % LANES), bf16
    )

    def prepare_scan(chunk):
        some = wide_rows(chunk)
        in_wide(chunk).wait()
        scan_shard_ref[some, 0:scan_width] = in_wide_ref[some, inner:].astype(bf16)

    def prepare_gate(chunk):
        some = wide_rows(chunk)
        gate_shard_ref[some, :] = in_wide_ref[some, 0:inner].astype(bf16)

    def prepare_out(chunk):
        @pl.when(chunk == 0)
        def _():
            out_wide.wait()

        some = pl.ds(pl.multiple_of(chunk * out_height, out_height), out_height)
        out_low_ref[some, :] = out_wide_ref[some, :].astype(bf16)

    scan_ring = weight_ring(scan_shard_ref, scan_all_ref, HEIGHT, ring_sems[0:5], prepare_scan)
    gate_ring = weight_ring(gate_shard_ref, gate_all_ref, HEIGHT, ring_sems[5:10], prepare_gate)
    out_ring = weight_ring(out_low_ref, out_all_ref, out_height, ring_sems[10:15], prepare_out)
    spacing = 3
    rings = (
        (scan_ring, 0, in_chunks),
        (gate_ring, in_chunks, in_chunks),
        (out_ring, 2 * in_chunks, out_chunks),
    )

    def round_(step):
        for ring, first, chunks in rings:
            ring.round(step - first, chunks, spacing)

    def rounds(first, end):
        def one(step, carry):
            round_(step)
            return carry

        lax.fori_loop(first, end, one, 0)

    def complete(at):
        ring, first, chunks = rings[at]
        return first + chunks + spacing * ring.reach

    def wait_pairs(at):
        ring, _, chunks = rings[at]

        def one(chunk, carry):
            ring.wait_pair(chunk)
            return carry

        lax.fori_loop(0, chunks, one, 0)

    rounds(0, 2)

    for i in range(1, group):
        small_copy(i, lax.rem(me + i, group), me).wait_send()
        small_copy(i, me, lax.rem(me + group - i, group)).wait_recv()
    taps_ref[...] = jnp.zeros_like(taps_ref)
    for device in range(group):
        small = small_all_ref[device].astype(f32)
        pre_scale_ref[0:1, device * own_in : (device + 1) * own_in] = small[0:1, 0:own_in]
        taps_ref[0:5, device * conv_own : (device + 1) * conv_own] = small[1:6, 0:conv_own]
        post_scale_ref[0:1, device * own_out : (device + 1) * own_out] = small[6:7, 0:own_out]
    pre_scale_ref[1:8, :] = jnp.zeros((7, model_width), f32)

    skip_parts = jnp.concatenate(
        thirds(jnp.broadcast_to(heads_ref[2:3, :], (8, LANES))), axis=1
    )

    def spread_skip(tile, carry):
        cols = pl.ds(pl.multiple_of(tile * LANES, LANES), LANES)
        skip_ref[0:1, cols] = mm(skip_parts, head_lanes(tile, per_tile, 3), 1, 0)[0:1, :]
        return carry

    lax.fori_loop(0, tiles, spread_skip, 0)

    def norm(at, carry):
        some = pl.ds(pl.multiple_of(at * HEIGHT, HEIGHT), HEIGHT)
        hidden = hidden_ref[some, :].astype(f32)
        root = lax.rsqrt(jnp.mean(hidden * hidden, axis=-1, keepdims=True) + norm_eps)
        normed_ref[some, :] = (hidden * root * pre_scale_ref[0:1, :]).astype(bf16)
        return carry

    lax.fori_loop(0, rows // HEIGHT, norm, 0)

    def turn(source_ref, target_ref):
        def one(at, carry):
            cols = pl.ds(pl.multiple_of(at * LANES, LANES), LANES)
            target_ref[cols, :] = source_ref[:, cols].astype(f32).T.astype(bf16)
            return carry

        lax.fori_loop(0, source_ref.shape[1] // LANES, one, 0)

    turn(normed_ref, normed_t_ref)
    rounds(2, complete(0))
    wait_pairs(0)

    def weight_copy(all_ref, at, width):
        slot = lax.rem(at, 2)
        cols = pl.ds(pl.multiple_of(at * WIDE, WIDE), width)
        return pltpu.make_async_copy(
            all_ref.at[:, :, :, cols],
            weights_ref.at[slot, :, :, :, pl.ds(0, width)],
            weight_sem.at[slot],
        )

    def columns(all_ref, action):
        total = all_ref.shape[3]
        full = total // WIDE
        rest = total % WIDE

        def fetch(at, act):
            @pl.when(at < full)
            def _():
                act(weight_copy(all_ref, at, WIDE))

            if rest:

                @pl.when(at == full)
                def _():
                    act(weight_copy(all_ref, at, rest))

        fetch(0, lambda copy: copy.start())

        def one(at, carry):
            fetch(at + 1, lambda copy: copy.start())
            fetch(at, lambda copy: copy.wait())
            weights = weights_ref[lax.rem(at, 2)].reshape(model_width, WIDE)
            action(at, WIDE, mm(normed_ref[...], weights, 1, 0))
            return carry

        lax.fori_loop(0, full, one, 0)
        if rest:
            fetch(full, lambda copy: copy.wait())
            weights = weights_ref[full % 2, :, :, :, 0:rest].reshape(model_width, rest)
            action(full, rest, mm(normed_ref[...], weights, 1, 0))

    def keep_scan(at, width, product):
        cols = pl.ds(at * WIDE if isinstance(at, int) else pl.multiple_of(at * WIDE, WIDE), width)
        u_ref[:, cols] = product.astype(bf16)

    columns(scan_all_ref, keep_scan)
    halo_copy = seq_copy(
        u_ref.at[pl.ds(rows - HALO, HALO), pl.ds(0, conv_width)],
        halo_ref,
        halo_sem.at[0],
        halo_sem.at[1],
        right,
    )

    @pl.when(rank < last)
    def _():
        halo_copy.start()

    round_(complete(0))
    step = jax.nn.softplus(u_ref[:, conv_width:].astype(f32) + heads_ref[0:1, :])
    decay = -step * jnp.exp(heads_ref[1:2, :])
    lower = (iota((rows, rows), 0) >= iota((rows, rows), 1)).astype(f32).astype(bf16)
    cum = sum(mm(lower, part, 1, 0) for part in thirds(decay))
    step_ref[...] = step
    cum_ref[...] = cum
    cumt_ref[...] = cum.T

    @pl.when(rank > 0)
    def _():
        halo_copy.wait_recv()

    @pl.when(rank == 0)
    def _():
        halo_ref[...] = jnp.zeros_like(halo_ref)

    pre_b, sig_b = conv_tile(conv_ref, halo_ref, u_ref, taps_ref, inner, rows)
    b_parts = halves(pre_b * sig_b)
    pre_c, sig_c = conv_tile(conv_ref, halo_ref, u_ref, taps_ref, inner + N, rows)
    c_parts = halves(pre_c * sig_c)
    scores = mm3(c_parts, b_parts, 1, 1)
    causal = iota((rows, rows), 0) >= iota((rows, rows), 1)
    score_ref[...] = jnp.where(causal, scores, 0.0)
    cum_parts = jnp.concatenate(thirds(cum), axis=1)
    step_parts = jnp.concatenate(thirds(step), axis=1)
    lane = iota((rows, LANES), 1)
    width = LANES // per_tile

    def chain(tile):
        return seq_copy(
            leave_ref.at[tile], enter_ref.at[tile], send_sem.at[tile], recv_sem.at[tile], right
        )

    def one(tile, carry):
        start = pl.multiple_of(tile * LANES, LANES)
        cols = pl.ds(start, LANES)
        pick = head_lanes(tile, per_tile, 3)
        cum_l = mm(cum_parts, pick, 1, 0)
        step_l = mm(step_parts, pick, 1, 0)
        pre, sig = conv_tile(conv_ref, halo_ref, u_ref, taps_ref, start, rows)
        values = pre * sig
        x = values * step_l
        total = cum_l[rows - 1 : rows, :]
        fresh = mm3(b_parts, halves(x * jnp.exp(total - cum_l)), 0, 0)

        @pl.when(rank > 0)
        def _():
            chain(tile).wait_recv()

        @pl.when(rank == 0)
        def _():
            enter_ref[tile] = jnp.zeros((N, LANES), f32)

        enter = enter_ref[tile]
        leave_ref[tile] = jnp.exp(total) * enter + fresh

        @pl.when(rank < last)
        def _():
            chain(tile).start()

        result = mm3(c_parts, halves(enter), 1, 0) * jnp.exp(cum_l)
        for h in range(per_tile):
            row = cumt_ref[pl.ds(tile * per_tile + h, 1), :]
            col = cum_l[:, h * width : h * width + 1]
            kernel = jnp.exp(jnp.minimum(col - row, 0.0)) * score_ref[...]
            own = (lane // width) == h
            result = result + mm3(halves(kernel), halves(jnp.where(own, x, 0.0)), 1, 0)
        ypre_ref[:, cols] = result
        mixer_ref[:, cols] = (result + skip_ref[0:1, cols] * values).astype(bf16)

        @pl.when(lax.rem(tile, pace) == pace - 1)
        def _():
            round_(in_loop + tile // pace)

        return carry

    in_loop = complete(0) + 1
    pace = 4
    lax.fori_loop(0, tiles, one, 0)
    at_round = in_loop + tiles // pace
    rounds(at_round, max(at_round, complete(1)))
    at_round = max(at_round, complete(1))
    wait_pairs(1)

    gated_ref_sum = score_ref

    def keep_gate(at, width, product):
        cols = pl.ds(at * WIDE if isinstance(at, int) else pl.multiple_of(at * WIDE, WIDE), width)
        gated = mixer_ref[:, cols].astype(f32) * (product * jax.nn.sigmoid(product))
        gate_ref[:, cols] = product
        gated_ref[:, cols] = gated
        square = gated * gated
        total = square[:, 0:LANES]
        for part in range(1, width // LANES):
            total = total + square[:, part * LANES : (part + 1) * LANES]
        gated_ref_sum[:, 0:LANES] += total

    gated_ref_sum[:, 0:LANES] = jnp.zeros((rows, LANES), f32)
    columns(gate_all_ref, keep_gate)
    end_round = complete(2)
    rounds(at_round, min(at_round + 1, end_round))
    at_round = min(at_round + 1, end_round)
    root = lax.rsqrt(
        jnp.sum(gated_ref_sum[:, 0:LANES], axis=-1, keepdims=True) / inner + norm_eps
    )

    def keep_post(at, carry):
        cols = pl.ds(pl.multiple_of(at * WIDE, WIDE), WIDE)
        whitened = gated_ref[:, cols] * root
        gated_ref[:, cols] = whitened
        post_ref[:, cols] = (whitened * post_scale_ref[0:1, cols]).astype(bf16)
        return carry

    lax.fori_loop(0, inner // WIDE, keep_post, 0)
    turn(post_ref, post_t_ref)
    rounds(at_round, end_round)
    wait_pairs(2)
    normed_turn = PlaneTurn(
        normed_t_ref,
        normed_turned_ref,
        own_in,
        rows,
        (turn_send.at[0], turn_recv.at[0], own_sem.at[0]),
    )
    post_turn = PlaneTurn(
        post_t_ref,
        post_turned_ref,
        own_out,
        rows,
        (turn_send.at[1], turn_recv.at[1], own_sem.at[1]),
    )
    post_turn.start()
    normed_turn.start()

    span = 2 * own_out

    def out_copy(chip):
        slot = chip % 2
        return pltpu.make_async_copy(
            out_all_ref.at[chip], out_weights_ref.at[slot], weight_sem.at[slot]
        )

    out_copy(0).start()
    overlap = jnp.zeros((rows, LANES), f32)
    for chip in range(group // 2):
        if chip + 1 < group // 2:
            out_copy(chip + 1).start()
        out_copy(chip).wait()
        cols = slice(chip * span, (chip + 1) * span)
        weights = out_weights_ref[chip % 2].reshape(span, model_width)
        dpost = mm(cot_ref[...], weights, 1, 1)
        dpost_ref[:, cols] = dpost
        pulled = dpost * gated_ref[:, cols]
        post_grad_ref[0:1, cols] = jnp.sum(pulled, axis=0, keepdims=True)
        pulled = pulled * post_scale_ref[0:1, cols]
        for part in range(span // LANES):
            overlap = overlap + pulled[:, part * LANES : (part + 1) * LANES]
    mean = jnp.sum(overlap, axis=-1, keepdims=True) / inner

    def keep_back(at, carry):
        cols = pl.ds(pl.multiple_of(at * WIDE, WIDE), WIDE)
        gate = gate_ref[:, cols]
        sig = jax.nn.sigmoid(gate)
        dgated = root * (dpost_ref[:, cols] * post_scale_ref[0:1, cols] - gated_ref[:, cols] * mean)
        dy_ref[:, cols] = (dgated * (gate * sig)).astype(bf16)
        gate_grad_ref[:, cols] = (
            dgated * mixer_ref[:, cols].astype(f32) * sig * (1.0 + gate * (1.0 - sig))
        ).astype(bf16)
        return carry

    lax.fori_loop(0, inner // WIDE, keep_back, 0)

    @pl.when(rank < last)
    def _():
        halo_copy.wait_send()

        def drain(tile, carry):
            chain(tile).wait_send()
            return carry

        lax.fori_loop(0, tiles, drain, 0)

    for ring, _, chunks in rings:

        def finish(chunk, carry, ring=ring):
            ring.finish(chunk)
            return carry

        lax.fori_loop(0, chunks, finish, 0)

    def backward():
        core = lax.rem(me, 2)
        cot_chunks = EARLY

        def cot_block(chunk, origin, part):
            ref = cot_all_ref.at[chunk, core, origin]
            return ref if part is None else ref.at[pl.ds(part * (rows // 2), rows // 2), :]

        def cot_source(chunk, part, action):
            part_rows = pl.ds(0, rows) if part is None else pl.ds(part * (rows // 2), rows // 2)
            cols = pl.ds(pl.multiple_of(chunk * WIDE, WIDE), WIDE)
            action(cot_ref.at[part_rows, cols])

        ring = PlaneRing(
            cot_block, cot_source, lambda chunk, half: cot_all_ref.at[chunk, half], cot_ring_sems
        )

        left = jnp.maximum(rank - 1, 0)
        cum = cum_ref[...]
        step = step_ref[...]
        pre_b, sig_b = conv_tile(conv_ref, halo_ref, u_ref, taps_ref, inner, rows)
        b_parts = halves(pre_b * sig_b)
        pre_c, sig_c = conv_tile(conv_ref, halo_ref, u_ref, taps_ref, inner + N, rows)
        c_parts = halves(pre_c * sig_c)
        later = iota((rows, rows), 1) >= iota((rows, rows), 0)
        score_ref[...] = jnp.where(later, mm3(b_parts, c_parts, 1, 1), 0.0)
        dscore_ref[...] = jnp.zeros_like(dscore_ref)
        dread_ref[...] = jnp.zeros_like(dread_ref)
        dwrite_ref[...] = jnp.zeros_like(dwrite_ref)
        dcum_ref[...] = jnp.zeros_like(dcum_ref)
        dstep_ref[...] = jnp.zeros_like(dstep_ref)
        cum_parts = jnp.concatenate(thirds(cum), axis=1)
        step_parts = jnp.concatenate(thirds(step), axis=1)
        lane = iota((rows, LANES), 1)
        final_row = iota((rows, LANES), 0) == rows - 1
        width = LANES // per_tile

        def chain(tile):
            return seq_copy(
                leave_ref.at[tile], arrive_ref.at[tile], back_send.at[tile], back_recv.at[tile], left
            )

        def tap_grads(dpre, extra):
            sums = [
                jnp.sum(
                    dpre * conv_ref[HALO - 3 + k : HALO - 3 + k + rows, :], axis=0, keepdims=True
                )
                for k in range(4)
            ]
            sums.append(jnp.sum(dpre, axis=0, keepdims=True))
            sums.append(extra)
            sums.append(jnp.zeros((2, LANES), f32))
            return jnp.concatenate(sums, axis=0)

        def one(tile, carry):
            start = pl.multiple_of(tile * LANES, LANES)
            cols = pl.ds(start, LANES)
            pick = head_lanes(tile, per_tile, 3)
            cum_l = mm(cum_parts, pick, 1, 0)
            step_l = mm(step_parts, pick, 1, 0)
            total = cum_l[rows - 1 : rows, :]
            dy = dy_ref[:, cols].astype(f32)
            reads = halves(dy * jnp.exp(cum_l))
            denter = mm3(c_parts, reads, 0, 0)

            @pl.when(rank < last)
            def _():
                chain(tile).wait_recv()

            @pl.when(rank == last)
            def _():
                arrive_ref[tile] = jnp.zeros((N, LANES), f32)

            arrive = arrive_ref[tile]
            leave_ref[tile] = jnp.exp(total) * arrive + denter

            @pl.when(rank > 0)
            def _():
                chain(tile).start()

            pre, sig = conv_tile(conv_ref, halo_ref, u_ref, taps_ref, start, rows)
            values = pre * sig
            x = values * step_l
            x_parts = halves(x)
            tail = jnp.exp(total - cum_l)
            enter = enter_ref[tile]
            arrive_parts = halves(arrive)
            dx_state = mm3(b_parts, arrive_parts, 1, 0) * tail
            dx = dx_state
            for h in range(per_tile):
                row = cumt_ref[pl.ds(tile * per_tile + h, 1), :]
                col = cum_l[:, h * width : h * width + 1]
                spread = jnp.exp(jnp.minimum(row - col, 0.0))
                kernel = halves(spread * score_ref[...])
                own = jnp.where((lane // width) == h, dy, 0.0).astype(bf16)
                dx = dx + (mm(kernel[0], own, 1, 0) + mm(kernel[1], own, 1, 0))
                pairs = mm(x_parts[0], own, 1, 1) + mm(x_parts[1], own, 1, 1)
                dscore_ref[...] += spread * pairs
            dread_ref[...] += mm3(reads, halves(enter), 1, 1)
            dwrite_ref[...] += mm3(halves(x * tail), arrive_parts, 1, 1)
            ends = jnp.sum(x * dx_state, axis=0, keepdims=True) + jnp.exp(total) * jnp.sum(
                enter * arrive, axis=0, keepdims=True
            )
            dcum = dy * ypre_ref[:, cols] - x * dx + jnp.where(final_row, ends, 0.0)
            own_head = pick[0:LANES, :]
            for part in halves(dcum):
                dcum_ref[...] += mm(part, own_head, 1, 1)
            for part in halves(dx * values):
                dstep_ref[...] += mm(part, own_head, 1, 1)
            dvalues = step_l * dx + skip_ref[0:1, cols] * dy
            dpre = dvalues * sig * (1.0 + pre * (1.0 - sig))
            dpre_ref[0:rows, cols] = dpre
            packed_ref[:, cols] = tap_grads(dpre, jnp.sum(dy * values, axis=0, keepdims=True))

            ring.round(tile - COT_AT, cot_chunks, COT_SPACING)

            return carry

        lax.fori_loop(0, tiles, one, 0)
        for at in range(tiles - COT_AT, cot_chunks + COT_SPACING * ring.reach):
            ring.round(at, cot_chunks, COT_SPACING)

        dscore = halves(jnp.where(later, dscore_ref[...], 0.0))
        dshared = (
            dwrite_ref[...] + mm3(dscore, c_parts, 1, 0),
            dread_ref[...] + mm3(dscore, b_parts, 0, 0),
        )
        for i in range(2):
            start = inner + i * N
            pre, sig = conv_tile(conv_ref, halo_ref, u_ref, taps_ref, start, rows)
            dpre = dshared[i] * sig * (1.0 + pre * (1.0 - sig))
            dpre_ref[0:rows, start : start + N] = dpre
            packed_ref[:, start : start + N] = tap_grads(dpre, jnp.zeros((1, LANES), f32))

        edge = seq_copy(
            dpre_ref.at[pl.ds(0, 8), :],
            dpre_ref.at[pl.ds(rows, 8), :],
            edge_sem.at[0],
            edge_sem.at[1],
            left,
        )

        @pl.when(rank > 0)
        def _():
            edge.start()

        upper = (iota((rows, rows), 1) >= iota((rows, rows), 0)).astype(f32).astype(bf16)
        ddecay = sum(mm(upper, part, 1, 0) for part in thirds(dcum_ref[...]))
        exp_rate = jnp.exp(heads_ref[1:2, :])
        drate = (dstep_ref[...] - ddecay * exp_rate) * jax.nn.sigmoid(
            u_ref[:, conv_width:].astype(f32) + heads_ref[0:1, :]
        )
        packed_ref[:, conv_width:] = jnp.concatenate(
            [
                jnp.sum(drate, axis=0, keepdims=True),
                jnp.sum(ddecay * (-step * exp_rate), axis=0, keepdims=True),
                jnp.zeros((6, LANES), f32),
            ],
            axis=0,
        )
        packed_ref[6:7, 0:inner] = post_grad_ref[...]
        dproj_ref[:, conv_width : conv_width + LANES] = drate.astype(bf16)
        dproj_ref[:, conv_width + LANES :] = jnp.zeros(
            (rows, dproj_ref.shape[1] - conv_width - LANES), bf16
        )

        @pl.when(rank == last)
        def _():
            dpre_ref[rows : rows + 8, :] = jnp.zeros((8, conv_width), f32)

        @pl.when(rank < last)
        def _():
            edge.wait_recv()

        def unconv(tile, carry):
            cols = pl.ds(pl.multiple_of(tile * LANES, LANES), LANES)
            taps = taps_ref[:, cols]
            du = taps[3:4, :] * dpre_ref[0:rows, cols]
            for k in range(3):
                du = du + taps[k : k + 1, :] * dpre_ref[3 - k : 3 - k + rows, cols]
            dproj_ref[:, cols] = du.astype(bf16)
            return carry

        lax.fori_loop(0, conv_width // LANES, unconv, 0)

        @pl.when(rank > 0)
        def _():
            edge.wait_send()

            def drain(tile, carry):
                chain(tile).wait_send()
                return carry

            lax.fori_loop(0, tiles, drain, 0)


        def finish_ring(chunk, carry):
            ring.wait_pair(chunk)
            ring.finish(chunk)
            return carry

        lax.fori_loop(0, cot_chunks, finish_ring, 0)

    cot_ring_sems = ring_sems[15:]
    leaving = [
        pltpu.make_async_copy(post_ref, post_out_ref, leave_sem.at[0]),
        pltpu.make_async_copy(gate_grad_ref, gate_grad_out_ref, leave_sem.at[1]),
    ]
    for copy in leaving:
        copy.start()
    backward()
    for copy in leaving:
        copy.wait()
    post_turn.finish()
    normed_turn.finish()


def vmem(count):
    return [pl.BlockSpec(memory_space=pltpu.VMEM)] * count


def front(in_shard, out_shard, prenorm, convtaps, postnorm, hidden, cot, headcoefs, sizes):
    rows, inner, tiles, _ = sizes
    conv_width = inner + 2 * N
    shape = jax.ShapeDtypeStruct
    group = lax.axis_size("dp")
    own_in, proj_width = in_shard.shape
    own_out, model_width = out_shard.shape
    scan_width = -(-(proj_width - inner) // LANES) * LANES
    in_chunks = own_in // HEIGHT
    out_chunks = own_out // (2 * HEIGHT)
    small_lanes = -(-max(own_in, own_out, convtaps.shape[1]) // LANES) * LANES
    anywhere = pl.BlockSpec(memory_space=pl.ANY)
    dma = pltpu.SemaphoreType.DMA
    return pl.pallas_call(
        functools.partial(front_kernel, sizes),
        out_shape=(
            shape((8, model_width), f32),
            shape((rows, inner), bf16),
            shape((rows, inner), bf16),
            shape((own_in, group * rows), bf16),
            shape((own_out, group * rows), bf16),
            shape((rows, -(-scan_width // WIDE) * WIDE), bf16),
            shape((8, conv_width + LANES), f32),
            shape((group // 2, 2, own_in, scan_width), bf16),
            shape((group // 2, 2, own_in, inner), bf16),
            shape((group // 2, 2, own_out, model_width), bf16),
            shape((EARLY, 2, group // 2, rows, WIDE), bf16),
        ),
        in_specs=[anywhere] * 2 + vmem(6),
        out_specs=tuple(vmem(1) + [anywhere] * 4 + vmem(2) + [anywhere] * 4),
        scratch_shapes=[
            pltpu.VMEM((rows, scan_width), bf16),
            pltpu.VMEM((rows, inner), f32),
            pltpu.VMEM((tiles, N, LANES), f32),
            pltpu.VMEM((HALO, conv_width), bf16),
            pltpu.VMEM((rows, LANES), f32),
            pltpu.VMEM((rows, LANES), f32),
            pltpu.VMEM((LANES, rows), f32),
            pltpu.VMEM((8, conv_width), f32),
            pltpu.VMEM((rows, inner), bf16),
            pltpu.VMEM((inner, rows), bf16),
            pltpu.VMEM(in_shard.shape, f32),
            pltpu.VMEM(out_shard.shape, f32),
            pltpu.VMEM((own_in, scan_width), bf16),
            pltpu.VMEM((own_in, inner), bf16),
            pltpu.VMEM((own_out, model_width), bf16),
            pltpu.VMEM((group, 16, small_lanes), bf16),
            pltpu.VMEM((1, inner), f32),
            pltpu.VMEM((rows, model_width), bf16),
            pltpu.VMEM((2, group // 2, 2, own_in, WIDE), bf16),
            pltpu.VMEM((2, 2, own_out, model_width), bf16),
            pltpu.VMEM((HALO + rows, LANES), f32),
            pltpu.VMEM((rows, rows), f32),
            pltpu.VMEM((tiles, N, LANES), f32),
            pltpu.VMEM((rows, inner), bf16),
            pltpu.VMEM((rows, inner), f32),
            pltpu.VMEM((rows, inner), f32),
            pltpu.VMEM((rows, inner), f32),
            pltpu.VMEM((model_width, rows), bf16),
            pltpu.VMEM((rows, rows), f32),
            pltpu.VMEM((rows, N), f32),
            pltpu.VMEM((rows, N), f32),
            pltpu.VMEM((rows, LANES), f32),
            pltpu.VMEM((rows, LANES), f32),
            pltpu.VMEM((rows + 8, conv_width), f32),
            pltpu.VMEM((tiles, N, LANES), f32),
            pltpu.VMEM((1, inner), f32),
            pltpu.VMEM((rows, inner), bf16),
            pltpu.VMEM((rows, inner), bf16),
            pltpu.VMEM((16, small_lanes), bf16),
            pltpu.VMEM((8, LANES), f32),
            pltpu.VMEM((1, inner), f32),
            dma((tiles,)),
            dma((tiles,)),
            dma((2,)),
            dma((tiles,)),
            dma((tiles,)),
            dma((2,)),
            dma((2,)),
            dma((group,)),
            dma((group,)),
            dma((2, group)),
            dma((2, group)),
            dma((2,)),
            dma((in_chunks + 1,)),
            dma((2,)),
        ]
        + PlaneRing.semaphores(in_chunks)
        + PlaneRing.semaphores(in_chunks)
        + PlaneRing.semaphores(out_chunks)
        + PlaneRing.semaphores(EARLY),
        compiler_params=pltpu.CompilerParams(
            collective_id=1, has_side_effects=True, vmem_limit_bytes=60 * 2**20
        ),
        cost_estimate=pl.CostEstimate(
            flops=10**10, bytes_accessed=10**8, transcendentals=4 * 10**6
        ),
    )(in_shard, out_shard, prenorm, convtaps, postnorm, hidden, cot, headcoefs)


def plane_copy(src, dst, send, recv, to):
    return pltpu.make_async_remote_copy(
        src_ref=src,
        dst_ref=dst,
        send_sem=send,
        recv_sem=recv,
        device_id={"dp": to},
        device_id_type=MESH,
    )


class PlaneTurn:
    def __init__(self, source, target, height, width, sems):
        self.source, self.target, self.height, self.width = source, target, height, width
        self.send, self.recv, self.own_sem = sems
        self.me = lax.axis_index("dp")
        self.group = lax.axis_size("dp")

    def rows_for(self, device):
        return self.source.at[
            pl.ds(pl.multiple_of(device * self.height, self.height), self.height), :
        ]

    def columns_of(self, device):
        start = pl.multiple_of(slot_of(device, self.group) * self.width, self.width)
        return self.target.at[:, pl.ds(start, self.width)]

    def copy(self, i, peer, origin):
        return plane_copy(
            self.rows_for(peer), self.columns_of(origin), self.send.at[i], self.recv.at[i], peer
        )

    def own(self):
        return pltpu.make_async_copy(
            self.rows_for(self.me), self.columns_of(self.me), self.own_sem
        )

    def start(self):
        for i in range(1, self.group):
            self.copy(i, lax.rem(self.me + i, self.group), self.me).start()
        self.own().start()

    def arrive(self):
        for i in range(1, self.group):
            origin = lax.rem(self.me + self.group - i, self.group)
            self.copy(i, origin, origin).wait_recv()
        self.own().wait()

    def sent(self):
        for i in range(1, self.group):
            self.copy(i, lax.rem(self.me + i, self.group), self.me).wait_send()

    def finish(self):
        self.arrive()
        self.sent()


class PlaneRing:
    def __init__(self, block, source, pair_block, sems, prepare=None):
        group = lax.axis_size("dp")
        me = lax.axis_index("dp")
        self.block, self.source, self.pair_block = block, source, pair_block
        self.prepare = prepare
        self.ring_send, self.ring_recv, self.pair_send, self.pair_recv, self.own_sem = sems
        self.chips = group // 2
        self.reach = self.chips // 2
        self.me = me
        self.core = lax.rem(me, 2)
        self.chip = me // 2
        self.place = ring_place(self.chip, self.chips)

    @staticmethod
    def semaphores(chunks):
        group = lax.axis_size("dp")
        dma = pltpu.SemaphoreType.DMA
        return [dma((chunks, group // 2)), dma((chunks, group // 2))] + [dma((chunks,))] * 3

    def ring_chip(self, ahead):
        return ring_place(lax.rem(self.place + ahead + self.chips, self.chips), self.chips)

    def part(self, number, way):
        return None if number < self.reach else (0 if way == 1 else 1)

    def copy(self, chunk, number, way, origin, source=None):
        block = self.block(chunk, origin, self.part(number, way))
        at = 2 * (number - 1) + (0 if way == 1 else 1)
        return plane_copy(
            block if source is None else source,
            block,
            self.ring_send.at[chunk, at],
            self.ring_recv.at[chunk, at],
            2 * self.ring_chip(way) + self.core,
        )

    def hop(self, chunk, number, way, source=None):
        return self.copy(chunk, number, way, self.ring_chip(-way * (number - 1)), source)

    def hop_in(self, chunk, number, way):
        return self.copy(chunk, number, way, self.ring_chip(-way * number))

    def own_copy(self, chunk, source):
        return pltpu.make_async_copy(
            source, self.block(chunk, self.chip, None), self.own_sem.at[chunk]
        )

    def pair_copy(self, chunk, core):
        block = self.pair_block(chunk, core)
        return plane_copy(
            block,
            block,
            self.pair_send.at[chunk],
            self.pair_recv.at[chunk],
            self.me + 1 - 2 * self.core,
        )

    def stage(self, chunk, number):
        if number == 0:
            if self.prepare is not None:
                self.prepare(chunk)
            self.source(chunk, None, lambda ref: self.own_copy(chunk, ref).start())
            for way in (1, -1):
                self.source(
                    chunk,
                    self.part(1, way),
                    lambda ref, way=way: self.hop(chunk, 1, way, ref).start(),
                )
            return
        for way in (1, -1):
            self.hop_in(chunk, number, way).wait_recv()
            if number < self.reach:
                self.hop(chunk, number + 1, way).start()
        if number == self.reach:
            self.own_copy(chunk, self.block(chunk, self.chip, None)).wait()
            self.pair_copy(chunk, self.core).start()

    def wait_pair(self, chunk):
        self.pair_copy(chunk, 1 - self.core).wait_recv()

    def finish(self, chunk):
        for number in range(1, self.reach + 1):
            for way in (1, -1):
                self.hop(chunk, number, way).wait_send()
        self.pair_copy(chunk, self.core).wait_send()

    def round(self, step, chunks, spacing):
        for number in range(self.reach, -1, -1):
            chunk = step - number * spacing

            @pl.when((chunk >= 0) & (chunk < chunks))
            def _(chunk=chunk, number=number):
                self.stage(chunk, number)


def weight_ring(shard_ref, all_ref, height, sems, prepare):
    core = lax.rem(lax.axis_index("dp"), 2)

    def rows_of(chunk, part):
        size = height if part is None else height // 2
        start = chunk * height + (0 if part is None else part * size)
        return pl.ds(pl.multiple_of(start, size), size)

    return PlaneRing(
        lambda chunk, origin, part: all_ref.at[origin, core, rows_of(chunk, part), :],
        lambda chunk, part, action: action(shard_ref.at[rows_of(chunk, part), :]),
        lambda chunk, half: all_ref.at[:, half, rows_of(chunk, None), :],
        sems,
        prepare,
    )


HEIGHT = 32


def tail_kernel(
    sizes,
    normed_turned_ref,
    post_turned_ref,
    cot_ref,
    gate_far_ref,
    scan_far_ref,
    packed_in_ref,
    hidden_far_ref,
    own_cot_far_ref,
    post_far_ref,
    scale_ref,
    gate_matrix_ref,
    scan_matrix_ref,
    out_matrix_ref,
    in_ref,
    out_ref,
    small_out_ref,
    output_far_ref,
    input_grad_far_ref,
    gathered_ref,
    value_ref,
    inbox_ref,
    total_ref,
    loaded_ref,
    small_value_ref,
    small_inbox_ref,
    small_all_ref,
    weights_ref,
    normed_grad_ref,
    packed_ref,
    gate_ref,
    scan_ref,
    hidden_ref,
    own_cot_ref,
    post_ref,
    output_ref,
    input_grad_ref,
    far_sem,
    up_send,
    inbox_recv,
    other_recv,
    total_recv,
    left_send,
    right_send,
    store_sem,
    ring_send,
    ring_recv,
    pair_send,
    pair_recv,
    own_sem,
    load_sem,
    small_send,
    small_recv,
    weight_sem,
):
    rows, own_in, out_steps, gate_steps, steps, root, lag, spacing = sizes
    rest = out_steps // 2 - EARLY
    back_items = steps - out_steps
    chunks = back_items + rest
    rank = lax.axis_index("seq")
    last = lax.axis_size("seq") - 1
    me = lax.axis_index("dp")
    group = lax.axis_size("dp")
    chips = group // 2
    reach = chips // 2
    core = lax.rem(me, 2)
    arriving = [
        pltpu.make_async_copy(far, near, far_sem.at[at])
        for at, (far, near) in enumerate(
            (
                (gate_far_ref, gate_ref),
                (scan_far_ref, scan_ref),
                (hidden_far_ref, hidden_ref),
                (own_cot_far_ref, own_cot_ref),
                (post_far_ref, post_ref),
            )
        )
    ]
    leaving = (
        pltpu.make_async_copy(input_grad_ref, input_grad_far_ref, far_sem.at[5]),
        pltpu.make_async_copy(output_ref, output_far_ref, far_sem.at[6]),
    )
    barrier = pltpu.get_barrier_semaphore()
    greet_seq(barrier, rank, last)
    greet_plane(barrier, me, group)
    pl.semaphore_wait(barrier, seq_neighbours(rank, last) + group - 1)
    left = jnp.maximum(rank - 1, 0)
    right = jnp.minimum(rank + 1, last)

    model_width = hidden_ref.shape[1]

    def small_copy(i, peer, slot):
        return plane_copy(
            packed_ref, small_all_ref.at[slot], small_send.at[i], small_recv.at[i], peer
        )

    def block(chunk, origin, part):
        ref = gathered_ref.at[chunk, core, origin]
        return ref if part is None else ref.at[pl.ds(part * (rows // 2), rows // 2), :]

    def source(chunk, part, action):
        part_rows = pl.ds(0, rows) if part is None else pl.ds(part * (rows // 2), rows // 2)

        def one(ref, first):
            start = pl.multiple_of((chunk - first) * WIDE, WIDE)
            action(ref.at[part_rows, pl.ds(start, WIDE)])

        @pl.when(chunk < rest)
        def _():
            one(own_cot_far_ref, -EARLY)

        @pl.when((chunk >= rest) & (chunk < rest + gate_steps))
        def _():
            one(gate_far_ref, rest)

        @pl.when(chunk >= rest + gate_steps)
        def _():
            one(scan_far_ref, rest + gate_steps)

    ring = PlaneRing(
        block,
        source,
        lambda chunk, half: gathered_ref.at[chunk, half],
        (ring_send, ring_recv, pair_send, pair_recv, own_sem),
    )

    def order_of(step):
        return jnp.where(step < out_steps, step // 2, step - out_steps + out_steps // 2)

    def fetch(step, action):
        order = order_of(step)
        slot = lax.rem(order, 2)

        @pl.when((order < EARLY) & (lax.rem(step, 2) == 0))
        def _():
            action(
                pltpu.make_async_copy(cot_ref.at[order], loaded_ref.at[slot], load_sem.at[slot])
            )

        @pl.when((order >= EARLY) & ((step >= out_steps) | (lax.rem(step, 2) == 0)))
        def _():
            action(
                pltpu.make_async_copy(
                    gathered_ref.at[order - EARLY], loaded_ref.at[slot], load_sem.at[slot]
                )
            )

        return slot

    def compute(step):
        arrived = loaded_ref.at[fetch(step, lambda copy: copy.wait())]

        @pl.when(step < out_steps)
        def _():
            some = pl.ds(pl.multiple_of(lax.rem(step, 2) * own_in, own_in), own_in)
            value_ref[...] = mm(
                post_turned_ref[some, :], arrived[...].reshape(group * rows, WIDE), 1, 0
            )

        @pl.when(step >= out_steps)
        def _():
            value_ref[...] = mm(
                normed_turned_ref[...], arrived[...].reshape(group * rows, WIDE), 1, 0
            )

    fetch(0, lambda copy: copy.start())
    for copy in arriving:
        copy.start()

    def weight_copy(item, action):
        slot = lax.rem(item, 2)
        narrow = scan_matrix_ref.shape[1] % WIDE

        def one(matrix_ref, first, width):
            height = matrix_ref.shape[0]
            start = pl.multiple_of((item - first) * WIDE, WIDE)
            action(
                pltpu.make_async_copy(
                    matrix_ref.at[:, pl.ds(start, width)],
                    weights_ref.at[slot, pl.ds(0, height), pl.ds(0, width)],
                    weight_sem.at[slot],
                )
            )

        full = back_items - 1 if narrow else back_items

        @pl.when(item < gate_steps)
        def _():
            one(gate_matrix_ref, 0, WIDE)

        @pl.when((item >= gate_steps) & (item < full))
        def _():
            one(scan_matrix_ref, gate_steps, WIDE)

        if narrow:

            @pl.when(item == full)
            def _():
                one(scan_matrix_ref, gate_steps, narrow)

        @pl.when((item >= back_items) & (item < items))
        def _():
            one(out_matrix_ref, back_items, WIDE)

    items = back_items + model_width // WIDE

    def back_product(grad_ref, item, first, width):
        cols = pl.ds(pl.multiple_of((item - first) * WIDE, WIDE), width)
        weights = weights_ref[lax.rem(item, 2), 0:model_width, 0:width]
        normed_grad_ref[...] += mm(grad_ref[:, cols], weights, 1, 1)

    def norm_backward():
        def block(at, carry):
            some = pl.ds(pl.multiple_of(at * HEIGHT, HEIGHT), HEIGHT)
            hidden = hidden_ref[some, :].astype(f32)
            root_mean = lax.rsqrt(jnp.mean(hidden * hidden, axis=-1, keepdims=True) + norm_eps)
            plain = hidden * root_mean
            grad = normed_grad_ref[some, :]
            scaled = grad * scale_ref[0:1, :]
            input_grad_ref[some, :] = root_mean * (
                scaled - plain * jnp.mean(scaled * plain, axis=-1, keepdims=True)
            ) + own_cot_ref[some, :].astype(f32)
            return carry + jnp.sum(grad * plain, axis=0, keepdims=True)

        total = lax.fori_loop(0, rows // HEIGHT, block, jnp.zeros((1, model_width), f32))
        packed_ref[...] = packed_in_ref[...]
        packed_ref[7:8, 0:model_width] = total
        for i in range(1, group):
            small_copy(i, lax.rem(me + i, group), me).start()
        small_all_ref[me] = packed_ref[...]

    def local_product(item):
        narrow = scan_matrix_ref.shape[1] % WIDE
        full = back_items - 1 if narrow else back_items

        @pl.when(item == 0)
        def _():
            normed_grad_ref[...] = jnp.zeros_like(normed_grad_ref)
            for copy in arriving:
                copy.wait()

        weight_copy(item, lambda copy: copy.wait())
        weight_copy(item + 1, lambda copy: copy.start())

        @pl.when(item < gate_steps)
        def _():
            back_product(gate_ref, item, 0, WIDE)

        @pl.when((item >= gate_steps) & (item < full))
        def _():
            back_product(scan_ref, item, gate_steps, WIDE)

        if narrow:

            @pl.when(item == full)
            def _():
                back_product(scan_ref, item, gate_steps, narrow)

        @pl.when(item == back_items - 1)
        def _():
            norm_backward()
            leaving[0].start()

        @pl.when(item >= back_items)
        def _():
            cols = pl.ds(pl.multiple_of((item - back_items) * WIDE, WIDE), WIDE)
            output_ref[:, cols] = hidden_ref[:, cols].astype(f32) + mm(
                post_ref[...], weights_ref[lax.rem(item, 2)], 1, 0
            )

        @pl.when(item == items - 1)
        def _():
            leaving[1].start()

    weight_copy(0, lambda copy: copy.start())

    def piece(ref, part, parts):
        if parts == 1:
            return ref
        size = own_in // parts
        start = part * size if isinstance(part, int) else pl.multiple_of(part * size, size)
        return ref.at[pl.ds(start, size), :]

    def up_copy(source, target, step, part, parts, recv, to):
        return seq_copy(
            piece(source, part, parts),
            piece(target, part, parts),
            up_send.at[step, part],
            recv.at[step, part],
            to,
        )

    def down_copy(total, step, part, parts, send, to):
        return seq_copy(
            piece(total, part, parts),
            piece(total, part, parts),
            send.at[step, part],
            total_recv.at[step, part],
            to,
        )

    def up(value, inbox, total, step, parts, after):
        edge = ((rank == 0) | (rank == last)) & (rank != root)
        inner_place = (rank != root) & (rank > 0) & (rank < last)
        for part in range(parts):
            here = piece(value, part, parts)
            inbox_here = piece(inbox, part, parts)
            total_here = piece(total, part, parts)

            @pl.when(edge)
            def _(here=here, inbox_here=inbox_here):
                inbox_here[...] = here[...]

            @pl.when(inner_place)
            def _(here=here, inbox_here=inbox_here, part=part):
                up_copy(inbox, inbox, step, part, parts, inbox_recv, left).wait_recv()
                inbox_here[...] += here[...]

            @pl.when(rank < root)
            def _(part=part):
                up_copy(inbox, inbox, step, part, parts, inbox_recv, right).start()

            @pl.when(rank == root + 1)
            def _(part=part):
                up_copy(inbox, total, step, part, parts, other_recv, left).start()

            @pl.when(rank > root + 1)
            def _(part=part):
                up_copy(inbox, inbox, step, part, parts, inbox_recv, left).start()

            @pl.when(rank == root)
            def _(here=here, inbox_here=inbox_here, total_here=total_here, part=part):
                result = here[...]
                if root > 0:
                    up_copy(inbox, inbox, step, part, parts, inbox_recv, left).wait_recv()
                    result = result + inbox_here[...]
                if root < last:
                    up_copy(total, total, step, part, parts, other_recv, right).wait_recv()
                    result = result + total_here[...]
                total_here[...] = result
                if root > 0:
                    down_copy(total, step, part, parts, left_send, left).start()
                if root < last:
                    down_copy(total, step, part, parts, right_send, right).start()

            after(part)

    def down(total, step, part, parts):
        @pl.when(rank < root)
        def _():
            down_copy(total, step, part, parts, left_send, left).wait_recv()

            @pl.when(rank > 0)
            def _():
                down_copy(total, step, part, parts, left_send, left).start()

        @pl.when(rank > root)
        def _():
            down_copy(total, step, part, parts, right_send, right).wait_recv()

            @pl.when(rank < last)
            def _():
                down_copy(total, step, part, parts, right_send, right).start()

    def drain(inbox, total, step, parts):
        for part in range(parts):

            @pl.when(rank < root)
            def _(part=part):
                up_copy(inbox, inbox, step, part, parts, inbox_recv, right).wait_send()

            @pl.when(rank > root)
            def _(part=part):
                up_copy(inbox, inbox, step, part, parts, inbox_recv, left).wait_send()

            @pl.when((rank <= root) & (rank > 0))
            def _(part=part):
                down_copy(total, step, part, parts, left_send, left).wait_send()

            @pl.when((rank >= root) & (rank < last))
            def _(part=part):
                down_copy(total, step, part, parts, right_send, right).wait_send()

    def stored(step, action):
        @pl.when(step < out_steps)
        def _():
            some = pl.ds(pl.multiple_of(lax.rem(step, 2) * own_in, own_in), own_in)
            cols = pl.ds(pl.multiple_of(step // 2 * WIDE, WIDE), WIDE)
            action(
                pltpu.make_async_copy(
                    total_ref.at[step], out_ref.at[some, cols], store_sem.at[step]
                )
            )

        @pl.when(step >= out_steps)
        def _():
            cols = pl.ds(pl.multiple_of((step - out_steps) * WIDE, WIDE), WIDE)
            action(
                pltpu.make_async_copy(total_ref.at[step], in_ref.at[:, cols], store_sem.at[step])
            )

    behind = lag * (jnp.maximum(rank - root, 0) + jnp.maximum(root - rank, 0))

    def round_(step, carry):
        for stage in range(reach, -1, -1):
            chunk = step - stage * spacing

            @pl.when((chunk >= 0) & (chunk < chunks))
            def _(chunk=chunk, stage=stage):
                ring.stage(chunk, stage)

        follow = step + 1
        arrives = (follow >= out_steps) | ((order_of(follow) >= EARLY) & (lax.rem(follow, 2) == 0))

        @pl.when(arrives & (follow < steps))
        def _():
            ring.wait_pair(order_of(follow) - EARLY)

        @pl.when(step + 1 < steps)
        def _():
            fetch(step + 1, lambda copy: copy.start())

        def down_late(part):
            late = PARTS * step + part - behind
            late_step = late // PARTS
            late_part = lax.rem(late, PARTS)

            @pl.when((late >= 0) & (late_step < steps))
            def _():
                down(total_ref.at[late_step], late_step, late_part, PARTS)

                @pl.when(late_part == PARTS - 1)
                def _():
                    stored(late_step, lambda copy: copy.start())

            @pl.when(late == PARTS * steps)
            def _():
                down(small_out_ref, steps, 0, 1)

        @pl.when(step < steps)
        def _():
            compute(step)
            up(value_ref, inbox_ref.at[step], total_ref.at[step], step, PARTS, down_late)

        @pl.when(step == steps)
        def _():
            for i in range(1, group):
                small_copy(i, lax.rem(me + i, group), me).wait_send()
                origin = lax.rem(me + group - i, group)
                small_copy(i, origin, origin).wait_recv()
            small_value_ref[...] = jnp.sum(small_all_ref[...], axis=0)
            up(small_value_ref, small_inbox_ref, small_out_ref, steps, 1, lambda part: None)

        @pl.when(step >= steps)
        def _():
            for part in range(PARTS):
                down_late(part)

        @pl.when((step >= 1) & (step < 1 + items))
        def _():
            local_product(step - 1)

        return carry

    lax.fori_loop(0, steps + 1 + (behind + PARTS - 1) // PARTS, round_, 0)

    def finish(step, carry):
        drain(inbox_ref.at[step], total_ref.at[step], step, PARTS)
        stored(step, lambda copy: copy.wait())
        return carry

    lax.fori_loop(0, steps, finish, 0)
    drain(small_inbox_ref, small_out_ref, steps, 1)

    def finish_ring(chunk, carry):
        ring.finish(chunk)
        return carry

    lax.fori_loop(0, chunks, finish_ring, 0)
    for copy in leaving:
        copy.wait()


def reduce_gradients(
    normed_turned, post_turned, cot_early, gate_grad, scan_grad, packed, hidden, cot, post, scale, matrices
):
    size = lax.axis_size("seq")
    group = lax.axis_size("dp")
    rows = gate_grad.shape[0]
    own_in = normed_turned.shape[0]
    model_width = hidden.shape[1]
    out_steps = 2 * (model_width // WIDE)
    gate_steps = gate_grad.shape[1] // WIDE
    back_items = gate_steps + scan_grad.shape[1] // WIDE
    steps = out_steps + back_items
    chunks = back_items + out_steps // 2 - EARLY
    reach = group // 4
    spacing = min(3, (out_steps - 2) // reach)
    assert out_steps == 2 * EARLY
    sizes = (rows, own_in, out_steps, gate_steps, steps, size // 2, LAG, spacing)
    assert back_items + model_width // WIDE < steps
    shape = jax.ShapeDtypeStruct
    dma = pltpu.SemaphoreType.DMA
    small_shape = packed.shape
    anywhere = pl.BlockSpec(memory_space=pl.ANY)
    return pl.pallas_call(
        functools.partial(tail_kernel, sizes),
        out_shape=(
            shape((own_in, back_items * WIDE), f32),
            shape((2 * own_in, model_width), f32),
            shape(small_shape, f32),
            shape((rows, model_width), f32),
            shape((rows, model_width), f32),
            shape((chunks, 2, group // 2, rows, WIDE), bf16),
        ),
        in_specs=vmem(2) + [anywhere] * 3 + vmem(1) + [anywhere] * 3 + vmem(1) + [anywhere] * 3,
        out_specs=(anywhere, anywhere) + tuple(vmem(1)) + (anywhere,) * 3,
        scratch_shapes=[
            pltpu.VMEM((own_in, WIDE), f32),
            pltpu.VMEM((steps, own_in, WIDE), f32),
            pltpu.VMEM((steps, own_in, WIDE), f32),
            pltpu.VMEM((2, 2, group // 2, rows, WIDE), bf16),
            pltpu.VMEM(small_shape, f32),
            pltpu.VMEM(small_shape, f32),
            pltpu.VMEM((group,) + small_shape, f32),
            pltpu.VMEM((2, matrices[2].shape[0], WIDE), bf16),
            pltpu.VMEM((rows, model_width), f32),
            pltpu.VMEM(small_shape, f32),
            pltpu.VMEM(gate_grad.shape, bf16),
            pltpu.VMEM(scan_grad.shape, bf16),
            pltpu.VMEM(hidden.shape, bf16),
            pltpu.VMEM(cot.shape, bf16),
            pltpu.VMEM(post.shape, bf16),
            pltpu.VMEM((rows, model_width), f32),
            pltpu.VMEM((rows, model_width), f32),
            dma((7,)),
        ]
        + [dma((steps + 1, PARTS))] * 6
        + [
            dma((steps,)),
            *PlaneRing.semaphores(chunks),
            dma((2,)),
            *[dma((group,))] * 2,
            dma((2,)),
        ],
        compiler_params=pltpu.CompilerParams(
            collective_id=3, has_side_effects=True, vmem_limit_bytes=56 * 2**20
        ),
        cost_estimate=pl.CostEstimate(
            flops=2 * 10**10, bytes_accessed=2 * 10**8, transcendentals=0
        ),
    )(
        normed_turned,
        post_turned,
        cot_early,
        gate_grad,
        scan_grad,
        packed,
        hidden,
        cot,
        post,
        scale,
        *matrices,
    )


def adam_kernel(*refs):
    ins, outs = refs[:8], refs[8:]
    for matrix in range(2):
        gradient, weight, moment, square = (ref[...] for ref in ins[4 * matrix : 4 * matrix + 4])
        gradient = gradient[:, : weight.shape[1]]
        updated = adam_update(weight, moment, square, gradient, rate_matrix, weight_decay)
        for ref, value in zip(outs[4 * matrix : 4 * matrix + 4], (gradient,) + updated):
            ref[...] = value


def adam_matrices(matrices):
    blocks = 12
    flat = [array for four in matrices for array in four]
    out = [four[1] for four in matrices for _ in range(4)]

    def spec(array):
        return pl.BlockSpec((array.shape[0] // blocks, array.shape[1]), lambda at: (at, 0))

    results = pl.pallas_call(
        adam_kernel,
        grid=(blocks,),
        out_shape=[jax.ShapeDtypeStruct(array.shape, f32) for array in out],
        in_specs=[spec(array) for array in flat],
        out_specs=[spec(array) for array in out],
        compiler_params=pltpu.CompilerParams(vmem_limit_bytes=58 * 2**20),
    )(*flat)
    return results[:4], results[4:]


def on_device(
    hidden_in,
    out_grad,
    prenorm,
    inproject,
    convtaps,
    headcoefs,
    postnorm,
    outproject,
    prenorm_first,
    inproject_first,
    convtaps_first,
    headcoefs_first,
    postnorm_first,
    outproject_first,
    prenorm_second,
    inproject_second,
    convtaps_second,
    headcoefs_second,
    postnorm_second,
    outproject_second,
):
    group = lax.axis_size("dp")
    me = lax.axis_index("dp")
    seq_here, rows, model_width = hidden_in.shape
    assert seq_here == 1
    heads = headcoefs.shape[1]
    own_in, proj_width = inproject.shape
    own_out = outproject.shape[0]
    inner = own_out * group
    width = inner // heads
    per_tile = LANES // width
    tiles = inner // LANES
    sizes = (rows, inner, tiles, per_tile)
    conv_own = convtaps.shape[1]
    conv_width = conv_own * group

    tap_rows = convtaps.shape[0]
    hidden_low = hidden_in.reshape(rows, model_width)
    cot_low = out_grad.reshape(rows, model_width)
    (
        pre_scale,
        gate_grad,
        post_low,
        normed_turned,
        post_turned,
        scan_grad,
        packed,
        scan_matrix,
        gate_matrix,
        out_matrix,
        cot_early,
    ) = front(
        inproject,
        outproject,
        prenorm.reshape(1, -1),
        convtaps,
        postnorm.reshape(1, -1),
        hidden_low,
        cot_low,
        headcoefs,
        sizes,
    )
    scan_matrix = scan_matrix.reshape(model_width, -1)
    gate_matrix = gate_matrix.reshape(model_width, inner)
    out_matrix = out_matrix.reshape(inner, model_width)
    inproj_padded, outproj_owned, packed, output, input_gradient, _ = reduce_gradients(
        normed_turned,
        post_turned,
        cot_early,
        gate_grad,
        scan_grad,
        packed,
        hidden_low,
        cot_low,
        post_low,
        pre_scale,
        (gate_matrix, scan_matrix, out_matrix),
    )
    prenorm_owned = lax.dynamic_slice_in_dim(packed[7], me * own_in, own_in, 0)
    postnorm_owned = lax.dynamic_slice_in_dim(packed[6], me * own_out, own_out, 0)
    conv_owned = lax.dynamic_slice_in_dim(packed[:tap_rows], me * conv_own, conv_own, 1)
    head_total = jnp.concatenate(
        [
            packed[:2, conv_width : conv_width + heads],
            jnp.sum(packed[5:6, :inner].reshape(1, heads, width), axis=-1),
        ]
    )

    prenorm_new, prenorm_mom, prenorm_sq = adam_update(
        prenorm, prenorm_first, prenorm_second, prenorm_owned, rate_vector, 0.0
    )
    (
        (inproj_owned, inproj_new, inproj_mom, inproj_sq),
        (outproj_owned, outproj_new, outproj_mom, outproj_sq),
    ) = adam_matrices(
        (
            (inproj_padded, inproject, inproject_first, inproject_second),
            (outproj_owned, outproject, outproject_first, outproject_second),
        )
    )
    conv_new, conv_mom, conv_sq = adam_update(
        convtaps, convtaps_first, convtaps_second, conv_owned, rate_vector, 0.0
    )
    head_new, head_mom, head_sq = adam_update(
        headcoefs, headcoefs_first, headcoefs_second, head_total, rate_vector, 0.0
    )
    postnorm_new, postnorm_mom, postnorm_sq = adam_update(
        postnorm, postnorm_first, postnorm_second, postnorm_owned, rate_vector, 0.0
    )
    return (
        output.reshape(seq_here, rows, model_width),
        input_gradient.reshape(seq_here, rows, model_width),
        prenorm_owned,
        inproj_owned,
        conv_owned,
        head_total,
        postnorm_owned,
        outproj_owned,
        prenorm_new,
        inproj_new,
        conv_new,
        head_new,
        postnorm_new,
        outproj_new,
        prenorm_mom,
        inproj_mom,
        conv_mom,
        head_mom,
        postnorm_mom,
        outproj_mom,
        prenorm_sq,
        inproj_sq,
        conv_sq,
        head_sq,
        postnorm_sq,
        outproj_sq,
    )


def solution(mesh):
    weights = (P("dp"), P("dp", None), P(None, "dp"), P(), P("dp"), P("dp", None))
    tokens = (P("dp", "seq", None), P("dp", "seq", None))
    return jax.shard_map(
        on_device,
        mesh=mesh,
        in_specs=tokens + weights * 3,
        out_specs=tokens + weights * 4,
        check_vma=False,
    )
```

```python
import functools

import jax
import jax.numpy as jnp
from jax import lax
from jax.experimental import pallas as pl
from jax.experimental.pallas import tpu as pltpu
from jax.sharding import PartitionSpec as P

N = 128
LANES = 128
HALO = 16
WIDE = 256
HEIGHT = 32
PARTS = 2
LAG = 4
COT_AT = 8
EARLY = 6
COT_SPACING = 5

norm_eps = 1e-05
beta_moment = 0.9
beta_square = 0.95
adam_eps = 1e-08
adam_step = 3.0
rate_matrix = 0.005
rate_vector = 0.05
weight_decay = 0.1

f32 = jnp.float32
bf16 = jnp.bfloat16
MESH = pl.DeviceIdType.MESH


def adam_update(weight, moment, square, gradient, step_rate, decay_rate):
    moment_new = beta_moment * moment + (1.0 - beta_moment) * gradient
    square_new = beta_square * square + (1.0 - beta_square) * gradient * gradient
    moment_hat = moment_new / (1.0 - beta_moment**adam_step)
    square_hat = square_new / (1.0 - beta_square**adam_step)
    updated = weight - step_rate * (
        moment_hat / (jnp.sqrt(square_hat) + adam_eps) + decay_rate * weight
    )
    return (updated, moment_new, square_new)


def mm(a, b, ca, cb):
    return lax.dot_general(a, b, (((ca,), (cb,)), ((), ())), preferred_element_type=f32)


def halves(a):
    hi = a.astype(bf16)
    return hi, (a - hi.astype(f32)).astype(bf16)


def thirds(a):
    hi = a.astype(bf16)
    rest = a - hi.astype(f32)
    mid = rest.astype(bf16)
    return hi, mid, (rest - mid.astype(f32)).astype(bf16)


def mm3(a, b, ca, cb):
    return mm(a[0], b[0], ca, cb) + mm(a[0], b[1], ca, cb) + mm(a[1], b[0], ca, cb)


def iota(shape, dim):
    return lax.broadcasted_iota(jnp.int32, shape, dim)


def head_lanes(tile, heads_a_tile, copies):
    rows = iota((copies * LANES, LANES), 0)
    lane_head = tile * heads_a_tile + iota((copies * LANES, LANES), 1) // (LANES // heads_a_tile)
    return (rows % LANES == lane_head).astype(f32).astype(bf16)


def conv_tile(conv_ref, halo_ref, u_ref, taps_ref, start, rows):
    cols = pl.ds(start, LANES)
    conv_ref[0:HALO, :] = halo_ref[:, cols].astype(f32)
    conv_ref[HALO : HALO + rows, :] = u_ref[:, cols].astype(f32)
    taps = taps_ref[:, cols]
    pre = taps[4:5, :] + taps[0:1, :] * conv_ref[HALO - 3 : HALO - 3 + rows, :]
    for k in range(1, 4):
        pre = pre + taps[k : k + 1, :] * conv_ref[HALO - 3 + k : HALO - 3 + k + rows, :]
    return pre, jax.nn.sigmoid(pre)


def seq_copy(src, dst, send, recv, to):
    return pltpu.make_async_remote_copy(
        src_ref=src,
        dst_ref=dst,
        send_sem=send,
        recv_sem=recv,
        device_id={"seq": to},
        device_id_type=MESH,
    )


def greet_seq(barrier, rank, last):
    @pl.when(rank > 0)
    def _():
        pl.semaphore_signal(barrier, inc=1, device_id={"seq": rank - 1}, device_id_type=MESH)

    @pl.when(rank < last)
    def _():
        pl.semaphore_signal(barrier, inc=1, device_id={"seq": rank + 1}, device_id_type=MESH)


def seq_neighbours(rank, last):
    return jnp.minimum(rank, 1) + jnp.minimum(last - rank, 1)


def greet_plane(barrier, me, group):
    for i in range(1, group):
        pl.semaphore_signal(
            barrier, inc=1, device_id={"dp": lax.rem(me + i, group)}, device_id_type=MESH
        )


def slot_of(device, group):
    return lax.rem(device, 2) * (group // 2) + device // 2


def ring_place(at, chips):
    half = chips // 2
    turned = at // half
    return at * (1 - turned) + turned * (3 * half - 1 - at)


def front_kernel(
    sizes,
    in_shard_ref,
    out_shard_ref,
    prenorm_ref,
    convtaps_ref,
    postnorm_ref,
    hidden_ref,
    cot_ref,
    headcoefs_ref,
    pre_scale_ref,
    gate_grad_out_ref,
    post_out_ref,
    normed_turned_ref,
    post_turned_ref,
    dproj_ref,
    packed_ref,
    scan_all_ref,
    gate_all_ref,
    out_all_ref,
    cot_all_ref,
    u_ref,
    ypre_ref,
    enter_ref,
    halo_ref,
    step_ref,
    cum_ref,
    cumt_ref,
    taps_ref,
    dy_ref,
    post_t_ref,
    in_wide_ref,
    out_wide_ref,
    scan_shard_ref,
    gate_shard_ref,
    out_low_ref,
    small_all_ref,
    post_scale_ref,
    normed_ref,
    weights_ref,
    out_weights_ref,
    conv_ref,
    score_ref,
    leave_ref,
    mixer_ref,
    gate_ref,
    gated_ref,
    dpost_ref,
    normed_t_ref,
    dscore_ref,
    dread_ref,
    dwrite_ref,
    dcum_ref,
    dstep_ref,
    dpre_ref,
    arrive_ref,
    post_grad_ref,
    gate_grad_ref,
    post_ref,
    small_ref,
    heads_ref,
    skip_ref,
    send_sem,
    recv_sem,
    halo_sem,
    back_send,
    back_recv,
    edge_sem,
    leave_sem,
    small_send,
    small_recv,
    turn_send,
    turn_recv,
    own_sem,
    wide_sem,
    weight_sem,
    *ring_sems,
):
    rows, inner, tiles, per_tile = sizes
    conv_width = inner + 2 * N
    own_in = in_shard_ref.shape[0]
    own_out, model_width = out_shard_ref.shape
    scan_width = in_shard_ref.shape[1] - inner
    rank = lax.axis_index("seq")
    last = lax.axis_size("seq") - 1
    me = lax.axis_index("dp")
    group = lax.axis_size("dp")
    in_chunks = own_in // HEIGHT
    out_height = 2 * HEIGHT
    out_chunks = own_out // out_height

    def wide_rows(chunk):
        return pl.ds(pl.multiple_of(chunk * HEIGHT, HEIGHT), HEIGHT)

    def in_wide(chunk):
        some = wide_rows(chunk)
        return pltpu.make_async_copy(
            in_shard_ref.at[some, :], in_wide_ref.at[some, :], wide_sem.at[chunk]
        )

    out_wide = pltpu.make_async_copy(out_shard_ref, out_wide_ref, wide_sem.at[in_chunks])
    for chunk in range(in_chunks):
        in_wide(chunk).start()
    out_wide.start()
    conv_own = convtaps_ref.shape[1]
    small_rows = [
        jnp.concatenate([part, jnp.zeros((part.shape[0], width), f32)], axis=1)
        if width
        else part
        for part, width in (
            (ref[...], small_ref.shape[1] - ref.shape[1])
            for ref in (prenorm_ref, convtaps_ref, postnorm_ref)
        )
    ]
    small_rows.append(jnp.zeros((9, small_ref.shape[1]), f32))
    small_ref[...] = jnp.concatenate(small_rows, axis=0).astype(bf16)
    heads_ref[...] = jnp.zeros_like(heads_ref)
    heads_ref[0:3, 0 : headcoefs_ref.shape[1]] = headcoefs_ref[...]
    barrier = pltpu.get_barrier_semaphore()
    greet_seq(barrier, rank, last)
    greet_plane(barrier, me, group)
    pl.semaphore_wait(barrier, seq_neighbours(rank, last) + group - 1)
    right = jnp.minimum(rank + 1, last)
    left = jnp.maximum(rank - 1, 0)

    def small_copy(i, peer, slot):
        return plane_copy(
            small_ref, small_all_ref.at[slot], small_send.at[i], small_recv.at[i], peer
        )

    for i in range(1, group):
        small_copy(i, lax.rem(me + i, group), me).start()
    small_all_ref[me] = small_ref[...]
    scan_shard_ref[:, scan_width - scan_width % LANES :] = jnp.zeros(
        (own_in, scan_shard_ref.shape[1] - scan_width + scan_width % LANES), bf16
    )

    def prepare_scan(chunk):
        some = wide_rows(chunk)
        in_wide(chunk).wait()
        scan_shard_ref[some, 0:scan_width] = in_wide_ref[some, inner:].astype(bf16)

    def prepare_gate(chunk):
        some = wide_rows(chunk)
        gate_shard_ref[some, :] = in_wide_ref[some, 0:inner].astype(bf16)

    def prepare_out(chunk):
        @pl.when(chunk == 0)
        def _():
            out_wide.wait()

        some = pl.ds(pl.multiple_of(chunk * out_height, out_height), out_height)
        out_low_ref[some, :] = out_wide_ref[some, :].astype(bf16)

    scan_ring = weight_ring(scan_shard_ref, scan_all_ref, HEIGHT, ring_sems[0:5], prepare_scan)
    gate_ring = weight_ring(gate_shard_ref, gate_all_ref, HEIGHT, ring_sems[5:10], prepare_gate)
    out_ring = weight_ring(out_low_ref, out_all_ref, out_height, ring_sems[10:15], prepare_out)
    spacing = 3
    rings = (
        (scan_ring, 0, in_chunks),
        (gate_ring, in_chunks, in_chunks),
        (out_ring, 2 * in_chunks, out_chunks),
    )

    def round_(step):
        for ring, first, chunks in rings:
            ring.round(step - first, chunks, spacing)

    def rounds(first, end):
        def one(step, carry):
            round_(step)
            return carry

        lax.fori_loop(first, end, one, 0)

    def complete(at):
        ring, first, chunks = rings[at]
        return first + chunks + spacing * ring.reach

    def wait_pairs(at):
        ring, _, chunks = rings[at]

        def one(chunk, carry):
            ring.wait_pair(chunk)
            return carry

        lax.fori_loop(0, chunks, one, 0)

    rounds(0, 2)

    for i in range(1, group):
        small_copy(i, lax.rem(me + i, group), me).wait_send()
        small_copy(i, me, lax.rem(me + group - i, group)).wait_recv()
    taps_ref[...] = jnp.zeros_like(taps_ref)
    for device in range(group):
        small = small_all_ref[device].astype(f32)
        pre_scale_ref[0:1, device * own_in : (device + 1) * own_in] = small[0:1, 0:own_in]
        taps_ref[0:5, device * conv_own : (device + 1) * conv_own] = small[1:6, 0:conv_own]
        post_scale_ref[0:1, device * own_out : (device + 1) * own_out] = small[6:7, 0:own_out]
    pre_scale_ref[1:8, :] = jnp.zeros((7, model_width), f32)

    skip_parts = jnp.concatenate(
        thirds(jnp.broadcast_to(heads_ref[2:3, :], (8, LANES))), axis=1
    )

    def spread_skip(tile, carry):
        cols = pl.ds(pl.multiple_of(tile * LANES, LANES), LANES)
        skip_ref[0:1, cols] = mm(skip_parts, head_lanes(tile, per_tile, 3), 1, 0)[0:1, :]
        return carry

    lax.fori_loop(0, tiles, spread_skip, 0)

    def norm(at, carry):
        some = pl.ds(pl.multiple_of(at * HEIGHT, HEIGHT), HEIGHT)
        hidden = hidden_ref[some, :].astype(f32)
        root = lax.rsqrt(jnp.mean(hidden * hidden, axis=-1, keepdims=True) + norm_eps)
        normed_ref[some, :] = (hidden * root * pre_scale_ref[0:1, :]).astype(bf16)
        return carry

    lax.fori_loop(0, rows // HEIGHT, norm, 0)

    def turn(source_ref, target_ref):
        def one(at, carry):
            cols = pl.ds(pl.multiple_of(at * LANES, LANES), LANES)
            target_ref[cols, :] = source_ref[:, cols].astype(f32).T.astype(bf16)
            return carry

        lax.fori_loop(0, source_ref.shape[1] // LANES, one, 0)

    turn(normed_ref, normed_t_ref)
    rounds(2, complete(0))
    wait_pairs(0)

    def weight_copy(all_ref, at, width):
        slot = lax.rem(at, 2)
        cols = pl.ds(pl.multiple_of(at * WIDE, WIDE), width)
        return pltpu.make_async_copy(
            all_ref.at[:, :, :, cols],
            weights_ref.at[slot, :, :, :, pl.ds(0, width)],
            weight_sem.at[slot],
        )

    def columns(all_ref, action):
        total = all_ref.shape[3]
        full = total // WIDE
        rest = total % WIDE

        def fetch(at, act):
            @pl.when(at < full)
            def _():
                act(weight_copy(all_ref, at, WIDE))

            if rest:

                @pl.when(at == full)
                def _():
                    act(weight_copy(all_ref, at, rest))

        fetch(0, lambda copy: copy.start())

        def one(at, carry):
            fetch(at + 1, lambda copy: copy.start())
            fetch(at, lambda copy: copy.wait())
            weights = weights_ref[lax.rem(at, 2)].reshape(model_width, WIDE)
            action(at, WIDE, mm(normed_ref[...], weights, 1, 0))
            return carry

        lax.fori_loop(0, full, one, 0)
        if rest:
            fetch(full, lambda copy: copy.wait())
            weights = weights_ref[full % 2, :, :, :, 0:rest].reshape(model_width, rest)
            action(full, rest, mm(normed_ref[...], weights, 1, 0))

    def keep_scan(at, width, product):
        cols = pl.ds(at * WIDE if isinstance(at, int) else pl.multiple_of(at * WIDE, WIDE), width)
        u_ref[:, cols] = product.astype(bf16)

    columns(scan_all_ref, keep_scan)
    halo_copy = seq_copy(
        u_ref.at[pl.ds(rows - HALO, HALO), pl.ds(0, conv_width)],
        halo_ref,
        halo_sem.at[0],
        halo_sem.at[1],
        right,
    )

    @pl.when(rank < last)
    def _():
        halo_copy.start()

    round_(complete(0))
    step = jax.nn.softplus(u_ref[:, conv_width:].astype(f32) + heads_ref[0:1, :])
    decay = -step * jnp.exp(heads_ref[1:2, :])
    lower = (iota((rows, rows), 0) >= iota((rows, rows), 1)).astype(f32).astype(bf16)
    cum = sum(mm(lower, part, 1, 0) for part in thirds(decay))
    step_ref[...] = step
    cum_ref[...] = cum
    cumt_ref[...] = cum.T

    @pl.when(rank > 0)
    def _():
        halo_copy.wait_recv()

    @pl.when(rank == 0)
    def _():
        halo_ref[...] = jnp.zeros_like(halo_ref)

    pre_b, sig_b = conv_tile(conv_ref, halo_ref, u_ref, taps_ref, inner, rows)
    b_parts = halves(pre_b * sig_b)
    pre_c, sig_c = conv_tile(conv_ref, halo_ref, u_ref, taps_ref, inner + N, rows)
    c_parts = halves(pre_c * sig_c)
    scores = mm3(c_parts, b_parts, 1, 1)
    causal = iota((rows, rows), 0) >= iota((rows, rows), 1)
    score_ref[...] = jnp.where(causal, scores, 0.0)
    cum_parts = jnp.concatenate(thirds(cum), axis=1)
    step_parts = jnp.concatenate(thirds(step), axis=1)
    lane = iota((rows, LANES), 1)
    width = LANES // per_tile

    def chain(tile):
        return seq_copy(
            leave_ref.at[tile], enter_ref.at[tile], send_sem.at[tile], recv_sem.at[tile], right
        )

    def one(tile, carry):
        start = pl.multiple_of(tile * LANES, LANES)
        cols = pl.ds(start, LANES)
        pick = head_lanes(tile, per_tile, 3)
        cum_l = mm(cum_parts, pick, 1, 0)
        step_l = mm(step_parts, pick, 1, 0)
        pre, sig = conv_tile(conv_ref, halo_ref, u_ref, taps_ref, start, rows)
        values = pre * sig
        x = values * step_l
        total = cum_l[rows - 1 : rows, :]
        fresh = mm3(b_parts, halves(x * jnp.exp(total - cum_l)), 0, 0)

        @pl.when(rank > 0)
        def _():
            chain(tile).wait_recv()

        @pl.when(rank == 0)
        def _():
            enter_ref[tile] = jnp.zeros((N, LANES), f32)

        enter = enter_ref[tile]
        leave_ref[tile] = jnp.exp(total) * enter + fresh

        @pl.when(rank < last)
        def _():
            chain(tile).start()

        result = mm3(c_parts, halves(enter), 1, 0) * jnp.exp(cum_l)
        for h in range(per_tile):
            row = cumt_ref[pl.ds(tile * per_tile + h, 1), :]
            col = cum_l[:, h * width : h * width + 1]
            kernel = jnp.exp(jnp.minimum(col - row, 0.0)) * score_ref[...]
            own = (lane // width) == h
            result = result + mm3(halves(kernel), halves(jnp.where(own, x, 0.0)), 1, 0)
        ypre_ref[:, cols] = result
        mixer_ref[:, cols] = (result + skip_ref[0:1, cols] * values).astype(bf16)

        @pl.when(lax.rem(tile, pace) == pace - 1)
        def _():
            round_(in_loop + tile // pace)

        return carry

    in_loop = complete(0) + 1
    pace = 4
    lax.fori_loop(0, tiles, one, 0)
    at_round = in_loop + tiles // pace
    rounds(at_round, max(at_round, complete(1)))
    at_round = max(at_round, complete(1))
    wait_pairs(1)

    gated_ref_sum = score_ref

    def keep_gate(at, width, product):
        cols = pl.ds(at * WIDE if isinstance(at, int) else pl.multiple_of(at * WIDE, WIDE), width)
        gated = mixer_ref[:, cols].astype(f32) * (product * jax.nn.sigmoid(product))
        gate_ref[:, cols] = product
        gated_ref[:, cols] = gated
        square = gated * gated
        total = square[:, 0:LANES]
        for part in range(1, width // LANES):
            total = total + square[:, part * LANES : (part + 1) * LANES]
        gated_ref_sum[:, 0:LANES] += total

    gated_ref_sum[:, 0:LANES] = jnp.zeros((rows, LANES), f32)
    columns(gate_all_ref, keep_gate)
    end_round = complete(2)
    rounds(at_round, min(at_round + 1, end_round))
    at_round = min(at_round + 1, end_round)
    root = lax.rsqrt(
        jnp.sum(gated_ref_sum[:, 0:LANES], axis=-1, keepdims=True) / inner + norm_eps
    )

    def keep_post(at, carry):
        cols = pl.ds(pl.multiple_of(at * WIDE, WIDE), WIDE)
        whitened = gated_ref[:, cols] * root
        gated_ref[:, cols] = whitened
        post_ref[:, cols] = (whitened * post_scale_ref[0:1, cols]).astype(bf16)
        return carry

    lax.fori_loop(0, inner // WIDE, keep_post, 0)
    turn(post_ref, post_t_ref)
    rounds(at_round, end_round)
    wait_pairs(2)
    normed_turn = PlaneTurn(
        normed_t_ref,
        normed_turned_ref,
        own_in,
        rows,
        (turn_send.at[0], turn_recv.at[0], own_sem.at[0]),
    )
    post_turn = PlaneTurn(
        post_t_ref,
        post_turned_ref,
        own_out,
        rows,
        (turn_send.at[1], turn_recv.at[1], own_sem.at[1]),
    )
    post_turn.start()
    normed_turn.start()

    span = 2 * own_out

    def out_copy(chip):
        slot = chip % 2
        return pltpu.make_async_copy(
            out_all_ref.at[chip], out_weights_ref.at[slot], weight_sem.at[slot]
        )

    out_copy(0).start()
    overlap = jnp.zeros((rows, LANES), f32)
    for chip in range(group // 2):
        if chip + 1 < group // 2:
            out_copy(chip + 1).start()
        out_copy(chip).wait()
        cols = slice(chip * span, (chip + 1) * span)
        weights = out_weights_ref[chip % 2].reshape(span, model_width)
        dpost = mm(cot_ref[...], weights, 1, 1)
        dpost_ref[:, cols] = dpost
        pulled = dpost * gated_ref[:, cols]
        post_grad_ref[0:1, cols] = jnp.sum(pulled, axis=0, keepdims=True)
        pulled = pulled * post_scale_ref[0:1, cols]
        for part in range(span // LANES):
            overlap = overlap + pulled[:, part * LANES : (part + 1) * LANES]
    mean = jnp.sum(overlap, axis=-1, keepdims=True) / inner

    def keep_back(at, carry):
        cols = pl.ds(pl.multiple_of(at * WIDE, WIDE), WIDE)
        gate = gate_ref[:, cols]
        sig = jax.nn.sigmoid(gate)
        dgated = root * (dpost_ref[:, cols] * post_scale_ref[0:1, cols] - gated_ref[:, cols] * mean)
        dy_ref[:, cols] = (dgated * (gate * sig)).astype(bf16)
        gate_grad_ref[:, cols] = (
            dgated * mixer_ref[:, cols].astype(f32) * sig * (1.0 + gate * (1.0 - sig))
        ).astype(bf16)
        return carry

    lax.fori_loop(0, inner // WIDE, keep_back, 0)

    @pl.when(rank < last)
    def _():
        halo_copy.wait_send()

        def drain(tile, carry):
            chain(tile).wait_send()
            return carry

        lax.fori_loop(0, tiles, drain, 0)

    for ring, _, chunks in rings:

        def finish(chunk, carry, ring=ring):
            ring.finish(chunk)
            return carry

        lax.fori_loop(0, chunks, finish, 0)

    def backward():
        core = lax.rem(me, 2)
        cot_chunks = EARLY

        def cot_block(chunk, origin, part):
            ref = cot_all_ref.at[chunk, core, origin]
            return ref if part is None else ref.at[pl.ds(part * (rows // 2), rows // 2), :]

        def cot_source(chunk, part, action):
            part_rows = pl.ds(0, rows) if part is None else pl.ds(part * (rows // 2), rows // 2)
            cols = pl.ds(pl.multiple_of(chunk * WIDE, WIDE), WIDE)
            action(cot_ref.at[part_rows, cols])

        ring = PlaneRing(
            cot_block, cot_source, lambda chunk, half: cot_all_ref.at[chunk, half], cot_ring_sems
        )

        left = jnp.maximum(rank - 1, 0)
        cum = cum_ref[...]
        step = step_ref[...]
        pre_b, sig_b = conv_tile(conv_ref, halo_ref, u_ref, taps_ref, inner, rows)
        b_parts = halves(pre_b * sig_b)
        pre_c, sig_c = conv_tile(conv_ref, halo_ref, u_ref, taps_ref, inner + N, rows)
        c_parts = halves(pre_c * sig_c)
        later = iota((rows, rows), 1) >= iota((rows, rows), 0)
        score_ref[...] = jnp.where(later, mm3(b_parts, c_parts, 1, 1), 0.0)
        dscore_ref[...] = jnp.zeros_like(dscore_ref)
        dread_ref[...] = jnp.zeros_like(dread_ref)
        dwrite_ref[...] = jnp.zeros_like(dwrite_ref)
        dcum_ref[...] = jnp.zeros_like(dcum_ref)
        dstep_ref[...] = jnp.zeros_like(dstep_ref)
        cum_parts = jnp.concatenate(thirds(cum), axis=1)
        step_parts = jnp.concatenate(thirds(step), axis=1)
        lane = iota((rows, LANES), 1)
        final_row = iota((rows, LANES), 0) == rows - 1
        width = LANES // per_tile

        def chain(tile):
            return seq_copy(
                leave_ref.at[tile], arrive_ref.at[tile], back_send.at[tile], back_recv.at[tile], left
            )

        def tap_grads(dpre, extra):
            sums = [
                jnp.sum(
                    dpre * conv_ref[HALO - 3 + k : HALO - 3 + k + rows, :], axis=0, keepdims=True
                )
                for k in range(4)
            ]
            sums.append(jnp.sum(dpre, axis=0, keepdims=True))
            sums.append(extra)
            sums.append(jnp.zeros((2, LANES), f32))
            return jnp.concatenate(sums, axis=0)

        def one(tile, carry):
            start = pl.multiple_of(tile * LANES, LANES)
            cols = pl.ds(start, LANES)
            pick = head_lanes(tile, per_tile, 3)
            cum_l = mm(cum_parts, pick, 1, 0)
            step_l = mm(step_parts, pick, 1, 0)
            total = cum_l[rows - 1 : rows, :]
            dy = dy_ref[:, cols].astype(f32)
            reads = halves(dy * jnp.exp(cum_l))
            denter = mm3(c_parts, reads, 0, 0)

            @pl.when(rank < last)
            def _():
                chain(tile).wait_recv()

            @pl.when(rank == last)
            def _():
                arrive_ref[tile] = jnp.zeros((N, LANES), f32)

            arrive = arrive_ref[tile]
            leave_ref[tile] = jnp.exp(total) * arrive + denter

            @pl.when(rank > 0)
            def _():
                chain(tile).start()

            pre, sig = conv_tile(conv_ref, halo_ref, u_ref, taps_ref, start, rows)
            values = pre * sig
            x = values * step_l
            x_parts = halves(x)
            tail = jnp.exp(total - cum_l)
            enter = enter_ref[tile]
            arrive_parts = halves(arrive)
            dx_state = mm3(b_parts, arrive_parts, 1, 0) * tail
            dx = dx_state
            for h in range(per_tile):
                row = cumt_ref[pl.ds(tile * per_tile + h, 1), :]
                col = cum_l[:, h * width : h * width + 1]
                spread = jnp.exp(jnp.minimum(row - col, 0.0))
                kernel = halves(spread * score_ref[...])
                own = jnp.where((lane // width) == h, dy, 0.0).astype(bf16)
                dx = dx + (mm(kernel[0], own, 1, 0) + mm(kernel[1], own, 1, 0))
                pairs = mm(x_parts[0], own, 1, 1) + mm(x_parts[1], own, 1, 1)
                dscore_ref[...] += spread * pairs
            dread_ref[...] += mm3(reads, halves(enter), 1, 1)
            dwrite_ref[...] += mm3(halves(x * tail), arrive_parts, 1, 1)
            ends = jnp.sum(x * dx_state, axis=0, keepdims=True) + jnp.exp(total) * jnp.sum(
                enter * arrive, axis=0, keepdims=True
            )
            dcum = dy * ypre_ref[:, cols] - x * dx + jnp.where(final_row, ends, 0.0)
            own_head = pick[0:LANES, :]
            for part in halves(dcum):
                dcum_ref[...] += mm(part, own_head, 1, 1)
            for part in halves(dx * values):
                dstep_ref[...] += mm(part, own_head, 1, 1)
            dvalues = step_l * dx + skip_ref[0:1, cols] * dy
            dpre = dvalues * sig * (1.0 + pre * (1.0 - sig))
            dpre_ref[0:rows, cols] = dpre
            packed_ref[:, cols] = tap_grads(dpre, jnp.sum(dy * values, axis=0, keepdims=True))

            ring.round(tile - COT_AT, cot_chunks, COT_SPACING)

            return carry

        lax.fori_loop(0, tiles, one, 0)
        for at in range(tiles - COT_AT, cot_chunks + COT_SPACING * ring.reach):
            ring.round(at, cot_chunks, COT_SPACING)

        dscore = halves(jnp.where(later, dscore_ref[...], 0.0))
        dshared = (
            dwrite_ref[...] + mm3(dscore, c_parts, 1, 0),
            dread_ref[...] + mm3(dscore, b_parts, 0, 0),
        )
        for i in range(2):
            start = inner + i * N
            pre, sig = conv_tile(conv_ref, halo_ref, u_ref, taps_ref, start, rows)
            dpre = dshared[i] * sig * (1.0 + pre * (1.0 - sig))
            dpre_ref[0:rows, start : start + N] = dpre
            packed_ref[:, start : start + N] = tap_grads(dpre, jnp.zeros((1, LANES), f32))

        edge = seq_copy(
            dpre_ref.at[pl.ds(0, 8), :],
            dpre_ref.at[pl.ds(rows, 8), :],
            edge_sem.at[0],
            edge_sem.at[1],
            left,
        )

        @pl.when(rank > 0)
        def _():
            edge.start()

        upper = (iota((rows, rows), 1) >= iota((rows, rows), 0)).astype(f32).astype(bf16)
        ddecay = sum(mm(upper, part, 1, 0) for part in thirds(dcum_ref[...]))
        exp_rate = jnp.exp(heads_ref[1:2, :])
        drate = (dstep_ref[...] - ddecay * exp_rate) * jax.nn.sigmoid(
            u_ref[:, conv_width:].astype(f32) + heads_ref[0:1, :]
        )
        packed_ref[:, conv_width:] = jnp.concatenate(
            [
                jnp.sum(drate, axis=0, keepdims=True),
                jnp.sum(ddecay * (-step * exp_rate), axis=0, keepdims=True),
                jnp.zeros((6, LANES), f32),
            ],
            axis=0,
        )
        packed_ref[6:7, 0:inner] = post_grad_ref[...]
        dproj_ref[:, conv_width : conv_width + LANES] = drate.astype(bf16)
        dproj_ref[:, conv_width + LANES :] = jnp.zeros(
            (rows, dproj_ref.shape[1] - conv_width - LANES), bf16
        )

        @pl.when(rank == last)
        def _():
            dpre_ref[rows : rows + 8, :] = jnp.zeros((8, conv_width), f32)

        @pl.when(rank < last)
        def _():
            edge.wait_recv()

        def unconv(tile, carry):
            cols = pl.ds(pl.multiple_of(tile * LANES, LANES), LANES)
            taps = taps_ref[:, cols]
            du = taps[3:4, :] * dpre_ref[0:rows, cols]
            for k in range(3):
                du = du + taps[k : k + 1, :] * dpre_ref[3 - k : 3 - k + rows, cols]
            dproj_ref[:, cols] = du.astype(bf16)
            return carry

        lax.fori_loop(0, conv_width // LANES, unconv, 0)

        @pl.when(rank > 0)
        def _():
            edge.wait_send()

            def drain(tile, carry):
                chain(tile).wait_send()
                return carry

            lax.fori_loop(0, tiles, drain, 0)


        def finish_ring(chunk, carry):
            ring.wait_pair(chunk)
            ring.finish(chunk)
            return carry

        lax.fori_loop(0, cot_chunks, finish_ring, 0)

    cot_ring_sems = ring_sems[15:]
    leaving = [
        pltpu.make_async_copy(post_ref, post_out_ref, leave_sem.at[0]),
        pltpu.make_async_copy(gate_grad_ref, gate_grad_out_ref, leave_sem.at[1]),
    ]
    for copy in leaving:
        copy.start()
    backward()
    for copy in leaving:
        copy.wait()
    post_turn.finish()
    normed_turn.finish()


def vmem(count):
    return [pl.BlockSpec(memory_space=pltpu.VMEM)] * count


def front(in_shard, out_shard, prenorm, convtaps, postnorm, hidden, cot, headcoefs, sizes):
    rows, inner, tiles, _ = sizes
    conv_width = inner + 2 * N
    shape = jax.ShapeDtypeStruct
    group = lax.axis_size("dp")
    own_in, proj_width = in_shard.shape
    own_out, model_width = out_shard.shape
    scan_width = -(-(proj_width - inner) // LANES) * LANES
    in_chunks = own_in // HEIGHT
    out_chunks = own_out // (2 * HEIGHT)
    small_lanes = -(-max(own_in, own_out, convtaps.shape[1]) // LANES) * LANES
    anywhere = pl.BlockSpec(memory_space=pl.ANY)
    dma = pltpu.SemaphoreType.DMA
    return pl.pallas_call(
        functools.partial(front_kernel, sizes),
        out_shape=(
            shape((8, model_width), f32),
            shape((rows, inner), bf16),
            shape((rows, inner), bf16),
            shape((own_in, group * rows), bf16),
            shape((own_out, group * rows), bf16),
            shape((rows, -(-scan_width // WIDE) * WIDE), bf16),
            shape((8, conv_width + LANES), f32),
            shape((group // 2, 2, own_in, scan_width), bf16),
            shape((group // 2, 2, own_in, inner), bf16),
            shape((group // 2, 2, own_out, model_width), bf16),
            shape((EARLY, 2, group // 2, rows, WIDE), bf16),
        ),
        in_specs=[anywhere] * 2 + vmem(6),
        out_specs=tuple(vmem(1) + [anywhere] * 4 + vmem(2) + [anywhere] * 4),
        scratch_shapes=[
            pltpu.VMEM((rows, scan_width), bf16),
            pltpu.VMEM((rows, inner), f32),
            pltpu.VMEM((tiles, N, LANES), f32),
            pltpu.VMEM((HALO, conv_width), bf16),
            pltpu.VMEM((rows, LANES), f32),
            pltpu.VMEM((rows, LANES), f32),
            pltpu.VMEM((LANES, rows), f32),
            pltpu.VMEM((8, conv_width), f32),
            pltpu.VMEM((rows, inner), bf16),
            pltpu.VMEM((inner, rows), bf16),
            pltpu.VMEM(in_shard.shape, f32),
            pltpu.VMEM(out_shard.shape, f32),
            pltpu.VMEM((own_in, scan_width), bf16),
            pltpu.VMEM((own_in, inner), bf16),
            pltpu.VMEM((own_out, model_width), bf16),
            pltpu.VMEM((group, 16, small_lanes), bf16),
            pltpu.VMEM((1, inner), f32),
            pltpu.VMEM((rows, model_width), bf16),
            pltpu.VMEM((2, group // 2, 2, own_in, WIDE), bf16),
            pltpu.VMEM((2, 2, own_out, model_width), bf16),
            pltpu.VMEM((HALO + rows, LANES), f32),
            pltpu.VMEM((rows, rows), f32),
            pltpu.VMEM((tiles, N, LANES), f32),
            pltpu.VMEM((rows, inner), bf16),
            pltpu.VMEM((rows, inner), f32),
            pltpu.VMEM((rows, inner), f32),
            pltpu.VMEM((rows, inner), f32),
            pltpu.VMEM((model_width, rows), bf16),
            pltpu.VMEM((rows, rows), f32),
            pltpu.VMEM((rows, N), f32),
            pltpu.VMEM((rows, N), f32),
            pltpu.VMEM((rows, LANES), f32),
            pltpu.VMEM((rows, LANES), f32),
            pltpu.VMEM((rows + 8, conv_width), f32),
            pltpu.VMEM((tiles, N, LANES), f32),
            pltpu.VMEM((1, inner), f32),
            pltpu.VMEM((rows, inner), bf16),
            pltpu.VMEM((rows, inner), bf16),
            pltpu.VMEM((16, small_lanes), bf16),
            pltpu.VMEM((8, LANES), f32),
            pltpu.VMEM((1, inner), f32),
            dma((tiles,)),
            dma((tiles,)),
            dma((2,)),
            dma((tiles,)),
            dma((tiles,)),
            dma((2,)),
            dma((2,)),
            dma((group,)),
            dma((group,)),
            dma((2, group)),
            dma((2, group)),
            dma((2,)),
            dma((in_chunks + 1,)),
            dma((2,)),
        ]
        + PlaneRing.semaphores(in_chunks)
        + PlaneRing.semaphores(in_chunks)
        + PlaneRing.semaphores(out_chunks)
        + PlaneRing.semaphores(EARLY),
        compiler_params=pltpu.CompilerParams(
            collective_id=1, has_side_effects=True, vmem_limit_bytes=60 * 2**20
        ),
        cost_estimate=pl.CostEstimate(
            flops=10**10, bytes_accessed=10**8, transcendentals=4 * 10**6
        ),
    )(in_shard, out_shard, prenorm, convtaps, postnorm, hidden, cot, headcoefs)


def plane_copy(src, dst, send, recv, to):
    return pltpu.make_async_remote_copy(
        src_ref=src,
        dst_ref=dst,
        send_sem=send,
        recv_sem=recv,
        device_id={"dp": to},
        device_id_type=MESH,
    )


class PlaneTurn:
    def __init__(self, source, target, height, width, sems):
        self.source, self.target, self.height, self.width = source, target, height, width
        self.send, self.recv, self.own_sem = sems
        self.me = lax.axis_index("dp")
        self.group = lax.axis_size("dp")

    def rows_for(self, device):
        return self.source.at[
            pl.ds(pl.multiple_of(device * self.height, self.height), self.height), :
        ]

    def columns_of(self, device):
        start = pl.multiple_of(slot_of(device, self.group) * self.width, self.width)
        return self.target.at[:, pl.ds(start, self.width)]

    def copy(self, i, peer, origin):
        return plane_copy(
            self.rows_for(peer), self.columns_of(origin), self.send.at[i], self.recv.at[i], peer
        )

    def own(self):
        return pltpu.make_async_copy(
            self.rows_for(self.me), self.columns_of(self.me), self.own_sem
        )

    def start(self):
        for i in range(1, self.group):
            self.copy(i, lax.rem(self.me + i, self.group), self.me).start()
        self.own().start()

    def arrive(self):
        for i in range(1, self.group):
            origin = lax.rem(self.me + self.group - i, self.group)
            self.copy(i, origin, origin).wait_recv()
        self.own().wait()

    def sent(self):
        for i in range(1, self.group):
            self.copy(i, lax.rem(self.me + i, self.group), self.me).wait_send()

    def finish(self):
        self.arrive()
        self.sent()


class PlaneRing:
    def __init__(self, block, source, pair_block, sems, prepare=None):
        group = lax.axis_size("dp")
        me = lax.axis_index("dp")
        self.block, self.source, self.pair_block = block, source, pair_block
        self.prepare = prepare
        self.ring_send, self.ring_recv, self.pair_send, self.pair_recv, self.own_sem = sems
        self.chips = group // 2
        self.reach = self.chips // 2
        self.me = me
        self.core = lax.rem(me, 2)
        self.chip = me // 2
        self.place = ring_place(self.chip, self.chips)

    @staticmethod
    def semaphores(chunks):
        group = lax.axis_size("dp")
        dma = pltpu.SemaphoreType.DMA
        return [dma((chunks, group // 2)), dma((chunks, group // 2))] + [dma((chunks,))] * 3

    def ring_chip(self, ahead):
        return ring_place(lax.rem(self.place + ahead + self.chips, self.chips), self.chips)

    def part(self, number, way):
        return None if number < self.reach else (0 if way == 1 else 1)

    def copy(self, chunk, number, way, origin, source=None):
        block = self.block(chunk, origin, self.part(number, way))
        at = 2 * (number - 1) + (0 if way == 1 else 1)
        return plane_copy(
            block if source is None else source,
            block,
            self.ring_send.at[chunk, at],
            self.ring_recv.at[chunk, at],
            2 * self.ring_chip(way) + self.core,
        )

    def hop(self, chunk, number, way, source=None):
        return self.copy(chunk, number, way, self.ring_chip(-way * (number - 1)), source)

    def hop_in(self, chunk, number, way):
        return self.copy(chunk, number, way, self.ring_chip(-way * number))

    def own_copy(self, chunk, source):
        return pltpu.make_async_copy(
            source, self.block(chunk, self.chip, None), self.own_sem.at[chunk]
        )

    def pair_copy(self, chunk, core):
        block = self.pair_block(chunk, core)
        return plane_copy(
            block,
            block,
            self.pair_send.at[chunk],
            self.pair_recv.at[chunk],
            self.me + 1 - 2 * self.core,
        )

    def stage(self, chunk, number):
        if number == 0:
            if self.prepare is not None:
                self.prepare(chunk)
            self.source(chunk, None, lambda ref: self.own_copy(chunk, ref).start())
            for way in (1, -1):
                self.source(
                    chunk,
                    self.part(1, way),
                    lambda ref, way=way: self.hop(chunk, 1, way, ref).start(),
                )
            return
        for way in (1, -1):
            self.hop_in(chunk, number, way).wait_recv()
            if number < self.reach:
                self.hop(chunk, number + 1, way).start()
        if number == self.reach:
            self.own_copy(chunk, self.block(chunk, self.chip, None)).wait()
            self.pair_copy(chunk, self.core).start()

    def wait_pair(self, chunk):
        self.pair_copy(chunk, 1 - self.core).wait_recv()

    def finish(self, chunk):
        for number in range(1, self.reach + 1):
            for way in (1, -1):
                self.hop(chunk, number, way).wait_send()
        self.pair_copy(chunk, self.core).wait_send()

    def round(self, step, chunks, spacing):
        for number in range(self.reach, -1, -1):
            chunk = step - number * spacing

            @pl.when((chunk >= 0) & (chunk < chunks))
            def _(chunk=chunk, number=number):
                self.stage(chunk, number)


def weight_ring(shard_ref, all_ref, height, sems, prepare):
    core = lax.rem(lax.axis_index("dp"), 2)

    def rows_of(chunk, part):
        size = height if part is None else height // 2
        start = chunk * height + (0 if part is None else part * size)
        return pl.ds(pl.multiple_of(start, size), size)

    return PlaneRing(
        lambda chunk, origin, part: all_ref.at[origin, core, rows_of(chunk, part), :],
        lambda chunk, part, action: action(shard_ref.at[rows_of(chunk, part), :]),
        lambda chunk, half: all_ref.at[:, half, rows_of(chunk, None), :],
        sems,
        prepare,
    )


HEIGHT = 32


def tail_kernel(
    sizes,
    normed_turned_ref,
    post_turned_ref,
    cot_ref,
    gate_far_ref,
    scan_far_ref,
    packed_in_ref,
    hidden_far_ref,
    own_cot_far_ref,
    post_far_ref,
    scale_ref,
    gate_matrix_ref,
    scan_matrix_ref,
    out_matrix_ref,
    in_ref,
    out_ref,
    small_out_ref,
    output_far_ref,
    input_grad_far_ref,
    gathered_ref,
    value_ref,
    inbox_ref,
    total_ref,
    loaded_ref,
    small_value_ref,
    small_inbox_ref,
    small_all_ref,
    weights_ref,
    normed_grad_ref,
    packed_ref,
    gate_ref,
    scan_ref,
    hidden_ref,
    own_cot_ref,
    post_ref,
    output_ref,
    input_grad_ref,
    far_sem,
    up_send,
    inbox_recv,
    other_recv,
    total_recv,
    left_send,
    right_send,
    store_sem,
    ring_send,
    ring_recv,
    pair_send,
    pair_recv,
    own_sem,
    load_sem,
    small_send,
    small_recv,
    weight_sem,
):
    rows, own_in, out_steps, gate_steps, steps, root, lag, spacing = sizes
    rest = out_steps // 2 - EARLY
    back_items = steps - out_steps
    chunks = back_items + rest
    rank = lax.axis_index("seq")
    last = lax.axis_size("seq") - 1
    me = lax.axis_index("dp")
    group = lax.axis_size("dp")
    chips = group // 2
    reach = chips // 2
    core = lax.rem(me, 2)
    arriving = [
        pltpu.make_async_copy(far, near, far_sem.at[at])
        for at, (far, near) in enumerate(
            (
                (gate_far_ref, gate_ref),
                (scan_far_ref, scan_ref),
                (hidden_far_ref, hidden_ref),
                (own_cot_far_ref, own_cot_ref),
                (post_far_ref, post_ref),
            )
        )
    ]
    leaving = (
        pltpu.make_async_copy(input_grad_ref, input_grad_far_ref, far_sem.at[5]),
        pltpu.make_async_copy(output_ref, output_far_ref, far_sem.at[6]),
    )
    barrier = pltpu.get_barrier_semaphore()
    greet_seq(barrier, rank, last)
    greet_plane(barrier, me, group)
    pl.semaphore_wait(barrier, seq_neighbours(rank, last) + group - 1)
    left = jnp.maximum(rank - 1, 0)
    right = jnp.minimum(rank + 1, last)

    model_width = hidden_ref.shape[1]

    def small_copy(i, peer, slot):
        return plane_copy(
            packed_ref, small_all_ref.at[slot], small_send.at[i], small_recv.at[i], peer
        )

    def block(chunk, origin, part):
        ref = gathered_ref.at[chunk, core, origin]
        return ref if part is None else ref.at[pl.ds(part * (rows // 2), rows // 2), :]

    def source(chunk, part, action):
        part_rows = pl.ds(0, rows) if part is None else pl.ds(part * (rows // 2), rows // 2)

        def one(ref, first):
            start = pl.multiple_of((chunk - first) * WIDE, WIDE)
            action(ref.at[part_rows, pl.ds(start, WIDE)])

        @pl.when(chunk < rest)
        def _():
            one(own_cot_far_ref, -EARLY)

        @pl.when((chunk >= rest) & (chunk < rest + gate_steps))
        def _():
            one(gate_far_ref, rest)

        @pl.when(chunk >= rest + gate_steps)
        def _():
            one(scan_far_ref, rest + gate_steps)

    ring = PlaneRing(
        block,
        source,
        lambda chunk, half: gathered_ref.at[chunk, half],
        (ring_send, ring_recv, pair_send, pair_recv, own_sem),
    )

    def order_of(step):
        return jnp.where(step < out_steps, step // 2, step - out_steps + out_steps // 2)

    def fetch(step, action):
        order = order_of(step)
        slot = lax.rem(order, 2)

        @pl.when((order < EARLY) & (lax.rem(step, 2) == 0))
        def _():
            action(
                pltpu.make_async_copy(cot_ref.at[order], loaded_ref.at[slot], load_sem.at[slot])
            )

        @pl.when((order >= EARLY) & ((step >= out_steps) | (lax.rem(step, 2) == 0)))
        def _():
            action(
                pltpu.make_async_copy(
                    gathered_ref.at[order - EARLY], loaded_ref.at[slot], load_sem.at[slot]
                )
            )

        return slot

    def compute(step):
        arrived = loaded_ref.at[fetch(step, lambda copy: copy.wait())]

        @pl.when(step < out_steps)
        def _():
            some = pl.ds(pl.multiple_of(lax.rem(step, 2) * own_in, own_in), own_in)
            value_ref[...] = mm(
                post_turned_ref[some, :], arrived[...].reshape(group * rows, WIDE), 1, 0
            )

        @pl.when(step >= out_steps)
        def _():
            value_ref[...] = mm(
                normed_turned_ref[...], arrived[...].reshape(group * rows, WIDE), 1, 0
            )

    fetch(0, lambda copy: copy.start())
    for copy in arriving:
        copy.start()

    def weight_copy(item, action):
        slot = lax.rem(item, 2)
        narrow = scan_matrix_ref.shape[1] % WIDE

        def one(matrix_ref, first, width):
            height = matrix_ref.shape[0]
            start = pl.multiple_of((item - first) * WIDE, WIDE)
            action(
                pltpu.make_async_copy(
                    matrix_ref.at[:, pl.ds(start, width)],
                    weights_ref.at[slot, pl.ds(0, height), pl.ds(0, width)],
                    weight_sem.at[slot],
                )
            )

        full = back_items - 1 if narrow else back_items

        @pl.when(item < gate_steps)
        def _():
            one(gate_matrix_ref, 0, WIDE)

        @pl.when((item >= gate_steps) & (item < full))
        def _():
            one(scan_matrix_ref, gate_steps, WIDE)

        if narrow:

            @pl.when(item == full)
            def _():
                one(scan_matrix_ref, gate_steps, narrow)

        @pl.when((item >= back_items) & (item < items))
        def _():
            one(out_matrix_ref, back_items, WIDE)

    items = back_items + model_width // WIDE

    def back_product(grad_ref, item, first, width):
        cols = pl.ds(pl.multiple_of((item - first) * WIDE, WIDE), width)
        weights = weights_ref[lax.rem(item, 2), 0:model_width, 0:width]
        normed_grad_ref[...] += mm(grad_ref[:, cols], weights, 1, 1)

    def norm_backward():
        def block(at, carry):
            some = pl.ds(pl.multiple_of(at * HEIGHT, HEIGHT), HEIGHT)
            hidden = hidden_ref[some, :].astype(f32)
            root_mean = lax.rsqrt(jnp.mean(hidden * hidden, axis=-1, keepdims=True) + norm_eps)
            plain = hidden * root_mean
            grad = normed_grad_ref[some, :]
            scaled = grad * scale_ref[0:1, :]
            input_grad_ref[some, :] = root_mean * (
                scaled - plain * jnp.mean(scaled * plain, axis=-1, keepdims=True)
            ) + own_cot_ref[some, :].astype(f32)
            return carry + jnp.sum(grad * plain, axis=0, keepdims=True)

        total = lax.fori_loop(0, rows // HEIGHT, block, jnp.zeros((1, model_width), f32))
        packed_ref[...] = packed_in_ref[...]
        packed_ref[7:8, 0:model_width] = total
        for i in range(1, group):
            small_copy(i, lax.rem(me + i, group), me).start()
        small_all_ref[me] = packed_ref[...]

    def local_product(item):
        narrow = scan_matrix_ref.shape[1] % WIDE
        full = back_items - 1 if narrow else back_items

        @pl.when(item == 0)
        def _():
            normed_grad_ref[...] = jnp.zeros_like(normed_grad_ref)
            for copy in arriving:
                copy.wait()

        weight_copy(item, lambda copy: copy.wait())
        weight_copy(item + 1, lambda copy: copy.start())

        @pl.when(item < gate_steps)
        def _():
            back_product(gate_ref, item, 0, WIDE)

        @pl.when((item >= gate_steps) & (item < full))
        def _():
            back_product(scan_ref, item, gate_steps, WIDE)

        if narrow:

            @pl.when(item == full)
            def _():
                back_product(scan_ref, item, gate_steps, narrow)

        @pl.when(item == back_items - 1)
        def _():
            norm_backward()
            leaving[0].start()

        @pl.when(item >= back_items)
        def _():
            cols = pl.ds(pl.multiple_of((item - back_items) * WIDE, WIDE), WIDE)
            output_ref[:, cols] = hidden_ref[:, cols].astype(f32) + mm(
                post_ref[...], weights_ref[lax.rem(item, 2)], 1, 0
            )

        @pl.when(item == items - 1)
        def _():
            leaving[1].start()

    weight_copy(0, lambda copy: copy.start())

    def piece(ref, part, parts):
        if parts == 1:
            return ref
        size = own_in // parts
        start = part * size if isinstance(part, int) else pl.multiple_of(part * size, size)
        return ref.at[pl.ds(start, size), :]

    def up_copy(source, target, step, part, parts, recv, to):
        return seq_copy(
            piece(source, part, parts),
            piece(target, part, parts),
            up_send.at[step, part],
            recv.at[step, part],
            to,
        )

    def down_copy(total, step, part, parts, send, to):
        return seq_copy(
            piece(total, part, parts),
            piece(total, part, parts),
            send.at[step, part],
            total_recv.at[step, part],
            to,
        )

    def up(value, inbox, total, step, parts, after):
        edge = ((rank == 0) | (rank == last)) & (rank != root)
        inner_place = (rank != root) & (rank > 0) & (rank < last)
        for part in range(parts):
            here = piece(value, part, parts)
            inbox_here = piece(inbox, part, parts)
            total_here = piece(total, part, parts)

            @pl.when(edge)
            def _(here=here, inbox_here=inbox_here):
                inbox_here[...] = here[...]

            @pl.when(inner_place)
            def _(here=here, inbox_here=inbox_here, part=part):
                up_copy(inbox, inbox, step, part, parts, inbox_recv, left).wait_recv()
                inbox_here[...] += here[...]

            @pl.when(rank < root)
            def _(part=part):
                up_copy(inbox, inbox, step, part, parts, inbox_recv, right).start()

            @pl.when(rank == root + 1)
            def _(part=part):
                up_copy(inbox, total, step, part, parts, other_recv, left).start()

            @pl.when(rank > root + 1)
            def _(part=part):
                up_copy(inbox, inbox, step, part, parts, inbox_recv, left).start()

            @pl.when(rank == root)
            def _(here=here, inbox_here=inbox_here, total_here=total_here, part=part):
                result = here[...]
                if root > 0:
                    up_copy(inbox, inbox, step, part, parts, inbox_recv, left).wait_recv()
                    result = result + inbox_here[...]
                if root < last:
                    up_copy(total, total, step, part, parts, other_recv, right).wait_recv()
                    result = result + total_here[...]
                total_here[...] = result
                if root > 0:
                    down_copy(total, step, part, parts, left_send, left).start()
                if root < last:
                    down_copy(total, step, part, parts, right_send, right).start()

            after(part)

    def down(total, step, part, parts):
        @pl.when(rank < root)
        def _():
            down_copy(total, step, part, parts, left_send, left).wait_recv()

            @pl.when(rank > 0)
            def _():
                down_copy(total, step, part, parts, left_send, left).start()

        @pl.when(rank > root)
        def _():
            down_copy(total, step, part, parts, right_send, right).wait_recv()

            @pl.when(rank < last)
            def _():
                down_copy(total, step, part, parts, right_send, right).start()

    def drain(inbox, total, step, parts):
        for part in range(parts):

            @pl.when(rank < root)
            def _(part=part):
                up_copy(inbox, inbox, step, part, parts, inbox_recv, right).wait_send()

            @pl.when(rank > root)
            def _(part=part):
                up_copy(inbox, inbox, step, part, parts, inbox_recv, left).wait_send()

            @pl.when((rank <= root) & (rank > 0))
            def _(part=part):
                down_copy(total, step, part, parts, left_send, left).wait_send()

            @pl.when((rank >= root) & (rank < last))
            def _(part=part):
                down_copy(total, step, part, parts, right_send, right).wait_send()

    def stored(step, action):
        @pl.when(step < out_steps)
        def _():
            some = pl.ds(pl.multiple_of(lax.rem(step, 2) * own_in, own_in), own_in)
            cols = pl.ds(pl.multiple_of(step // 2 * WIDE, WIDE), WIDE)
            action(
                pltpu.make_async_copy(
                    total_ref.at[step], out_ref.at[some, cols], store_sem.at[step]
                )
            )

        @pl.when(step >= out_steps)
        def _():
            cols = pl.ds(pl.multiple_of((step - out_steps) * WIDE, WIDE), WIDE)
            action(
                pltpu.make_async_copy(total_ref.at[step], in_ref.at[:, cols], store_sem.at[step])
            )

    behind = lag * (jnp.maximum(rank - root, 0) + jnp.maximum(root - rank, 0))

    def round_(step, carry):
        for stage in range(reach, -1, -1):
            chunk = step - stage * spacing

            @pl.when((chunk >= 0) & (chunk < chunks))
            def _(chunk=chunk, stage=stage):
                ring.stage(chunk, stage)

        follow = step + 1
        arrives = (follow >= out_steps) | ((order_of(follow) >= EARLY) & (lax.rem(follow, 2) == 0))

        @pl.when(arrives & (follow < steps))
        def _():
            ring.wait_pair(order_of(follow) - EARLY)

        @pl.when(step + 1 < steps)
        def _():
            fetch(step + 1, lambda copy: copy.start())

        def down_late(part):
            late = PARTS * step + part - behind
            late_step = late // PARTS
            late_part = lax.rem(late, PARTS)

            @pl.when((late >= 0) & (late_step < steps))
            def _():
                down(total_ref.at[late_step], late_step, late_part, PARTS)

                @pl.when(late_part == PARTS - 1)
                def _():
                    stored(late_step, lambda copy: copy.start())

            @pl.when(late == PARTS * steps)
            def _():
                down(small_out_ref, steps, 0, 1)

        @pl.when(step < steps)
        def _():
            compute(step)
            up(value_ref, inbox_ref.at[step], total_ref.at[step], step, PARTS, down_late)

        @pl.when(step == steps)
        def _():
            for i in range(1, group):
                small_copy(i, lax.rem(me + i, group), me).wait_send()
                origin = lax.rem(me + group - i, group)
                small_copy(i, origin, origin).wait_recv()
            small_value_ref[...] = jnp.sum(small_all_ref[...], axis=0)
            up(small_value_ref, small_inbox_ref, small_out_ref, steps, 1, lambda part: None)

        @pl.when(step >= steps)
        def _():
            for part in range(PARTS):
                down_late(part)

        @pl.when((step >= 1) & (step < 1 + items))
        def _():
            local_product(step - 1)

        return carry

    lax.fori_loop(0, steps + 1 + (behind + PARTS - 1) // PARTS, round_, 0)

    def finish(step, carry):
        drain(inbox_ref.at[step], total_ref.at[step], step, PARTS)
        stored(step, lambda copy: copy.wait())
        return carry

    lax.fori_loop(0, steps, finish, 0)
    drain(small_inbox_ref, small_out_ref, steps, 1)

    def finish_ring(chunk, carry):
        ring.finish(chunk)
        return carry

    lax.fori_loop(0, chunks, finish_ring, 0)
    for copy in leaving:
        copy.wait()


def reduce_gradients(
    normed_turned, post_turned, cot_early, gate_grad, scan_grad, packed, hidden, cot, post, scale, matrices
):
    size = lax.axis_size("seq")
    group = lax.axis_size("dp")
    rows = gate_grad.shape[0]
    own_in = normed_turned.shape[0]
    model_width = hidden.shape[1]
    out_steps = 2 * (model_width // WIDE)
    gate_steps = gate_grad.shape[1] // WIDE
    back_items = gate_steps + scan_grad.shape[1] // WIDE
    steps = out_steps + back_items
    chunks = back_items + out_steps // 2 - EARLY
    reach = group // 4
    spacing = min(3, (out_steps - 2) // reach)
    assert out_steps == 2 * EARLY
    sizes = (rows, own_in, out_steps, gate_steps, steps, size // 2, LAG, spacing)
    assert back_items + model_width // WIDE < steps
    shape = jax.ShapeDtypeStruct
    dma = pltpu.SemaphoreType.DMA
    small_shape = packed.shape
    anywhere = pl.BlockSpec(memory_space=pl.ANY)
    return pl.pallas_call(
        functools.partial(tail_kernel, sizes),
        out_shape=(
            shape((own_in, back_items * WIDE), f32),
            shape((2 * own_in, model_width), f32),
            shape(small_shape, f32),
            shape((rows, model_width), f32),
            shape((rows, model_width), f32),
            shape((chunks, 2, group // 2, rows, WIDE), bf16),
        ),
        in_specs=vmem(2) + [anywhere] * 3 + vmem(1) + [anywhere] * 3 + vmem(1) + [anywhere] * 3,
        out_specs=(anywhere, anywhere) + tuple(vmem(1)) + (anywhere,) * 3,
        scratch_shapes=[
            pltpu.VMEM((own_in, WIDE), f32),
            pltpu.VMEM((steps, own_in, WIDE), f32),
            pltpu.VMEM((steps, own_in, WIDE), f32),
            pltpu.VMEM((2, 2, group // 2, rows, WIDE), bf16),
            pltpu.VMEM(small_shape, f32),
            pltpu.VMEM(small_shape, f32),
            pltpu.VMEM((group,) + small_shape, f32),
            pltpu.VMEM((2, matrices[2].shape[0], WIDE), bf16),
            pltpu.VMEM((rows, model_width), f32),
            pltpu.VMEM(small_shape, f32),
            pltpu.VMEM(gate_grad.shape, bf16),
            pltpu.VMEM(scan_grad.shape, bf16),
            pltpu.VMEM(hidden.shape, bf16),
            pltpu.VMEM(cot.shape, bf16),
            pltpu.VMEM(post.shape, bf16),
            pltpu.VMEM((rows, model_width), f32),
            pltpu.VMEM((rows, model_width), f32),
            dma((7,)),
        ]
        + [dma((steps + 1, PARTS))] * 6
        + [
            dma((steps,)),
            *PlaneRing.semaphores(chunks),
            dma((2,)),
            *[dma((group,))] * 2,
            dma((2,)),
        ],
        compiler_params=pltpu.CompilerParams(
            collective_id=3, has_side_effects=True, vmem_limit_bytes=56 * 2**20
        ),
        cost_estimate=pl.CostEstimate(
            flops=2 * 10**10, bytes_accessed=2 * 10**8, transcendentals=0
        ),
    )(
        normed_turned,
        post_turned,
        cot_early,
        gate_grad,
        scan_grad,
        packed,
        hidden,
        cot,
        post,
        scale,
        *matrices,
    )


def adam_kernel(*refs):
    ins, outs = refs[:8], refs[8:]
    for matrix in range(2):
        gradient, weight, moment, square = (ref[...] for ref in ins[4 * matrix : 4 * matrix + 4])
        gradient = gradient[:, : weight.shape[1]]
        updated = adam_update(weight, moment, square, gradient, rate_matrix, weight_decay)
        for ref, value in zip(outs[4 * matrix : 4 * matrix + 4], (gradient,) + updated):
            ref[...] = value


def adam_matrices(matrices):
    blocks = 4
    flat = [array for four in matrices for array in four]
    out = [four[1] for four in matrices for _ in range(4)]

    def spec(array):
        return pl.BlockSpec((array.shape[0] // blocks, array.shape[1]), lambda at: (at, 0))

    results = pl.pallas_call(
        adam_kernel,
        grid=(blocks,),
        out_shape=[jax.ShapeDtypeStruct(array.shape, f32) for array in out],
        in_specs=[spec(array) for array in flat],
        out_specs=[spec(array) for array in out],
        compiler_params=pltpu.CompilerParams(vmem_limit_bytes=58 * 2**20),
    )(*flat)
    return results[:4], results[4:]


def on_device(
    hidden_in,
    out_grad,
    prenorm,
    inproject,
    convtaps,
    headcoefs,
    postnorm,
    outproject,
    prenorm_first,
    inproject_first,
    convtaps_first,
    headcoefs_first,
    postnorm_first,
    outproject_first,
    prenorm_second,
    inproject_second,
    convtaps_second,
    headcoefs_second,
    postnorm_second,
    outproject_second,
):
    group = lax.axis_size("dp")
    me = lax.axis_index("dp")
    seq_here, rows, model_width = hidden_in.shape
    assert seq_here == 1
    heads = headcoefs.shape[1]
    own_in, proj_width = inproject.shape
    own_out = outproject.shape[0]
    inner = own_out * group
    width = inner // heads
    per_tile = LANES // width
    tiles = inner // LANES
    sizes = (rows, inner, tiles, per_tile)
    conv_own = convtaps.shape[1]
    conv_width = conv_own * group

    tap_rows = convtaps.shape[0]
    hidden_low = hidden_in.reshape(rows, model_width)
    cot_low = out_grad.reshape(rows, model_width)
    (
        pre_scale,
        gate_grad,
        post_low,
        normed_turned,
        post_turned,
        scan_grad,
        packed,
        scan_matrix,
        gate_matrix,
        out_matrix,
        cot_early,
    ) = front(
        inproject,
        outproject,
        prenorm.reshape(1, -1),
        convtaps,
        postnorm.reshape(1, -1),
        hidden_low,
        cot_low,
        headcoefs,
        sizes,
    )
    scan_matrix = scan_matrix.reshape(model_width, -1)
    gate_matrix = gate_matrix.reshape(model_width, inner)
    out_matrix = out_matrix.reshape(inner, model_width)
    inproj_padded, outproj_owned, packed, output, input_gradient, _ = reduce_gradients(
        normed_turned,
        post_turned,
        cot_early,
        gate_grad,
        scan_grad,
        packed,
        hidden_low,
        cot_low,
        post_low,
        pre_scale,
        (gate_matrix, scan_matrix, out_matrix),
    )
    prenorm_owned = lax.dynamic_slice_in_dim(packed[7], me * own_in, own_in, 0)
    postnorm_owned = lax.dynamic_slice_in_dim(packed[6], me * own_out, own_out, 0)
    conv_owned = lax.dynamic_slice_in_dim(packed[:tap_rows], me * conv_own, conv_own, 1)
    head_total = jnp.concatenate(
        [
            packed[:2, conv_width : conv_width + heads],
            jnp.sum(packed[5:6, :inner].reshape(1, heads, width), axis=-1),
        ]
    )

    prenorm_new, prenorm_mom, prenorm_sq = adam_update(
        prenorm, prenorm_first, prenorm_second, prenorm_owned, rate_vector, 0.0
    )
    (
        (inproj_owned, inproj_new, inproj_mom, inproj_sq),
        (outproj_owned, outproj_new, outproj_mom, outproj_sq),
    ) = adam_matrices(
        (
            (inproj_padded, inproject, inproject_first, inproject_second),
            (outproj_owned, outproject, outproject_first, outproject_second),
        )
    )
    conv_new, conv_mom, conv_sq = adam_update(
        convtaps, convtaps_first, convtaps_second, conv_owned, rate_vector, 0.0
    )
    head_new, head_mom, head_sq = adam_update(
        headcoefs, headcoefs_first, headcoefs_second, head_total, rate_vector, 0.0
    )
    postnorm_new, postnorm_mom, postnorm_sq = adam_update(
        postnorm, postnorm_first, postnorm_second, postnorm_owned, rate_vector, 0.0
    )
    return (
        output.reshape(seq_here, rows, model_width),
        input_gradient.reshape(seq_here, rows, model_width),
        prenorm_owned,
        inproj_owned,
        conv_owned,
        head_total,
        postnorm_owned,
        outproj_owned,
        prenorm_new,
        inproj_new,
        conv_new,
        head_new,
        postnorm_new,
        outproj_new,
        prenorm_mom,
        inproj_mom,
        conv_mom,
        head_mom,
        postnorm_mom,
        outproj_mom,
        prenorm_sq,
        inproj_sq,
        conv_sq,
        head_sq,
        postnorm_sq,
        outproj_sq,
    )


def solution(mesh):
    weights = (P("dp"), P("dp", None), P(None, "dp"), P(), P("dp"), P("dp", None))
    tokens = (P("dp", "seq", None), P("dp", "seq", None))
    return jax.shard_map(
        on_device,
        mesh=mesh,
        in_specs=tokens + weights * 3,
        out_specs=tokens + weights * 4,
        check_vma=False,
    )
```

```python
import functools

import jax
import jax.numpy as jnp
from jax import lax
from jax.experimental import pallas as pl
from jax.experimental.pallas import tpu as pltpu
from jax.sharding import PartitionSpec as P

N = 128
LANES = 128
HALO = 16
WIDE = 256
HEIGHT = 32
PARTS = 2
LAG = 4
COT_AT = 10
EARLY = 6
COT_SPACING = 5

norm_eps = 1e-05
beta_moment = 0.9
beta_square = 0.95
adam_eps = 1e-08
adam_step = 3.0
rate_matrix = 0.005
rate_vector = 0.05
weight_decay = 0.1

f32 = jnp.float32
bf16 = jnp.bfloat16
MESH = pl.DeviceIdType.MESH


def adam_update(weight, moment, square, gradient, step_rate, decay_rate):
    moment_new = beta_moment * moment + (1.0 - beta_moment) * gradient
    square_new = beta_square * square + (1.0 - beta_square) * gradient * gradient
    moment_hat = moment_new / (1.0 - beta_moment**adam_step)
    square_hat = square_new / (1.0 - beta_square**adam_step)
    updated = weight - step_rate * (
        moment_hat / (jnp.sqrt(square_hat) + adam_eps) + decay_rate * weight
    )
    return (updated, moment_new, square_new)


def mm(a, b, ca, cb):
    return lax.dot_general(a, b, (((ca,), (cb,)), ((), ())), preferred_element_type=f32)


def halves(a):
    hi = a.astype(bf16)
    return hi, (a - hi.astype(f32)).astype(bf16)


def thirds(a):
    hi = a.astype(bf16)
    rest = a - hi.astype(f32)
    mid = rest.astype(bf16)
    return hi, mid, (rest - mid.astype(f32)).astype(bf16)


def mm3(a, b, ca, cb):
    return mm(a[0], b[0], ca, cb) + mm(a[0], b[1], ca, cb) + mm(a[1], b[0], ca, cb)


def iota(shape, dim):
    return lax.broadcasted_iota(jnp.int32, shape, dim)


def head_lanes(tile, heads_a_tile, copies):
    rows = iota((copies * LANES, LANES), 0)
    lane_head = tile * heads_a_tile + iota((copies * LANES, LANES), 1) // (LANES // heads_a_tile)
    return (rows % LANES == lane_head).astype(f32).astype(bf16)


def conv_tile(conv_ref, halo_ref, u_ref, taps_ref, start, rows):
    cols = pl.ds(start, LANES)
    conv_ref[0:HALO, :] = halo_ref[:, cols].astype(f32)
    conv_ref[HALO : HALO + rows, :] = u_ref[:, cols].astype(f32)
    taps = taps_ref[:, cols]
    pre = taps[4:5, :] + taps[0:1, :] * conv_ref[HALO - 3 : HALO - 3 + rows, :]
    for k in range(1, 4):
        pre = pre + taps[k : k + 1, :] * conv_ref[HALO - 3 + k : HALO - 3 + k + rows, :]
    return pre, jax.nn.sigmoid(pre)


def seq_copy(src, dst, send, recv, to):
    return pltpu.make_async_remote_copy(
        src_ref=src,
        dst_ref=dst,
        send_sem=send,
        recv_sem=recv,
        device_id={"seq": to},
        device_id_type=MESH,
    )


def greet_seq(barrier, rank, last):
    @pl.when(rank > 0)
    def _():
        pl.semaphore_signal(barrier, inc=1, device_id={"seq": rank - 1}, device_id_type=MESH)

    @pl.when(rank < last)
    def _():
        pl.semaphore_signal(barrier, inc=1, device_id={"seq": rank + 1}, device_id_type=MESH)


def seq_neighbours(rank, last):
    return jnp.minimum(rank, 1) + jnp.minimum(last - rank, 1)


def greet_plane(barrier, me, group):
    for i in range(1, group):
        pl.semaphore_signal(
            barrier, inc=1, device_id={"dp": lax.rem(me + i, group)}, device_id_type=MESH
        )


def slot_of(device, group):
    return lax.rem(device, 2) * (group // 2) + device // 2


def ring_place(at, chips):
    half = chips // 2
    turned = at // half
    return at * (1 - turned) + turned * (3 * half - 1 - at)


def front_kernel(
    sizes,
    in_shard_ref,
    out_shard_ref,
    prenorm_ref,
    convtaps_ref,
    postnorm_ref,
    hidden_ref,
    cot_ref,
    headcoefs_ref,
    pre_scale_ref,
    gate_grad_out_ref,
    post_out_ref,
    normed_turned_ref,
    post_turned_ref,
    dproj_ref,
    packed_ref,
    scan_all_ref,
    gate_all_ref,
    out_all_ref,
    cot_all_ref,
    u_ref,
    ypre_ref,
    enter_ref,
    halo_ref,
    step_ref,
    cum_ref,
    cumt_ref,
    taps_ref,
    dy_ref,
    post_t_ref,
    in_wide_ref,
    out_wide_ref,
    scan_shard_ref,
    gate_shard_ref,
    out_low_ref,
    small_all_ref,
    post_scale_ref,
    normed_ref,
    weights_ref,
    out_weights_ref,
    conv_ref,
    score_ref,
    leave_ref,
    mixer_ref,
    gate_ref,
    gated_ref,
    dpost_ref,
    normed_t_ref,
    dscore_ref,
    dread_ref,
    dwrite_ref,
    dcum_ref,
    dstep_ref,
    dpre_ref,
    arrive_ref,
    post_grad_ref,
    gate_grad_ref,
    post_ref,
    small_ref,
    heads_ref,
    skip_ref,
    send_sem,
    recv_sem,
    halo_sem,
    back_send,
    back_recv,
    edge_sem,
    leave_sem,
    small_send,
    small_recv,
    turn_send,
    turn_recv,
    own_sem,
    wide_sem,
    weight_sem,
    *ring_sems,
):
    rows, inner, tiles, per_tile = sizes
    conv_width = inner + 2 * N
    own_in = in_shard_ref.shape[0]
    own_out, model_width = out_shard_ref.shape
    scan_width = in_shard_ref.shape[1] - inner
    rank = lax.axis_index("seq")
    last = lax.axis_size("seq") - 1
    me = lax.axis_index("dp")
    group = lax.axis_size("dp")
    in_chunks = own_in // HEIGHT
    out_height = 2 * HEIGHT
    out_chunks = own_out // out_height

    def wide_rows(chunk):
        return pl.ds(pl.multiple_of(chunk * HEIGHT, HEIGHT), HEIGHT)

    def in_wide(chunk):
        some = wide_rows(chunk)
        return pltpu.make_async_copy(
            in_shard_ref.at[some, :], in_wide_ref.at[some, :], wide_sem.at[chunk]
        )

    out_wide = pltpu.make_async_copy(out_shard_ref, out_wide_ref, wide_sem.at[in_chunks])
    for chunk in range(in_chunks):
        in_wide(chunk).start()
    out_wide.start()
    conv_own = convtaps_ref.shape[1]
    small_rows = [
        jnp.concatenate([part, jnp.zeros((part.shape[0], width), f32)], axis=1)
        if width
        else part
        for part, width in (
            (ref[...], small_ref.shape[1] - ref.shape[1])
            for ref in (prenorm_ref, convtaps_ref, postnorm_ref)
        )
    ]
    small_rows.append(jnp.zeros((9, small_ref.shape[1]), f32))
    small_ref[...] = jnp.concatenate(small_rows, axis=0).astype(bf16)
    heads_ref[...] = jnp.zeros_like(heads_ref)
    heads_ref[0:3, 0 : headcoefs_ref.shape[1]] = headcoefs_ref[...]
    barrier = pltpu.get_barrier_semaphore()
    greet_seq(barrier, rank, last)
    greet_plane(barrier, me, group)
    pl.semaphore_wait(barrier, seq_neighbours(rank, last) + group - 1)
    right = jnp.minimum(rank + 1, last)
    left = jnp.maximum(rank - 1, 0)

    def small_copy(i, peer, slot):
        return plane_copy(
            small_ref, small_all_ref.at[slot], small_send.at[i], small_recv.at[i], peer
        )

    for i in range(1, group):
        small_copy(i, lax.rem(me + i, group), me).start()
    small_all_ref[me] = small_ref[...]
    scan_shard_ref[:, scan_width - scan_width % LANES :] = jnp.zeros(
        (own_in, scan_shard_ref.shape[1] - scan_width + scan_width % LANES), bf16
    )

    def prepare_scan(chunk):
        some = wide_rows(chunk)
        in_wide(chunk).wait()
        scan_shard_ref[some, 0:scan_width] = in_wide_ref[some, inner:].astype(bf16)

    def prepare_gate(chunk):
        some = wide_rows(chunk)
        gate_shard_ref[some, :] = in_wide_ref[some, 0:inner].astype(bf16)

    def prepare_out(chunk):
        @pl.when(chunk == 0)
        def _():
            out_wide.wait()

        some = pl.ds(pl.multiple_of(chunk * out_height, out_height), out_height)
        out_low_ref[some, :] = out_wide_ref[some, :].astype(bf16)

    scan_ring = weight_ring(scan_shard_ref, scan_all_ref, HEIGHT, ring_sems[0:5], prepare_scan)
    gate_ring = weight_ring(gate_shard_ref, gate_all_ref, HEIGHT, ring_sems[5:10], prepare_gate)
    out_ring = weight_ring(out_low_ref, out_all_ref, out_height, ring_sems[10:15], prepare_out)
    spacing = 3
    rings = (
        (scan_ring, 0, in_chunks),
        (gate_ring, in_chunks, in_chunks),
        (out_ring, 2 * in_chunks, out_chunks),
    )

    def round_(step):
        for ring, first, chunks in rings:
            ring.round(step - first, chunks, spacing)

    def rounds(first, end):
        def one(step, carry):
            round_(step)
            return carry

        lax.fori_loop(first, end, one, 0)

    def complete(at):
        ring, first, chunks = rings[at]
        return first + chunks + spacing * ring.reach

    def wait_pairs(at):
        ring, _, chunks = rings[at]

        def one(chunk, carry):
            ring.wait_pair(chunk)
            return carry

        lax.fori_loop(0, chunks, one, 0)

    rounds(0, 2)

    for i in range(1, group):
        small_copy(i, lax.rem(me + i, group), me).wait_send()
        small_copy(i, me, lax.rem(me + group - i, group)).wait_recv()
    taps_ref[...] = jnp.zeros_like(taps_ref)
    for device in range(group):
        small = small_all_ref[device].astype(f32)
        pre_scale_ref[0:1, device * own_in : (device + 1) * own_in] = small[0:1, 0:own_in]
        taps_ref[0:5, device * conv_own : (device + 1) * conv_own] = small[1:6, 0:conv_own]
        post_scale_ref[0:1, device * own_out : (device + 1) * own_out] = small[6:7, 0:own_out]
    pre_scale_ref[1:8, :] = jnp.zeros((7, model_width), f32)

    skip_parts = jnp.concatenate(
        thirds(jnp.broadcast_to(heads_ref[2:3, :], (8, LANES))), axis=1
    )

    def spread_skip(tile, carry):
        cols = pl.ds(pl.multiple_of(tile * LANES, LANES), LANES)
        skip_ref[0:1, cols] = mm(skip_parts, head_lanes(tile, per_tile, 3), 1, 0)[0:1, :]
        return carry

    lax.fori_loop(0, tiles, spread_skip, 0)

    def norm(at, carry):
        some = pl.ds(pl.multiple_of(at * HEIGHT, HEIGHT), HEIGHT)
        hidden = hidden_ref[some, :].astype(f32)
        root = lax.rsqrt(jnp.mean(hidden * hidden, axis=-1, keepdims=True) + norm_eps)
        normed_ref[some, :] = (hidden * root * pre_scale_ref[0:1, :]).astype(bf16)
        return carry

    lax.fori_loop(0, rows // HEIGHT, norm, 0)

    def turn(source_ref, target_ref):
        def one(at, carry):
            cols = pl.ds(pl.multiple_of(at * LANES, LANES), LANES)
            target_ref[cols, :] = source_ref[:, cols].astype(f32).T.astype(bf16)
            return carry

        lax.fori_loop(0, source_ref.shape[1] // LANES, one, 0)

    turn(normed_ref, normed_t_ref)
    rounds(2, complete(0))
    wait_pairs(0)

    def weight_copy(all_ref, at, width):
        slot = lax.rem(at, 2)
        cols = pl.ds(pl.multiple_of(at * WIDE, WIDE), width)
        return pltpu.make_async_copy(
            all_ref.at[:, :, :, cols],
            weights_ref.at[slot, :, :, :, pl.ds(0, width)],
            weight_sem.at[slot],
        )

    def columns(all_ref, action):
        total = all_ref.shape[3]
        full = total // WIDE
        rest = total % WIDE

        def fetch(at, act):
            @pl.when(at < full)
            def _():
                act(weight_copy(all_ref, at, WIDE))

            if rest:

                @pl.when(at == full)
                def _():
                    act(weight_copy(all_ref, at, rest))

        fetch(0, lambda copy: copy.start())

        def one(at, carry):
            fetch(at + 1, lambda copy: copy.start())
            fetch(at, lambda copy: copy.wait())
            weights = weights_ref[lax.rem(at, 2)].reshape(model_width, WIDE)
            action(at, WIDE, mm(normed_ref[...], weights, 1, 0))
            return carry

        lax.fori_loop(0, full, one, 0)
        if rest:
            fetch(full, lambda copy: copy.wait())
            weights = weights_ref[full % 2, :, :, :, 0:rest].reshape(model_width, rest)
            action(full, rest, mm(normed_ref[...], weights, 1, 0))

    def keep_scan(at, width, product):
        cols = pl.ds(at * WIDE if isinstance(at, int) else pl.multiple_of(at * WIDE, WIDE), width)
        u_ref[:, cols] = product.astype(bf16)

    columns(scan_all_ref, keep_scan)
    halo_copy = seq_copy(
        u_ref.at[pl.ds(rows - HALO, HALO), pl.ds(0, conv_width)],
        halo_ref,
        halo_sem.at[0],
        halo_sem.at[1],
        right,
    )

    @pl.when(rank < last)
    def _():
        halo_copy.start()

    round_(complete(0))
    step = jax.nn.softplus(u_ref[:, conv_width:].astype(f32) + heads_ref[0:1, :])
    decay = -step * jnp.exp(heads_ref[1:2, :])
    lower = (iota((rows, rows), 0) >= iota((rows, rows), 1)).astype(f32).astype(bf16)
    cum = sum(mm(lower, part, 1, 0) for part in thirds(decay))
    step_ref[...] = step
    cum_ref[...] = cum
    cumt_ref[...] = cum.T

    @pl.when(rank > 0)
    def _():
        halo_copy.wait_recv()

    @pl.when(rank == 0)
    def _():
        halo_ref[...] = jnp.zeros_like(halo_ref)

    pre_b, sig_b = conv_tile(conv_ref, halo_ref, u_ref, taps_ref, inner, rows)
    b_parts = halves(pre_b * sig_b)
    pre_c, sig_c = conv_tile(conv_ref, halo_ref, u_ref, taps_ref, inner + N, rows)
    c_parts = halves(pre_c * sig_c)
    scores = mm3(c_parts, b_parts, 1, 1)
    causal = iota((rows, rows), 0) >= iota((rows, rows), 1)
    score_ref[...] = jnp.where(causal, scores, 0.0)
    cum_parts = jnp.concatenate(thirds(cum), axis=1)
    step_parts = jnp.concatenate(thirds(step), axis=1)
    lane = iota((rows, LANES), 1)
    width = LANES // per_tile

    def chain(tile):
        return seq_copy(
            leave_ref.at[tile], enter_ref.at[tile], send_sem.at[tile], recv_sem.at[tile], right
        )

    def one(tile, carry):
        start = pl.multiple_of(tile * LANES, LANES)
        cols = pl.ds(start, LANES)
        pick = head_lanes(tile, per_tile, 3)
        cum_l = mm(cum_parts, pick, 1, 0)
        step_l = mm(step_parts, pick, 1, 0)
        pre, sig = conv_tile(conv_ref, halo_ref, u_ref, taps_ref, start, rows)
        values = pre * sig
        x = values * step_l
        total = cum_l[rows - 1 : rows, :]
        fresh = mm3(b_parts, halves(x * jnp.exp(total - cum_l)), 0, 0)

        @pl.when(rank > 0)
        def _():
            chain(tile).wait_recv()

        @pl.when(rank == 0)
        def _():
            enter_ref[tile] = jnp.zeros((N, LANES), f32)

        enter = enter_ref[tile]
        leave_ref[tile] = jnp.exp(total) * enter + fresh

        @pl.when(rank < last)
        def _():
            chain(tile).start()

        result = mm3(c_parts, halves(enter), 1, 0) * jnp.exp(cum_l)
        for h in range(per_tile):
            row = cumt_ref[pl.ds(tile * per_tile + h, 1), :]
            col = cum_l[:, h * width : h * width + 1]
            kernel = jnp.exp(jnp.minimum(col - row, 0.0)) * score_ref[...]
            own = (lane // width) == h
            result = result + mm3(halves(kernel), halves(jnp.where(own, x, 0.0)), 1, 0)
        ypre_ref[:, cols] = result
        mixer_ref[:, cols] = (result + skip_ref[0:1, cols] * values).astype(bf16)

        @pl.when(lax.rem(tile, pace) == pace - 1)
        def _():
            round_(in_loop + tile // pace)

        return carry

    in_loop = complete(0) + 1
    pace = 4
    lax.fori_loop(0, tiles, one, 0)
    at_round = in_loop + tiles // pace
    rounds(at_round, max(at_round, complete(1)))
    at_round = max(at_round, complete(1))
    wait_pairs(1)

    gated_ref_sum = score_ref

    def keep_gate(at, width, product):
        cols = pl.ds(at * WIDE if isinstance(at, int) else pl.multiple_of(at * WIDE, WIDE), width)
        gated = mixer_ref[:, cols].astype(f32) * (product * jax.nn.sigmoid(product))
        gate_ref[:, cols] = product
        gated_ref[:, cols] = gated
        square = gated * gated
        total = square[:, 0:LANES]
        for part in range(1, width // LANES):
            total = total + square[:, part * LANES : (part + 1) * LANES]
        gated_ref_sum[:, 0:LANES] += total

    gated_ref_sum[:, 0:LANES] = jnp.zeros((rows, LANES), f32)
    columns(gate_all_ref, keep_gate)
    end_round = complete(2)
    rounds(at_round, min(at_round + 1, end_round))
    at_round = min(at_round + 1, end_round)
    root = lax.rsqrt(
        jnp.sum(gated_ref_sum[:, 0:LANES], axis=-1, keepdims=True) / inner + norm_eps
    )

    def keep_post(at, carry):
        cols = pl.ds(pl.multiple_of(at * WIDE, WIDE), WIDE)
        whitened = gated_ref[:, cols] * root
        gated_ref[:, cols] = whitened
        post_ref[:, cols] = (whitened * post_scale_ref[0:1, cols]).astype(bf16)
        return carry

    lax.fori_loop(0, inner // WIDE, keep_post, 0)
    turn(post_ref, post_t_ref)
    rounds(at_round, end_round)
    wait_pairs(2)
    normed_turn = PlaneTurn(
        normed_t_ref,
        normed_turned_ref,
        own_in,
        rows,
        (turn_send.at[0], turn_recv.at[0], own_sem.at[0]),
    )
    post_turn = PlaneTurn(
        post_t_ref,
        post_turned_ref,
        own_out,
        rows,
        (turn_send.at[1], turn_recv.at[1], own_sem.at[1]),
    )
    post_turn.start()
    normed_turn.start()

    span = 2 * own_out

    def out_copy(chip):
        slot = chip % 2
        return pltpu.make_async_copy(
            out_all_ref.at[chip], out_weights_ref.at[slot], weight_sem.at[slot]
        )

    out_copy(0).start()
    overlap = jnp.zeros((rows, LANES), f32)
    for chip in range(group // 2):
        if chip + 1 < group // 2:
            out_copy(chip + 1).start()
        out_copy(chip).wait()
        cols = slice(chip * span, (chip + 1) * span)
        weights = out_weights_ref[chip % 2].reshape(span, model_width)
        dpost = mm(cot_ref[...], weights, 1, 1)
        dpost_ref[:, cols] = dpost
        pulled = dpost * gated_ref[:, cols]
        post_grad_ref[0:1, cols] = jnp.sum(pulled, axis=0, keepdims=True)
        pulled = pulled * post_scale_ref[0:1, cols]
        for part in range(span // LANES):
            overlap = overlap + pulled[:, part * LANES : (part + 1) * LANES]
    mean = jnp.sum(overlap, axis=-1, keepdims=True) / inner

    def keep_back(at, carry):
        cols = pl.ds(pl.multiple_of(at * WIDE, WIDE), WIDE)
        gate = gate_ref[:, cols]
        sig = jax.nn.sigmoid(gate)
        dgated = root * (dpost_ref[:, cols] * post_scale_ref[0:1, cols] - gated_ref[:, cols] * mean)
        dy_ref[:, cols] = (dgated * (gate * sig)).astype(bf16)
        gate_grad_ref[:, cols] = (
            dgated * mixer_ref[:, cols].astype(f32) * sig * (1.0 + gate * (1.0 - sig))
        ).astype(bf16)
        return carry

    lax.fori_loop(0, inner // WIDE, keep_back, 0)

    @pl.when(rank < last)
    def _():
        halo_copy.wait_send()

        def drain(tile, carry):
            chain(tile).wait_send()
            return carry

        lax.fori_loop(0, tiles, drain, 0)

    for ring, _, chunks in rings:

        def finish(chunk, carry, ring=ring):
            ring.finish(chunk)
            return carry

        lax.fori_loop(0, chunks, finish, 0)

    def backward():
        core = lax.rem(me, 2)
        cot_chunks = EARLY

        def cot_block(chunk, origin, part):
            ref = cot_all_ref.at[chunk, core, origin]
            return ref if part is None else ref.at[pl.ds(part * (rows // 2), rows // 2), :]

        def cot_source(chunk, part, action):
            part_rows = pl.ds(0, rows) if part is None else pl.ds(part * (rows // 2), rows // 2)
            cols = pl.ds(pl.multiple_of(chunk * WIDE, WIDE), WIDE)
            action(cot_ref.at[part_rows, cols])

        ring = PlaneRing(
            cot_block, cot_source, lambda chunk, half: cot_all_ref.at[chunk, half], cot_ring_sems
        )

        left = jnp.maximum(rank - 1, 0)
        cum = cum_ref[...]
        step = step_ref[...]
        pre_b, sig_b = conv_tile(conv_ref, halo_ref, u_ref, taps_ref, inner, rows)
        b_parts = halves(pre_b * sig_b)
        pre_c, sig_c = conv_tile(conv_ref, halo_ref, u_ref, taps_ref, inner + N, rows)
        c_parts = halves(pre_c * sig_c)
        later = iota((rows, rows), 1) >= iota((rows, rows), 0)
        score_ref[...] = jnp.where(later, mm3(b_parts, c_parts, 1, 1), 0.0)
        dscore_ref[...] = jnp.zeros_like(dscore_ref)
        dread_ref[...] = jnp.zeros_like(dread_ref)
        dwrite_ref[...] = jnp.zeros_like(dwrite_ref)
        dcum_ref[...] = jnp.zeros_like(dcum_ref)
        dstep_ref[...] = jnp.zeros_like(dstep_ref)
        cum_parts = jnp.concatenate(thirds(cum), axis=1)
        step_parts = jnp.concatenate(thirds(step), axis=1)
        lane = iota((rows, LANES), 1)
        final_row = iota((rows, LANES), 0) == rows - 1
        width = LANES // per_tile

        def chain(tile):
            return seq_copy(
                leave_ref.at[tile], arrive_ref.at[tile], back_send.at[tile], back_recv.at[tile], left
            )

        def tap_grads(dpre, extra):
            sums = [
                jnp.sum(
                    dpre * conv_ref[HALO - 3 + k : HALO - 3 + k + rows, :], axis=0, keepdims=True
                )
                for k in range(4)
            ]
            sums.append(jnp.sum(dpre, axis=0, keepdims=True))
            sums.append(extra)
            sums.append(jnp.zeros((2, LANES), f32))
            return jnp.concatenate(sums, axis=0)

        def one(tile, carry):
            start = pl.multiple_of(tile * LANES, LANES)
            cols = pl.ds(start, LANES)
            pick = head_lanes(tile, per_tile, 3)
            cum_l = mm(cum_parts, pick, 1, 0)
            step_l = mm(step_parts, pick, 1, 0)
            total = cum_l[rows - 1 : rows, :]
            dy = dy_ref[:, cols].astype(f32)
            reads = halves(dy * jnp.exp(cum_l))
            denter = mm3(c_parts, reads, 0, 0)

            @pl.when(rank < last)
            def _():
                chain(tile).wait_recv()

            @pl.when(rank == last)
            def _():
                arrive_ref[tile] = jnp.zeros((N, LANES), f32)

            arrive = arrive_ref[tile]
            leave_ref[tile] = jnp.exp(total) * arrive + denter

            @pl.when(rank > 0)
            def _():
                chain(tile).start()

            pre, sig = conv_tile(conv_ref, halo_ref, u_ref, taps_ref, start, rows)
            values = pre * sig
            x = values * step_l
            x_parts = halves(x)
            tail = jnp.exp(total - cum_l)
            enter = enter_ref[tile]
            arrive_parts = halves(arrive)
            dx_state = mm3(b_parts, arrive_parts, 1, 0) * tail
            dx = dx_state
            for h in range(per_tile):
                row = cumt_ref[pl.ds(tile * per_tile + h, 1), :]
                col = cum_l[:, h * width : h * width + 1]
                spread = jnp.exp(jnp.minimum(row - col, 0.0))
                kernel = halves(spread * score_ref[...])
                own = jnp.where((lane // width) == h, dy, 0.0).astype(bf16)
                dx = dx + (mm(kernel[0], own, 1, 0) + mm(kernel[1], own, 1, 0))
                pairs = mm(x_parts[0], own, 1, 1) + mm(x_parts[1], own, 1, 1)
                dscore_ref[...] += spread * pairs
            dread_ref[...] += mm3(reads, halves(enter), 1, 1)
            dwrite_ref[...] += mm3(halves(x * tail), arrive_parts, 1, 1)
            ends = jnp.sum(x * dx_state, axis=0, keepdims=True) + jnp.exp(total) * jnp.sum(
                enter * arrive, axis=0, keepdims=True
            )
            dcum = dy * ypre_ref[:, cols] - x * dx + jnp.where(final_row, ends, 0.0)
            own_head = pick[0:LANES, :]
            for part in halves(dcum):
                dcum_ref[...] += mm(part, own_head, 1, 1)
            for part in halves(dx * values):
                dstep_ref[...] += mm(part, own_head, 1, 1)
            dvalues = step_l * dx + skip_ref[0:1, cols] * dy
            dpre = dvalues * sig * (1.0 + pre * (1.0 - sig))
            dpre_ref[0:rows, cols] = dpre
            packed_ref[:, cols] = tap_grads(dpre, jnp.sum(dy * values, axis=0, keepdims=True))

            ring.round(tile - COT_AT, cot_chunks, COT_SPACING)

            return carry

        lax.fori_loop(0, tiles, one, 0)
        for at in range(tiles - COT_AT, cot_chunks + COT_SPACING * ring.reach):
            ring.round(at, cot_chunks, COT_SPACING)

        dscore = halves(jnp.where(later, dscore_ref[...], 0.0))
        dshared = (
            dwrite_ref[...] + mm3(dscore, c_parts, 1, 0),
            dread_ref[...] + mm3(dscore, b_parts, 0, 0),
        )
        for i in range(2):
            start = inner + i * N
            pre, sig = conv_tile(conv_ref, halo_ref, u_ref, taps_ref, start, rows)
            dpre = dshared[i] * sig * (1.0 + pre * (1.0 - sig))
            dpre_ref[0:rows, start : start + N] = dpre
            packed_ref[:, start : start + N] = tap_grads(dpre, jnp.zeros((1, LANES), f32))

        edge = seq_copy(
            dpre_ref.at[pl.ds(0, 8), :],
            dpre_ref.at[pl.ds(rows, 8), :],
            edge_sem.at[0],
            edge_sem.at[1],
            left,
        )

        @pl.when(rank > 0)
        def _():
            edge.start()

        upper = (iota((rows, rows), 1) >= iota((rows, rows), 0)).astype(f32).astype(bf16)
        ddecay = sum(mm(upper, part, 1, 0) for part in thirds(dcum_ref[...]))
        exp_rate = jnp.exp(heads_ref[1:2, :])
        drate = (dstep_ref[...] - ddecay * exp_rate) * jax.nn.sigmoid(
            u_ref[:, conv_width:].astype(f32) + heads_ref[0:1, :]
        )
        packed_ref[:, conv_width:] = jnp.concatenate(
            [
                jnp.sum(drate, axis=0, keepdims=True),
                jnp.sum(ddecay * (-step * exp_rate), axis=0, keepdims=True),
                jnp.zeros((6, LANES), f32),
            ],
            axis=0,
        )
        packed_ref[6:7, 0:inner] = post_grad_ref[...]
        dproj_ref[:, conv_width : conv_width + LANES] = drate.astype(bf16)
        dproj_ref[:, conv_width + LANES :] = jnp.zeros(
            (rows, dproj_ref.shape[1] - conv_width - LANES), bf16
        )

        @pl.when(rank == last)
        def _():
            dpre_ref[rows : rows + 8, :] = jnp.zeros((8, conv_width), f32)

        @pl.when(rank < last)
        def _():
            edge.wait_recv()

        def unconv(tile, carry):
            cols = pl.ds(pl.multiple_of(tile * LANES, LANES), LANES)
            taps = taps_ref[:, cols]
            du = taps[3:4, :] * dpre_ref[0:rows, cols]
            for k in range(3):
                du = du + taps[k : k + 1, :] * dpre_ref[3 - k : 3 - k + rows, cols]
            dproj_ref[:, cols] = du.astype(bf16)
            return carry

        lax.fori_loop(0, conv_width // LANES, unconv, 0)

        @pl.when(rank > 0)
        def _():
            edge.wait_send()

            def drain(tile, carry):
                chain(tile).wait_send()
                return carry

            lax.fori_loop(0, tiles, drain, 0)


        def finish_ring(chunk, carry):
            ring.wait_pair(chunk)
            ring.finish(chunk)
            return carry

        lax.fori_loop(0, cot_chunks, finish_ring, 0)

    cot_ring_sems = ring_sems[15:]
    leaving = [
        pltpu.make_async_copy(post_ref, post_out_ref, leave_sem.at[0]),
        pltpu.make_async_copy(gate_grad_ref, gate_grad_out_ref, leave_sem.at[1]),
    ]
    for copy in leaving:
        copy.start()
    backward()
    for copy in leaving:
        copy.wait()
    post_turn.finish()
    normed_turn.finish()


def vmem(count):
    return [pl.BlockSpec(memory_space=pltpu.VMEM)] * count


def front(in_shard, out_shard, prenorm, convtaps, postnorm, hidden, cot, headcoefs, sizes):
    rows, inner, tiles, _ = sizes
    conv_width = inner + 2 * N
    shape = jax.ShapeDtypeStruct
    group = lax.axis_size("dp")
    own_in, proj_width = in_shard.shape
    own_out, model_width = out_shard.shape
    scan_width = -(-(proj_width - inner) // LANES) * LANES
    in_chunks = own_in // HEIGHT
    out_chunks = own_out // (2 * HEIGHT)
    small_lanes = -(-max(own_in, own_out, convtaps.shape[1]) // LANES) * LANES
    anywhere = pl.BlockSpec(memory_space=pl.ANY)
    dma = pltpu.SemaphoreType.DMA
    return pl.pallas_call(
        functools.partial(front_kernel, sizes),
        out_shape=(
            shape((8, model_width), f32),
            shape((rows, inner), bf16),
            shape((rows, inner), bf16),
            shape((own_in, group * rows), bf16),
            shape((own_out, group * rows), bf16),
            shape((rows, -(-scan_width // WIDE) * WIDE), bf16),
            shape((8, conv_width + LANES), f32),
            shape((group // 2, 2, own_in, scan_width), bf16),
            shape((group // 2, 2, own_in, inner), bf16),
            shape((group // 2, 2, own_out, model_width), bf16),
            shape((EARLY, 2, group // 2, rows, WIDE), bf16),
        ),
        in_specs=[anywhere] * 2 + vmem(6),
        out_specs=tuple(vmem(1) + [anywhere] * 4 + vmem(2) + [anywhere] * 4),
        scratch_shapes=[
            pltpu.VMEM((rows, scan_width), bf16),
            pltpu.VMEM((rows, inner), f32),
            pltpu.VMEM((tiles, N, LANES), f32),
            pltpu.VMEM((HALO, conv_width), bf16),
            pltpu.VMEM((rows, LANES), f32),
            pltpu.VMEM((rows, LANES), f32),
            pltpu.VMEM((LANES, rows), f32),
            pltpu.VMEM((8, conv_width), f32),
            pltpu.VMEM((rows, inner), bf16),
            pltpu.VMEM((inner, rows), bf16),
            pltpu.VMEM(in_shard.shape, f32),
            pltpu.VMEM(out_shard.shape, f32),
            pltpu.VMEM((own_in, scan_width), bf16),
            pltpu.VMEM((own_in, inner), bf16),
            pltpu.VMEM((own_out, model_width), bf16),
            pltpu.VMEM((group, 16, small_lanes), bf16),
            pltpu.VMEM((1, inner), f32),
            pltpu.VMEM((rows, model_width), bf16),
            pltpu.VMEM((2, group // 2, 2, own_in, WIDE), bf16),
            pltpu.VMEM((2, 2, own_out, model_width), bf16),
            pltpu.VMEM((HALO + rows, LANES), f32),
            pltpu.VMEM((rows, rows), f32),
            pltpu.VMEM((tiles, N, LANES), f32),
            pltpu.VMEM((rows, inner), bf16),
            pltpu.VMEM((rows, inner), f32),
            pltpu.VMEM((rows, inner), f32),
            pltpu.VMEM((rows, inner), f32),
            pltpu.VMEM((model_width, rows), bf16),
            pltpu.VMEM((rows, rows), f32),
            pltpu.VMEM((rows, N), f32),
            pltpu.VMEM((rows, N), f32),
            pltpu.VMEM((rows, LANES), f32),
            pltpu.VMEM((rows, LANES), f32),
            pltpu.VMEM((rows + 8, conv_width), f32),
            pltpu.VMEM((tiles, N, LANES), f32),
            pltpu.VMEM((1, inner), f32),
            pltpu.VMEM((rows, inner), bf16),
            pltpu.VMEM((rows, inner), bf16),
            pltpu.VMEM((16, small_lanes), bf16),
            pltpu.VMEM((8, LANES), f32),
            pltpu.VMEM((1, inner), f32),
            dma((tiles,)),
            dma((tiles,)),
            dma((2,)),
            dma((tiles,)),
            dma((tiles,)),
            dma((2,)),
            dma((2,)),
            dma((group,)),
            dma((group,)),
            dma((2, group)),
            dma((2, group)),
            dma((2,)),
            dma((in_chunks + 1,)),
            dma((2,)),
        ]
        + PlaneRing.semaphores(in_chunks)
        + PlaneRing.semaphores(in_chunks)
        + PlaneRing.semaphores(out_chunks)
        + PlaneRing.semaphores(EARLY),
        compiler_params=pltpu.CompilerParams(
            collective_id=1, has_side_effects=True, vmem_limit_bytes=60 * 2**20
        ),
        cost_estimate=pl.CostEstimate(
            flops=10**10, bytes_accessed=10**8, transcendentals=4 * 10**6
        ),
    )(in_shard, out_shard, prenorm, convtaps, postnorm, hidden, cot, headcoefs)


def plane_copy(src, dst, send, recv, to):
    return pltpu.make_async_remote_copy(
        src_ref=src,
        dst_ref=dst,
        send_sem=send,
        recv_sem=recv,
        device_id={"dp": to},
        device_id_type=MESH,
    )


class PlaneTurn:
    def __init__(self, source, target, height, width, sems):
        self.source, self.target, self.height, self.width = source, target, height, width
        self.send, self.recv, self.own_sem = sems
        self.me = lax.axis_index("dp")
        self.group = lax.axis_size("dp")

    def rows_for(self, device):
        return self.source.at[
            pl.ds(pl.multiple_of(device * self.height, self.height), self.height), :
        ]

    def columns_of(self, device):
        start = pl.multiple_of(slot_of(device, self.group) * self.width, self.width)
        return self.target.at[:, pl.ds(start, self.width)]

    def copy(self, i, peer, origin):
        return plane_copy(
            self.rows_for(peer), self.columns_of(origin), self.send.at[i], self.recv.at[i], peer
        )

    def own(self):
        return pltpu.make_async_copy(
            self.rows_for(self.me), self.columns_of(self.me), self.own_sem
        )

    def start(self):
        for i in range(1, self.group):
            self.copy(i, lax.rem(self.me + i, self.group), self.me).start()
        self.own().start()

    def arrive(self):
        for i in range(1, self.group):
            origin = lax.rem(self.me + self.group - i, self.group)
            self.copy(i, origin, origin).wait_recv()
        self.own().wait()

    def sent(self):
        for i in range(1, self.group):
            self.copy(i, lax.rem(self.me + i, self.group), self.me).wait_send()

    def finish(self):
        self.arrive()
        self.sent()


class PlaneRing:
    def __init__(self, block, source, pair_block, sems, prepare=None):
        group = lax.axis_size("dp")
        me = lax.axis_index("dp")
        self.block, self.source, self.pair_block = block, source, pair_block
        self.prepare = prepare
        self.ring_send, self.ring_recv, self.pair_send, self.pair_recv, self.own_sem = sems
        self.chips = group // 2
        self.reach = self.chips // 2
        self.me = me
        self.core = lax.rem(me, 2)
        self.chip = me // 2
        self.place = ring_place(self.chip, self.chips)

    @staticmethod
    def semaphores(chunks):
        group = lax.axis_size("dp")
        dma = pltpu.SemaphoreType.DMA
        return [dma((chunks, group // 2)), dma((chunks, group // 2))] + [dma((chunks,))] * 3

    def ring_chip(self, ahead):
        return ring_place(lax.rem(self.place + ahead + self.chips, self.chips), self.chips)

    def part(self, number, way):
        return None if number < self.reach else (0 if way == 1 else 1)

    def copy(self, chunk, number, way, origin, source=None):
        block = self.block(chunk, origin, self.part(number, way))
        at = 2 * (number - 1) + (0 if way == 1 else 1)
        return plane_copy(
            block if source is None else source,
            block,
            self.ring_send.at[chunk, at],
            self.ring_recv.at[chunk, at],
            2 * self.ring_chip(way) + self.core,
        )

    def hop(self, chunk, number, way, source=None):
        return self.copy(chunk, number, way, self.ring_chip(-way * (number - 1)), source)

    def hop_in(self, chunk, number, way):
        return self.copy(chunk, number, way, self.ring_chip(-way * number))

    def own_copy(self, chunk, source):
        return pltpu.make_async_copy(
            source, self.block(chunk, self.chip, None), self.own_sem.at[chunk]
        )

    def pair_copy(self, chunk, core):
        block = self.pair_block(chunk, core)
        return plane_copy(
            block,
            block,
            self.pair_send.at[chunk],
            self.pair_recv.at[chunk],
            self.me + 1 - 2 * self.core,
        )

    def stage(self, chunk, number):
        if number == 0:
            if self.prepare is not None:
                self.prepare(chunk)
            self.source(chunk, None, lambda ref: self.own_copy(chunk, ref).start())
            for way in (1, -1):
                self.source(
                    chunk,
                    self.part(1, way),
                    lambda ref, way=way: self.hop(chunk, 1, way, ref).start(),
                )
            return
        for way in (1, -1):
            self.hop_in(chunk, number, way).wait_recv()
            if number < self.reach:
                self.hop(chunk, number + 1, way).start()
        if number == self.reach:
            self.own_copy(chunk, self.block(chunk, self.chip, None)).wait()
            self.pair_copy(chunk, self.core).start()

    def wait_pair(self, chunk):
        self.pair_copy(chunk, 1 - self.core).wait_recv()

    def finish(self, chunk):
        for number in range(1, self.reach + 1):
            for way in (1, -1):
                self.hop(chunk, number, way).wait_send()
        self.pair_copy(chunk, self.core).wait_send()

    def round(self, step, chunks, spacing):
        for number in range(self.reach, -1, -1):
            chunk = step - number * spacing

            @pl.when((chunk >= 0) & (chunk < chunks))
            def _(chunk=chunk, number=number):
                self.stage(chunk, number)


def weight_ring(shard_ref, all_ref, height, sems, prepare):
    core = lax.rem(lax.axis_index("dp"), 2)

    def rows_of(chunk, part):
        size = height if part is None else height // 2
        start = chunk * height + (0 if part is None else part * size)
        return pl.ds(pl.multiple_of(start, size), size)

    return PlaneRing(
        lambda chunk, origin, part: all_ref.at[origin, core, rows_of(chunk, part), :],
        lambda chunk, part, action: action(shard_ref.at[rows_of(chunk, part), :]),
        lambda chunk, half: all_ref.at[:, half, rows_of(chunk, None), :],
        sems,
        prepare,
    )


HEIGHT = 32


def tail_kernel(
    sizes,
    normed_turned_ref,
    post_turned_ref,
    cot_ref,
    gate_far_ref,
    scan_far_ref,
    packed_in_ref,
    hidden_far_ref,
    own_cot_far_ref,
    post_far_ref,
    scale_ref,
    gate_matrix_ref,
    scan_matrix_ref,
    out_matrix_ref,
    in_ref,
    out_ref,
    small_out_ref,
    output_far_ref,
    input_grad_far_ref,
    gathered_ref,
    value_ref,
    inbox_ref,
    total_ref,
    loaded_ref,
    small_value_ref,
    small_inbox_ref,
    small_all_ref,
    weights_ref,
    normed_grad_ref,
    packed_ref,
    gate_ref,
    scan_ref,
    hidden_ref,
    own_cot_ref,
    post_ref,
    output_ref,
    input_grad_ref,
    far_sem,
    up_send,
    inbox_recv,
    other_recv,
    total_recv,
    left_send,
    right_send,
    store_sem,
    ring_send,
    ring_recv,
    pair_send,
    pair_recv,
    own_sem,
    load_sem,
    small_send,
    small_recv,
    weight_sem,
):
    rows, own_in, out_steps, gate_steps, steps, root, lag, spacing = sizes
    rest = out_steps // 2 - EARLY
    back_items = steps - out_steps
    chunks = back_items + rest
    rank = lax.axis_index("seq")
    last = lax.axis_size("seq") - 1
    me = lax.axis_index("dp")
    group = lax.axis_size("dp")
    chips = group // 2
    reach = chips // 2
    core = lax.rem(me, 2)
    arriving = [
        pltpu.make_async_copy(far, near, far_sem.at[at])
        for at, (far, near) in enumerate(
            (
                (gate_far_ref, gate_ref),
                (scan_far_ref, scan_ref),
                (hidden_far_ref, hidden_ref),
                (own_cot_far_ref, own_cot_ref),
                (post_far_ref, post_ref),
            )
        )
    ]
    leaving = (
        pltpu.make_async_copy(input_grad_ref, input_grad_far_ref, far_sem.at[5]),
        pltpu.make_async_copy(output_ref, output_far_ref, far_sem.at[6]),
    )
    barrier = pltpu.get_barrier_semaphore()
    greet_seq(barrier, rank, last)
    greet_plane(barrier, me, group)
    pl.semaphore_wait(barrier, seq_neighbours(rank, last) + group - 1)
    left = jnp.maximum(rank - 1, 0)
    right = jnp.minimum(rank + 1, last)

    model_width = hidden_ref.shape[1]

    def small_copy(i, peer, slot):
        return plane_copy(
            packed_ref, small_all_ref.at[slot], small_send.at[i], small_recv.at[i], peer
        )

    def block(chunk, origin, part):
        ref = gathered_ref.at[chunk, core, origin]
        return ref if part is None else ref.at[pl.ds(part * (rows // 2), rows // 2), :]

    def source(chunk, part, action):
        part_rows = pl.ds(0, rows) if part is None else pl.ds(part * (rows // 2), rows // 2)

        def one(ref, first):
            start = pl.multiple_of((chunk - first) * WIDE, WIDE)
            action(ref.at[part_rows, pl.ds(start, WIDE)])

        @pl.when(chunk < rest)
        def _():
            one(own_cot_far_ref, -EARLY)

        @pl.when((chunk >= rest) & (chunk < rest + gate_steps))
        def _():
            one(gate_far_ref, rest)

        @pl.when(chunk >= rest + gate_steps)
        def _():
            one(scan_far_ref, rest + gate_steps)

    ring = PlaneRing(
        block,
        source,
        lambda chunk, half: gathered_ref.at[chunk, half],
        (ring_send, ring_recv, pair_send, pair_recv, own_sem),
    )

    def order_of(step):
        return jnp.where(step < out_steps, step // 2, step - out_steps + out_steps // 2)

    def fetch(step, action):
        order = order_of(step)
        slot = lax.rem(order, 2)

        @pl.when((order < EARLY) & (lax.rem(step, 2) == 0))
        def _():
            action(
                pltpu.make_async_copy(cot_ref.at[order], loaded_ref.at[slot], load_sem.at[slot])
            )

        @pl.when((order >= EARLY) & ((step >= out_steps) | (lax.rem(step, 2) == 0)))
        def _():
            action(
                pltpu.make_async_copy(
                    gathered_ref.at[order - EARLY], loaded_ref.at[slot], load_sem.at[slot]
                )
            )

        return slot

    def compute(step):
        arrived = loaded_ref.at[fetch(step, lambda copy: copy.wait())]

        @pl.when(step < out_steps)
        def _():
            some = pl.ds(pl.multiple_of(lax.rem(step, 2) * own_in, own_in), own_in)
            value_ref[...] = mm(
                post_turned_ref[some, :], arrived[...].reshape(group * rows, WIDE), 1, 0
            )

        @pl.when(step >= out_steps)
        def _():
            value_ref[...] = mm(
                normed_turned_ref[...], arrived[...].reshape(group * rows, WIDE), 1, 0
            )

    fetch(0, lambda copy: copy.start())
    for copy in arriving:
        copy.start()

    def weight_copy(item, action):
        slot = lax.rem(item, 2)
        narrow = scan_matrix_ref.shape[1] % WIDE

        def one(matrix_ref, first, width):
            height = matrix_ref.shape[0]
            start = pl.multiple_of((item - first) * WIDE, WIDE)
            action(
                pltpu.make_async_copy(
                    matrix_ref.at[:, pl.ds(start, width)],
                    weights_ref.at[slot, pl.ds(0, height), pl.ds(0, width)],
                    weight_sem.at[slot],
                )
            )

        full = back_items - 1 if narrow else back_items

        @pl.when(item < gate_steps)
        def _():
            one(gate_matrix_ref, 0, WIDE)

        @pl.when((item >= gate_steps) & (item < full))
        def _():
            one(scan_matrix_ref, gate_steps, WIDE)

        if narrow:

            @pl.when(item == full)
            def _():
                one(scan_matrix_ref, gate_steps, narrow)

        @pl.when((item >= back_items) & (item < items))
        def _():
            one(out_matrix_ref, back_items, WIDE)

    items = back_items + model_width // WIDE

    def back_product(grad_ref, item, first, width):
        cols = pl.ds(pl.multiple_of((item - first) * WIDE, WIDE), width)
        weights = weights_ref[lax.rem(item, 2), 0:model_width, 0:width]
        normed_grad_ref[...] += mm(grad_ref[:, cols], weights, 1, 1)

    def norm_backward():
        def block(at, carry):
            some = pl.ds(pl.multiple_of(at * HEIGHT, HEIGHT), HEIGHT)
            hidden = hidden_ref[some, :].astype(f32)
            root_mean = lax.rsqrt(jnp.mean(hidden * hidden, axis=-1, keepdims=True) + norm_eps)
            plain = hidden * root_mean
            grad = normed_grad_ref[some, :]
            scaled = grad * scale_ref[0:1, :]
            input_grad_ref[some, :] = root_mean * (
                scaled - plain * jnp.mean(scaled * plain, axis=-1, keepdims=True)
            ) + own_cot_ref[some, :].astype(f32)
            return carry + jnp.sum(grad * plain, axis=0, keepdims=True)

        total = lax.fori_loop(0, rows // HEIGHT, block, jnp.zeros((1, model_width), f32))
        packed_ref[...] = packed_in_ref[...]
        packed_ref[7:8, 0:model_width] = total
        for i in range(1, group):
            small_copy(i, lax.rem(me + i, group), me).start()
        small_all_ref[me] = packed_ref[...]

    def local_product(item):
        narrow = scan_matrix_ref.shape[1] % WIDE
        full = back_items - 1 if narrow else back_items

        @pl.when(item == 0)
        def _():
            normed_grad_ref[...] = jnp.zeros_like(normed_grad_ref)
            for copy in arriving:
                copy.wait()

        weight_copy(item, lambda copy: copy.wait())
        weight_copy(item + 1, lambda copy: copy.start())

        @pl.when(item < gate_steps)
        def _():
            back_product(gate_ref, item, 0, WIDE)

        @pl.when((item >= gate_steps) & (item < full))
        def _():
            back_product(scan_ref, item, gate_steps, WIDE)

        if narrow:

            @pl.when(item == full)
            def _():
                back_product(scan_ref, item, gate_steps, narrow)

        @pl.when(item == back_items - 1)
        def _():
            norm_backward()
            leaving[0].start()

        @pl.when(item >= back_items)
        def _():
            cols = pl.ds(pl.multiple_of((item - back_items) * WIDE, WIDE), WIDE)
            output_ref[:, cols] = hidden_ref[:, cols].astype(f32) + mm(
                post_ref[...], weights_ref[lax.rem(item, 2)], 1, 0
            )

        @pl.when(item == items - 1)
        def _():
            leaving[1].start()

    weight_copy(0, lambda copy: copy.start())

    def piece(ref, part, parts):
        if parts == 1:
            return ref
        size = own_in // parts
        start = part * size if isinstance(part, int) else pl.multiple_of(part * size, size)
        return ref.at[pl.ds(start, size), :]

    def up_copy(source, target, step, part, parts, recv, to):
        return seq_copy(
            piece(source, part, parts),
            piece(target, part, parts),
            up_send.at[step, part],
            recv.at[step, part],
            to,
        )

    def down_copy(total, step, part, parts, send, to):
        return seq_copy(
            piece(total, part, parts),
            piece(total, part, parts),
            send.at[step, part],
            total_recv.at[step, part],
            to,
        )

    def up(value, inbox, total, step, parts, after):
        edge = ((rank == 0) | (rank == last)) & (rank != root)
        inner_place = (rank != root) & (rank > 0) & (rank < last)
        for part in range(parts):
            here = piece(value, part, parts)
            inbox_here = piece(inbox, part, parts)
            total_here = piece(total, part, parts)

            @pl.when(edge)
            def _(here=here, inbox_here=inbox_here):
                inbox_here[...] = here[...]

            @pl.when(inner_place)
            def _(here=here, inbox_here=inbox_here, part=part):
                up_copy(inbox, inbox, step, part, parts, inbox_recv, left).wait_recv()
                inbox_here[...] += here[...]

            @pl.when(rank < root)
            def _(part=part):
                up_copy(inbox, inbox, step, part, parts, inbox_recv, right).start()

            @pl.when(rank == root + 1)
            def _(part=part):
                up_copy(inbox, total, step, part, parts, other_recv, left).start()

            @pl.when(rank > root + 1)
            def _(part=part):
                up_copy(inbox, inbox, step, part, parts, inbox_recv, left).start()

            @pl.when(rank == root)
            def _(here=here, inbox_here=inbox_here, total_here=total_here, part=part):
                result = here[...]
                if root > 0:
                    up_copy(inbox, inbox, step, part, parts, inbox_recv, left).wait_recv()
                    result = result + inbox_here[...]
                if root < last:
                    up_copy(total, total, step, part, parts, other_recv, right).wait_recv()
                    result = result + total_here[...]
                total_here[...] = result
                if root > 0:
                    down_copy(total, step, part, parts, left_send, left).start()
                if root < last:
                    down_copy(total, step, part, parts, right_send, right).start()

            after(part)

    def down(total, step, part, parts):
        @pl.when(rank < root)
        def _():
            down_copy(total, step, part, parts, left_send, left).wait_recv()

            @pl.when(rank > 0)
            def _():
                down_copy(total, step, part, parts, left_send, left).start()

        @pl.when(rank > root)
        def _():
            down_copy(total, step, part, parts, right_send, right).wait_recv()

            @pl.when(rank < last)
            def _():
                down_copy(total, step, part, parts, right_send, right).start()

    def drain(inbox, total, step, parts):
        for part in range(parts):

            @pl.when(rank < root)
            def _(part=part):
                up_copy(inbox, inbox, step, part, parts, inbox_recv, right).wait_send()

            @pl.when(rank > root)
            def _(part=part):
                up_copy(inbox, inbox, step, part, parts, inbox_recv, left).wait_send()

            @pl.when((rank <= root) & (rank > 0))
            def _(part=part):
                down_copy(total, step, part, parts, left_send, left).wait_send()

            @pl.when((rank >= root) & (rank < last))
            def _(part=part):
                down_copy(total, step, part, parts, right_send, right).wait_send()

    def stored(step, action):
        @pl.when(step < out_steps)
        def _():
            some = pl.ds(pl.multiple_of(lax.rem(step, 2) * own_in, own_in), own_in)
            cols = pl.ds(pl.multiple_of(step // 2 * WIDE, WIDE), WIDE)
            action(
                pltpu.make_async_copy(
                    total_ref.at[step], out_ref.at[some, cols], store_sem.at[step]
                )
            )

        @pl.when(step >= out_steps)
        def _():
            cols = pl.ds(pl.multiple_of((step - out_steps) * WIDE, WIDE), WIDE)
            action(
                pltpu.make_async_copy(total_ref.at[step], in_ref.at[:, cols], store_sem.at[step])
            )

    behind = lag * (jnp.maximum(rank - root, 0) + jnp.maximum(root - rank, 0))

    def round_(step, carry):
        for stage in range(reach, -1, -1):
            chunk = step - stage * spacing

            @pl.when((chunk >= 0) & (chunk < chunks))
            def _(chunk=chunk, stage=stage):
                ring.stage(chunk, stage)

        follow = step + 1
        arrives = (follow >= out_steps) | ((order_of(follow) >= EARLY) & (lax.rem(follow, 2) == 0))

        @pl.when(arrives & (follow < steps))
        def _():
            ring.wait_pair(order_of(follow) - EARLY)

        @pl.when(step + 1 < steps)
        def _():
            fetch(step + 1, lambda copy: copy.start())

        def down_late(part):
            late = PARTS * step + part - behind
            late_step = late // PARTS
            late_part = lax.rem(late, PARTS)

            @pl.when((late >= 0) & (late_step < steps))
            def _():
                down(total_ref.at[late_step], late_step, late_part, PARTS)

                @pl.when(late_part == PARTS - 1)
                def _():
                    stored(late_step, lambda copy: copy.start())

            @pl.when(late == PARTS * steps)
            def _():
                down(small_out_ref, steps, 0, 1)

        @pl.when(step < steps)
        def _():
            compute(step)
            up(value_ref, inbox_ref.at[step], total_ref.at[step], step, PARTS, down_late)

        @pl.when(step == steps)
        def _():
            for i in range(1, group):
                small_copy(i, lax.rem(me + i, group), me).wait_send()
                origin = lax.rem(me + group - i, group)
                small_copy(i, origin, origin).wait_recv()
            small_value_ref[...] = jnp.sum(small_all_ref[...], axis=0)
            up(small_value_ref, small_inbox_ref, small_out_ref, steps, 1, lambda part: None)

        @pl.when(step >= steps)
        def _():
            for part in range(PARTS):
                down_late(part)

        @pl.when((step >= 1) & (step < 1 + items))
        def _():
            local_product(step - 1)

        return carry

    lax.fori_loop(0, steps + 1 + (behind + PARTS - 1) // PARTS, round_, 0)

    def finish(step, carry):
        drain(inbox_ref.at[step], total_ref.at[step], step, PARTS)
        stored(step, lambda copy: copy.wait())
        return carry

    lax.fori_loop(0, steps, finish, 0)
    drain(small_inbox_ref, small_out_ref, steps, 1)

    def finish_ring(chunk, carry):
        ring.finish(chunk)
        return carry

    lax.fori_loop(0, chunks, finish_ring, 0)
    for copy in leaving:
        copy.wait()


def reduce_gradients(
    normed_turned, post_turned, cot_early, gate_grad, scan_grad, packed, hidden, cot, post, scale, matrices
):
    size = lax.axis_size("seq")
    group = lax.axis_size("dp")
    rows = gate_grad.shape[0]
    own_in = normed_turned.shape[0]
    model_width = hidden.shape[1]
    out_steps = 2 * (model_width // WIDE)
    gate_steps = gate_grad.shape[1] // WIDE
    back_items = gate_steps + scan_grad.shape[1] // WIDE
    steps = out_steps + back_items
    chunks = back_items + out_steps // 2 - EARLY
    reach = group // 4
    spacing = min(3, (out_steps - 2) // reach)
    assert out_steps == 2 * EARLY
    sizes = (rows, own_in, out_steps, gate_steps, steps, size // 2 - 1, LAG, spacing)
    assert back_items + model_width // WIDE < steps
    shape = jax.ShapeDtypeStruct
    dma = pltpu.SemaphoreType.DMA
    small_shape = packed.shape
    anywhere = pl.BlockSpec(memory_space=pl.ANY)
    return pl.pallas_call(
        functools.partial(tail_kernel, sizes),
        out_shape=(
            shape((own_in, back_items * WIDE), f32),
            shape((2 * own_in, model_width), f32),
            shape(small_shape, f32),
            shape((rows, model_width), f32),
            shape((rows, model_width), f32),
            shape((chunks, 2, group // 2, rows, WIDE), bf16),
        ),
        in_specs=vmem(2) + [anywhere] * 3 + vmem(1) + [anywhere] * 3 + vmem(1) + [anywhere] * 3,
        out_specs=(anywhere, anywhere) + tuple(vmem(1)) + (anywhere,) * 3,
        scratch_shapes=[
            pltpu.VMEM((own_in, WIDE), f32),
            pltpu.VMEM((steps, own_in, WIDE), f32),
            pltpu.VMEM((steps, own_in, WIDE), f32),
            pltpu.VMEM((2, 2, group // 2, rows, WIDE), bf16),
            pltpu.VMEM(small_shape, f32),
            pltpu.VMEM(small_shape, f32),
            pltpu.VMEM((group,) + small_shape, f32),
            pltpu.VMEM((2, matrices[2].shape[0], WIDE), bf16),
            pltpu.VMEM((rows, model_width), f32),
            pltpu.VMEM(small_shape, f32),
            pltpu.VMEM(gate_grad.shape, bf16),
            pltpu.VMEM(scan_grad.shape, bf16),
            pltpu.VMEM(hidden.shape, bf16),
            pltpu.VMEM(cot.shape, bf16),
            pltpu.VMEM(post.shape, bf16),
            pltpu.VMEM((rows, model_width), f32),
            pltpu.VMEM((rows, model_width), f32),
            dma((7,)),
        ]
        + [dma((steps + 1, PARTS))] * 6
        + [
            dma((steps,)),
            *PlaneRing.semaphores(chunks),
            dma((2,)),
            *[dma((group,))] * 2,
            dma((2,)),
        ],
        compiler_params=pltpu.CompilerParams(
            collective_id=3, has_side_effects=True, vmem_limit_bytes=56 * 2**20
        ),
        cost_estimate=pl.CostEstimate(
            flops=2 * 10**10, bytes_accessed=2 * 10**8, transcendentals=0
        ),
    )(
        normed_turned,
        post_turned,
        cot_early,
        gate_grad,
        scan_grad,
        packed,
        hidden,
        cot,
        post,
        scale,
        *matrices,
    )


def adam_kernel(*refs):
    ins, outs = refs[:8], refs[8:]
    for matrix in range(2):
        gradient, weight, moment, square = (ref[...] for ref in ins[4 * matrix : 4 * matrix + 4])
        gradient = gradient[:, : weight.shape[1]]
        updated = adam_update(weight, moment, square, gradient, rate_matrix, weight_decay)
        for ref, value in zip(outs[4 * matrix : 4 * matrix + 4], (gradient,) + updated):
            ref[...] = value


def adam_matrices(matrices):
    blocks = 4
    flat = [array for four in matrices for array in four]
    out = [four[1] for four in matrices for _ in range(4)]

    def spec(array):
        return pl.BlockSpec((array.shape[0] // blocks, array.shape[1]), lambda at: (at, 0))

    results = pl.pallas_call(
        adam_kernel,
        grid=(blocks,),
        out_shape=[jax.ShapeDtypeStruct(array.shape, f32) for array in out],
        in_specs=[spec(array) for array in flat],
        out_specs=[spec(array) for array in out],
        compiler_params=pltpu.CompilerParams(vmem_limit_bytes=58 * 2**20),
    )(*flat)
    return results[:4], results[4:]


def on_device(
    hidden_in,
    out_grad,
    prenorm,
    inproject,
    convtaps,
    headcoefs,
    postnorm,
    outproject,
    prenorm_first,
    inproject_first,
    convtaps_first,
    headcoefs_first,
    postnorm_first,
    outproject_first,
    prenorm_second,
    inproject_second,
    convtaps_second,
    headcoefs_second,
    postnorm_second,
    outproject_second,
):
    group = lax.axis_size("dp")
    me = lax.axis_index("dp")
    seq_here, rows, model_width = hidden_in.shape
    assert seq_here == 1
    heads = headcoefs.shape[1]
    own_in, proj_width = inproject.shape
    own_out = outproject.shape[0]
    inner = own_out * group
    width = inner // heads
    per_tile = LANES // width
    tiles = inner // LANES
    sizes = (rows, inner, tiles, per_tile)
    conv_own = convtaps.shape[1]
    conv_width = conv_own * group

    tap_rows = convtaps.shape[0]
    hidden_low = hidden_in.reshape(rows, model_width)
    cot_low = out_grad.reshape(rows, model_width)
    (
        pre_scale,
        gate_grad,
        post_low,
        normed_turned,
        post_turned,
        scan_grad,
        packed,
        scan_matrix,
        gate_matrix,
        out_matrix,
        cot_early,
    ) = front(
        inproject,
        outproject,
        prenorm.reshape(1, -1),
        convtaps,
        postnorm.reshape(1, -1),
        hidden_low,
        cot_low,
        headcoefs,
        sizes,
    )
    scan_matrix = scan_matrix.reshape(model_width, -1)
    gate_matrix = gate_matrix.reshape(model_width, inner)
    out_matrix = out_matrix.reshape(inner, model_width)
    inproj_padded, outproj_owned, packed, output, input_gradient, _ = reduce_gradients(
        normed_turned,
        post_turned,
        cot_early,
        gate_grad,
        scan_grad,
        packed,
        hidden_low,
        cot_low,
        post_low,
        pre_scale,
        (gate_matrix, scan_matrix, out_matrix),
    )
    prenorm_owned = lax.dynamic_slice_in_dim(packed[7], me * own_in, own_in, 0)
    postnorm_owned = lax.dynamic_slice_in_dim(packed[6], me * own_out, own_out, 0)
    conv_owned = lax.dynamic_slice_in_dim(packed[:tap_rows], me * conv_own, conv_own, 1)
    head_total = jnp.concatenate(
        [
            packed[:2, conv_width : conv_width + heads],
            jnp.sum(packed[5:6, :inner].reshape(1, heads, width), axis=-1),
        ]
    )

    prenorm_new, prenorm_mom, prenorm_sq = adam_update(
        prenorm, prenorm_first, prenorm_second, prenorm_owned, rate_vector, 0.0
    )
    (
        (inproj_owned, inproj_new, inproj_mom, inproj_sq),
        (outproj_owned, outproj_new, outproj_mom, outproj_sq),
    ) = adam_matrices(
        (
            (inproj_padded, inproject, inproject_first, inproject_second),
            (outproj_owned, outproject, outproject_first, outproject_second),
        )
    )
    conv_new, conv_mom, conv_sq = adam_update(
        convtaps, convtaps_first, convtaps_second, conv_owned, rate_vector, 0.0
    )
    head_new, head_mom, head_sq = adam_update(
        headcoefs, headcoefs_first, headcoefs_second, head_total, rate_vector, 0.0
    )
    postnorm_new, postnorm_mom, postnorm_sq = adam_update(
        postnorm, postnorm_first, postnorm_second, postnorm_owned, rate_vector, 0.0
    )
    return (
        output.reshape(seq_here, rows, model_width),
        input_gradient.reshape(seq_here, rows, model_width),
        prenorm_owned,
        inproj_owned,
        conv_owned,
        head_total,
        postnorm_owned,
        outproj_owned,
        prenorm_new,
        inproj_new,
        conv_new,
        head_new,
        postnorm_new,
        outproj_new,
        prenorm_mom,
        inproj_mom,
        conv_mom,
        head_mom,
        postnorm_mom,
        outproj_mom,
        prenorm_sq,
        inproj_sq,
        conv_sq,
        head_sq,
        postnorm_sq,
        outproj_sq,
    )


def solution(mesh):
    weights = (P("dp"), P("dp", None), P(None, "dp"), P(), P("dp"), P("dp", None))
    tokens = (P("dp", "seq", None), P("dp", "seq", None))
    return jax.shard_map(
        on_device,
        mesh=mesh,
        in_specs=tokens + weights * 3,
        out_specs=tokens + weights * 4,
        check_vma=False,
    )
```
